32 devices in a mesh: section: 2 (over x), seq: 8 (over z, core), tp: 2 (over y).
Axes of the slice: x: 2, y: 2, z: 4, core: 2. Of those that a mesh axis runs over, the one named last changes fastest.
Arguments:
- image: bfloat16 [2, 1024, 3072], P('section', 'seq'), may hold values from -6 to 6
- text_kv: bfloat16 [2, 512, 2, 2048], P('section', 'seq', None, 'tp'), may hold values from -6 to 6
- modulation: float32 [2, 3, 3072], P('section'), may hold values from -3 to 3
- w_qkv: bfloat16 [3072, 3, 2048], P('seq', None, 'tp'), may hold values from -0.109375 to 0.109375
- w_out: bfloat16 [2048, 3072], P('tp'), may hold values from -6 to 6
- q_gain: float32 [128], replicated, may hold values from 0.1 to 1.9
- k_gain: float32 [128], replicated, may hold values from 0.1 to 1.9
- region_mask: int32 [8, 8], P('seq'), may hold values from 0 to 1, as said below
Outputs:
- block_out: bfloat16 [2, 1024, 3072], P('section', 'seq', 'tp')
The draws below stay inside these ranges and needn't reach their ends.
Inputs may be any that keep to these rules, and one draw needn't show every extreme that they name: `region_mask`: each query tile reads its own drawn share of condition tiles, from none or one eighth up to all of them.
All inputs are finite; a program needn't handle non-finite values.
Results may differ from the reference program's by a relative error of at most 0.011.
Values may be sent and summed in bfloat16 or wider, within the bound.
No kernel may reach another device: no remote copies, remote signals or barrier semaphores. Data moves between devices by JAX's collectives and lax.ppermute only.
A program may use at most 128 MiB of HBM per device.

```python
import jax
import jax.numpy as jnp
from jax import lax

D = 3072
HEADS = 16
HEAD_DIM = 128
GRID_W = 64
TILE = 128
TXT = 512
IMG = 1024
QT = 8
N_SECTION = 2


def draw_region_mask(key, part):
    key = jax.random.fold_in(key, 7)
    level_key, tile_key = jax.random.split(key)
    level = jax.random.randint(level_key, (QT, 1), 0, 9)
    raw = jax.random.randint(tile_key, (QT, QT), 0, 8)
    return (raw < level).astype(jnp.int32)


def levels(rng, dims, cuts, least, largest):
    def one(axis_at, shards_of):
        steps = jax.random.uniform(jax.random.fold_in(jax.random.fold_in(rng, 6), axis_at), (shards_of,), jnp.float32, least / len(cuts), largest / len(cuts))
        return jnp.repeat(jnp.exp(steps), dims[axis_at] // shards_of).reshape((-1,) + (1,) * (len(dims) - axis_at - 1))

    level = one(*cuts[0])
    for cut in cuts[1:]:
        level = level * one(*cut)
    return level


def noise(key, dims, spread, limit, pieces=(), held_as=jnp.bfloat16):
    drawn = spread * jax.random.normal(key, dims, jnp.float32)
    if pieces:
        drawn = drawn * levels(key, dims, pieces, -0.22, 0.18)
    return jnp.clip(drawn, -limit, limit).astype(held_as)


def setup_inputs(seed: int = 0) -> dict:
    splits = jax.random.split(jax.random.key(seed), 9)
    return {
        "image": noise(splits[0], (N_SECTION, IMG, D), 1.0, 6.0, ((0, 2), (1, 8))),
        "text_kv": noise(splits[1], (N_SECTION, TXT, 2, HEADS * HEAD_DIM), 1.0, 6.0, ((0, 2), (1, 8), (3, 2))),
        "modulation": noise(splits[2], (N_SECTION, 3, D), 0.5, 3.0, ((0, 2),), jnp.float32),
        "w_qkv": noise(splits[3], (D, 3, HEADS * HEAD_DIM), D ** -0.5, 0.109375, ((0, 8), (2, 2))),
        "w_out": noise(splits[4], (HEADS * HEAD_DIM, D), 1.0, 6.0, ((0, 2),)),
        "q_gain": jnp.clip(1.0 + 0.18 * jax.random.normal(splits[5], (HEAD_DIM,), jnp.float32), 0.1, 1.9),
        "k_gain": jnp.clip(1.0 + 0.18 * jax.random.normal(splits[6], (HEAD_DIM,), jnp.float32), 0.1, 1.9),
        "region_mask": draw_region_mask(jax.random.fold_in(splits[8], 71), 0),
    }


def rms_rows(x, gain):
    return x * lax.rsqrt(lax.optimization_barrier(jnp.mean(x * x, axis=-1, keepdims=True)) + 1e-06) * gain

def axis_freqs(width):
    return 10000.0 ** (-jnp.arange(0, width, 2).astype(jnp.float32) / width)

def rope_tables(rows_index, time_index):
    first = HEAD_DIM // 8
    rest = (HEAD_DIM - first) // 2
    row_pos = (rows_index // GRID_W).astype(jnp.float32)
    col_pos = (rows_index % GRID_W).astype(jnp.float32)
    time_pos = jnp.zeros_like(row_pos) + time_index
    angles = jnp.concatenate([time_pos[:, None] * axis_freqs(first)[None], row_pos[:, None] * axis_freqs(rest)[None], col_pos[:, None] * axis_freqs(rest)[None]], axis=-1)
    return (jnp.cos(angles), jnp.sin(angles))

def apply_rope(x, cosine, sine):
    rows, heads_here = (x.shape[0], x.shape[1])
    pairs = x.reshape(rows, heads_here, HEAD_DIM // 2, 2)
    first = pairs[..., 0]
    second = pairs[..., 1]
    cosine = cosine[:, None, :]
    sine = sine[:, None, :]
    rotated = jnp.stack([first * cosine - second * sine, first * sine + second * cosine], axis=-1)
    return rotated.reshape(rows, heads_here, HEAD_DIM)

def project_group(image, modulation, w_qkv, q_gain, k_gain, time_index):
    tokens = image.astype(jnp.float32)
    mean = lax.optimization_barrier(jnp.mean(tokens, axis=-1, keepdims=True))
    var = lax.optimization_barrier(jnp.mean((tokens - mean) ** 2, axis=-1, keepdims=True))
    normed = ((tokens - mean) * lax.rsqrt(var + 1e-06) * (1.0 + modulation[1]) + modulation[0]).astype(jnp.bfloat16)
    flat = w_qkv.reshape(w_qkv.shape[0], -1)
    qkv = jnp.dot(normed, flat, preferred_element_type=jnp.float32).reshape(image.shape[0], 3, HEADS, HEAD_DIM)
    cosine, sine = rope_tables(jnp.arange(image.shape[0]), time_index)
    query = apply_rope(rms_rows(qkv[:, 0], q_gain), cosine, sine).astype(jnp.bfloat16)
    keys = apply_rope(rms_rows(qkv[:, 1], k_gain), cosine, sine).astype(jnp.bfloat16)
    values = qkv[:, 2].astype(jnp.bfloat16)
    return (query, keys, values)

def attend_head(query, own_k, own_v, cond_k, cond_v, cond_mask):
    scale = 1.0 / HEAD_DIM ** 0.5
    scores = jnp.dot(query, own_k.T, preferred_element_type=jnp.float32) * scale
    weights = jnp.exp(scores)
    den = lax.optimization_barrier(jnp.sum(weights, axis=-1))
    num = jnp.dot(weights.astype(jnp.bfloat16), own_v, preferred_element_type=jnp.float32)
    cscores = jnp.dot(query, cond_k.T, preferred_element_type=jnp.float32) * scale
    cweights = jnp.where(cond_mask, jnp.exp(cscores), 0.0)
    den = den + lax.optimization_barrier(jnp.sum(cweights, axis=-1))
    num = num + jnp.dot(cweights.astype(jnp.bfloat16), cond_v, preferred_element_type=jnp.float32)
    return (num / den[:, None]).astype(jnp.bfloat16)

def reference(image, text_kv, modulation, w_qkv, w_out, q_gain, k_gain, region_mask):
    full_mask = jnp.repeat(jnp.repeat(region_mask, TILE, axis=0), TILE, axis=1) > 0
    projected = [project_group(image[g], modulation[g], w_qkv, q_gain, k_gain, 1.0 - g) for g in range(2)]
    results = []
    for g in range(2):
        query, keys, values = projected[g]
        text_k = text_kv[g, :, 0].reshape(TXT, HEADS, HEAD_DIM)
        text_v = text_kv[g, :, 1].reshape(TXT, HEADS, HEAD_DIM)
        own_k = jnp.concatenate([keys, text_k], axis=0)
        own_v = jnp.concatenate([values, text_v], axis=0)
        cond_k = projected[0][1]
        cond_v = projected[0][2]
        cond_mask = full_mask & (g == 1)

        def one_head(head):
            return attend_head(query[:, head], own_k[:, head], own_v[:, head], cond_k[:, head], cond_v[:, head], cond_mask)
        attn = lax.map(one_head, jnp.arange(HEADS))
        attn = jnp.transpose(attn, (1, 0, 2)).reshape(IMG, HEADS * HEAD_DIM)
        branch = jnp.dot(attn, w_out, preferred_element_type=jnp.float32)
        out = image[g].astype(jnp.float32) + modulation[g, 2] * branch
        results.append(out.astype(jnp.bfloat16))
    return jnp.stack(results, axis=0)
```

```python
import functools

import jax
import jax.numpy as jnp
from jax import lax
from jax.experimental import pallas as pl
from jax.experimental.pallas import tpu as pltpu
from jax.sharding import PartitionSpec as P

HEAD_DIM = 128
GRID_W = 64
TILE = 128
VMEM_LIMIT = 48 * 1024 * 1024


def axis_freqs(width):
    return 10000.0 ** (-jnp.arange(0, width, 2).astype(jnp.float32) / width)


def rope_tables(rows_index, time_index):
    first = HEAD_DIM // 8
    rest = (HEAD_DIM - first) // 2
    row_pos = (rows_index // GRID_W).astype(jnp.float32)
    col_pos = (rows_index % GRID_W).astype(jnp.float32)
    time_pos = jnp.zeros_like(row_pos) + time_index
    angles = jnp.concatenate(
        [
            time_pos[:, None] * axis_freqs(first)[None],
            row_pos[:, None] * axis_freqs(rest)[None],
            col_pos[:, None] * axis_freqs(rest)[None],
        ],
        axis=-1,
    )
    return (jnp.cos(angles), jnp.sin(angles))


def layer_norm(tokens, mods):
    mean = jnp.mean(tokens, axis=-1, keepdims=True)
    var = jnp.mean((tokens - mean) ** 2, axis=-1, keepdims=True)
    return ((tokens - mean) * lax.rsqrt(var + 1e-06) * (1.0 + mods[1]) + mods[0]).astype(
        jnp.bfloat16
    )


def project_kernel(x_ref, w_ref, cos_ref, sin_ref, gain_ref, q_ref, kv_ref):
    qkv = jnp.dot(x_ref[...], w_ref[...], preferred_element_type=jnp.float32)
    cosine = cos_ref[...]
    sine = sin_ref[...]
    even = lax.broadcasted_iota(jnp.int32, cosine.shape, 1) % 2 == 0

    def rotated(x, gain):
        x = x * lax.rsqrt(jnp.mean(x * x, axis=-1, keepdims=True) + 1e-06) * gain
        other = jnp.where(even, pltpu.roll(x, HEAD_DIM - 1, 1), pltpu.roll(x, 1, 1))
        return (x * cosine + other * sine).astype(jnp.bfloat16)

    q_ref[...] = rotated(qkv[:, :HEAD_DIM], gain_ref[0:1, :])
    kv_ref[0] = rotated(qkv[:, HEAD_DIM : 2 * HEAD_DIM], gain_ref[1:2, :])
    kv_ref[1] = qkv[:, 2 * HEAD_DIM :].astype(jnp.bfloat16)


def project_head(x, w, cosine, sine, gains):
    rows, depth = x.shape
    block = 256
    return pl.pallas_call(
        project_kernel,
        grid=(rows // block,),
        in_specs=[
            pl.BlockSpec((block, depth), lambda i: (i, 0)),
            pl.BlockSpec(w.shape, lambda i: (0, 0)),
            pl.BlockSpec((block, HEAD_DIM), lambda i: (i, 0)),
            pl.BlockSpec((block, HEAD_DIM), lambda i: (i, 0)),
            pl.BlockSpec((2, HEAD_DIM), lambda i: (0, 0)),
        ],
        out_specs=[
            pl.BlockSpec((block, HEAD_DIM), lambda i: (i, 0)),
            pl.BlockSpec((2, block, HEAD_DIM), lambda i: (0, i, 0)),
        ],
        out_shape=[
            jax.ShapeDtypeStruct((rows, HEAD_DIM), jnp.bfloat16),
            jax.ShapeDtypeStruct((2, rows, HEAD_DIM), jnp.bfloat16),
        ],
        compiler_params=pltpu.CompilerParams(vmem_limit_bytes=VMEM_LIMIT),
        cost_estimate=pl.CostEstimate(
            flops=2 * rows * depth * 3 * HEAD_DIM,
            bytes_accessed=2 * (rows * depth + w.size),
            transcendentals=0,
        ),
        name="project_head",
    )(x, w, cosine, sine, gains)


def weights_of(query, keys):
    scores = lax.dot_general(
        query, keys, (((1,), (1,)), ((), ())), preferred_element_type=jnp.float32
    )
    return jnp.exp(scores * (1.0 / HEAD_DIM**0.5))


def own_kernel(q_ref, kv_ref, text_ref, num_ref, den_ref):
    query = q_ref[...]
    num = jnp.zeros(num_ref.shape, jnp.float32)
    den = jnp.zeros((num_ref.shape[0], 1), jnp.float32)
    for ref in (kv_ref, text_ref):
        weights = weights_of(query, ref[0])
        den = den + jnp.sum(weights, axis=-1, keepdims=True)
        num = num + jnp.dot(
            weights.astype(jnp.bfloat16), ref[1], preferred_element_type=jnp.float32
        )
    num_ref[...] = num
    den_ref[...] = jnp.broadcast_to(den, den_ref.shape)


def cond_kernel(mask_ref, q_ref, cond_ref, num_in, den_in, out_ref, num_ref, den_ref):
    step = pl.program_id(0)
    query = q_ref[...]
    rows = query.shape[0]
    tiles = mask_ref.shape[1]
    per_block = rows // TILE
    num_ref[...] = num_in[...]
    den_ref[...] = den_in[...]
    row_tile = lax.broadcasted_iota(jnp.int32, (rows, TILE), 0) // TILE

    for j in range(tiles):
        on = [mask_ref[step * per_block + r, j] for r in range(per_block)]
        some = functools.reduce(jnp.maximum, on)

        @pl.when(some > 0)
        def _(j=j, on=on):
            keep = jnp.zeros((rows, TILE), jnp.float32)
            for r in range(per_block):
                keep = jnp.where(row_tile == r, (on[r] > 0).astype(jnp.float32), keep)
            at = pl.ds(j * TILE, TILE)
            weights = weights_of(query, cond_ref[0, at, :]) * keep
            den_ref[...] += jnp.sum(weights, axis=-1, keepdims=True)
            num_ref[...] += jnp.dot(
                weights.astype(jnp.bfloat16), cond_ref[1, at, :], preferred_element_type=jnp.float32
            )

    out_ref[...] = (num_ref[...] / den_ref[...]).astype(jnp.bfloat16)


def attend_own(query, kv, text):
    rows = query.shape[0]
    block = 256
    row_spec = pl.BlockSpec((block, HEAD_DIM), lambda i: (i, 0))
    keys = kv.shape[1] + text.shape[1]
    return pl.pallas_call(
        own_kernel,
        grid=(rows // block,),
        in_specs=[
            row_spec,
            pl.BlockSpec(kv.shape, lambda i: (0, 0, 0)),
            pl.BlockSpec(text.shape, lambda i: (0, 0, 0)),
        ],
        out_specs=[row_spec, row_spec],
        out_shape=[jax.ShapeDtypeStruct((rows, HEAD_DIM), jnp.float32)] * 2,
        compiler_params=pltpu.CompilerParams(vmem_limit_bytes=VMEM_LIMIT),
        cost_estimate=pl.CostEstimate(
            flops=4 * rows * keys * HEAD_DIM,
            bytes_accessed=2 * (kv.size + text.size) + 10 * query.size,
            transcendentals=rows * keys,
        ),
        name="attend_own",
    )(query, kv, text)


def attend_cond(mask, query, cond, num, den):
    rows = query.shape[0]
    block = 256
    row_spec = pl.BlockSpec((block, HEAD_DIM), lambda i: (i, 0))
    keys = cond.shape[1]
    return pl.pallas_call(
        cond_kernel,
        grid=(rows // block,),
        in_specs=[
            pl.BlockSpec(memory_space=pltpu.SMEM),
            row_spec,
            pl.BlockSpec(cond.shape, lambda i: (0, 0, 0)),
            row_spec,
            row_spec,
        ],
        out_specs=row_spec,
        out_shape=jax.ShapeDtypeStruct((rows, HEAD_DIM), jnp.bfloat16),
        scratch_shapes=[
            pltpu.VMEM((block, HEAD_DIM), jnp.float32),
            pltpu.VMEM((block, HEAD_DIM), jnp.float32),
        ],
        compiler_params=pltpu.CompilerParams(vmem_limit_bytes=VMEM_LIMIT),
        cost_estimate=pl.CostEstimate(
            flops=4 * rows * keys * HEAD_DIM,
            bytes_accessed=2 * cond.size + 10 * query.size,
            transcendentals=rows * keys,
        ),
        name="attend_cond",
    )(mask, query, cond, num, den)


def head_body(image, text_kv, modulation, w_qkv, w_out, q_gain, k_gain, region_mask):
    seq = lax.axis_size("seq")
    img_rows = image.shape[1]
    depth = w_qkv.shape[0]
    rows = img_rows * seq
    section_index = lax.axis_index("section")
    tokens = image[0].astype(jnp.float32)
    mods = modulation[0]

    text = lax.all_to_all(
        text_kv[0].reshape(-1, 2, seq, HEAD_DIM).transpose(2, 1, 0, 3), "seq", 0, 0
    )
    text = text.transpose(1, 0, 2, 3).reshape(2, -1, HEAD_DIM)
    mask = lax.all_gather(region_mask, "seq", axis=0, tiled=True) * (section_index == 1).astype(
        jnp.int32
    )
    w_mine = lax.all_to_all(
        w_qkv.reshape(depth, 3, seq, HEAD_DIM).transpose(2, 0, 1, 3), "seq", 0, 0
    ).reshape(depth * seq, 3 * HEAD_DIM)
    x = lax.all_gather(layer_norm(tokens, mods), "seq", axis=0, tiled=True)

    time_index = (section_index == 0).astype(jnp.float32)
    cosine, sine = rope_tables(jnp.arange(rows, dtype=jnp.int32), time_index)
    cosine = jnp.repeat(cosine, 2, axis=-1)
    sine = jnp.stack([-sine, sine], axis=-1).reshape(rows, HEAD_DIM)
    query, kv = project_head(x, w_mine, cosine, sine, jnp.stack([q_gain, k_gain]))
    cond = lax.ppermute(kv, "section", [(0, 1)])
    num, den = attend_own(query, kv, text)
    attn = attend_cond(mask, query, cond, num, den)

    attn = lax.all_to_all(attn.reshape(seq, img_rows, HEAD_DIM), "seq", 0, 0)
    attn = attn.transpose(1, 0, 2).reshape(img_rows, seq * HEAD_DIM)
    term = jnp.dot(attn, w_out, preferred_element_type=jnp.float32)
    branch = lax.psum_scatter(
        term.astype(jnp.bfloat16), "tp", scatter_dimension=1, tiled=True
    ).astype(jnp.float32)
    cols = branch.shape[1]
    offset = lax.axis_index("tp") * cols
    residual = lax.dynamic_slice_in_dim(image[0], offset, cols, 1).astype(jnp.float32)
    gate = lax.dynamic_slice_in_dim(mods[2], offset, cols, 0)
    return (residual + gate[None, :] * branch).astype(jnp.bfloat16)[None]


def rms_rows(x, gain):
    return x * lax.rsqrt(jnp.mean(x * x, axis=-1, keepdims=True) + 1e-06) * gain


def apply_rope(x, cosine, sine):
    rows, heads_here = (x.shape[0], x.shape[1])
    pairs = x.reshape(rows, heads_here, HEAD_DIM // 2, 2)
    first = pairs[..., 0]
    second = pairs[..., 1]
    cosine = cosine[:, None, :]
    sine = sine[:, None, :]
    rotated = jnp.stack([first * cosine - second * sine, first * sine + second * cosine], axis=-1)
    return rotated.reshape(rows, heads_here, HEAD_DIM)


def attend_piece(carry, keys_vals, query, keep):
    num, den = carry
    rows = keys_vals.shape[0]
    heads_local = query.shape[1]
    piece_k = keys_vals[:, 0].reshape(rows, heads_local, HEAD_DIM)
    piece_v = keys_vals[:, 1].reshape(rows, heads_local, HEAD_DIM)
    scores = jnp.einsum("qhd,khd->hqk", query, piece_k, preferred_element_type=jnp.float32) * (
        1.0 / HEAD_DIM**0.5
    )
    weights = jnp.exp(scores)
    if keep is not None:
        weights = jnp.where(keep[None], weights, 0.0)
    den = den + jnp.sum(weights, axis=-1)
    num = num + jnp.einsum(
        "hqk,khd->hqd", weights.astype(jnp.bfloat16), piece_v, preferred_element_type=jnp.float32
    )
    return (num, den)


def token_body(image, text_kv, modulation, w_qkv, w_out, q_gain, k_gain, region_mask):
    img_rows = image.shape[1]
    width_local = w_qkv.shape[2]
    heads_local = width_local // HEAD_DIM
    tokens = image[0].astype(jnp.float32)
    mods = modulation[0]
    normed = layer_norm(tokens, mods)
    qkv = jnp.einsum(
        "td,dcf->tcf",
        normed,
        lax.all_gather(w_qkv, "seq", axis=0, tiled=True),
        preferred_element_type=jnp.float32,
    )
    section_index = lax.axis_index("section")
    time_index = (section_index == 0).astype(jnp.float32)
    rows_index = lax.axis_index("seq") * img_rows + jnp.arange(img_rows, dtype=jnp.int32)
    cosine, sine = rope_tables(rows_index, time_index)
    query = apply_rope(
        rms_rows(qkv[:, 0].reshape(img_rows, heads_local, HEAD_DIM), q_gain), cosine, sine
    ).astype(jnp.bfloat16)
    keys = apply_rope(
        rms_rows(qkv[:, 1].reshape(img_rows, heads_local, HEAD_DIM), k_gain), cosine, sine
    ).astype(jnp.bfloat16)
    values = qkv[:, 2].astype(jnp.bfloat16)
    image_kv = jnp.stack([keys.reshape(img_rows, width_local), values], axis=1)
    own_kv = jnp.concatenate([image_kv, text_kv[0]], axis=0)
    enabled = (section_index == 1).astype(jnp.int32)
    local_mask = region_mask * enabled
    init = (
        jnp.zeros((heads_local, img_rows, HEAD_DIM), jnp.float32),
        jnp.zeros((heads_local, img_rows), jnp.float32),
    )
    carry = attend_piece(init, lax.all_gather(own_kv, "seq", axis=0, tiled=True), query, None)
    cond_local = lax.ppermute(image_kv, "section", [(0, 1)])
    keep = jnp.repeat(jnp.repeat(local_mask, TILE, axis=0), TILE, axis=1) > 0
    carry = attend_piece(carry, lax.all_gather(cond_local, "seq", axis=0, tiled=True), query, keep)
    num, den = carry
    attn = (num / den[..., None]).astype(jnp.bfloat16)
    attn = jnp.transpose(attn, (1, 0, 2)).reshape(img_rows, width_local)
    term = jnp.dot(attn, w_out, preferred_element_type=jnp.float32)
    branch = lax.psum_scatter(
        term.astype(jnp.bfloat16), "tp", scatter_dimension=1, tiled=True
    ).astype(jnp.float32)
    cols = branch.shape[1]
    offset = lax.axis_index("tp") * cols
    residual = lax.dynamic_slice_in_dim(tokens, offset, cols, 1)
    gate = lax.dynamic_slice_in_dim(mods[2], offset, cols, 0)
    out = residual + gate[None, :] * branch
    return out.astype(jnp.bfloat16)[None]


def body(*arrays):
    w_qkv = arrays[3]
    one_head_each = w_qkv.shape[2] // HEAD_DIM == lax.axis_size("seq")
    return (head_body if one_head_each else token_body)(*arrays)


def solution(mesh):
    return jax.shard_map(
        body,
        mesh=mesh,
        in_specs=(
            P("section", "seq", None),
            P("section", "seq", None, "tp"),
            P("section", None, None),
            P("seq", None, "tp"),
            P("tp", None),
            P(),
            P(),
            P("seq", None),
        ),
        out_specs=P("section", "seq", "tp"),
        check_vma=False,
    )
```

```python
import jax
import jax.numpy as jnp
from jax import lax
from jax.experimental import pallas as pl
from jax.experimental.pallas import tpu as pltpu
from jax.sharding import PartitionSpec as P

HEAD_DIM = 128
GRID_W = 64
TILE = 128
VMEM_LIMIT = 48 * 1024 * 1024


def axis_freqs(width):
    return 10000.0 ** (-jnp.arange(0, width, 2).astype(jnp.float32) / width)


def rope_tables(rows_index, time_index):
    first = HEAD_DIM // 8
    rest = (HEAD_DIM - first) // 2
    row_pos = (rows_index // GRID_W).astype(jnp.float32)
    col_pos = (rows_index % GRID_W).astype(jnp.float32)
    time_pos = jnp.zeros_like(row_pos) + time_index
    angles = jnp.concatenate(
        [
            time_pos[:, None] * axis_freqs(first)[None],
            row_pos[:, None] * axis_freqs(rest)[None],
            col_pos[:, None] * axis_freqs(rest)[None],
        ],
        axis=-1,
    )
    return (jnp.cos(angles), jnp.sin(angles))


def layer_norm(tokens, mods):
    mean = jnp.mean(tokens, axis=-1, keepdims=True)
    var = jnp.mean((tokens - mean) ** 2, axis=-1, keepdims=True)
    return ((tokens - mean) * lax.rsqrt(var + 1e-06) * (1.0 + mods[1]) + mods[0]).astype(
        jnp.bfloat16
    )


def normed_rotated(x, gain, cosine, sine):
    x = x * lax.rsqrt(jnp.mean(x * x, axis=-1, keepdims=True) + 1e-06) * gain
    even = lax.broadcasted_iota(jnp.int32, x.shape, 1) % 2 == 0
    other = jnp.where(even, pltpu.roll(x, HEAD_DIM - 1, 1), pltpu.roll(x, 1, 1))
    return (x * cosine + other * sine).astype(jnp.bfloat16)


def gather_weights(into, section, mine, peer, kinds):
    sources, _, half, _ = mine.shape
    for ref, at in ((mine, section), (peer, 1 - section)):
        for s in range(sources):
            rows = pl.ds(pl.multiple_of(s * 2 * half + at * half, half), half)
            for place, kind in enumerate(kinds):
                into[rows, place * HEAD_DIM : (place + 1) * HEAD_DIM] = ref[s, kind]


def kv_kernel(section_ref, x_ref, mine, peer, cos_ref, sin_ref, gain_ref, kv_ref, w_ref):
    @pl.when(pl.program_id(0) == 0)
    def _():
        gather_weights(w_ref, section_ref[0], mine, peer, (1, 2))

    both = jnp.dot(x_ref[...], w_ref[...], preferred_element_type=jnp.float32)
    kv_ref[0] = normed_rotated(both[:, :HEAD_DIM], gain_ref[1:2, :], cos_ref[...], sin_ref[...])
    kv_ref[1] = both[:, HEAD_DIM:].astype(jnp.bfloat16)


def weights_of(query, keys):
    scores = lax.dot_general(
        query, keys, (((1,), (1,)), ((), ())), preferred_element_type=jnp.float32
    )
    return jnp.exp(scores * (1.0 / HEAD_DIM**0.5))


def own_kernel(
    section_ref, x_ref, mine, peer, cos_ref, sin_ref, gain_ref, kv_ref, text_ref,
    q_ref, num_ref, den_ref, w_ref,
):
    @pl.when(pl.program_id(0) == 0)
    def _():
        gather_weights(w_ref, section_ref[0], mine, peer, (0,))

    query = jnp.dot(x_ref[...], w_ref[...], preferred_element_type=jnp.float32)
    query = normed_rotated(query, gain_ref[0:1, :], cos_ref[...], sin_ref[...])
    q_ref[...] = query
    num = jnp.zeros(num_ref.shape, jnp.float32)
    den = jnp.zeros((num_ref.shape[0], 1), jnp.float32)
    count = text_ref.shape[1] // 2 - 8
    text_k = text_ref[:, :count, :].reshape(-1, HEAD_DIM)
    text_v = text_ref[:, count : 2 * count, :].reshape(-1, HEAD_DIM)
    for keys, values in ((kv_ref[0], kv_ref[1]), (text_k, text_v)):
        weights = weights_of(query, keys)
        den = den + jnp.sum(weights, axis=-1, keepdims=True)
        num = num + jnp.dot(weights.astype(jnp.bfloat16), values, preferred_element_type=jnp.float32)
    num_ref[...] = num
    den_ref[...] = jnp.broadcast_to(den, den_ref.shape)


def cond_kernel(section_ref, keep_ref, q_ref, cond_ref, num_ref, den_ref, out_ref):
    section = section_ref[0]

    @pl.when(section == 0)
    def _():
        out_ref[...] = (num_ref[...] / den_ref[...]).astype(jnp.bfloat16)

    @pl.when(section != 0)
    def _():
        weights = weights_of(q_ref[...], cond_ref[0])
        rows, keys = weights.shape
        weights = weights.reshape(rows // TILE, TILE, keys) * keep_ref[0][:, None, :]
        weights = weights.reshape(rows, keys)
        den = den_ref[...] + jnp.sum(weights, axis=-1, keepdims=True)
        num = num_ref[...] + jnp.dot(
            weights.astype(jnp.bfloat16), cond_ref[1], preferred_element_type=jnp.float32
        )
        out_ref[...] = (num / den).astype(jnp.bfloat16)


BLOCK = 256


def whole(array):
    return pl.BlockSpec(array.shape, lambda i, *_: (0,) * array.ndim)


def by_rows(width):
    return pl.BlockSpec((BLOCK, width), lambda i, *_: (i, 0))


def call(kernel, name, grid, in_specs, out_specs, out_shape, scratch, flops, moved, exps, args):
    return pl.pallas_call(
        kernel,
        grid_spec=pltpu.PrefetchScalarGridSpec(
            num_scalar_prefetch=1,
            grid=grid,
            in_specs=in_specs,
            out_specs=out_specs,
            scratch_shapes=scratch,
        ),
        out_shape=out_shape,
        compiler_params=pltpu.CompilerParams(vmem_limit_bytes=VMEM_LIMIT),
        cost_estimate=pl.CostEstimate(flops=flops, bytes_accessed=moved, transcendentals=exps),
        name=name,
    )(*args)


def project_kv(section, x, mine, peer, cosine, sine, gains):
    rows, depth = x.shape
    return call(
        kv_kernel, "project_kv", (rows // BLOCK,),
        [
            by_rows(depth), whole(mine), whole(peer), by_rows(HEAD_DIM), by_rows(HEAD_DIM),
            whole(gains),
        ],
        pl.BlockSpec((2, BLOCK, HEAD_DIM), lambda i, *_: (0, i, 0)),
        jax.ShapeDtypeStruct((2, rows, HEAD_DIM), jnp.bfloat16),
        [pltpu.VMEM((depth, 2 * HEAD_DIM), jnp.bfloat16)],
        4 * rows * depth * HEAD_DIM, 2 * (x.size + 2 * mine.size), 0,
        (section, x, mine, peer, cosine, sine, gains),
    )


def attend_own(section, x, mine, peer, cosine, sine, gains, kv, text):
    rows, depth = x.shape
    keys = rows + text.shape[0] * (text.shape[1] // 2 - 8)
    return call(
        own_kernel, "attend_own", (rows // BLOCK,),
        [
            by_rows(depth), whole(mine), whole(peer), by_rows(HEAD_DIM), by_rows(HEAD_DIM),
            whole(gains), whole(kv), whole(text),
        ],
        [by_rows(HEAD_DIM)] * 3,
        [
            jax.ShapeDtypeStruct((rows, HEAD_DIM), jnp.bfloat16),
            jax.ShapeDtypeStruct((rows, HEAD_DIM), jnp.float32),
            jax.ShapeDtypeStruct((rows, HEAD_DIM), jnp.float32),
        ],
        [pltpu.VMEM((depth, HEAD_DIM), jnp.bfloat16)],
        2 * rows * depth * HEAD_DIM + 4 * rows * keys * HEAD_DIM,
        2 * (x.size + 2 * mine.size), rows * keys,
        (section, x, mine, peer, cosine, sine, gains, kv, text),
    )


def attend_cond(section, keep, query, cond, num, den):
    rows, keys = query.shape[0], cond.shape[1]
    keep = keep.reshape(rows // BLOCK, BLOCK // TILE, keys)
    return call(
        cond_kernel, "attend_cond", (rows // BLOCK,),
        [
            pl.BlockSpec((1, BLOCK // TILE, keys), lambda i, *_: (i, 0, 0)),
            by_rows(HEAD_DIM), whole(cond), by_rows(HEAD_DIM), by_rows(HEAD_DIM),
        ],
        by_rows(HEAD_DIM),
        jax.ShapeDtypeStruct((rows, HEAD_DIM), jnp.bfloat16),
        [],
        4 * rows * keys * HEAD_DIM, 2 * cond.size + 10 * query.size, rows * keys,
        (section, keep, query, cond, num, den),
    )


def sent_kernel(half_ref, attn_ref, w_ref, out_ref):
    attn = jnp.concatenate([attn_ref[s] for s in range(attn_ref.shape[0])], axis=1)
    out_ref[...] = jnp.dot(attn, w_ref[...], preferred_element_type=jnp.float32).astype(jnp.bfloat16)


def kept_kernel(half_ref, attn_ref, w_ref, image_ref, gate_ref, out_ref):
    attn = jnp.concatenate([attn_ref[s] for s in range(attn_ref.shape[0])], axis=1)
    branch = jnp.dot(attn, w_ref[...], preferred_element_type=jnp.float32)
    out_ref[...] = image_ref[...].astype(jnp.float32) + gate_ref[...] * branch


def project_out(half, attn, w_out, image=None, gate=None):
    sources, rows, _ = attn.shape
    depth, width = w_out.shape[0], w_out.shape[1] // 2
    block = 512
    steps = width // block

    def columns(height):
        return pl.BlockSpec((height, block), lambda i, half: (0, half[0] * steps + i))

    kept = image is not None
    return call(
        kept_kernel if kept else sent_kernel, "out_kept" if kept else "out_sent", (steps,),
        [whole(attn), columns(depth)] + ([columns(rows), columns(1)] if kept else []),
        pl.BlockSpec((rows, block), lambda i, half: (0, i)),
        jax.ShapeDtypeStruct((rows, width), jnp.float32 if kept else jnp.bfloat16),
        [],
        2 * rows * depth * width, 2 * depth * width, 0,
        (half, attn, w_out) + ((image, gate) if kept else ()),
    )


def head_body(image, text_kv, modulation, w_qkv, w_out, q_gain, k_gain, region_mask):
    seq = lax.axis_size("seq")
    img_rows = image.shape[1]
    depth = w_qkv.shape[0]
    rows = img_rows * seq
    section = lax.axis_index("section")
    tp = lax.axis_index("tp")
    mods = modulation[0]
    section_at = section.astype(jnp.int32).reshape(1)

    half = depth // 2
    w_half = lax.dynamic_slice_in_dim(w_qkv.transpose(1, 0, 2), section * half, half, 1)
    w_half = w_half.reshape(3, half, seq, HEAD_DIM).transpose(2, 0, 1, 3)
    mine = lax.all_to_all(w_half, "seq", 0, 0)
    peer = lax.ppermute(mine, "section", [(0, 1), (1, 0)])

    part = img_rows // lax.axis_size("tp")
    tokens = lax.dynamic_slice_in_dim(image[0], tp * part, part, 0).astype(jnp.float32)
    x = lax.all_gather(layer_norm(tokens, mods), ("seq", "tp"), axis=0, tiled=True)

    text = text_kv[0].reshape(-1, 2, seq, HEAD_DIM).transpose(2, 1, 0, 3)
    text = text.reshape(seq, -1, HEAD_DIM)
    mask = region_mask.astype(jnp.bfloat16)
    mask = jnp.pad(mask, ((0, 16 - mask.shape[0]), (0, HEAD_DIM - mask.shape[1])))
    text = lax.all_to_all(
        jnp.concatenate([text, jnp.broadcast_to(mask, (seq,) + mask.shape)], axis=1), "seq", 0, 0
    )
    keep = text[:, -16 : -16 + region_mask.shape[0], : region_mask.shape[1]].astype(jnp.float32)
    keep = jnp.repeat(keep.reshape(-1, region_mask.shape[1]), TILE, axis=1)

    time_index = (section == 0).astype(jnp.float32)
    cosine, sine = rope_tables(jnp.arange(rows, dtype=jnp.int32), time_index)
    cosine = jnp.repeat(cosine, 2, axis=-1)
    sine = jnp.stack([-sine, sine], axis=-1).reshape(rows, HEAD_DIM)
    gains = jnp.stack([q_gain, k_gain])
    kv = project_kv(section_at, x, mine, peer, cosine, sine, gains)
    cond = lax.ppermute(kv, "section", [(0, 1)])
    query, num, den = attend_own(section_at, x, mine, peer, cosine, sine, gains, kv, text)
    attn = attend_cond(section_at, keep, query, cond, num, den)

    attn = lax.all_to_all(attn.reshape(seq, img_rows, HEAD_DIM), "seq", 0, 0)
    tp_at = tp.astype(jnp.int32).reshape(1)
    gate = mods[2:3]
    other = lax.ppermute(project_out(1 - tp_at, attn, w_out), "tp", [(0, 1), (1, 0)])
    kept = project_out(tp_at, attn, w_out, image[0], gate)
    gate = lax.dynamic_slice_in_dim(gate, tp * other.shape[1], other.shape[1], 1)
    return (kept + gate * other.astype(jnp.float32)).astype(jnp.bfloat16)[None]


def rms_rows(x, gain):
    return x * lax.rsqrt(jnp.mean(x * x, axis=-1, keepdims=True) + 1e-06) * gain


def apply_rope(x, cosine, sine):
    rows, heads_here = (x.shape[0], x.shape[1])
    pairs = x.reshape(rows, heads_here, HEAD_DIM // 2, 2)
    first = pairs[..., 0]
    second = pairs[..., 1]
    cosine = cosine[:, None, :]
    sine = sine[:, None, :]
    rotated = jnp.stack([first * cosine - second * sine, first * sine + second * cosine], axis=-1)
    return rotated.reshape(rows, heads_here, HEAD_DIM)


def attend_piece(carry, keys_vals, query, keep):
    num, den = carry
    rows = keys_vals.shape[0]
    heads_local = query.shape[1]
    piece_k = keys_vals[:, 0].reshape(rows, heads_local, HEAD_DIM)
    piece_v = keys_vals[:, 1].reshape(rows, heads_local, HEAD_DIM)
    scores = jnp.einsum("qhd,khd->hqk", query, piece_k, preferred_element_type=jnp.float32) * (
        1.0 / HEAD_DIM**0.5
    )
    weights = jnp.exp(scores)
    if keep is not None:
        weights = jnp.where(keep[None], weights, 0.0)
    den = den + jnp.sum(weights, axis=-1)
    num = num + jnp.einsum(
        "hqk,khd->hqd", weights.astype(jnp.bfloat16), piece_v, preferred_element_type=jnp.float32
    )
    return (num, den)


def token_body(image, text_kv, modulation, w_qkv, w_out, q_gain, k_gain, region_mask):
    img_rows = image.shape[1]
    width_local = w_qkv.shape[2]
    heads_local = width_local // HEAD_DIM
    tokens = image[0].astype(jnp.float32)
    mods = modulation[0]
    normed = layer_norm(tokens, mods)
    qkv = jnp.einsum(
        "td,dcf->tcf",
        normed,
        lax.all_gather(w_qkv, "seq", axis=0, tiled=True),
        preferred_element_type=jnp.float32,
    )
    section_index = lax.axis_index("section")
    time_index = (section_index == 0).astype(jnp.float32)
    rows_index = lax.axis_index("seq") * img_rows + jnp.arange(img_rows, dtype=jnp.int32)
    cosine, sine = rope_tables(rows_index, time_index)
    query = apply_rope(
        rms_rows(qkv[:, 0].reshape(img_rows, heads_local, HEAD_DIM), q_gain), cosine, sine
    ).astype(jnp.bfloat16)
    keys = apply_rope(
        rms_rows(qkv[:, 1].reshape(img_rows, heads_local, HEAD_DIM), k_gain), cosine, sine
    ).astype(jnp.bfloat16)
    values = qkv[:, 2].astype(jnp.bfloat16)
    image_kv = jnp.stack([keys.reshape(img_rows, width_local), values], axis=1)
    own_kv = jnp.concatenate([image_kv, text_kv[0]], axis=0)
    enabled = (section_index == 1).astype(jnp.int32)
    local_mask = region_mask * enabled
    init = (
        jnp.zeros((heads_local, img_rows, HEAD_DIM), jnp.float32),
        jnp.zeros((heads_local, img_rows), jnp.float32),
    )
    carry = attend_piece(init, lax.all_gather(own_kv, "seq", axis=0, tiled=True), query, None)
    cond_local = lax.ppermute(image_kv, "section", [(0, 1)])
    keep = jnp.repeat(jnp.repeat(local_mask, TILE, axis=0), TILE, axis=1) > 0
    carry = attend_piece(carry, lax.all_gather(cond_local, "seq", axis=0, tiled=True), query, keep)
    num, den = carry
    attn = (num / den[..., None]).astype(jnp.bfloat16)
    attn = jnp.transpose(attn, (1, 0, 2)).reshape(img_rows, width_local)
    term = jnp.dot(attn, w_out, preferred_element_type=jnp.float32)
    branch = lax.psum_scatter(
        term.astype(jnp.bfloat16), "tp", scatter_dimension=1, tiled=True
    ).astype(jnp.float32)
    cols = branch.shape[1]
    offset = lax.axis_index("tp") * cols
    residual = lax.dynamic_slice_in_dim(tokens, offset, cols, 1)
    gate = lax.dynamic_slice_in_dim(mods[2], offset, cols, 0)
    out = residual + gate[None, :] * branch
    return out.astype(jnp.bfloat16)[None]


def body(*arrays):
    image, w_qkv, region_mask = arrays[0], arrays[3], arrays[7]
    one_head_each = (
        w_qkv.shape[2] // HEAD_DIM == lax.axis_size("seq")
        and lax.axis_size("section") == 2
        and lax.axis_size("tp") == 2
        and w_qkv.shape[0] % 32 == 0
        and image.shape[1] % 32 == 0
        and image.shape[1] * lax.axis_size("seq") % BLOCK == 0
        and arrays[4].shape[1] % 1024 == 0
        and region_mask.shape[0] <= 16
        and region_mask.shape[1] <= HEAD_DIM
    )
    return (head_body if one_head_each else token_body)(*arrays)


def solution(mesh):
    return jax.shard_map(
        body,
        mesh=mesh,
        in_specs=(
            P("section", "seq", None),
            P("section", "seq", None, "tp"),
            P("section", None, None),
            P("seq", None, "tp"),
            P("tp", None),
            P(),
            P(),
            P("seq", None),
        ),
        out_specs=P("section", "seq", "tp"),
        check_vma=False,
    )
```

```python
import jax
import jax.numpy as jnp
from jax import lax
from jax.experimental import pallas as pl
from jax.experimental.pallas import tpu as pltpu
from jax.sharding import PartitionSpec as P

HEAD_DIM = 128
GRID_W = 64
TILE = 128
VMEM_LIMIT = 30 * 1024 * 1024


def axis_freqs(width):
    return 10000.0 ** (-jnp.arange(0, width, 2).astype(jnp.float32) / width)


def rope_tables(rows_index, time_index):
    first = HEAD_DIM // 8
    rest = (HEAD_DIM - first) // 2
    row_pos = (rows_index // GRID_W).astype(jnp.float32)
    col_pos = (rows_index % GRID_W).astype(jnp.float32)
    time_pos = jnp.zeros_like(row_pos) + time_index
    angles = jnp.concatenate(
        [
            time_pos[:, None] * axis_freqs(first)[None],
            row_pos[:, None] * axis_freqs(rest)[None],
            col_pos[:, None] * axis_freqs(rest)[None],
        ],
        axis=-1,
    )
    return (jnp.cos(angles), jnp.sin(angles))


def layer_norm(tokens, mods):
    mean = jnp.mean(tokens, axis=-1, keepdims=True)
    var = jnp.mean((tokens - mean) ** 2, axis=-1, keepdims=True)
    return ((tokens - mean) * lax.rsqrt(var + 1e-06) * (1.0 + mods[1:2]) + mods[0:1]).astype(
        jnp.bfloat16
    )


CHUNKS = 2
BLOCK = 256
VMEM = pl.BlockSpec(memory_space=pltpu.VMEM)
SMEM = pl.BlockSpec(memory_space=pltpu.SMEM)


def call(kernel, name, out_shape, flops, moved, exps, **spec):
    return pl.pallas_call(
        kernel,
        out_shape=out_shape,
        compiler_params=pltpu.CompilerParams(vmem_limit_bytes=VMEM_LIMIT),
        cost_estimate=pl.CostEstimate(flops=flops, bytes_accessed=moved, transcendentals=exps),
        name=name,
        **spec,
    )


def norm_kernel(tp_ref, image_ref, mods_ref, *out_refs):
    normed = layer_norm(image_ref[...].astype(jnp.float32), mods_ref[...])
    rows = normed.shape[0] // len(out_refs)
    for c, out_ref in enumerate(out_refs):
        out_ref[...] = normed[c * rows : (c + 1) * rows]


def norm_part(tp, parts, image, mods):
    rows, depth = image.shape
    part = rows // parts
    small = pl.BlockSpec((part // CHUNKS, depth), lambda i, tp: (0, 0))
    return call(
        norm_kernel, "norm_part",
        [jax.ShapeDtypeStruct((part // CHUNKS, depth), jnp.bfloat16)] * CHUNKS,
        10 * part * depth, 4 * part * depth, 0,
        grid_spec=pltpu.PrefetchScalarGridSpec(
            num_scalar_prefetch=1,
            grid=(1,),
            in_specs=[
                pl.BlockSpec((part, depth), lambda i, tp: (tp[0], 0)),
                pl.BlockSpec(mods.shape, lambda i, tp: (0, 0)),
            ],
            out_specs=[small] * CHUNKS,
        ),
    )(tp, image, mods)


def normed_rotated(x, gain, cosine, sine):
    x = x * lax.rsqrt(jnp.mean(x * x, axis=-1, keepdims=True) + 1e-06) * gain
    even = lax.broadcasted_iota(jnp.int32, x.shape, 1) % 2 == 0
    other = jnp.where(even, pltpu.roll(x, HEAD_DIM - 1, 1), pltpu.roll(x, 1, 1))
    return (x * cosine + other * sine).astype(jnp.bfloat16)


def project_kernel(kinds, section_ref, x_ref, mine, peer, cos_ref, sin_ref, gain_ref, *refs):
    out_refs, acc_ref = refs[:-1], refs[-1]
    step = pl.program_id(0)
    half = peer.shape[1] // 3
    first = section_ref[0] == 0

    def piece(s, kind):
        at = slice(kind * half, (kind + 1) * half)
        a, b = mine[s, at, :], peer[s, at, :]
        return jnp.concatenate([jnp.where(first, a, b), jnp.where(first, b, a)], axis=0)

    w = jnp.concatenate(
        [
            jnp.concatenate([piece(s, kind) for s in range(mine.shape[0])], axis=0)
            for kind in kinds
        ],
        axis=1,
    )
    part = jnp.dot(x_ref[...], w, preferred_element_type=jnp.float32)

    @pl.when(step == 0)
    def _():
        acc_ref[...] = part

    @pl.when(step > 0)
    def _():
        acc_ref[...] += part

    @pl.when(step == pl.num_programs(0) - 1)
    def _():
        for place, kind in enumerate(kinds):
            value = acc_ref[:, place * HEAD_DIM : (place + 1) * HEAD_DIM]
            if kind < 2:
                value = normed_rotated(
                    value, gain_ref[kind : kind + 1, :], cos_ref[...], sin_ref[...]
                )
            if kind == 0:
                out_refs[0][...] = value
            else:
                out_refs[-1][kind - 1] = value.astype(jnp.bfloat16)


def project(kinds, section, x, mine, peer, cosine, sine, gains):
    rows, depth = x.shape
    sources = mine.shape[0]
    steps = 4
    out_shape, out_specs = [], []
    if 0 in kinds:
        out_shape.append(jax.ShapeDtypeStruct((rows, HEAD_DIM), jnp.bfloat16))
        out_specs.append(pl.BlockSpec((rows, HEAD_DIM), lambda k, s: (0, 0)))
    if 1 in kinds:
        out_shape.append(jax.ShapeDtypeStruct((2, rows, HEAD_DIM), jnp.bfloat16))
        out_specs.append(pl.BlockSpec((2, rows, HEAD_DIM), lambda k, s: (0, 0, 0)))

    def pieces(array):
        return pl.BlockSpec((sources // steps,) + array.shape[1:], lambda k, s: (k, 0, 0))

    return call(
        lambda *refs: project_kernel(kinds, *refs), "project_" + "".join("qkv"[k] for k in kinds),
        out_shape,
        2 * len(kinds) * rows * depth * HEAD_DIM, 2 * (x.size + mine.size + peer.size), 0,
        grid_spec=pltpu.PrefetchScalarGridSpec(
            num_scalar_prefetch=1,
            grid=(steps,),
            in_specs=[
                pl.BlockSpec((rows, depth // steps), lambda k, s: (0, k)),
                pieces(mine),
                pieces(peer),
                pl.BlockSpec((rows, HEAD_DIM), lambda k, s: (0, 0)),
                pl.BlockSpec((rows, HEAD_DIM), lambda k, s: (0, 0)),
                pl.BlockSpec((2, HEAD_DIM), lambda k, s: (0, 0)),
            ],
            out_specs=out_specs,
            scratch_shapes=[pltpu.VMEM((rows, len(kinds) * HEAD_DIM), jnp.float32)],
        ),
    )(section, x, mine, peer, cosine, sine, gains)


def weights_of(query, keys):
    scores = lax.dot_general(
        query, keys, (((1,), (1,)), ((), ())), preferred_element_type=jnp.float32
    )
    return jnp.exp(scores * (1.0 / HEAD_DIM**0.5))


def summed(weights, values):
    den = jnp.sum(weights, axis=-1, keepdims=True)
    num = jnp.dot(weights.astype(jnp.bfloat16), values, preferred_element_type=jnp.float32)
    return num, den


def kept_weights(query, cond_ref, keep):
    weights = weights_of(query, cond_ref[0])
    rows, keys = weights.shape
    tiles = keep.shape[0]
    return (weights.reshape(tiles, rows // tiles, keys) * keep[:, None, :]).reshape(rows, keys)


def own_kernel(section_ref, keep_ref, qa, qb, kva, kvb, text, conda, num_ref, den_ref):
    rows = qa.shape[0]
    tiles = keep_ref.shape[0] * BLOCK // rows
    for c, q_ref in enumerate((qa, qb)):
        for b in range(rows // BLOCK):
            query = q_ref[b * BLOCK : (b + 1) * BLOCK, :]
            at = pl.ds(c * rows + b * BLOCK, BLOCK)
            num, den = 0.0, 0.0
            for ref in (kva, kvb, text):
                more = summed(weights_of(query, ref[0]), ref[1])
                num, den = num + more[0], den + more[1]
            num_ref[at, :] = num
            den_ref[at, :] = jnp.broadcast_to(den, num.shape)

    @pl.when(section_ref[0] != 0)
    def _():
        for c, q_ref in enumerate((qa, qb)):
            for b in range(rows // BLOCK):
                query = q_ref[b * BLOCK : (b + 1) * BLOCK, :]
                at = pl.ds(c * rows + b * BLOCK, BLOCK)
                keep = keep_ref[b * tiles : (b + 1) * tiles, :]
                num, den = summed(kept_weights(query, conda, keep), conda[1])
                num_ref[at, :] += num
                den_ref[at, :] += jnp.broadcast_to(den, num.shape)


def cond_kernel(section_ref, keep_ref, qa, qb, condb, num_ref, den_ref, out_ref):
    rows = qa.shape[0]
    tiles = keep_ref.shape[0] * BLOCK // rows

    def store(c, b, num, den):
        value = (num / den).astype(jnp.bfloat16).reshape(tiles, -1, HEAD_DIM)
        out_ref[b * tiles : (b + 1) * tiles, c] = value

    @pl.when(section_ref[0] == 0)
    def _():
        for c in range(CHUNKS):
            for b in range(rows // BLOCK):
                at = pl.ds(c * rows + b * BLOCK, BLOCK)
                store(c, b, num_ref[at, :], den_ref[at, :])

    @pl.when(section_ref[0] != 0)
    def _():
        for c, q_ref in enumerate((qa, qb)):
            for b in range(rows // BLOCK):
                query = q_ref[b * BLOCK : (b + 1) * BLOCK, :]
                at = pl.ds(c * rows + b * BLOCK, BLOCK)
                keep = keep_ref[b * tiles : (b + 1) * tiles, :]
                num, den = summed(kept_weights(query, condb, keep), condb[1])
                store(c, b, num_ref[at, :] + num, den_ref[at, :] + den)


def attend_own(section, keep, queries, kvs, text, cond):
    rows = 2 * queries[0].shape[0]
    keys = rows + text.shape[1] + cond.shape[1]
    return call(
        own_kernel, "attend_own", [jax.ShapeDtypeStruct((rows, HEAD_DIM), jnp.float32)] * 2,
        4 * rows * keys * HEAD_DIM, 2 * rows * HEAD_DIM * 10, rows * keys,
        in_specs=[SMEM] + [VMEM] * 7,
        out_specs=[VMEM] * 2,
    )(section, keep, *queries, *kvs, text, cond)


def attend_cond(section, keep, queries, cond, num, den):
    rows, seq = num.shape[0], keep.shape[0]
    keys = cond.shape[1]
    return call(
        cond_kernel, "attend_cond",
        jax.ShapeDtypeStruct((seq, CHUNKS, rows // seq // CHUNKS, HEAD_DIM), jnp.bfloat16),
        4 * rows * keys * HEAD_DIM, 2 * rows * HEAD_DIM * 8, rows * keys,
        in_specs=[SMEM] + [VMEM] * 6,
        out_specs=VMEM,
    )(section, keep, *queries, cond, num, den)


def token_rows(attn_ref):
    heads, chunks, held, _ = attn_ref.shape
    parts = 2
    piece = held // parts
    return jnp.concatenate(
        [
            jnp.concatenate(
                [
                    attn_ref[h, c, t * piece : (t + 1) * piece, :]
                    for t in range(parts)
                    for c in range(chunks)
                ],
                axis=0,
            )
            for h in range(heads)
        ],
        axis=1,
    )


def sent_kernel(half_ref, attn_ref, w_ref, out_ref):
    branch = jnp.dot(token_rows(attn_ref), w_ref[...], preferred_element_type=jnp.float32)
    out_ref[...] = branch.astype(jnp.bfloat16)


def kept_kernel(half_ref, attn_ref, w_ref, image_ref, gate_ref, out_ref):
    branch = jnp.dot(token_rows(attn_ref), w_ref[...], preferred_element_type=jnp.float32)
    out_ref[...] = image_ref[...].astype(jnp.float32) + gate_ref[...] * branch


def project_out(half, attn, w_out, image=None, gate=None):
    rows = attn.shape[1] * attn.shape[2]
    depth, width = w_out.shape[0], w_out.shape[1] // 2
    block = 512
    steps = width // block

    def columns(height):
        return pl.BlockSpec((height, block), lambda i, half: (0, half[0] * steps + i))

    kept = image is not None
    return call(
        kept_kernel if kept else sent_kernel, "out_kept" if kept else "out_sent",
        jax.ShapeDtypeStruct((rows, width), jnp.float32 if kept else jnp.bfloat16),
        2 * rows * depth * width, 2 * depth * width, 0,
        grid_spec=pltpu.PrefetchScalarGridSpec(
            num_scalar_prefetch=1,
            grid=(steps,),
            in_specs=[pl.BlockSpec(attn.shape, lambda i, half: (0, 0, 0, 0)), columns(depth)]
            + ([columns(rows), columns(1)] if kept else []),
            out_specs=pl.BlockSpec((rows, block), lambda i, half: (0, i)),
        ),
    )(half, attn, w_out, *((image, gate) if kept else ()))


def lane_tables(rows_index, time_index):
    first = HEAD_DIM // 8
    rest = (HEAD_DIM - first) // 2
    freqs = jnp.concatenate([axis_freqs(first), axis_freqs(rest), axis_freqs(rest)])
    freqs = jnp.repeat(freqs, 2)[None]
    lane = jnp.arange(HEAD_DIM, dtype=jnp.int32)[None]
    row_pos = (rows_index // GRID_W).astype(jnp.float32)[:, None]
    col_pos = (rows_index % GRID_W).astype(jnp.float32)[:, None]
    ids = jnp.where(lane < first, time_index, jnp.where(lane < first + rest, row_pos, col_pos))
    angles = ids * freqs
    return jnp.cos(angles), jnp.sin(angles) * jnp.where(lane % 2 == 0, -1.0, 1.0)


def head_body(image, text_kv, modulation, w_qkv, w_out, q_gain, k_gain, region_mask):
    seq = lax.axis_size("seq")
    parts = lax.axis_size("tp")
    img_rows = image.shape[1]
    depth = w_qkv.shape[0]
    section = lax.axis_index("section")
    tp = lax.axis_index("tp")
    mods = modulation[0]
    section_at = section.astype(jnp.int32).reshape(1)
    tp_at = tp.astype(jnp.int32).reshape(1)

    piece = img_rows // parts // CHUNKS
    normed = norm_part(tp_at, parts, image[0], mods)
    xs = [lax.all_gather(n, ("seq", "tp"), axis=0, tiled=True) for n in normed]

    half = depth // 2
    w_half = lax.dynamic_slice_in_dim(w_qkv.transpose(1, 0, 2), section * half, half, 1)
    w_half = w_half.reshape(3, half, seq, HEAD_DIM).transpose(2, 0, 1, 3).reshape(seq, -1, HEAD_DIM)
    text = text_kv[0].reshape(-1, 2, seq, HEAD_DIM).transpose(2, 0, 1, 3).reshape(seq, -1, HEAD_DIM)
    mask = jnp.pad(
        region_mask.astype(jnp.bfloat16), ((0, 15), (0, HEAD_DIM - region_mask.shape[1]))
    )
    mask = jnp.broadcast_to(mask, (seq,) + mask.shape)
    mine = lax.all_to_all(jnp.concatenate([w_half, text, mask], axis=1), "seq", 0, 0)
    w_rows = 3 * half
    peer = lax.ppermute(mine[:, :w_rows], "section", [(0, 1), (1, 0)])
    text = mine[:, w_rows:-16].reshape(-1, 2, HEAD_DIM).transpose(1, 0, 2)
    keep = mine[:, -16, : region_mask.shape[1]].astype(jnp.float32)
    keep = jnp.repeat(keep, parts * piece, axis=1)

    time_index = (section == 0).astype(jnp.float32)
    index = jnp.arange(seq * parts * piece, dtype=jnp.int32)
    index = index // piece * (CHUNKS * piece) + index % piece
    tables = [lane_tables(index + c * piece, time_index) for c in range(CHUNKS)]
    gains = jnp.stack([q_gain, k_gain])

    q_a, kv_a = project((0, 1, 2), section_at, xs[0], mine, peer, *tables[0], gains)
    cond_a = lax.ppermute(kv_a, "section", [(0, 1)])
    (kv_b,) = project((1, 2), section_at, xs[1], mine, peer, *tables[1], gains)
    cond_b = lax.ppermute(kv_b, "section", [(0, 1)])
    (q_b,) = project((0,), section_at, xs[1], mine, peer, *tables[1], gains)
    queries = (q_a, q_b)
    num, den = attend_own(section_at, keep, queries, (kv_a, kv_b), text, cond_a)
    attn = attend_cond(section_at, keep, queries, cond_b, num, den)

    attn = lax.all_to_all(attn, "seq", 0, 0)
    gate = mods[2:3]
    other = lax.ppermute(project_out(1 - tp_at, attn, w_out), "tp", [(0, 1), (1, 0)])
    kept = project_out(tp_at, attn, w_out, image[0], gate)
    gate = lax.dynamic_slice_in_dim(gate, tp * other.shape[1], other.shape[1], 1)
    return (kept + gate * other.astype(jnp.float32)).astype(jnp.bfloat16)[None]


def rms_rows(x, gain):
    return x * lax.rsqrt(jnp.mean(x * x, axis=-1, keepdims=True) + 1e-06) * gain


def apply_rope(x, cosine, sine):
    rows, heads_here = (x.shape[0], x.shape[1])
    pairs = x.reshape(rows, heads_here, HEAD_DIM // 2, 2)
    first = pairs[..., 0]
    second = pairs[..., 1]
    cosine = cosine[:, None, :]
    sine = sine[:, None, :]
    rotated = jnp.stack([first * cosine - second * sine, first * sine + second * cosine], axis=-1)
    return rotated.reshape(rows, heads_here, HEAD_DIM)


def attend_piece(carry, keys_vals, query, keep):
    num, den = carry
    rows = keys_vals.shape[0]
    heads_local = query.shape[1]
    piece_k = keys_vals[:, 0].reshape(rows, heads_local, HEAD_DIM)
    piece_v = keys_vals[:, 1].reshape(rows, heads_local, HEAD_DIM)
    scores = jnp.einsum("qhd,khd->hqk", query, piece_k, preferred_element_type=jnp.float32) * (
        1.0 / HEAD_DIM**0.5
    )
    weights = jnp.exp(scores)
    if keep is not None:
        weights = jnp.where(keep[None], weights, 0.0)
    den = den + jnp.sum(weights, axis=-1)
    num = num + jnp.einsum(
        "hqk,khd->hqd", weights.astype(jnp.bfloat16), piece_v, preferred_element_type=jnp.float32
    )
    return (num, den)


def token_body(image, text_kv, modulation, w_qkv, w_out, q_gain, k_gain, region_mask):
    img_rows = image.shape[1]
    width_local = w_qkv.shape[2]
    heads_local = width_local // HEAD_DIM
    tokens = image[0].astype(jnp.float32)
    mods = modulation[0]
    normed = layer_norm(tokens, mods)
    qkv = jnp.einsum(
        "td,dcf->tcf",
        normed,
        lax.all_gather(w_qkv, "seq", axis=0, tiled=True),
        preferred_element_type=jnp.float32,
    )
    section_index = lax.axis_index("section")
    time_index = (section_index == 0).astype(jnp.float32)
    rows_index = lax.axis_index("seq") * img_rows + jnp.arange(img_rows, dtype=jnp.int32)
    cosine, sine = rope_tables(rows_index, time_index)
    query = apply_rope(
        rms_rows(qkv[:, 0].reshape(img_rows, heads_local, HEAD_DIM), q_gain), cosine, sine
    ).astype(jnp.bfloat16)
    keys = apply_rope(
        rms_rows(qkv[:, 1].reshape(img_rows, heads_local, HEAD_DIM), k_gain), cosine, sine
    ).astype(jnp.bfloat16)
    values = qkv[:, 2].astype(jnp.bfloat16)
    image_kv = jnp.stack([keys.reshape(img_rows, width_local), values], axis=1)
    own_kv = jnp.concatenate([image_kv, text_kv[0]], axis=0)
    enabled = (section_index == 1).astype(jnp.int32)
    local_mask = region_mask * enabled
    init = (
        jnp.zeros((heads_local, img_rows, HEAD_DIM), jnp.float32),
        jnp.zeros((heads_local, img_rows), jnp.float32),
    )
    carry = attend_piece(init, lax.all_gather(own_kv, "seq", axis=0, tiled=True), query, None)
    cond_local = lax.ppermute(image_kv, "section", [(0, 1)])
    keep = jnp.repeat(jnp.repeat(local_mask, TILE, axis=0), TILE, axis=1) > 0
    carry = attend_piece(carry, lax.all_gather(cond_local, "seq", axis=0, tiled=True), query, keep)
    num, den = carry
    attn = (num / den[..., None]).astype(jnp.bfloat16)
    attn = jnp.transpose(attn, (1, 0, 2)).reshape(img_rows, width_local)
    term = jnp.dot(attn, w_out, preferred_element_type=jnp.float32)
    branch = lax.psum_scatter(
        term.astype(jnp.bfloat16), "tp", scatter_dimension=1, tiled=True
    ).astype(jnp.float32)
    cols = branch.shape[1]
    offset = lax.axis_index("tp") * cols
    residual = lax.dynamic_slice_in_dim(tokens, offset, cols, 1)
    gate = lax.dynamic_slice_in_dim(mods[2], offset, cols, 0)
    out = residual + gate[None, :] * branch
    return out.astype(jnp.bfloat16)[None]


def body(*arrays):
    image, w_qkv, region_mask = arrays[0], arrays[3], arrays[7]
    seq = lax.axis_size("seq")
    one_head_each = (
        w_qkv.shape[2] // HEAD_DIM == seq
        and seq % 4 == 0
        and lax.axis_size("section") == 2
        and lax.axis_size("tp") == 2
        and w_qkv.shape[0] % 128 == 0
        and image.shape[1] == TILE
        and image.shape[1] * seq % (2 * BLOCK) == 0
        and arrays[1].shape[1] % 16 == 0
        and arrays[4].shape[1] % 1024 == 0
        and region_mask.shape[1] <= HEAD_DIM
    )
    return (head_body if one_head_each else token_body)(*arrays)


def solution(mesh):
    return jax.shard_map(
        body,
        mesh=mesh,
        in_specs=(
            P("section", "seq", None),
            P("section", "seq", None, "tp"),
            P("section", None, None),
            P("seq", None, "tp"),
            P("tp", None),
            P(),
            P(),
            P("seq", None),
        ),
        out_specs=P("section", "seq", "tp"),
        check_vma=False,
    )
```

```python
import jax
import jax.numpy as jnp
from jax import lax
from jax.experimental import pallas as pl
from jax.experimental.pallas import tpu as pltpu
from jax.sharding import PartitionSpec as P

HEAD_DIM = 128
GRID_W = 64
TILE = 128
VMEM_LIMIT = 56 * 1024 * 1024


def axis_freqs(width):
    return 10000.0 ** (-jnp.arange(0, width, 2).astype(jnp.float32) / width)


def rope_tables(rows_index, time_index):
    first = HEAD_DIM // 8
    rest = (HEAD_DIM - first) // 2
    row_pos = (rows_index // GRID_W).astype(jnp.float32)
    col_pos = (rows_index % GRID_W).astype(jnp.float32)
    time_pos = jnp.zeros_like(row_pos) + time_index
    angles = jnp.concatenate(
        [
            time_pos[:, None] * axis_freqs(first)[None],
            row_pos[:, None] * axis_freqs(rest)[None],
            col_pos[:, None] * axis_freqs(rest)[None],
        ],
        axis=-1,
    )
    return (jnp.cos(angles), jnp.sin(angles))


def layer_norm(tokens, mods):
    mean = jnp.mean(tokens, axis=-1, keepdims=True)
    var = jnp.mean((tokens - mean) ** 2, axis=-1, keepdims=True)
    return ((tokens - mean) * lax.rsqrt(var + 1e-06) * (1.0 + mods[1:2]) + mods[0:1]).astype(
        jnp.bfloat16
    )


VMEM = pl.BlockSpec(memory_space=pltpu.VMEM)
SMEM = pl.BlockSpec(memory_space=pltpu.SMEM)


def call(kernel, name, out_shape, flops, moved, exps, limit=VMEM_LIMIT, **spec):
    return pl.pallas_call(
        kernel,
        out_shape=out_shape,
        compiler_params=pltpu.CompilerParams(vmem_limit_bytes=limit),
        cost_estimate=pl.CostEstimate(flops=flops, bytes_accessed=moved, transcendentals=exps),
        name=name,
        **spec,
    )


def norm_kernel(tp_ref, image_ref, mods_ref, shared_ref, direct_ref):
    normed = layer_norm(image_ref[...].astype(jnp.float32), mods_ref[...])
    half = direct_ref.shape[0]
    piece = shared_ref.shape[0]
    direct_ref[...] = normed[half:]
    for t in range(half // piece):

        @pl.when(tp_ref[0] == t)
        def _(t=t):
            shared_ref[...] = normed[t * piece : (t + 1) * piece]


def norm_tokens(tp, image, mods):
    rows, depth = image.shape
    return call(
        norm_kernel, "norm_tokens",
        [
            jax.ShapeDtypeStruct((rows // 4, depth), jnp.bfloat16),
            jax.ShapeDtypeStruct((rows // 2, depth), jnp.bfloat16),
        ],
        10 * rows * depth, 4 * rows * depth, 0,
        in_specs=[SMEM, VMEM, VMEM],
        out_specs=[VMEM, VMEM],
    )(tp, image, mods)


def normed_rotated(x, gain, cosine, sine):
    x = x * lax.rsqrt(jnp.mean(x * x, axis=-1, keepdims=True) + 1e-06) * gain
    even = lax.broadcasted_iota(jnp.int32, x.shape, 1) % 2 == 0
    other = jnp.where(even, pltpu.roll(x, HEAD_DIM - 1, 1), pltpu.roll(x, 1, 1))
    return (x * cosine + other * sine).astype(jnp.bfloat16)


def project_kernel(kinds, counts, section_ref, x_ref, cos_ref, sin_ref, gain_ref, *refs):
    pairs = [refs[2 * i : 2 * i + 2] for i in range(len(counts))]
    out_refs, acc_ref = refs[2 * len(counts) : -1], refs[-1]
    step = pl.program_id(0)
    first = section_ref[0] == 0

    def piece(mine, peer, s, place):
        half = peer.shape[1] // place[1]
        at = slice(place[0] * half, (place[0] + 1) * half)
        a, b = mine[s, at, :], peer[s, at, :]
        return jnp.concatenate([jnp.where(first, a, b), jnp.where(first, b, a)], axis=0)

    w = jnp.concatenate(
        [
            jnp.concatenate(
                [piece(mine, peer, s, (k, count)) for s in range(mine.shape[0])], axis=0
            )
            for (mine, peer), count in zip(pairs, counts)
            for k in range(count)
        ],
        axis=1,
    )
    part = jnp.dot(x_ref[...], w, preferred_element_type=jnp.float32)

    @pl.when(step == 0)
    def _():
        acc_ref[...] = part

    @pl.when(step > 0)
    def _():
        acc_ref[...] += part

    @pl.when(step == pl.num_programs(0) - 1)
    def _():
        for place, kind in enumerate(kinds):
            value = acc_ref[:, place * HEAD_DIM : (place + 1) * HEAD_DIM]
            if kind < 2:
                value = normed_rotated(
                    value, gain_ref[kind : kind + 1, :], cos_ref[...], sin_ref[...]
                )
            if kind == 0:
                out_refs[-1][...] = value
            else:
                out_refs[0][kind - 1] = value.astype(jnp.bfloat16)


def project(kinds, section, x, tables, gains, *pairs):
    rows, depth = x.shape
    sources = pairs[0][0].shape[0]
    steps = 4
    out_shape, out_specs = [], []
    if 1 in kinds:
        out_shape.append(jax.ShapeDtypeStruct((2, rows, HEAD_DIM), jnp.bfloat16))
        out_specs.append(pl.BlockSpec((2, rows, HEAD_DIM), lambda k, s: (0, 0, 0)))
    if 0 in kinds:
        out_shape.append(jax.ShapeDtypeStruct((rows, HEAD_DIM), jnp.bfloat16))
        out_specs.append(pl.BlockSpec((rows, HEAD_DIM), lambda k, s: (0, 0)))

    def pieces(array):
        return pl.BlockSpec((sources // steps,) + array.shape[1:], lambda k, s: (k, 0, 0))

    half = depth // sources // 2
    counts = [peer.shape[1] // half for _, peer in pairs]
    weights = [array for pair in pairs for array in pair]
    table = pl.BlockSpec((rows, HEAD_DIM), lambda k, s: (0, 0))
    return call(
        lambda *refs: project_kernel(kinds, counts, *refs),
        "project_" + "".join("qkv"[k] for k in kinds),
        out_shape,
        2 * len(kinds) * rows * depth * HEAD_DIM, 2 * (x.size + sum(w.size for w in weights)), 0,
        grid_spec=pltpu.PrefetchScalarGridSpec(
            num_scalar_prefetch=1,
            grid=(steps,),
            in_specs=[pl.BlockSpec((rows, depth // steps), lambda k, s: (0, k))]
            + [table, table, pl.BlockSpec((2, HEAD_DIM), lambda k, s: (0, 0))]
            + [pieces(w) for w in weights],
            out_specs=out_specs,
            scratch_shapes=[pltpu.VMEM((rows, len(kinds) * HEAD_DIM), jnp.float32)],
        ),
    )(section, x, *tables, gains, *weights)


def weights_of(query, keys):
    scores = lax.dot_general(
        query, keys, (((1,), (1,)), ((), ())), preferred_element_type=jnp.float32
    )
    return jnp.exp(scores * (1.0 / HEAD_DIM**0.5))


def summed(weights, values):
    den = jnp.sum(weights, axis=-1, keepdims=True)
    num = jnp.dot(weights.astype(jnp.bfloat16), values, preferred_element_type=jnp.float32)
    return num, den


def kept_weights(query, cond_ref, keep):
    weights = weights_of(query, cond_ref[0])
    rows, keys = weights.shape
    tiles = keep.shape[0]
    return (weights.reshape(tiles, rows // tiles, keys) * keep[:, None, :]).reshape(rows, keys)


def query_blocks(qa, qb, tiles):
    rows = qa.shape[0]
    for b in range(2):
        piece = rows // 2 // tiles
        yield qa, b * rows // 2, b * rows // 2, slice(0, tiles), slice(b * piece, (b + 1) * piece)
    piece = rows // tiles
    for b in range(2):
        at = slice(b * tiles // 2, (b + 1) * tiles // 2)
        yield qb, b * rows // 2, rows + b * rows // 2, at, slice(piece, 2 * piece)


def own_kernel(section_ref, keep_ref, qa, qb, kva, kvb, text, conda, num_ref, den_ref):
    size = qa.shape[0] // 2
    for q_ref, start, place, _, _ in query_blocks(qa, qb, keep_ref.shape[0]):
        query = q_ref[start : start + size, :]
        num, den = 0.0, 0.0
        for ref in (kva, kvb, text):
            more = summed(weights_of(query, ref[0]), ref[1])
            num, den = num + more[0], den + more[1]
        num_ref[place : place + size, :] = num
        den_ref[place : place + size, :] = jnp.broadcast_to(den, num.shape)

    @pl.when(section_ref[0] != 0)
    def _():
        for q_ref, start, place, tiles, _ in query_blocks(qa, qb, keep_ref.shape[0]):
            query = q_ref[start : start + size, :]
            num, den = summed(kept_weights(query, conda, keep_ref[tiles, :]), conda[1])
            num_ref[place : place + size, :] += num
            den_ref[place : place + size, :] += jnp.broadcast_to(den, num.shape)


def cond_kernel(section_ref, keep_ref, qa, qb, condb, num_ref, den_ref, out_ref):
    size = qa.shape[0] // 2

    def store(tiles, shard_rows, num, den):
        value = (num / den).astype(jnp.bfloat16)
        out_ref[tiles, shard_rows, :] = value.reshape(tiles.stop - tiles.start, -1, HEAD_DIM)

    @pl.when(section_ref[0] == 0)
    def _():
        for _, _, place, tiles, shard_rows in query_blocks(qa, qb, keep_ref.shape[0]):
            at = slice(place, place + size)
            store(tiles, shard_rows, num_ref[at, :], den_ref[at, :])

    @pl.when(section_ref[0] != 0)
    def _():
        for q_ref, start, place, tiles, shard_rows in query_blocks(qa, qb, keep_ref.shape[0]):
            query = q_ref[start : start + size, :]
            at = slice(place, place + size)
            num, den = summed(kept_weights(query, condb, keep_ref[tiles, :]), condb[1])
            store(tiles, shard_rows, num_ref[at, :] + num, den_ref[at, :] + den)


def attend_own(section, keep, queries, kvs, text, cond):
    rows = 2 * queries[0].shape[0]
    keys = rows + text.shape[1] + cond.shape[1]
    return call(
        own_kernel, "attend_own", [jax.ShapeDtypeStruct((rows, HEAD_DIM), jnp.float32)] * 2,
        4 * rows * keys * HEAD_DIM, 2 * rows * HEAD_DIM * 10, rows * keys,
        in_specs=[SMEM] + [VMEM] * 7,
        out_specs=[VMEM] * 2,
    )(section, keep, *queries, *kvs, text, cond)


def attend_cond(section, keep, queries, cond, num, den):
    rows, seq = num.shape[0], keep.shape[0]
    keys = cond.shape[1]
    return call(
        cond_kernel, "attend_cond",
        jax.ShapeDtypeStruct((seq, rows // seq, HEAD_DIM), jnp.bfloat16),
        4 * rows * keys * HEAD_DIM, 2 * rows * HEAD_DIM * 8, rows * keys,
        in_specs=[SMEM] + [VMEM] * 6,
        out_specs=VMEM,
    )(section, keep, *queries, cond, num, den)


def token_rows(attn_ref):
    return jnp.concatenate([attn_ref[h] for h in range(attn_ref.shape[0])], axis=1)


def sent_kernel(half_ref, attn_ref, w_ref, out_ref):
    branch = jnp.dot(token_rows(attn_ref), w_ref[...], preferred_element_type=jnp.float32)
    out_ref[...] = branch.astype(jnp.bfloat16)


def kept_kernel(half_ref, attn_ref, w_ref, image_ref, gate_ref, out_ref):
    branch = jnp.dot(token_rows(attn_ref), w_ref[...], preferred_element_type=jnp.float32)
    out_ref[...] = image_ref[...].astype(jnp.float32) + gate_ref[...] * branch


def project_out(half, attn, w_out, image=None, gate=None):
    rows = attn.shape[1]
    depth, width = w_out.shape[0], w_out.shape[1] // 2
    block = 512
    steps = width // block

    def columns(height):
        return pl.BlockSpec((height, block), lambda i, half: (0, half[0] * steps + i))

    kept = image is not None
    return call(
        kept_kernel if kept else sent_kernel, "out_kept" if kept else "out_sent",
        jax.ShapeDtypeStruct((rows, width), jnp.float32 if kept else jnp.bfloat16),
        2 * rows * depth * width, 2 * depth * width, 0, 24 * 1024 * 1024,
        grid_spec=pltpu.PrefetchScalarGridSpec(
            num_scalar_prefetch=1,
            grid=(steps,),
            in_specs=[pl.BlockSpec(attn.shape, lambda i, half: (0, 0, 0)), columns(depth)]
            + ([columns(rows), columns(1)] if kept else []),
            out_specs=pl.BlockSpec((rows, block), lambda i, half: (0, i)),
        ),
    )(half, attn, w_out, *((image, gate) if kept else ()))


def lane_tables(rows_index, time_index):
    first = HEAD_DIM // 8
    rest = (HEAD_DIM - first) // 2
    freqs = jnp.concatenate([axis_freqs(first), axis_freqs(rest), axis_freqs(rest)])
    freqs = jnp.repeat(freqs, 2)[None]
    lane = jnp.arange(HEAD_DIM, dtype=jnp.int32)[None]
    row_pos = (rows_index // GRID_W).astype(jnp.float32)[:, None]
    col_pos = (rows_index % GRID_W).astype(jnp.float32)[:, None]
    ids = jnp.where(lane < first, time_index, jnp.where(lane < first + rest, row_pos, col_pos))
    angles = ids * freqs
    return jnp.cos(angles), jnp.sin(angles) * jnp.where(lane % 2 == 0, -1.0, 1.0)


def head_body(image, text_kv, modulation, w_qkv, w_out, q_gain, k_gain, region_mask):
    seq = lax.axis_size("seq")
    img_rows = image.shape[1]
    depth = w_qkv.shape[0]
    section = lax.axis_index("section")
    tp = lax.axis_index("tp")
    core = lax.axis_index("seq") % 2
    mods = modulation[0]
    section_at = section.astype(jnp.int32).reshape(1)
    tp_at = tp.astype(jnp.int32).reshape(1)
    both = [(0, 1), (1, 0)]

    half = depth // 2
    w_half = lax.dynamic_slice_in_dim(w_qkv.transpose(1, 0, 2), section * half, half, 1)
    w_half = w_half.reshape(3, half, seq, HEAD_DIM).transpose(2, 0, 1, 3)
    text = text_kv[0].reshape(-1, 2, seq, HEAD_DIM).transpose(2, 0, 1, 3).reshape(seq, -1, HEAD_DIM)
    mask = jnp.pad(
        region_mask.astype(jnp.bfloat16), ((0, 15), (0, HEAD_DIM - region_mask.shape[1]))
    )
    mask = jnp.broadcast_to(mask, (seq,) + mask.shape)
    kv_mine = lax.all_to_all(w_half[:, 1:].reshape(seq, -1, HEAD_DIM), "seq", 0, 0)
    kv_peer = lax.ppermute(kv_mine, "section", both)
    q_mine = lax.all_to_all(jnp.concatenate([w_half[:, 0], text, mask], axis=1), "seq", 0, 0)
    q_peer = lax.ppermute(q_mine[:, :half], "section", both)
    text = q_mine[:, half:-16].reshape(-1, 2, HEAD_DIM).transpose(1, 0, 2)
    keep = q_mine[:, -16, : region_mask.shape[1]].astype(jnp.float32)

    shared, direct = norm_tokens(tp_at, image[0], mods)
    ours = lax.all_gather(shared, "seq", axis=0, tiled=True)
    count = ours.shape[0] // 2
    theirs = lax.ppermute(lax.dynamic_slice_in_dim(ours, core * count, count, 0), "tp", both)
    swapped = lax.ppermute(theirs, "seq", [(s, s ^ 1) for s in range(seq)])
    theirs = jnp.concatenate(
        [jnp.where(core == 0, theirs, swapped), jnp.where(core == 0, swapped, theirs)], axis=0
    )
    x_a = jnp.concatenate(
        [jnp.where(tp == 0, ours, theirs), jnp.where(tp == 0, theirs, ours)], axis=0
    )
    x_b = lax.all_gather(direct, "seq", axis=0, tiled=True)

    time_index = (section == 0).astype(jnp.float32)
    index = jnp.arange(x_a.shape[0], dtype=jnp.int32)
    piece = img_rows // 4
    index_a = index // piece % seq * img_rows + index // (seq * piece) * piece + index % piece
    index_b = index // (2 * piece) * img_rows + 2 * piece + index % (2 * piece)
    tables_a = lane_tables(index_a, time_index)
    tables_b = lane_tables(index_b, time_index)
    gains = jnp.stack([q_gain, k_gain])
    keep_a = jnp.tile(jnp.repeat(keep, piece, axis=1), (1, 2))
    keep_b = jnp.repeat(keep, 2 * piece, axis=1)

    kv_pair, q_pair = (kv_mine, kv_peer), (q_mine, q_peer)
    (kv_a,) = project((1, 2), section_at, x_a, tables_a, gains, kv_pair)
    cond_a = lax.ppermute(kv_a, "section", [(0, 1)])
    (q_a,) = project((0,), section_at, x_a, tables_a, gains, q_pair)
    (kv_b,) = project((1, 2), section_at, x_b, tables_b, gains, kv_pair)
    cond_b = lax.ppermute(kv_b, "section", [(0, 1)])
    (q_b,) = project((0,), section_at, x_b, tables_b, gains, q_pair)
    queries = (q_a, q_b)
    num, den = attend_own(section_at, keep_a, queries, (kv_a, kv_b), text, cond_a)
    attn = attend_cond(section_at, keep_b, queries, cond_b, num, den)

    attn = lax.all_to_all(attn, "seq", 0, 0)
    gate = mods[2:3]
    other = lax.ppermute(project_out(1 - tp_at, attn, w_out), "tp", both)
    kept = project_out(tp_at, attn, w_out, image[0], gate)
    gate = lax.dynamic_slice_in_dim(gate, tp * other.shape[1], other.shape[1], 1)
    return (kept + gate * other.astype(jnp.float32)).astype(jnp.bfloat16)[None]


def rms_rows(x, gain):
    return x * lax.rsqrt(jnp.mean(x * x, axis=-1, keepdims=True) + 1e-06) * gain


def apply_rope(x, cosine, sine):
    rows, heads_here = (x.shape[0], x.shape[1])
    pairs = x.reshape(rows, heads_here, HEAD_DIM // 2, 2)
    first = pairs[..., 0]
    second = pairs[..., 1]
    cosine = cosine[:, None, :]
    sine = sine[:, None, :]
    rotated = jnp.stack([first * cosine - second * sine, first * sine + second * cosine], axis=-1)
    return rotated.reshape(rows, heads_here, HEAD_DIM)


def attend_piece(carry, keys_vals, query, keep):
    num, den = carry
    rows = keys_vals.shape[0]
    heads_local = query.shape[1]
    piece_k = keys_vals[:, 0].reshape(rows, heads_local, HEAD_DIM)
    piece_v = keys_vals[:, 1].reshape(rows, heads_local, HEAD_DIM)
    scores = jnp.einsum("qhd,khd->hqk", query, piece_k, preferred_element_type=jnp.float32) * (
        1.0 / HEAD_DIM**0.5
    )
    weights = jnp.exp(scores)
    if keep is not None:
        weights = jnp.where(keep[None], weights, 0.0)
    den = den + jnp.sum(weights, axis=-1)
    num = num + jnp.einsum(
        "hqk,khd->hqd", weights.astype(jnp.bfloat16), piece_v, preferred_element_type=jnp.float32
    )
    return (num, den)


def token_body(image, text_kv, modulation, w_qkv, w_out, q_gain, k_gain, region_mask):
    img_rows = image.shape[1]
    width_local = w_qkv.shape[2]
    heads_local = width_local // HEAD_DIM
    tokens = image[0].astype(jnp.float32)
    mods = modulation[0]
    normed = layer_norm(tokens, mods)
    qkv = jnp.einsum(
        "td,dcf->tcf",
        normed,
        lax.all_gather(w_qkv, "seq", axis=0, tiled=True),
        preferred_element_type=jnp.float32,
    )
    section_index = lax.axis_index("section")
    time_index = (section_index == 0).astype(jnp.float32)
    rows_index = lax.axis_index("seq") * img_rows + jnp.arange(img_rows, dtype=jnp.int32)
    cosine, sine = rope_tables(rows_index, time_index)
    query = apply_rope(
        rms_rows(qkv[:, 0].reshape(img_rows, heads_local, HEAD_DIM), q_gain), cosine, sine
    ).astype(jnp.bfloat16)
    keys = apply_rope(
        rms_rows(qkv[:, 1].reshape(img_rows, heads_local, HEAD_DIM), k_gain), cosine, sine
    ).astype(jnp.bfloat16)
    values = qkv[:, 2].astype(jnp.bfloat16)
    image_kv = jnp.stack([keys.reshape(img_rows, width_local), values], axis=1)
    own_kv = jnp.concatenate([image_kv, text_kv[0]], axis=0)
    enabled = (section_index == 1).astype(jnp.int32)
    local_mask = region_mask * enabled
    init = (
        jnp.zeros((heads_local, img_rows, HEAD_DIM), jnp.float32),
        jnp.zeros((heads_local, img_rows), jnp.float32),
    )
    carry = attend_piece(init, lax.all_gather(own_kv, "seq", axis=0, tiled=True), query, None)
    cond_local = lax.ppermute(image_kv, "section", [(0, 1)])
    keep = jnp.repeat(jnp.repeat(local_mask, TILE, axis=0), TILE, axis=1) > 0
    carry = attend_piece(carry, lax.all_gather(cond_local, "seq", axis=0, tiled=True), query, keep)
    num, den = carry
    attn = (num / den[..., None]).astype(jnp.bfloat16)
    attn = jnp.transpose(attn, (1, 0, 2)).reshape(img_rows, width_local)
    term = jnp.dot(attn, w_out, preferred_element_type=jnp.float32)
    branch = lax.psum_scatter(
        term.astype(jnp.bfloat16), "tp", scatter_dimension=1, tiled=True
    ).astype(jnp.float32)
    cols = branch.shape[1]
    offset = lax.axis_index("tp") * cols
    residual = lax.dynamic_slice_in_dim(tokens, offset, cols, 1)
    gate = lax.dynamic_slice_in_dim(mods[2], offset, cols, 0)
    out = residual + gate[None, :] * branch
    return out.astype(jnp.bfloat16)[None]


def body(*arrays):
    image, w_qkv, region_mask = arrays[0], arrays[3], arrays[7]
    seq = lax.axis_size("seq")
    one_head_each = (
        w_qkv.shape[2] // HEAD_DIM == seq
        and seq % 4 == 0
        and lax.axis_size("section") == 2
        and lax.axis_size("tp") == 2
        and w_qkv.shape[0] % 128 == 0
        and image.shape[1] == TILE
        and region_mask.shape == (1, seq)
        and arrays[1].shape[1] % 16 == 0
        and arrays[4].shape[1] % 1024 == 0
    )
    return (head_body if one_head_each else token_body)(*arrays)


def solution(mesh):
    return jax.shard_map(
        body,
        mesh=mesh,
        in_specs=(
            P("section", "seq", None),
            P("section", "seq", None, "tp"),
            P("section", None, None),
            P("seq", None, "tp"),
            P("tp", None),
            P(),
            P(),
            P("seq", None),
        ),
        out_specs=P("section", "seq", "tp"),
        check_vma=False,
    )
```

```python
import jax
import jax.numpy as jnp
from jax import lax
from jax.experimental import pallas as pl
from jax.experimental.pallas import tpu as pltpu
from jax.sharding import PartitionSpec as P

HEAD_DIM = 128
GRID_W = 64
TILE = 128
VMEM_LIMIT = 20 * 1024 * 1024


def axis_freqs(width):
    return 10000.0 ** (-jnp.arange(0, width, 2).astype(jnp.float32) / width)


def rope_tables(rows_index, time_index):
    first = HEAD_DIM // 8
    rest = (HEAD_DIM - first) // 2
    row_pos = (rows_index // GRID_W).astype(jnp.float32)
    col_pos = (rows_index % GRID_W).astype(jnp.float32)
    time_pos = jnp.zeros_like(row_pos) + time_index
    angles = jnp.concatenate(
        [
            time_pos[:, None] * axis_freqs(first)[None],
            row_pos[:, None] * axis_freqs(rest)[None],
            col_pos[:, None] * axis_freqs(rest)[None],
        ],
        axis=-1,
    )
    return (jnp.cos(angles), jnp.sin(angles))


def layer_norm(tokens, mods):
    mean = jnp.mean(tokens, axis=-1, keepdims=True)
    var = jnp.mean((tokens - mean) ** 2, axis=-1, keepdims=True)
    return ((tokens - mean) * lax.rsqrt(var + 1e-06) * (1.0 + mods[1:2]) + mods[0:1]).astype(
        jnp.bfloat16
    )


VMEM = pl.BlockSpec(memory_space=pltpu.VMEM)
SMEM = pl.BlockSpec(memory_space=pltpu.SMEM)


def call(kernel, name, out_shape, flops, moved, exps, limit=VMEM_LIMIT, **spec):
    return pl.pallas_call(
        kernel,
        out_shape=out_shape,
        compiler_params=pltpu.CompilerParams(vmem_limit_bytes=limit),
        cost_estimate=pl.CostEstimate(flops=flops, bytes_accessed=moved, transcendentals=exps),
        name=name,
        **spec,
    )


def norm_kernel(tp_ref, image_ref, mods_ref, full_ref, part_ref):
    mods = jnp.concatenate([mods_ref[0], mods_ref[1]], axis=0)
    normed = layer_norm(image_ref[...].astype(jnp.float32), mods)
    part = part_ref.shape[0]
    for t in range(2):

        @pl.when(tp_ref[0] == t)
        def _(t=t):
            ours, theirs = normed[t * part : (t + 1) * part], normed[(1 - t) * part : (2 - t) * part]
            full_ref[:part, :] = ours
            full_ref[part:, :] = theirs
            part_ref[...] = ours


def norm_tokens(tp, image, mods):
    rows, depth = image.shape
    return call(
        norm_kernel, "norm_tokens",
        [
            jax.ShapeDtypeStruct((rows, depth), jnp.bfloat16),
            jax.ShapeDtypeStruct((rows // 2, depth), jnp.bfloat16),
        ],
        10 * rows * depth, 4 * rows * depth, 0,
        in_specs=[SMEM, VMEM, VMEM],
        out_specs=[VMEM, VMEM],
    )(tp, image, mods)


def normed_rotated(x, gain, cosine, sine):
    x = x * lax.rsqrt(jnp.mean(x * x, axis=-1, keepdims=True) + 1e-06) * gain
    even = lax.broadcasted_iota(jnp.int32, x.shape, 1) % 2 == 0
    other = jnp.where(even, pltpu.roll(x, HEAD_DIM - 1, 1), pltpu.roll(x, 1, 1))
    return (x * cosine + other * sine).astype(jnp.bfloat16)


def project_kernel(kinds, pieces, section_ref, mine, peer, cos_ref, sin_ref, gain_ref, *refs):
    x_refs, out_refs, acc_ref = refs[:pieces], refs[pieces:-1], refs[-1]
    step = pl.program_id(0)
    half = peer.shape[1] // 3
    first = section_ref[0] == 0

    def rows_of(s, kind):
        at = slice(kind * half, (kind + 1) * half)
        a, b = mine[s, at, :], peer[s, at, :]
        return jnp.concatenate([jnp.where(first, a, b), jnp.where(first, b, a)], axis=0)

    w = jnp.concatenate(
        [
            jnp.concatenate([rows_of(s, kind) for s in range(mine.shape[0])], axis=0)
            for kind in kinds
        ],
        axis=1,
    )
    x = jnp.concatenate([ref[...] for ref in x_refs], axis=0)
    part = jnp.dot(x, w, preferred_element_type=jnp.float32)

    @pl.when(step == 0)
    def _():
        acc_ref[...] = part

    @pl.when(step > 0)
    def _():
        acc_ref[...] += part

    @pl.when(step == pl.num_programs(0) - 1)
    def _():
        for place, kind in enumerate(kinds):
            value = acc_ref[:, place * HEAD_DIM : (place + 1) * HEAD_DIM]
            if kind < 2:
                value = normed_rotated(
                    value, gain_ref[kind : kind + 1, :], cos_ref[...], sin_ref[...]
                )
            if kind == 0:
                out_refs[0][...] = value
            else:
                out_refs[0][kind - 1] = value.astype(jnp.bfloat16)


def project(kinds, section, pieces, mine, peer, cosine, sine, gains):
    depth = pieces[0].shape[1]
    rows = sum(p.shape[0] for p in pieces)
    sources = mine.shape[0]
    steps = 4
    shape = (rows, HEAD_DIM) if kinds == (0,) else (2, rows, HEAD_DIM)

    def weights(array):
        return pl.BlockSpec((sources // steps,) + array.shape[1:], lambda k, s: (k, 0, 0))

    table = pl.BlockSpec((rows, HEAD_DIM), lambda k, s: (0, 0))
    return call(
        lambda *refs: project_kernel(kinds, len(pieces), *refs),
        "project_" + "".join("qkv"[k] for k in kinds),
        jax.ShapeDtypeStruct(shape, jnp.bfloat16),
        2 * len(kinds) * rows * depth * HEAD_DIM, 2 * (rows * depth + mine.size + peer.size), 0,
        grid_spec=pltpu.PrefetchScalarGridSpec(
            num_scalar_prefetch=1,
            grid=(steps,),
            in_specs=[weights(mine), weights(peer)]
            + [table, table, pl.BlockSpec((2, HEAD_DIM), lambda k, s: (0, 0))]
            + [pl.BlockSpec((p.shape[0], depth // steps), lambda k, s: (0, k)) for p in pieces],
            out_specs=pl.BlockSpec(shape, lambda k, s: (0,) * len(shape)),
            scratch_shapes=[pltpu.VMEM((rows, len(kinds) * HEAD_DIM), jnp.float32)],
        ),
    )(section, mine, peer, cosine, sine, gains, *pieces)


def weights_of(query, keys):
    scores = lax.dot_general(
        query, keys, (((1,), (1,)), ((), ())), preferred_element_type=jnp.float32
    )
    return jnp.exp(scores * (1.0 / HEAD_DIM**0.5))


def summed(weights, values):
    den = jnp.sum(weights, axis=-1, keepdims=True)
    num = jnp.dot(weights.astype(jnp.bfloat16), values, preferred_element_type=jnp.float32)
    return num, den


def kept_weights(query, cond_ref, keep):
    weights = weights_of(query, cond_ref[0])
    rows, keys = weights.shape
    groups = keep.shape[0]
    return (weights.reshape(groups, rows // groups, keys) * keep[:, None, :]).reshape(rows, keys)


BLOCK = 256


def own_kernel(section_ref, keep_ref, q_ref, kva, kvb, text, conda, num_ref, den_ref):
    rows = q_ref.shape[0]
    groups = keep_ref.shape[0] * BLOCK // rows
    for b in range(rows // BLOCK):
        at = slice(b * BLOCK, (b + 1) * BLOCK)
        num, den = 0.0, 0.0
        for ref in (kva, kvb, text):
            more = summed(weights_of(q_ref[at, :], ref[0]), ref[1])
            num, den = num + more[0], den + more[1]
        num_ref[at, :] = num
        den_ref[at, :] = jnp.broadcast_to(den, num.shape)

    @pl.when(section_ref[0] != 0)
    def _():
        for b in range(rows // BLOCK):
            at = slice(b * BLOCK, (b + 1) * BLOCK)
            keep = keep_ref[b * groups : (b + 1) * groups, :]
            num, den = summed(kept_weights(q_ref[at, :], conda, keep), conda[1])
            num_ref[at, :] += num
            den_ref[at, :] += jnp.broadcast_to(den, num.shape)


def cond_kernel(section_ref, place_ref, keep_ref, q_ref, condb, num_ref, den_ref, out_ref):
    rows = q_ref.shape[0]
    groups = keep_ref.shape[0] * BLOCK // rows
    size = BLOCK // groups

    def store(b, num, den):
        value = (num / den).astype(jnp.bfloat16)
        for g in range(groups):
            shard, part = place_ref[0, b * groups + g], place_ref[1, b * groups + g]
            at = pl.ds(pl.multiple_of(part * size, size), size)
            out_ref[shard, at, :] = value[g * size : (g + 1) * size]

    @pl.when(section_ref[0] == 0)
    def _():
        for b in range(rows // BLOCK):
            at = slice(b * BLOCK, (b + 1) * BLOCK)
            store(b, num_ref[at, :], den_ref[at, :])

    @pl.when(section_ref[0] != 0)
    def _():
        for b in range(rows // BLOCK):
            at = slice(b * BLOCK, (b + 1) * BLOCK)
            keep = keep_ref[b * groups : (b + 1) * groups, :]
            num, den = summed(kept_weights(q_ref[at, :], condb, keep), condb[1])
            store(b, num_ref[at, :] + num, den_ref[at, :] + den)


def attend_own(section, keep, query, kvs, text, cond):
    rows = query.shape[0]
    keys = rows + text.shape[1] + cond.shape[1]
    return call(
        own_kernel, "attend_own", [jax.ShapeDtypeStruct((rows, HEAD_DIM), jnp.float32)] * 2,
        4 * rows * keys * HEAD_DIM, 2 * rows * HEAD_DIM * 10, rows * keys,
        in_specs=[SMEM] + [VMEM] * 6,
        out_specs=[VMEM] * 2,
    )(section, keep, query, *kvs, text, cond)


def attend_cond(section, place, keep, query, cond, num, den, seq):
    rows = num.shape[0]
    keys = cond.shape[1]
    return call(
        cond_kernel, "attend_cond",
        jax.ShapeDtypeStruct((seq, rows // seq, HEAD_DIM), jnp.bfloat16),
        4 * rows * keys * HEAD_DIM, 2 * rows * HEAD_DIM * 8, rows * keys,
        in_specs=[SMEM, SMEM] + [VMEM] * 5,
        out_specs=VMEM,
    )(section, place, keep, query, cond, num, den)


def token_rows(attn_ref):
    return jnp.concatenate([attn_ref[h] for h in range(attn_ref.shape[0])], axis=1)


def sent_kernel(half_ref, attn_ref, w_ref, out_ref):
    branch = jnp.dot(token_rows(attn_ref), w_ref[...], preferred_element_type=jnp.float32)
    out_ref[...] = branch.astype(jnp.bfloat16)


def kept_kernel(half_ref, attn_ref, w_ref, image_ref, gate_ref, out_ref):
    branch = jnp.dot(token_rows(attn_ref), w_ref[...], preferred_element_type=jnp.float32)
    out_ref[...] = image_ref[...].astype(jnp.float32) + gate_ref[...] * branch


def project_out(half, attn, w_out, image=None, gate=None):
    rows = attn.shape[1]
    depth, width = w_out.shape[0], w_out.shape[1] // 2
    block = 512
    steps = width // block

    def columns(height):
        return pl.BlockSpec((height, block), lambda i, half: (0, half[0] * steps + i))

    kept = image is not None
    return call(
        kept_kernel if kept else sent_kernel, "out_kept" if kept else "out_sent",
        jax.ShapeDtypeStruct((rows, width), jnp.float32 if kept else jnp.bfloat16),
        2 * rows * depth * width, 2 * depth * width, 0,
        grid_spec=pltpu.PrefetchScalarGridSpec(
            num_scalar_prefetch=1,
            grid=(steps,),
            in_specs=[pl.BlockSpec(attn.shape, lambda i, half: (0, 0, 0)), columns(depth)]
            + ([columns(rows), columns(1)] if kept else []),
            out_specs=pl.BlockSpec((rows, block), lambda i, half: (0, i)),
        ),
    )(half, attn, w_out, *((image, gate) if kept else ()))


def lane_tables(rows_index, time_index):
    first = HEAD_DIM // 8
    rest = (HEAD_DIM - first) // 2
    freqs = jnp.concatenate([axis_freqs(first), axis_freqs(rest), axis_freqs(rest)])
    freqs = jnp.repeat(freqs, 2)[None]
    lane = jnp.arange(HEAD_DIM, dtype=jnp.int32)[None]
    row_pos = (rows_index // GRID_W).astype(jnp.float32)[:, None]
    col_pos = (rows_index % GRID_W).astype(jnp.float32)[:, None]
    ids = jnp.where(lane < first, time_index, jnp.where(lane < first + rest, row_pos, col_pos))
    angles = ids * freqs
    return jnp.cos(angles), jnp.sin(angles) * jnp.where(lane % 2 == 0, -1.0, 1.0)


def z_pairs(seq, pairs):
    return [(2 * a + core, 2 * b + core) for a, b in pairs for core in range(2)]


def head_body(image, text_kv, modulation, w_qkv, w_out, q_gain, k_gain, region_mask):
    seq = lax.axis_size("seq")
    img_rows = image.shape[1]
    depth = w_qkv.shape[0]
    section = lax.axis_index("section")
    tp = lax.axis_index("tp")
    chip, core = lax.axis_index("seq") // 2, lax.axis_index("seq") % 2
    mods = modulation[0]
    section_at = section.astype(jnp.int32).reshape(1)
    tp_at = tp.astype(jnp.int32).reshape(1)
    both = [(0, 1), (1, 0)]

    half = depth // 2
    w_half = lax.dynamic_slice_in_dim(w_qkv.transpose(1, 0, 2), section * half, half, 1)
    w_half = w_half.reshape(3, half, seq, HEAD_DIM).transpose(2, 0, 1, 3).reshape(seq, -1, HEAD_DIM)
    text = text_kv[0].reshape(-1, 2, seq, HEAD_DIM).transpose(2, 0, 1, 3).reshape(seq, -1, HEAD_DIM)
    mask = jnp.pad(
        region_mask.astype(jnp.bfloat16), ((0, 15), (0, HEAD_DIM - region_mask.shape[1]))
    )
    mask = jnp.broadcast_to(mask, (seq,) + mask.shape)
    mine = lax.all_to_all(jnp.concatenate([w_half, text, mask], axis=1), "seq", 0, 0)
    peer = lax.ppermute(mine[:, : 3 * half], "section", both)
    text = mine[:, 3 * half : -16].reshape(-1, 2, HEAD_DIM).transpose(1, 0, 2)
    keep = mine[:, -16, : region_mask.shape[1]].astype(jnp.float32)

    full, part = norm_tokens(tp_at, image[0], modulation.transpose(1, 0, 2))

    def along_z(x, pairs):
        return lax.ppermute(x, "seq", z_pairs(seq, pairs))

    near = along_z(part, [(0, 1), (1, 0), (2, 3), (3, 2)])
    middle = along_z(part, [(1, 2), (2, 1)])
    far = along_z(near, [(1, 2), (2, 1)])
    middle_end = along_z(middle, [(1, 0), (2, 3)])
    far_end = along_z(far, [(1, 0), (2, 3)])
    inner = (chip == 1) | (chip == 2)
    third = jnp.where(inner, middle, middle_end)
    fourth = jnp.where(inner, far, far_end)
    groups = [full]
    for came in (near, third, fourth):
        groups.append(jnp.concatenate([came, lax.ppermute(came, "tp", both)], axis=0))
    pieces = [
        (g, lax.ppermute(g, "seq", [(s, s ^ 1) for s in range(seq)])) for g in groups
    ]

    upper = chip >= 2
    chips = jnp.stack([chip, chip ^ 1, jnp.where(upper, 1, 2), jnp.where(upper, 0, 3)])
    cores = jnp.stack([core, 1 - core])
    parts = jnp.stack([tp, 1 - tp])
    shards = chips[:, None, None] * 2 + cores[None, :, None] + 0 * parts[None, None, :]
    parts = parts[None, None, :] + 0 * shards
    shards, parts = shards.reshape(-1).astype(jnp.int32), parts.reshape(-1).astype(jnp.int32)
    size = img_rows // 2
    first_row = shards * img_rows + parts * size
    rows_index = (first_row[:, None] + jnp.arange(size, dtype=jnp.int32)[None]).reshape(-1)
    cosine, sine = lane_tables(rows_index, (section == 0).astype(jnp.float32))
    gains = jnp.stack([q_gain, k_gain])
    chosen = (shards[:, None] == jnp.arange(seq)[None]).astype(jnp.float32)
    keep = jnp.repeat(chosen @ keep @ chosen.T, size, axis=1)

    rows = rows_index.shape[0] // 2
    a, b = list(pieces[0] + pieces[1]), list(pieces[2] + pieces[3])
    kv_a = project((1, 2), section_at, a, mine, peer, cosine[:rows], sine[:rows], gains)
    cond_a = lax.ppermute(kv_a, "section", [(0, 1)])
    kv_b = project((1, 2), section_at, b, mine, peer, cosine[rows:], sine[rows:], gains)
    cond_b = lax.ppermute(kv_b, "section", [(0, 1)])
    query = project((0,), section_at, a + b, mine, peer, cosine, sine, gains)
    num, den = attend_own(section_at, keep[:, :rows], query, (kv_a, kv_b), text, cond_a)
    place = jnp.stack([shards, parts])
    attn = attend_cond(section_at, place, keep[:, rows:], query, cond_b, num, den, seq)

    attn = lax.all_to_all(attn, "seq", 0, 0)
    gate = mods[2:3]
    other = lax.ppermute(project_out(1 - tp_at, attn, w_out), "tp", both)
    kept = project_out(tp_at, attn, w_out, image[0], gate)
    gate = lax.dynamic_slice_in_dim(gate, tp * other.shape[1], other.shape[1], 1)
    return (kept + gate * other.astype(jnp.float32)).astype(jnp.bfloat16)[None]


def rms_rows(x, gain):
    return x * lax.rsqrt(jnp.mean(x * x, axis=-1, keepdims=True) + 1e-06) * gain


def apply_rope(x, cosine, sine):
    rows, heads_here = (x.shape[0], x.shape[1])
    pairs = x.reshape(rows, heads_here, HEAD_DIM // 2, 2)
    first = pairs[..., 0]
    second = pairs[..., 1]
    cosine = cosine[:, None, :]
    sine = sine[:, None, :]
    rotated = jnp.stack([first * cosine - second * sine, first * sine + second * cosine], axis=-1)
    return rotated.reshape(rows, heads_here, HEAD_DIM)


def attend_piece(carry, keys_vals, query, keep):
    num, den = carry
    rows = keys_vals.shape[0]
    heads_local = query.shape[1]
    piece_k = keys_vals[:, 0].reshape(rows, heads_local, HEAD_DIM)
    piece_v = keys_vals[:, 1].reshape(rows, heads_local, HEAD_DIM)
    scores = jnp.einsum("qhd,khd->hqk", query, piece_k, preferred_element_type=jnp.float32) * (
        1.0 / HEAD_DIM**0.5
    )
    weights = jnp.exp(scores)
    if keep is not None:
        weights = jnp.where(keep[None], weights, 0.0)
    den = den + jnp.sum(weights, axis=-1)
    num = num + jnp.einsum(
        "hqk,khd->hqd", weights.astype(jnp.bfloat16), piece_v, preferred_element_type=jnp.float32
    )
    return (num, den)


def token_body(image, text_kv, modulation, w_qkv, w_out, q_gain, k_gain, region_mask):
    img_rows = image.shape[1]
    width_local = w_qkv.shape[2]
    heads_local = width_local // HEAD_DIM
    tokens = image[0].astype(jnp.float32)
    mods = modulation[0]
    normed = layer_norm(tokens, mods)
    qkv = jnp.einsum(
        "td,dcf->tcf",
        normed,
        lax.all_gather(w_qkv, "seq", axis=0, tiled=True),
        preferred_element_type=jnp.float32,
    )
    section_index = lax.axis_index("section")
    time_index = (section_index == 0).astype(jnp.float32)
    rows_index = lax.axis_index("seq") * img_rows + jnp.arange(img_rows, dtype=jnp.int32)
    cosine, sine = rope_tables(rows_index, time_index)
    query = apply_rope(
        rms_rows(qkv[:, 0].reshape(img_rows, heads_local, HEAD_DIM), q_gain), cosine, sine
    ).astype(jnp.bfloat16)
    keys = apply_rope(
        rms_rows(qkv[:, 1].reshape(img_rows, heads_local, HEAD_DIM), k_gain), cosine, sine
    ).astype(jnp.bfloat16)
    values = qkv[:, 2].astype(jnp.bfloat16)
    image_kv = jnp.stack([keys.reshape(img_rows, width_local), values], axis=1)
    own_kv = jnp.concatenate([image_kv, text_kv[0]], axis=0)
    enabled = (section_index == 1).astype(jnp.int32)
    local_mask = region_mask * enabled
    init = (
        jnp.zeros((heads_local, img_rows, HEAD_DIM), jnp.float32),
        jnp.zeros((heads_local, img_rows), jnp.float32),
    )
    carry = attend_piece(init, lax.all_gather(own_kv, "seq", axis=0, tiled=True), query, None)
    cond_local = lax.ppermute(image_kv, "section", [(0, 1)])
    keep = jnp.repeat(jnp.repeat(local_mask, TILE, axis=0), TILE, axis=1) > 0
    carry = attend_piece(carry, lax.all_gather(cond_local, "seq", axis=0, tiled=True), query, keep)
    num, den = carry
    attn = (num / den[..., None]).astype(jnp.bfloat16)
    attn = jnp.transpose(attn, (1, 0, 2)).reshape(img_rows, width_local)
    term = jnp.dot(attn, w_out, preferred_element_type=jnp.float32)
    branch = lax.psum_scatter(
        term.astype(jnp.bfloat16), "tp", scatter_dimension=1, tiled=True
    ).astype(jnp.float32)
    cols = branch.shape[1]
    offset = lax.axis_index("tp") * cols
    residual = lax.dynamic_slice_in_dim(tokens, offset, cols, 1)
    gate = lax.dynamic_slice_in_dim(mods[2], offset, cols, 0)
    out = residual + gate[None, :] * branch
    return out.astype(jnp.bfloat16)[None]


def body(*arrays):
    image, w_qkv, region_mask = arrays[0], arrays[3], arrays[7]
    seq = lax.axis_size("seq")
    one_head_each = (
        w_qkv.shape[2] // HEAD_DIM == seq == 8
        and lax.axis_size("section") == 2
        and lax.axis_size("tp") == 2
        and w_qkv.shape[0] % 128 == 0
        and image.shape[1] == TILE
        and region_mask.shape == (1, seq)
        and arrays[1].shape[1] % 16 == 0
        and arrays[4].shape[1] % 1024 == 0
    )
    return (head_body if one_head_each else token_body)(*arrays)


def solution(mesh):
    return jax.shard_map(
        body,
        mesh=mesh,
        in_specs=(
            P("section", "seq", None),
            P("section", "seq", None, "tp"),
            P("section", None, None),
            P("seq", None, "tp"),
            P("tp", None),
            P(),
            P(),
            P("seq", None),
        ),
        out_specs=P("section", "seq", "tp"),
        check_vma=False,
    )
```

```python
import jax
import jax.numpy as jnp
from jax import lax
from jax.experimental import pallas as pl
from jax.experimental.pallas import tpu as pltpu
from jax.sharding import PartitionSpec as P

HEAD_DIM = 128
GRID_W = 64
TILE = 128
VMEM_LIMIT = 20 * 1024 * 1024


def axis_freqs(width):
    return 10000.0 ** (-jnp.arange(0, width, 2).astype(jnp.float32) / width)


def rope_tables(rows_index, time_index):
    first = HEAD_DIM // 8
    rest = (HEAD_DIM - first) // 2
    row_pos = (rows_index // GRID_W).astype(jnp.float32)
    col_pos = (rows_index % GRID_W).astype(jnp.float32)
    time_pos = jnp.zeros_like(row_pos) + time_index
    angles = jnp.concatenate(
        [
            time_pos[:, None] * axis_freqs(first)[None],
            row_pos[:, None] * axis_freqs(rest)[None],
            col_pos[:, None] * axis_freqs(rest)[None],
        ],
        axis=-1,
    )
    return (jnp.cos(angles), jnp.sin(angles))


def layer_norm(tokens, mods):
    mean = jnp.mean(tokens, axis=-1, keepdims=True)
    var = jnp.mean((tokens - mean) ** 2, axis=-1, keepdims=True)
    return ((tokens - mean) * lax.rsqrt(var + 1e-06) * (1.0 + mods[1:2]) + mods[0:1]).astype(
        jnp.bfloat16
    )


VMEM = pl.BlockSpec(memory_space=pltpu.VMEM)
SMEM = pl.BlockSpec(memory_space=pltpu.SMEM)


def call(kernel, name, out_shape, flops, moved, exps, limit=VMEM_LIMIT, **spec):
    return pl.pallas_call(
        kernel,
        out_shape=out_shape,
        compiler_params=pltpu.CompilerParams(vmem_limit_bytes=limit),
        cost_estimate=pl.CostEstimate(flops=flops, bytes_accessed=moved, transcendentals=exps),
        name=name,
        **spec,
    )


def norm_kernel(tp_ref, image_ref, mods_ref, full_ref, part_ref):
    mods = jnp.concatenate([mods_ref[0], mods_ref[1]], axis=0)
    normed = layer_norm(image_ref[...].astype(jnp.float32), mods)
    part = part_ref.shape[0]
    for t in range(2):

        @pl.when(tp_ref[0] == t)
        def _(t=t):
            ours, theirs = normed[t * part : (t + 1) * part], normed[(1 - t) * part : (2 - t) * part]
            full_ref[:part, :] = ours
            full_ref[part:, :] = theirs
            part_ref[...] = ours


def norm_tokens(tp, image, mods):
    rows, depth = image.shape
    return call(
        norm_kernel, "norm_tokens",
        [
            jax.ShapeDtypeStruct((rows, depth), jnp.bfloat16),
            jax.ShapeDtypeStruct((rows // 2, depth), jnp.bfloat16),
        ],
        10 * rows * depth, 4 * rows * depth, 0,
        in_specs=[SMEM, VMEM, VMEM],
        out_specs=[VMEM, VMEM],
    )(tp, image, mods)


def normed_rotated(x, gain, cosine, sine):
    x = x * lax.rsqrt(jnp.mean(x * x, axis=-1, keepdims=True) + 1e-06) * gain
    even = lax.broadcasted_iota(jnp.int32, x.shape, 1) % 2 == 0
    other = jnp.where(even, pltpu.roll(x, HEAD_DIM - 1, 1), pltpu.roll(x, 1, 1))
    return (x * cosine + other * sine).astype(jnp.bfloat16)


def project_kernel(kinds, section_ref, *refs):
    weight_refs, (cos_ref, sin_ref, gain_ref) = refs[:3], refs[3:6]
    outputs = 2 if kinds == (0, 1, 2) else 1
    x_refs, out_refs, acc_ref = refs[6 : -1 - outputs], refs[-1 - outputs : -1], refs[-1]
    step = pl.program_id(0)
    first = section_ref[0] == 0

    def rows_of(s, kind):
        mine, peer, direct = (
            ref[s, kind * (ref.shape[1] // 3) : (kind + 1) * (ref.shape[1] // 3), :]
            for ref in weight_refs
        )
        return jnp.concatenate(
            [jnp.where(first, mine, peer), jnp.where(first, peer, mine), direct], axis=0
        )

    w = jnp.concatenate(
        [
            jnp.concatenate([rows_of(s, kind) for s in range(weight_refs[0].shape[0])], axis=0)
            for kind in kinds
        ],
        axis=1,
    )
    x = jnp.concatenate([ref[...] for ref in x_refs], axis=0)
    part = jnp.dot(x, w, preferred_element_type=jnp.float32)

    @pl.when(step == 0)
    def _():
        acc_ref[...] = part

    @pl.when(step > 0)
    def _():
        acc_ref[...] += part

    @pl.when(step == pl.num_programs(0) - 1)
    def _():
        for place, kind in enumerate(kinds):
            value = acc_ref[:, place * HEAD_DIM : (place + 1) * HEAD_DIM]
            if kind < 2:
                value = normed_rotated(
                    value, gain_ref[kind : kind + 1, :], cos_ref[...], sin_ref[...]
                )
            if kind == 0:
                out_refs[0][...] = value
            else:
                out_refs[-1][kind - 1] = value.astype(jnp.bfloat16)


def project(kinds, chunk, section, pieces, weights, cosine, sine, gains):
    depth = pieces[0].shape[1]
    rows = sum(p.shape[0] for p in pieces)
    sources = weights[0].shape[0]
    steps = 4
    out_shape, out_specs = [], []
    for shape in ((rows, HEAD_DIM),) * (0 in kinds) + ((2, rows, HEAD_DIM),) * (1 in kinds):
        out_shape.append(jax.ShapeDtypeStruct(shape, jnp.bfloat16))
        out_specs.append(pl.BlockSpec(shape, lambda k, s, n=len(shape): (0,) * n))
    table = pl.BlockSpec((rows, HEAD_DIM), lambda k, s: (chunk, 0))
    return call(
        lambda *refs: project_kernel(kinds, *refs),
        "project_" + "".join("qkv"[k] for k in kinds),
        out_shape,
        2 * len(kinds) * rows * depth * HEAD_DIM,
        2 * (rows * depth + sum(w.size for w in weights)), 0,
        grid_spec=pltpu.PrefetchScalarGridSpec(
            num_scalar_prefetch=1,
            grid=(steps,),
            in_specs=[
                pl.BlockSpec((sources // steps,) + w.shape[1:], lambda k, s: (k, 0, 0))
                for w in weights
            ]
            + [table, table, pl.BlockSpec((2, HEAD_DIM), lambda k, s: (0, 0))]
            + [pl.BlockSpec((p.shape[0], depth // steps), lambda k, s: (0, k)) for p in pieces],
            out_specs=out_specs,
            scratch_shapes=[pltpu.VMEM((rows, len(kinds) * HEAD_DIM), jnp.float32)],
        ),
    )(section, *weights, cosine, sine, gains, *pieces)


def weights_of(query, keys):
    scores = lax.dot_general(
        query, keys, (((1,), (1,)), ((), ())), preferred_element_type=jnp.float32
    )
    return jnp.exp(scores * (1.0 / HEAD_DIM**0.5))


def summed(weights, values):
    den = jnp.sum(weights, axis=-1, keepdims=True)
    num = jnp.dot(weights.astype(jnp.bfloat16), values, preferred_element_type=jnp.float32)
    return num, den


def kept_weights(query, cond_ref, keep):
    weights = weights_of(query, cond_ref[0])
    rows, keys = weights.shape
    groups = keep.shape[0]
    return (weights.reshape(groups, rows // groups, keys) * keep[:, None, :]).reshape(rows, keys)


BLOCK = 256


def query_blocks(q_refs):
    for c, ref in enumerate(q_refs):
        for b in range(ref.shape[0] // BLOCK):
            yield ref[b * BLOCK : (b + 1) * BLOCK, :], c * (ref.shape[0] // BLOCK) + b


def own_kernel(section_ref, keep_ref, qa, qb, kva, kvb, text, conda, num_ref, den_ref):
    groups = keep_ref.shape[0] * BLOCK // num_ref.shape[0]
    keys = conda.shape[1]
    for query, b in query_blocks((qa, qb)):
        at = slice(b * BLOCK, (b + 1) * BLOCK)
        num, den = 0.0, 0.0
        for ref in (kva, kvb, text):
            more = summed(weights_of(query, ref[0]), ref[1])
            num, den = num + more[0], den + more[1]
        num_ref[at, :] = num
        den_ref[at, :] = jnp.broadcast_to(den, num.shape)

    @pl.when(section_ref[0] != 0)
    def _():
        for query, b in query_blocks((qa, qb)):
            at = slice(b * BLOCK, (b + 1) * BLOCK)
            keep = keep_ref[b * groups : (b + 1) * groups, :keys]
            num, den = summed(kept_weights(query, conda, keep), conda[1])
            num_ref[at, :] += num
            den_ref[at, :] += jnp.broadcast_to(den, num.shape)


def cond_kernel(section_ref, place_ref, keep_ref, qa, qb, condb, num_ref, den_ref, out_ref):
    rows = num_ref.shape[0]
    groups = keep_ref.shape[0] * BLOCK // rows
    size = BLOCK // groups
    keys = condb.shape[1]

    def store(b, num, den):
        value = (num / den).astype(jnp.bfloat16)
        for g in range(groups):
            shard, part = place_ref[0, b * groups + g], place_ref[1, b * groups + g]
            at = pl.ds(pl.multiple_of(part * size, size), size)
            out_ref[shard, at, :] = value[g * size : (g + 1) * size]

    @pl.when(section_ref[0] == 0)
    def _():
        for b in range(rows // BLOCK):
            at = slice(b * BLOCK, (b + 1) * BLOCK)
            store(b, num_ref[at, :], den_ref[at, :])

    @pl.when(section_ref[0] != 0)
    def _():
        for query, b in query_blocks((qa, qb)):
            at = slice(b * BLOCK, (b + 1) * BLOCK)
            keep = keep_ref[b * groups : (b + 1) * groups, -keys:]
            num, den = summed(kept_weights(query, condb, keep), condb[1])
            store(b, num_ref[at, :] + num, den_ref[at, :] + den)


def attend_own(section, keep, queries, kvs, text, cond):
    rows = 2 * queries[0].shape[0]
    keys = rows + text.shape[1] + cond.shape[1]
    return call(
        own_kernel, "attend_own", [jax.ShapeDtypeStruct((rows, HEAD_DIM), jnp.float32)] * 2,
        4 * rows * keys * HEAD_DIM, 2 * rows * HEAD_DIM * 10, rows * keys,
        in_specs=[SMEM] + [VMEM] * 7,
        out_specs=[VMEM] * 2,
    )(section, keep, *queries, *kvs, text, cond)


def attend_cond(section, place, keep, queries, cond, num, den, seq):
    rows = num.shape[0]
    keys = cond.shape[1]
    return call(
        cond_kernel, "attend_cond",
        jax.ShapeDtypeStruct((seq, rows // seq, HEAD_DIM), jnp.bfloat16),
        4 * rows * keys * HEAD_DIM, 2 * rows * HEAD_DIM * 8, rows * keys,
        in_specs=[SMEM, SMEM] + [VMEM] * 6,
        out_specs=VMEM,
    )(section, place, keep, *queries, cond, num, den)


def token_rows(attn_ref):
    return jnp.concatenate([attn_ref[h] for h in range(attn_ref.shape[0])], axis=1)


def load_kernel(half_ref, w_ref, sent_ref, kept_ref, sems):
    width = sent_ref.shape[1]
    copies = []
    for i, out_ref in enumerate((sent_ref, kept_ref)):
        half = half_ref[0] if i else 1 - half_ref[0]
        columns = pl.ds(pl.multiple_of(half * width, width), width)
        copies.append(pltpu.make_async_copy(w_ref.at[:, columns], out_ref, sems.at[i]))
    for copy in copies:
        copy.start()
    for copy in copies:
        copy.wait()


def load_out(half, w_out):
    shape = jax.ShapeDtypeStruct((w_out.shape[0], w_out.shape[1] // 2), w_out.dtype)
    return call(
        load_kernel, "load_out", [shape] * 2, 0, 4 * w_out.size, 0,
        in_specs=[SMEM, pl.BlockSpec(memory_space=pl.ANY)],
        out_specs=[VMEM, VMEM],
        scratch_shapes=[pltpu.SemaphoreType.DMA((2,))],
    )(half, w_out)


def sent_kernel(attn_ref, w_ref, out_ref):
    branch = jnp.dot(token_rows(attn_ref), w_ref[...], preferred_element_type=jnp.float32)
    out_ref[...] = branch.astype(jnp.bfloat16)


def kept_kernel(attn_ref, w_ref, image_ref, gate_ref, out_ref):
    branch = jnp.dot(token_rows(attn_ref), w_ref[...], preferred_element_type=jnp.float32)
    out_ref[...] = image_ref[...].astype(jnp.float32) + gate_ref[...] * branch


def project_out(attn, w, image=None, gate=None):
    rows = attn.shape[1]
    depth, width = w.shape
    kept = image is not None
    args = (attn, w) + ((image, gate) if kept else ())
    return call(
        kept_kernel if kept else sent_kernel, "out_kept" if kept else "out_sent",
        jax.ShapeDtypeStruct((rows, width), jnp.float32 if kept else jnp.bfloat16),
        2 * rows * depth * width, 2 * depth * width, 0,
        in_specs=[VMEM] * len(args),
        out_specs=VMEM,
    )(*args)


def lane_tables(rows_index, time_index):
    first = HEAD_DIM // 8
    rest = (HEAD_DIM - first) // 2
    freqs = jnp.concatenate([axis_freqs(first), axis_freqs(rest), axis_freqs(rest)])
    freqs = jnp.repeat(freqs, 2)[None]
    lane = jnp.arange(HEAD_DIM, dtype=jnp.int32)[None]
    row_pos = (rows_index // GRID_W).astype(jnp.float32)[:, None]
    col_pos = (rows_index % GRID_W).astype(jnp.float32)[:, None]
    ids = jnp.where(lane < first, time_index, jnp.where(lane < first + rest, row_pos, col_pos))
    angles = ids * freqs
    return jnp.cos(angles), jnp.sin(angles) * jnp.where(lane % 2 == 0, -1.0, 1.0)


def z_pairs(seq, pairs):
    return [(2 * a + core, 2 * b + core) for a, b in pairs for core in range(2)]


def head_body(image, text_kv, modulation, w_qkv, w_out, q_gain, k_gain, region_mask):
    seq = lax.axis_size("seq")
    img_rows = image.shape[1]
    depth = w_qkv.shape[0]
    section = lax.axis_index("section")
    tp = lax.axis_index("tp")
    chip, core = lax.axis_index("seq") // 2, lax.axis_index("seq") % 2
    mods = modulation[0]
    section_at = section.astype(jnp.int32).reshape(1)
    tp_at = tp.astype(jnp.int32).reshape(1)
    both = [(0, 1), (1, 0)]

    rows3 = w_qkv.transpose(1, 0, 2)
    half = depth * 3 // 8

    def for_heads(rows):
        return rows.reshape(3, -1, seq, HEAD_DIM).transpose(2, 0, 1, 3).reshape(seq, -1, HEAD_DIM)

    mine = for_heads(lax.dynamic_slice_in_dim(rows3, section * half, half, 1))
    mine = lax.all_to_all(mine, "seq", 0, 0)

    full, part = norm_tokens(tp_at, image[0], modulation.transpose(1, 0, 2))

    def along_z(x, pairs):
        return lax.ppermute(x, "seq", z_pairs(seq, pairs))

    def to_core(x):
        return lax.ppermute(x, "seq", [(s, s ^ 1) for s in range(seq)])

    near = along_z(part, [(0, 1), (1, 0), (2, 3), (3, 2)])
    middle = along_z(part, [(1, 2), (2, 1)])
    far = along_z(near, [(1, 2), (2, 1)])
    middle_end = along_z(middle, [(1, 0), (2, 3)])
    far_end = along_z(far, [(1, 0), (2, 3)])
    inner = (chip == 1) | (chip == 2)
    third = jnp.where(inner, middle, middle_end)
    fourth = jnp.where(inner, far, far_end)
    pieces = [(full, to_core(full))]
    for came in (near, third):
        group = jnp.concatenate([came, lax.ppermute(came, "tp", both)], axis=0)
        pieces.append((group, to_core(group)))
    fourth, mine = lax.optimization_barrier((fourth, mine))
    passed = lax.ppermute(fourth, "tp", both)
    pieces.append((fourth, passed, to_core(fourth), to_core(passed)))

    peer = lax.ppermute(mine, "section", both)
    text = text_kv[0].reshape(-1, 2, seq, HEAD_DIM).transpose(2, 0, 1, 3).reshape(seq, -1, HEAD_DIM)
    mask = jnp.pad(
        region_mask.astype(jnp.bfloat16), ((0, 15), (0, HEAD_DIM - region_mask.shape[1]))
    )
    mask = jnp.broadcast_to(mask, (seq,) + mask.shape)
    direct = jnp.concatenate([for_heads(rows3[:, 2 * half :]), text, mask], axis=1)
    direct, mine = lax.optimization_barrier((direct, mine))
    direct = lax.all_to_all(direct, "seq", 0, 0)
    w_sent, w_kept = load_out(tp_at, w_out)
    direct, w_sent, w_kept = lax.optimization_barrier((direct, w_sent, w_kept))
    text = direct[:, -16 - 2 * text_kv.shape[1] : -16].reshape(-1, 2, HEAD_DIM).transpose(1, 0, 2)
    keep = direct[:, -16, : region_mask.shape[1]].astype(jnp.float32)
    direct = direct[:, : 3 * (depth - 2 * half)]

    upper = chip >= 2
    chips = jnp.stack([chip, chip ^ 1, jnp.where(upper, 1, 2), jnp.where(upper, 0, 3)])
    cores = jnp.stack([core, 1 - core])
    parts = jnp.stack([tp, 1 - tp])
    shards = chips[:, None, None] * 2 + cores[None, :, None] + 0 * parts[None, None, :]
    parts = parts[None, None, :] + 0 * shards
    shards, parts = shards.reshape(-1).astype(jnp.int32), parts.reshape(-1).astype(jnp.int32)
    size = img_rows // 2
    first_row = shards * img_rows + parts * size
    rows_index = (first_row[:, None] + jnp.arange(size, dtype=jnp.int32)[None]).reshape(-1)
    cosine, sine = lane_tables(rows_index, (section == 0).astype(jnp.float32))
    gains = jnp.stack([q_gain, k_gain])
    chosen = (shards[:, None] == jnp.arange(seq)[None]).astype(jnp.float32)
    keep = jnp.repeat(chosen @ keep @ chosen.T, size, axis=1)

    a, b = pieces[0] + pieces[1], pieces[2] + pieces[3]
    weights = (mine, peer, direct)
    q_a, kv_a = project((0, 1, 2), 0, section_at, a, weights, cosine, sine, gains)
    cond_a = lax.ppermute(kv_a, "section", [(0, 1)])
    (kv_b,) = project((1, 2), 1, section_at, b, weights, cosine, sine, gains)
    cond_b = lax.ppermute(kv_b, "section", [(0, 1)])
    (q_b,) = project((0,), 1, section_at, b, weights, cosine, sine, gains)
    queries = (q_a, q_b)
    num, den = attend_own(section_at, keep, queries, (kv_a, kv_b), text, cond_a)
    place = jnp.stack([shards, parts])
    attn = attend_cond(section_at, place, keep, queries, cond_b, num, den, seq)

    attn = lax.all_to_all(attn, "seq", 0, 0)
    other = lax.ppermute(project_out(attn, w_sent), "tp", both)
    cols = other.shape[1]
    gate = lax.dynamic_slice_in_dim(mods[2:3], tp * cols, cols, 1)
    residual = lax.dynamic_slice_in_dim(image[0], tp * cols, cols, 1)
    kept = project_out(attn, w_kept, residual, gate)
    return (kept + gate * other.astype(jnp.float32)).astype(jnp.bfloat16)[None]


def rms_rows(x, gain):
    return x * lax.rsqrt(jnp.mean(x * x, axis=-1, keepdims=True) + 1e-06) * gain


def apply_rope(x, cosine, sine):
    rows, heads_here = (x.shape[0], x.shape[1])
    pairs = x.reshape(rows, heads_here, HEAD_DIM // 2, 2)
    first = pairs[..., 0]
    second = pairs[..., 1]
    cosine = cosine[:, None, :]
    sine = sine[:, None, :]
    rotated = jnp.stack([first * cosine - second * sine, first * sine + second * cosine], axis=-1)
    return rotated.reshape(rows, heads_here, HEAD_DIM)


def attend_piece(carry, keys_vals, query, keep):
    num, den = carry
    rows = keys_vals.shape[0]
    heads_local = query.shape[1]
    piece_k = keys_vals[:, 0].reshape(rows, heads_local, HEAD_DIM)
    piece_v = keys_vals[:, 1].reshape(rows, heads_local, HEAD_DIM)
    scores = jnp.einsum("qhd,khd->hqk", query, piece_k, preferred_element_type=jnp.float32) * (
        1.0 / HEAD_DIM**0.5
    )
    weights = jnp.exp(scores)
    if keep is not None:
        weights = jnp.where(keep[None], weights, 0.0)
    den = den + jnp.sum(weights, axis=-1)
    num = num + jnp.einsum(
        "hqk,khd->hqd", weights.astype(jnp.bfloat16), piece_v, preferred_element_type=jnp.float32
    )
    return (num, den)


def token_body(image, text_kv, modulation, w_qkv, w_out, q_gain, k_gain, region_mask):
    img_rows = image.shape[1]
    width_local = w_qkv.shape[2]
    heads_local = width_local // HEAD_DIM
    tokens = image[0].astype(jnp.float32)
    mods = modulation[0]
    normed = layer_norm(tokens, mods)
    qkv = jnp.einsum(
        "td,dcf->tcf",
        normed,
        lax.all_gather(w_qkv, "seq", axis=0, tiled=True),
        preferred_element_type=jnp.float32,
    )
    section_index = lax.axis_index("section")
    time_index = (section_index == 0).astype(jnp.float32)
    rows_index = lax.axis_index("seq") * img_rows + jnp.arange(img_rows, dtype=jnp.int32)
    cosine, sine = rope_tables(rows_index, time_index)
    query = apply_rope(
        rms_rows(qkv[:, 0].reshape(img_rows, heads_local, HEAD_DIM), q_gain), cosine, sine
    ).astype(jnp.bfloat16)
    keys = apply_rope(
        rms_rows(qkv[:, 1].reshape(img_rows, heads_local, HEAD_DIM), k_gain), cosine, sine
    ).astype(jnp.bfloat16)
    values = qkv[:, 2].astype(jnp.bfloat16)
    image_kv = jnp.stack([keys.reshape(img_rows, width_local), values], axis=1)
    own_kv = jnp.concatenate([image_kv, text_kv[0]], axis=0)
    enabled = (section_index == 1).astype(jnp.int32)
    local_mask = region_mask * enabled
    init = (
        jnp.zeros((heads_local, img_rows, HEAD_DIM), jnp.float32),
        jnp.zeros((heads_local, img_rows), jnp.float32),
    )
    carry = attend_piece(init, lax.all_gather(own_kv, "seq", axis=0, tiled=True), query, None)
    cond_local = lax.ppermute(image_kv, "section", [(0, 1)])
    keep = jnp.repeat(jnp.repeat(local_mask, TILE, axis=0), TILE, axis=1) > 0
    carry = attend_piece(carry, lax.all_gather(cond_local, "seq", axis=0, tiled=True), query, keep)
    num, den = carry
    attn = (num / den[..., None]).astype(jnp.bfloat16)
    attn = jnp.transpose(attn, (1, 0, 2)).reshape(img_rows, width_local)
    term = jnp.dot(attn, w_out, preferred_element_type=jnp.float32)
    branch = lax.psum_scatter(
        term.astype(jnp.bfloat16), "tp", scatter_dimension=1, tiled=True
    ).astype(jnp.float32)
    cols = branch.shape[1]
    offset = lax.axis_index("tp") * cols
    residual = lax.dynamic_slice_in_dim(tokens, offset, cols, 1)
    gate = lax.dynamic_slice_in_dim(mods[2], offset, cols, 0)
    out = residual + gate[None, :] * branch
    return out.astype(jnp.bfloat16)[None]


def body(*arrays):
    image, w_qkv, region_mask = arrays[0], arrays[3], arrays[7]
    seq = lax.axis_size("seq")
    one_head_each = (
        w_qkv.shape[2] // HEAD_DIM == seq == 8
        and lax.axis_size("section") == 2
        and lax.axis_size("tp") == 2
        and w_qkv.shape[0] % 128 == 0
        and image.shape[1] == TILE
        and region_mask.shape == (1, seq)
        and arrays[1].shape[1] % 16 == 0
        and arrays[4].shape[1] % 1024 == 0
    )
    return (head_body if one_head_each else token_body)(*arrays)


def solution(mesh):
    return jax.shard_map(
        body,
        mesh=mesh,
        in_specs=(
            P("section", "seq", None),
            P("section", "seq", None, "tp"),
            P("section", None, None),
            P("seq", None, "tp"),
            P("tp", None),
            P(),
            P(),
            P("seq", None),
        ),
        out_specs=P("section", "seq", "tp"),
        check_vma=False,
    )
```

```python
import jax
import jax.numpy as jnp
from jax import lax
from jax.experimental import pallas as pl
from jax.experimental.pallas import tpu as pltpu
from jax.sharding import PartitionSpec as P

HEAD_DIM = 128
GRID_W = 64
TILE = 128
VMEM_LIMIT = 20 * 1024 * 1024


def axis_freqs(width):
    return 10000.0 ** (-jnp.arange(0, width, 2).astype(jnp.float32) / width)


def rope_tables(rows_index, time_index):
    first = HEAD_DIM // 8
    rest = (HEAD_DIM - first) // 2
    row_pos = (rows_index // GRID_W).astype(jnp.float32)
    col_pos = (rows_index % GRID_W).astype(jnp.float32)
    time_pos = jnp.zeros_like(row_pos) + time_index
    angles = jnp.concatenate(
        [
            time_pos[:, None] * axis_freqs(first)[None],
            row_pos[:, None] * axis_freqs(rest)[None],
            col_pos[:, None] * axis_freqs(rest)[None],
        ],
        axis=-1,
    )
    return (jnp.cos(angles), jnp.sin(angles))


def layer_norm(tokens, mods):
    mean = jnp.mean(tokens, axis=-1, keepdims=True)
    var = jnp.mean((tokens - mean) ** 2, axis=-1, keepdims=True)
    return ((tokens - mean) * lax.rsqrt(var + 1e-06) * (1.0 + mods[1:2]) + mods[0:1]).astype(
        jnp.bfloat16
    )


VMEM = pl.BlockSpec(memory_space=pltpu.VMEM)
SMEM = pl.BlockSpec(memory_space=pltpu.SMEM)


def call(kernel, name, out_shape, flops, moved, exps, limit=VMEM_LIMIT, **spec):
    return pl.pallas_call(
        kernel,
        out_shape=out_shape,
        compiler_params=pltpu.CompilerParams(vmem_limit_bytes=limit),
        cost_estimate=pl.CostEstimate(flops=flops, bytes_accessed=moved, transcendentals=exps),
        name=name,
        **spec,
    )


def norm_kernel(tp_ref, image_ref, mods_ref, full_ref, part_ref):
    mods = jnp.concatenate([mods_ref[0], mods_ref[1]], axis=0)
    normed = layer_norm(image_ref[...].astype(jnp.float32), mods)
    part = part_ref.shape[0]
    for t in range(2):

        @pl.when(tp_ref[0] == t)
        def _(t=t):
            ours, theirs = normed[t * part : (t + 1) * part], normed[(1 - t) * part : (2 - t) * part]
            full_ref[:part, :] = ours
            full_ref[part:, :] = theirs
            part_ref[...] = ours


def norm_tokens(tp, image, mods):
    rows, depth = image.shape
    return call(
        norm_kernel, "norm_tokens",
        [
            jax.ShapeDtypeStruct((rows, depth), jnp.bfloat16),
            jax.ShapeDtypeStruct((rows // 2, depth), jnp.bfloat16),
        ],
        10 * rows * depth, 4 * rows * depth, 0,
        in_specs=[SMEM, VMEM, VMEM],
        out_specs=[VMEM, VMEM],
    )(tp, image, mods)


def normed_rotated(x, gain, cosine, sine):
    x = x * lax.rsqrt(jnp.mean(x * x, axis=-1, keepdims=True) + 1e-06) * gain
    even = lax.broadcasted_iota(jnp.int32, x.shape, 1) % 2 == 0
    other = jnp.where(even, pltpu.roll(x, HEAD_DIM - 1, 1), pltpu.roll(x, 1, 1))
    return (x * cosine + other * sine).astype(jnp.bfloat16)


def copy_all(pairs, sems):
    copies = [pltpu.make_async_copy(s, d, sems.at[i]) for i, (s, d) in enumerate(pairs)]
    for copy in copies:
        copy.start()
    for copy in copies:
        copy.wait()


def pack_kernel(*refs):
    x_refs, out_ref, sems = refs[:-2], refs[-2], refs[-1]
    at, pairs = 0, []
    for ref in x_refs:
        pairs.append((ref, out_ref.at[pl.ds(at, ref.shape[0]), :]))
        at += ref.shape[0]
    copy_all(pairs, sems)


def pack(pieces):
    rows, depth = sum(p.shape[0] for p in pieces), pieces[0].shape[1]
    return call(
        pack_kernel, "pack_tokens", jax.ShapeDtypeStruct((rows, depth), jnp.bfloat16),
        0, 4 * rows * depth, 0,
        in_specs=[pl.BlockSpec(memory_space=pl.ANY)] * len(pieces),
        out_specs=VMEM,
        scratch_shapes=[pltpu.SemaphoreType.DMA((len(pieces),))],
    )(*pieces)


def first_kv_kernel(section_ref, x_ref, mine, peer, cos_ref, sin_ref, gain_ref, kv_ref, w_ref):
    first = section_ref[0] == 0
    sources, held, _ = mine.shape
    half = held // 2
    for s in range(sources):
        for kind in range(2):
            at = slice(kind * half, (kind + 1) * half)
            lanes = slice(kind * HEAD_DIM, (kind + 1) * HEAD_DIM)
            a, b = mine[s, at, :], peer[s, at, :]
            w_ref[2 * s * half : (2 * s + 1) * half, lanes] = jnp.where(first, a, b)
            w_ref[(2 * s + 1) * half : (2 * s + 2) * half, lanes] = jnp.where(first, b, a)
    kv_kernel(0, x_ref, w_ref, cos_ref, sin_ref, gain_ref, kv_ref)


def kv_kernel(chunk, x_ref, w_ref, cos_ref, sin_ref, gain_ref, kv_ref):
    both = jnp.dot(x_ref[...], w_ref[...], preferred_element_type=jnp.float32)
    at = slice(chunk * x_ref.shape[0], (chunk + 1) * x_ref.shape[0])
    kv_ref[0] = normed_rotated(
        both[:, :HEAD_DIM], gain_ref[1:2, :], cos_ref[at, :], sin_ref[at, :]
    )
    kv_ref[1] = both[:, HEAD_DIM:].astype(jnp.bfloat16)


def first_kv(section, x, mine, peer, cosine, sine, gains):
    rows, depth = x.shape
    return call(
        first_kv_kernel, "first_kv",
        [
            jax.ShapeDtypeStruct((2, rows, HEAD_DIM), jnp.bfloat16),
            jax.ShapeDtypeStruct((depth, 2 * HEAD_DIM), jnp.bfloat16),
        ],
        4 * rows * depth * HEAD_DIM, 2 * (x.size + 4 * mine.size), 0,
        in_specs=[SMEM] + [VMEM] * 6,
        out_specs=[VMEM, VMEM],
    )(section, x, mine, peer, cosine, sine, gains)


def second_kv(x, w, cosine, sine, gains):
    rows, depth = x.shape
    return call(
        lambda *refs: kv_kernel(1, *refs), "second_kv",
        jax.ShapeDtypeStruct((2, rows, HEAD_DIM), jnp.bfloat16),
        4 * rows * depth * HEAD_DIM, 2 * (x.size + w.size), 0,
        in_specs=[VMEM] * 5,
        out_specs=VMEM,
    )(x, w, cosine, sine, gains)


def weights_of(query, keys):
    scores = lax.dot_general(
        query, keys, (((1,), (1,)), ((), ())), preferred_element_type=jnp.float32
    )
    return jnp.exp(scores * (1.0 / HEAD_DIM**0.5))


def summed(weights, values):
    den = jnp.sum(weights, axis=-1, keepdims=True)
    num = jnp.dot(weights.astype(jnp.bfloat16), values, preferred_element_type=jnp.float32)
    return num, den


def kept_weights(query, cond_ref, keep):
    weights = weights_of(query, cond_ref[0])
    rows, keys = weights.shape
    groups = keep.shape[0]
    return (weights.reshape(groups, rows // groups, keys) * keep[:, None, :]).reshape(rows, keys)


BLOCK = 256


def own_kernel(
    xa, xb, direct, cos_ref, sin_ref, gain_ref, rows_ref, keys_ref, kva, kvb,
    q_ref, num_ref, den_ref, keep_ref,
):
    depth = xa.shape[1]
    sources, held, _ = direct.shape
    w = direct[:, : depth // sources, :].reshape(depth, HEAD_DIM)
    count = (held - 16 - depth // sources) // 2
    at = depth // sources
    text = (
        direct[:, at : at + count, :].reshape(-1, HEAD_DIM),
        direct[:, at + count : at + 2 * count, :].reshape(-1, HEAD_DIM),
    )
    for c, x_ref in enumerate((xa, xb)):
        for b in range(x_ref.shape[0] // BLOCK):
            start = c * x_ref.shape[0] + b * BLOCK
            at = slice(start, start + BLOCK)
            query = jnp.dot(
                x_ref[b * BLOCK : (b + 1) * BLOCK, :], w, preferred_element_type=jnp.float32
            )
            query = normed_rotated(query, gain_ref[0:1, :], cos_ref[at, :], sin_ref[at, :])
            q_ref[at, :] = query
            num, den = 0.0, 0.0
            for keys, values in ((kva[0], kva[1]), (kvb[0], kvb[1]), text):
                more = summed(weights_of(query, keys), values)
                num, den = num + more[0], den + more[1]
            num_ref[at, :] = num
            den_ref[at, :] = jnp.broadcast_to(den, num.shape)
    mask = jnp.concatenate(
        [direct[s, held - 16 : held, :].astype(jnp.float32)[:1] for s in range(sources)], axis=0
    )
    mask = jnp.dot(rows_ref[...], mask, preferred_element_type=jnp.float32)
    keep_ref[...] = jnp.dot(mask, keys_ref[...], preferred_element_type=jnp.float32)


def cond_sum(keep_ref, q_ref, cond, chunk, b):
    groups = keep_ref.shape[0] * BLOCK // q_ref.shape[0]
    keys = cond.shape[1]
    keep = keep_ref[b * groups : (b + 1) * groups, chunk * keys : (chunk + 1) * keys]
    return summed(kept_weights(q_ref[b * BLOCK : (b + 1) * BLOCK, :], cond, keep), cond[1])


def first_cond_kernel(section_ref, keep_ref, q_ref, cond, num_in, den_in, num_ref, den_ref):
    @pl.when(section_ref[0] == 0)
    def _():
        num_ref[...] = num_in[...]
        den_ref[...] = den_in[...]

    @pl.when(section_ref[0] != 0)
    def _():
        for b in range(num_ref.shape[0] // BLOCK):
            at = slice(b * BLOCK, (b + 1) * BLOCK)
            num, den = cond_sum(keep_ref, q_ref, cond, 0, b)
            num_ref[at, :] = num_in[at, :] + num
            den_ref[at, :] = den_in[at, :] + den


def second_cond_kernel(section_ref, place_ref, keep_ref, q_ref, cond, num_ref, den_ref, out_ref):
    groups = keep_ref.shape[0] * BLOCK // num_ref.shape[0]
    size = BLOCK // groups

    def store(b, num, den):
        value = (num / den).astype(jnp.bfloat16)
        for g in range(groups):
            shard, part = place_ref[0, b * groups + g], place_ref[1, b * groups + g]
            at = pl.ds(pl.multiple_of(part * size, size), size)
            out_ref[shard, at, :] = value[g * size : (g + 1) * size]

    @pl.when(section_ref[0] == 0)
    def _():
        for b in range(num_ref.shape[0] // BLOCK):
            at = slice(b * BLOCK, (b + 1) * BLOCK)
            store(b, num_ref[at, :], den_ref[at, :])

    @pl.when(section_ref[0] != 0)
    def _():
        for b in range(num_ref.shape[0] // BLOCK):
            at = slice(b * BLOCK, (b + 1) * BLOCK)
            num, den = cond_sum(keep_ref, q_ref, cond, 1, b)
            store(b, num_ref[at, :] + num, den_ref[at, :] + den)


def attend_own(xs, direct, cosine, sine, gains, row_tiles, key_tiles, kvs):
    rows, depth = 2 * xs[0].shape[0], xs[0].shape[1]
    keys = rows + 512
    return call(
        own_kernel, "attend_own",
        [
            jax.ShapeDtypeStruct((rows, HEAD_DIM), jnp.bfloat16),
            jax.ShapeDtypeStruct((rows, HEAD_DIM), jnp.float32),
            jax.ShapeDtypeStruct((rows, HEAD_DIM), jnp.float32),
            jax.ShapeDtypeStruct((row_tiles.shape[0], rows), jnp.float32),
        ],
        2 * rows * HEAD_DIM * (2 * keys + depth), 2 * rows * depth, rows * keys,
        in_specs=[VMEM] * 10,
        out_specs=[VMEM] * 4,
    )(*xs, direct, cosine, sine, gains, row_tiles, key_tiles, *kvs)


def attend_first(section, keep, query, cond, num, den):
    rows, keys = num.shape[0], cond.shape[1]
    return call(
        first_cond_kernel, "attend_first", [jax.ShapeDtypeStruct(num.shape, jnp.float32)] * 2,
        4 * rows * keys * HEAD_DIM, 2 * rows * HEAD_DIM * 8, rows * keys,
        in_specs=[SMEM] + [VMEM] * 5,
        out_specs=[VMEM] * 2,
    )(section, keep, query, cond, num, den)


def attend_second(section, place, keep, query, cond, num, den, seq):
    rows, keys = num.shape[0], cond.shape[1]
    return call(
        second_cond_kernel, "attend_second",
        jax.ShapeDtypeStruct((seq, rows // seq, HEAD_DIM), jnp.bfloat16),
        4 * rows * keys * HEAD_DIM, 2 * rows * HEAD_DIM * 8, rows * keys,
        in_specs=[SMEM, SMEM] + [VMEM] * 5,
        out_specs=VMEM,
    )(section, place, keep, query, cond, num, den)


def token_rows(attn_ref):
    return jnp.concatenate([attn_ref[h] for h in range(attn_ref.shape[0])], axis=1)


def load_kernel(half_ref, w_ref, sent_ref, kept_ref, sems):
    width = sent_ref.shape[1]
    pairs = []
    for half, out_ref in ((1 - half_ref[0], sent_ref), (half_ref[0], kept_ref)):
        columns = pl.ds(pl.multiple_of(half * width, width), width)
        pairs.append((w_ref.at[:, columns], out_ref))
    copy_all(pairs, sems)


def load_out(half, w_out):
    shape = jax.ShapeDtypeStruct((w_out.shape[0], w_out.shape[1] // 2), w_out.dtype)
    return call(
        load_kernel, "load_out", [shape] * 2, 0, 4 * w_out.size, 0,
        in_specs=[SMEM, pl.BlockSpec(memory_space=pl.ANY)],
        out_specs=[VMEM, VMEM],
        scratch_shapes=[pltpu.SemaphoreType.DMA((2,))],
    )(half, w_out)


def sent_kernel(attn_ref, w_ref, out_ref):
    branch = jnp.dot(token_rows(attn_ref), w_ref[...], preferred_element_type=jnp.float32)
    out_ref[...] = branch.astype(jnp.bfloat16)


def kept_kernel(attn_ref, w_ref, image_ref, gate_ref, out_ref):
    branch = jnp.dot(token_rows(attn_ref), w_ref[...], preferred_element_type=jnp.float32)
    out_ref[...] = image_ref[...].astype(jnp.float32) + gate_ref[...] * branch


def project_out(attn, w, image=None, gate=None):
    rows = attn.shape[1]
    depth, width = w.shape
    kept = image is not None
    args = (attn, w) + ((image, gate) if kept else ())
    return call(
        kept_kernel if kept else sent_kernel, "out_kept" if kept else "out_sent",
        jax.ShapeDtypeStruct((rows, width), jnp.float32 if kept else jnp.bfloat16),
        2 * rows * depth * width, 2 * depth * width, 0,
        in_specs=[VMEM] * len(args),
        out_specs=VMEM,
    )(*args)


def lane_tables(rows_index, time_index):
    first = HEAD_DIM // 8
    rest = (HEAD_DIM - first) // 2
    freqs = jnp.concatenate([axis_freqs(first), axis_freqs(rest), axis_freqs(rest)])
    freqs = jnp.repeat(freqs, 2)[None]
    lane = jnp.arange(HEAD_DIM, dtype=jnp.int32)[None]
    row_pos = (rows_index // GRID_W).astype(jnp.float32)[:, None]
    col_pos = (rows_index % GRID_W).astype(jnp.float32)[:, None]
    ids = jnp.where(lane < first, time_index, jnp.where(lane < first + rest, row_pos, col_pos))
    angles = ids * freqs
    return jnp.cos(angles), jnp.sin(angles) * jnp.where(lane % 2 == 0, -1.0, 1.0)


def z_pairs(seq, pairs):
    return [(2 * a + core, 2 * b + core) for a, b in pairs for core in range(2)]


def head_body(image, text_kv, modulation, w_qkv, w_out, q_gain, k_gain, region_mask):
    seq = lax.axis_size("seq")
    img_rows = image.shape[1]
    depth = w_qkv.shape[0]
    section = lax.axis_index("section")
    tp = lax.axis_index("tp")
    chip, core = lax.axis_index("seq") // 2, lax.axis_index("seq") % 2
    mods = modulation[0]
    section_at = section.astype(jnp.int32).reshape(1)
    tp_at = tp.astype(jnp.int32).reshape(1)
    both = [(0, 1), (1, 0)]

    upper = chip >= 2
    chips = jnp.stack([chip, chip ^ 1, jnp.where(upper, 1, 2), jnp.where(upper, 0, 3)])
    cores = jnp.stack([core, 1 - core])
    parts = jnp.stack([tp, 1 - tp])
    shards = chips[:, None, None] * 2 + cores[None, :, None] + 0 * parts[None, None, :]
    parts = parts[None, None, :] + 0 * shards
    shards, parts = shards.reshape(-1).astype(jnp.int32), parts.reshape(-1).astype(jnp.int32)
    size = img_rows // 2
    first_row = shards * img_rows + parts * size
    rows_index = (first_row[:, None] + jnp.arange(size, dtype=jnp.int32)[None]).reshape(-1)
    cosine, sine = lane_tables(rows_index, (section == 0).astype(jnp.float32))
    gains = jnp.stack([q_gain, k_gain])
    row_tiles = (shards[:, None] == jnp.arange(seq)[None]).astype(jnp.float32)
    key_tiles = jnp.arange(HEAD_DIM)[:, None] == jnp.repeat(shards, size)[None]
    key_tiles = key_tiles.astype(jnp.float32)
    place = jnp.stack([shards, parts])

    rows3 = w_qkv.transpose(1, 0, 2)
    half = depth // 2

    def for_heads(rows):
        rows = rows.reshape(rows.shape[0], -1, seq, HEAD_DIM).transpose(2, 0, 1, 3)
        return rows.reshape(seq, -1, HEAD_DIM)

    mine = for_heads(lax.dynamic_slice_in_dim(rows3[1:], section * half, half, 1))
    mine = lax.all_to_all(mine, "seq", 0, 0)

    full, part = norm_tokens(tp_at, image[0], modulation.transpose(1, 0, 2))

    def along_z(x, pairs):
        return lax.ppermute(x, "seq", z_pairs(seq, pairs))

    def to_core(x):
        return lax.ppermute(x, "seq", [(s, s ^ 1) for s in range(seq)])

    def shared(came):
        passed = lax.ppermute(came, "tp", both)
        return [came, passed, to_core(came), to_core(passed)]

    near = along_z(part, [(0, 1), (1, 0), (2, 3), (3, 2)])
    middle = along_z(part, [(1, 2), (2, 1)])
    far = along_z(near, [(1, 2), (2, 1)])
    middle_end = along_z(middle, [(1, 0), (2, 3)])
    far_end = along_z(far, [(1, 0), (2, 3)])
    inner = (chip == 1) | (chip == 2)
    third = jnp.where(inner, middle, middle_end)
    x_a = pack([full, to_core(full)] + shared(near))
    third, mine = lax.optimization_barrier((third, mine))
    peer = lax.ppermute(mine, "section", both)

    text = text_kv[0].reshape(-1, 2, seq, HEAD_DIM).transpose(2, 1, 0, 3).reshape(seq, -1, HEAD_DIM)
    mask = jnp.pad(
        region_mask.astype(jnp.bfloat16), ((0, 15), (0, HEAD_DIM - region_mask.shape[1]))
    )
    mask = jnp.broadcast_to(mask, (seq,) + mask.shape)
    direct = jnp.concatenate([for_heads(rows3[:1]), text, mask], axis=1)
    direct, mine = lax.optimization_barrier((direct, mine))
    direct = lax.all_to_all(direct, "seq", 0, 0)

    fourth = jnp.where(inner, far, far_end)
    w_sent, w_kept = load_out(tp_at, w_out)
    cols = w_sent.shape[1]
    gate = lax.dynamic_slice_in_dim(mods[2:3], tp * cols, cols, 1)
    residual = lax.dynamic_slice_in_dim(image[0], tp * cols, cols, 1)
    early = (cosine, sine, gains, row_tiles, key_tiles, place, gate, residual, w_sent, w_kept, x_a)
    fourth, early = lax.optimization_barrier((fourth, early))
    cosine, sine, gains, row_tiles, key_tiles, place, gate, residual, w_sent, w_kept, x_a = early
    x_b = pack(shared(third) + shared(fourth))

    kv_a, w_kv = first_kv(section_at, x_a, mine, peer, cosine, sine, gains)
    cond_a = lax.ppermute(kv_a, "section", [(0, 1)])
    kv_b = second_kv(x_b, w_kv, cosine, sine, gains)
    cond_b = lax.ppermute(kv_b, "section", [(0, 1)])
    query, num, den, keep = attend_own(
        (x_a, x_b), direct, cosine, sine, gains, row_tiles, key_tiles, (kv_a, kv_b)
    )
    num, den = attend_first(section_at, keep, query, cond_a, num, den)
    attn = attend_second(section_at, place, keep, query, cond_b, num, den, seq)

    attn = lax.all_to_all(attn, "seq", 0, 0)
    other = lax.ppermute(project_out(attn, w_sent), "tp", both)
    kept = project_out(attn, w_kept, residual, gate)
    return (kept + gate * other.astype(jnp.float32)).astype(jnp.bfloat16)[None]


def rms_rows(x, gain):
    return x * lax.rsqrt(jnp.mean(x * x, axis=-1, keepdims=True) + 1e-06) * gain


def apply_rope(x, cosine, sine):
    rows, heads_here = (x.shape[0], x.shape[1])
    pairs = x.reshape(rows, heads_here, HEAD_DIM // 2, 2)
    first = pairs[..., 0]
    second = pairs[..., 1]
    cosine = cosine[:, None, :]
    sine = sine[:, None, :]
    rotated = jnp.stack([first * cosine - second * sine, first * sine + second * cosine], axis=-1)
    return rotated.reshape(rows, heads_here, HEAD_DIM)


def attend_piece(carry, keys_vals, query, keep):
    num, den = carry
    rows = keys_vals.shape[0]
    heads_local = query.shape[1]
    piece_k = keys_vals[:, 0].reshape(rows, heads_local, HEAD_DIM)
    piece_v = keys_vals[:, 1].reshape(rows, heads_local, HEAD_DIM)
    scores = jnp.einsum("qhd,khd->hqk", query, piece_k, preferred_element_type=jnp.float32) * (
        1.0 / HEAD_DIM**0.5
    )
    weights = jnp.exp(scores)
    if keep is not None:
        weights = jnp.where(keep[None], weights, 0.0)
    den = den + jnp.sum(weights, axis=-1)
    num = num + jnp.einsum(
        "hqk,khd->hqd", weights.astype(jnp.bfloat16), piece_v, preferred_element_type=jnp.float32
    )
    return (num, den)


def token_body(image, text_kv, modulation, w_qkv, w_out, q_gain, k_gain, region_mask):
    img_rows = image.shape[1]
    width_local = w_qkv.shape[2]
    heads_local = width_local // HEAD_DIM
    tokens = image[0].astype(jnp.float32)
    mods = modulation[0]
    normed = layer_norm(tokens, mods)
    qkv = jnp.einsum(
        "td,dcf->tcf",
        normed,
        lax.all_gather(w_qkv, "seq", axis=0, tiled=True),
        preferred_element_type=jnp.float32,
    )
    section_index = lax.axis_index("section")
    time_index = (section_index == 0).astype(jnp.float32)
    rows_index = lax.axis_index("seq") * img_rows + jnp.arange(img_rows, dtype=jnp.int32)
    cosine, sine = rope_tables(rows_index, time_index)
    query = apply_rope(
        rms_rows(qkv[:, 0].reshape(img_rows, heads_local, HEAD_DIM), q_gain), cosine, sine
    ).astype(jnp.bfloat16)
    keys = apply_rope(
        rms_rows(qkv[:, 1].reshape(img_rows, heads_local, HEAD_DIM), k_gain), cosine, sine
    ).astype(jnp.bfloat16)
    values = qkv[:, 2].astype(jnp.bfloat16)
    image_kv = jnp.stack([keys.reshape(img_rows, width_local), values], axis=1)
    own_kv = jnp.concatenate([image_kv, text_kv[0]], axis=0)
    enabled = (section_index == 1).astype(jnp.int32)
    local_mask = region_mask * enabled
    init = (
        jnp.zeros((heads_local, img_rows, HEAD_DIM), jnp.float32),
        jnp.zeros((heads_local, img_rows), jnp.float32),
    )
    carry = attend_piece(init, lax.all_gather(own_kv, "seq", axis=0, tiled=True), query, None)
    cond_local = lax.ppermute(image_kv, "section", [(0, 1)])
    keep = jnp.repeat(jnp.repeat(local_mask, TILE, axis=0), TILE, axis=1) > 0
    carry = attend_piece(carry, lax.all_gather(cond_local, "seq", axis=0, tiled=True), query, keep)
    num, den = carry
    attn = (num / den[..., None]).astype(jnp.bfloat16)
    attn = jnp.transpose(attn, (1, 0, 2)).reshape(img_rows, width_local)
    term = jnp.dot(attn, w_out, preferred_element_type=jnp.float32)
    branch = lax.psum_scatter(
        term.astype(jnp.bfloat16), "tp", scatter_dimension=1, tiled=True
    ).astype(jnp.float32)
    cols = branch.shape[1]
    offset = lax.axis_index("tp") * cols
    residual = lax.dynamic_slice_in_dim(tokens, offset, cols, 1)
    gate = lax.dynamic_slice_in_dim(mods[2], offset, cols, 0)
    out = residual + gate[None, :] * branch
    return out.astype(jnp.bfloat16)[None]


def body(*arrays):
    image, w_qkv, region_mask = arrays[0], arrays[3], arrays[7]
    seq = lax.axis_size("seq")
    one_head_each = (
        w_qkv.shape[2] // HEAD_DIM == seq == 8
        and lax.axis_size("section") == 2
        and lax.axis_size("tp") == 2
        and w_qkv.shape[0] % 128 == 0
        and image.shape[1] == TILE
        and region_mask.shape == (1, seq)
        and arrays[1].shape[1] % 16 == 0
        and arrays[4].shape[1] % 1024 == 0
    )
    return (head_body if one_head_each else token_body)(*arrays)


def solution(mesh):
    return jax.shard_map(
        body,
        mesh=mesh,
        in_specs=(
            P("section", "seq", None),
            P("section", "seq", None, "tp"),
            P("section", None, None),
            P("seq", None, "tp"),
            P("tp", None),
            P(),
            P(),
            P("seq", None),
        ),
        out_specs=P("section", "seq", "tp"),
        check_vma=False,
    )
```

```python
import jax
import jax.numpy as jnp
from jax import lax
from jax.experimental import pallas as pl
from jax.experimental.pallas import tpu as pltpu
from jax.sharding import PartitionSpec as P

HEAD_DIM = 128
GRID_W = 64
TILE = 128
VMEM_LIMIT = 56 * 1024 * 1024


def axis_freqs(width):
    return 10000.0 ** (-jnp.arange(0, width, 2).astype(jnp.float32) / width)


def rope_tables(rows_index, time_index):
    first = HEAD_DIM // 8
    rest = (HEAD_DIM - first) // 2
    row_pos = (rows_index // GRID_W).astype(jnp.float32)
    col_pos = (rows_index % GRID_W).astype(jnp.float32)
    time_pos = jnp.zeros_like(row_pos) + time_index
    angles = jnp.concatenate(
        [
            time_pos[:, None] * axis_freqs(first)[None],
            row_pos[:, None] * axis_freqs(rest)[None],
            col_pos[:, None] * axis_freqs(rest)[None],
        ],
        axis=-1,
    )
    return (jnp.cos(angles), jnp.sin(angles))


def layer_norm(tokens, mods):
    mean = jnp.mean(tokens, axis=-1, keepdims=True)
    var = jnp.mean((tokens - mean) ** 2, axis=-1, keepdims=True)
    return ((tokens - mean) * lax.rsqrt(var + 1e-06) * (1.0 + mods[1:2]) + mods[0:1]).astype(
        jnp.bfloat16
    )


VMEM = pl.BlockSpec(memory_space=pltpu.VMEM)
SMEM = pl.BlockSpec(memory_space=pltpu.SMEM)
ANY = pl.BlockSpec(memory_space=pl.ANY)


def call(kernel, name, out_shape, flops, moved, exps, limit=VMEM_LIMIT, **spec):
    return pl.pallas_call(
        kernel,
        out_shape=out_shape,
        compiler_params=pltpu.CompilerParams(vmem_limit_bytes=limit),
        cost_estimate=pl.CostEstimate(flops=flops, bytes_accessed=moved, transcendentals=exps),
        name=name,
        **spec,
    )


def started(pairs, sems, first=0):
    copies = [pltpu.make_async_copy(s, d, sems.at[first + i]) for i, (s, d) in enumerate(pairs)]
    for copy in copies:
        copy.start()
    return copies


def finished(copies):
    for copy in copies:
        copy.wait()


def norm_kernel(tp_ref, image_hbm, mods_hbm, full_ref, part_ref, image_ref, mods_ref, sems):
    rows = image_ref.shape[0] // 4
    pairs = [
        (image_hbm.at[pl.ds(i * rows, rows), :], image_ref.at[pl.ds(i * rows, rows), :])
        for i in range(4)
    ]
    finished(started(pairs + [(mods_hbm, mods_ref)], sems))
    mods = jnp.concatenate([mods_ref[0], mods_ref[1]], axis=0)
    normed = layer_norm(image_ref[...].astype(jnp.float32), mods)
    part = part_ref.shape[0]
    for t in range(2):

        @pl.when(tp_ref[0] == t)
        def _(t=t):
            ours, theirs = normed[t * part : (t + 1) * part], normed[(1 - t) * part : (2 - t) * part]
            full_ref[:part, :] = ours
            full_ref[part:, :] = theirs
            part_ref[...] = ours


def norm_tokens(tp, image, mods):
    rows, depth = image.shape
    return call(
        norm_kernel, "norm_tokens",
        [
            jax.ShapeDtypeStruct((rows, depth), jnp.bfloat16),
            jax.ShapeDtypeStruct((rows // 2, depth), jnp.bfloat16),
        ],
        10 * rows * depth, 4 * rows * depth, 0,
        in_specs=[SMEM, ANY, ANY],
        out_specs=[VMEM, VMEM],
        scratch_shapes=[
            pltpu.VMEM(image.shape, image.dtype),
            pltpu.VMEM(mods.shape, mods.dtype),
            pltpu.SemaphoreType.DMA((5,)),
        ],
    )(tp, image, mods)


def kv_weights_kernel(section_ref, w_ref, out_ref, sems):
    heads, held, _ = out_ref.shape
    half = held // 2
    rows = pl.ds(pl.multiple_of(section_ref[0] * half, half), half)
    finished(
        started(
            [
                (
                    w_ref.at[1 + kind, rows, pl.ds(s * HEAD_DIM, HEAD_DIM)],
                    out_ref.at[s, pl.ds(kind * half, half), :],
                )
                for s in range(heads)
                for kind in range(2)
            ],
            sems,
        )
    )


def kv_weights(section, w):
    _, depth, width = w.shape
    shape = (width // HEAD_DIM, depth, HEAD_DIM)
    return call(
        kv_weights_kernel, "kv_weights", jax.ShapeDtypeStruct(shape, w.dtype),
        0, 4 * depth * width, 0,
        in_specs=[SMEM, ANY],
        out_specs=ANY,
        scratch_shapes=[pltpu.SemaphoreType.DMA((2 * shape[0],))],
    )(section, w)


def direct_kernel(w_ref, text_ref, mask_ref, out_ref, sems):
    heads = out_ref.shape[0]
    depth, count, last = w_ref.shape[1], text_ref.shape[1], mask_ref.shape[0]
    pairs = []
    for s in range(heads):
        lanes = pl.ds(s * HEAD_DIM, HEAD_DIM)
        pairs.append((w_ref.at[0, :, lanes], out_ref.at[s, pl.ds(0, depth), :]))
        pairs.append((text_ref.at[s], out_ref.at[s, pl.ds(depth, count), :]))
        pairs.append((mask_ref, out_ref.at[s, pl.ds(depth + count, last), :]))
    finished(started(pairs, sems))


def direct_rows(w, text, mask):
    heads, count, _ = text.shape
    shape = (heads, w.shape[1] + count + mask.shape[0], HEAD_DIM)
    return call(
        direct_kernel, "direct_rows", jax.ShapeDtypeStruct(shape, w.dtype),
        0, 4 * heads * shape[1] * HEAD_DIM, 0,
        in_specs=[ANY, ANY, ANY],
        out_specs=ANY,
        scratch_shapes=[pltpu.SemaphoreType.DMA((3 * heads,))],
    )(w, text, mask)


def normed_rotated(x, gain, cosine, sine):
    x = x * lax.rsqrt(jnp.mean(x * x, axis=-1, keepdims=True) + 1e-06) * gain
    even = lax.broadcasted_iota(jnp.int32, x.shape, 1) % 2 == 0
    other = jnp.where(even, pltpu.roll(x, HEAD_DIM - 1, 1), pltpu.roll(x, 1, 1))
    return (x * cosine + other * sine).astype(jnp.bfloat16)


def table_of(tabs_ref, which, start, rows):
    groups = tabs_ref.shape[1] - GRID_W
    columns = tabs_ref[which, groups:, :]
    lane = lax.broadcasted_iota(jnp.int32, columns.shape, 1)
    first = HEAD_DIM // 8
    by_row = lane < first + (HEAD_DIM - first) // 2
    return jnp.concatenate(
        [
            jnp.where(by_row, tabs_ref[which, g : g + 1, :], columns)
            for g in range(start // GRID_W, (start + rows) // GRID_W)
        ],
        axis=0,
    )


def piece_copies(piece_refs, x_ref):
    at, pairs = 0, []
    for ref in piece_refs:
        pairs.append((ref, x_ref.at[pl.ds(at, ref.shape[0]), :]))
        at += ref.shape[0]
    return pairs


def kv_kernel(chunk, section_ref, tabs_ref, gain_ref, mine_hbm, peer_a, peer_b, *refs):
    piece_refs, (kv_ref, x_ref, mine, peer, w_ref, sems) = refs[:-6], refs[-6:]
    sources, held, _ = mine.shape
    half = held // 2
    some = sources // 2
    weights = started(
        [
            (mine_hbm, mine),
            (peer_a, peer.at[pl.ds(0, some)]),
            (peer_b, peer.at[pl.ds(some, some)]),
        ],
        sems,
    )
    tokens = started(piece_copies(piece_refs, x_ref), sems, 3)
    finished(weights)
    first = section_ref[0] == 0
    for s in range(sources):
        for kind in range(2):
            at = slice(kind * half, (kind + 1) * half)
            lanes = slice(kind * HEAD_DIM, (kind + 1) * HEAD_DIM)
            a, b = mine[s, at, :], peer[s, at, :]
            w_ref[2 * s * half : (2 * s + 1) * half, lanes] = jnp.where(first, a, b)
            w_ref[(2 * s + 1) * half : (2 * s + 2) * half, lanes] = jnp.where(first, b, a)
    finished(tokens)
    both = jnp.dot(x_ref[...], w_ref[...], preferred_element_type=jnp.float32)
    rows = x_ref.shape[0]
    kv_ref[0] = normed_rotated(
        both[:, :HEAD_DIM],
        gain_ref[1:2, :],
        table_of(tabs_ref, 0, chunk * rows, rows),
        table_of(tabs_ref, 1, chunk * rows, rows),
    )
    kv_ref[1] = both[:, HEAD_DIM:].astype(jnp.bfloat16)


def project_kv(chunk, section, tabs, gains, mine, peers, pieces):
    depth = pieces[0].shape[1]
    rows = sum(p.shape[0] for p in pieces)
    return call(
        lambda *refs: kv_kernel(chunk, *refs), "project_kv" + "ab"[chunk],
        jax.ShapeDtypeStruct((2, rows, HEAD_DIM), jnp.bfloat16),
        4 * rows * depth * HEAD_DIM, 2 * (rows * depth + 2 * mine.size), 0,
        in_specs=[SMEM, VMEM, VMEM] + [ANY] * (3 + len(pieces)),
        out_specs=VMEM,
        scratch_shapes=[
            pltpu.VMEM((rows, depth), jnp.bfloat16),
            pltpu.VMEM(mine.shape, jnp.bfloat16),
            pltpu.VMEM(mine.shape, jnp.bfloat16),
            pltpu.VMEM((depth, 2 * HEAD_DIM), jnp.bfloat16),
            pltpu.SemaphoreType.DMA((3 + len(pieces),)),
        ],
    )(section, tabs, gains, mine, *peers, *pieces)


def weights_of(query, keys):
    scores = lax.dot_general(
        query, keys, (((1,), (1,)), ((), ())), preferred_element_type=jnp.float32
    )
    return jnp.exp(scores * (1.0 / HEAD_DIM**0.5))


def summed(weights, values):
    den = jnp.sum(weights, axis=-1, keepdims=True)
    num = jnp.dot(weights.astype(jnp.bfloat16), values, preferred_element_type=jnp.float32)
    return num, den


def kept_weights(query, cond_ref, keep):
    weights = weights_of(query, cond_ref[0])
    rows, keys = weights.shape
    groups = keep.shape[0]
    return (weights.reshape(groups, rows // groups, keys) * keep[:, None, :]).reshape(rows, keys)


BLOCK = 256


def own_kernel(tabs_ref, gain_ref, rows_ref, keys_ref, kva, kvb, direct_hbm, *refs):
    piece_refs = refs[:-7]
    q_ref, num_ref, den_ref, keep_ref, x_ref, direct, sems = refs[-7:]
    rows, depth = x_ref.shape
    sources, held, _ = direct.shape
    copies = started(
        [(direct_hbm.at[s], direct.at[s]) for s in range(sources)]
        + piece_copies(piece_refs, x_ref),
        sems,
    )
    finished(copies)
    wide = depth // sources
    w = direct[:, :wide, :].reshape(depth, HEAD_DIM)
    count = (held - 16 - wide) // 2
    text = (
        direct[:, wide : wide + count, :].reshape(-1, HEAD_DIM),
        direct[:, wide + count : wide + 2 * count, :].reshape(-1, HEAD_DIM),
    )
    for b in range(rows // BLOCK):
        at = slice(b * BLOCK, (b + 1) * BLOCK)
        query = jnp.dot(x_ref[at, :], w, preferred_element_type=jnp.float32)
        query = normed_rotated(
            query,
            gain_ref[0:1, :],
            table_of(tabs_ref, 0, b * BLOCK, BLOCK),
            table_of(tabs_ref, 1, b * BLOCK, BLOCK),
        )
        q_ref[at, :] = query
        num, den = 0.0, 0.0
        for keys, values in ((kva[0], kva[1]), (kvb[0], kvb[1]), text):
            more = summed(weights_of(query, keys), values)
            num, den = num + more[0], den + more[1]
        num_ref[at, :] = num
        den_ref[at, :] = jnp.broadcast_to(den, num.shape)
    mask = jnp.concatenate(
        [direct[s, held - 16 : held, :].astype(jnp.float32)[:1] for s in range(sources)], axis=0
    )
    mask = jnp.dot(rows_ref[...], mask, preferred_element_type=jnp.float32)
    mask = jnp.dot(mask, keys_ref[...], preferred_element_type=jnp.float32)
    size = rows // keep_ref.shape[0]
    for g in range(keep_ref.shape[0]):
        keep_ref[:, g * size : (g + 1) * size] = jnp.broadcast_to(
            mask[:, g : g + 1], (keep_ref.shape[0], size)
        )


def cond_sum(keep_ref, q_ref, cond, chunk, b):
    groups = keep_ref.shape[0] * BLOCK // q_ref.shape[0]
    keys = cond.shape[1]
    keep = keep_ref[b * groups : (b + 1) * groups, chunk * keys : (chunk + 1) * keys]
    return summed(kept_weights(q_ref[b * BLOCK : (b + 1) * BLOCK, :], cond, keep), cond[1])


def first_cond_kernel(section_ref, keep_ref, q_ref, cond, num_in, den_in, num_ref, den_ref):
    @pl.when(section_ref[0] == 0)
    def _():
        num_ref[...] = num_in[...]
        den_ref[...] = den_in[...]

    @pl.when(section_ref[0] != 0)
    def _():
        for b in range(num_ref.shape[0] // BLOCK):
            at = slice(b * BLOCK, (b + 1) * BLOCK)
            num, den = cond_sum(keep_ref, q_ref, cond, 0, b)
            num_ref[at, :] = num_in[at, :] + num
            den_ref[at, :] = den_in[at, :] + den


def second_cond_kernel(section_ref, place_ref, keep_ref, q_ref, cond, num_ref, den_ref, out_ref):
    groups = keep_ref.shape[0] * BLOCK // num_ref.shape[0]
    size = BLOCK // groups

    def store(b, num, den):
        value = (num / den).astype(jnp.bfloat16)
        for g in range(groups):
            shard, part = place_ref[0, b * groups + g], place_ref[1, b * groups + g]
            at = pl.ds(pl.multiple_of(part * size, size), size)
            out_ref[shard, at, :] = value[g * size : (g + 1) * size]

    @pl.when(section_ref[0] == 0)
    def _():
        for b in range(num_ref.shape[0] // BLOCK):
            at = slice(b * BLOCK, (b + 1) * BLOCK)
            store(b, num_ref[at, :], den_ref[at, :])

    @pl.when(section_ref[0] != 0)
    def _():
        for b in range(num_ref.shape[0] // BLOCK):
            at = slice(b * BLOCK, (b + 1) * BLOCK)
            num, den = cond_sum(keep_ref, q_ref, cond, 1, b)
            store(b, num_ref[at, :] + num, den_ref[at, :] + den)


def attend_own(tabs, gains, row_tiles, key_tiles, kvs, direct, pieces):
    depth = pieces[0].shape[1]
    rows = sum(p.shape[0] for p in pieces)
    keys = rows + rows // 2
    return call(
        own_kernel, "attend_own",
        [
            jax.ShapeDtypeStruct((rows, HEAD_DIM), jnp.bfloat16),
            jax.ShapeDtypeStruct((rows, HEAD_DIM), jnp.float32),
            jax.ShapeDtypeStruct((rows, HEAD_DIM), jnp.float32),
            jax.ShapeDtypeStruct((row_tiles.shape[0], rows), jnp.float32),
        ],
        2 * rows * HEAD_DIM * (2 * keys + depth), 2 * rows * depth, rows * keys,
        in_specs=[VMEM] * 6 + [ANY] * (1 + len(pieces)),
        out_specs=[VMEM] * 4,
        scratch_shapes=[
            pltpu.VMEM((rows, depth), jnp.bfloat16),
            pltpu.VMEM(direct.shape, jnp.bfloat16),
            pltpu.SemaphoreType.DMA((direct.shape[0] + len(pieces),)),
        ],
    )(tabs, gains, row_tiles, key_tiles, *kvs, direct, *pieces)


def attend_first(section, keep, query, cond, num, den):
    rows, keys = num.shape[0], cond.shape[1]
    return call(
        first_cond_kernel, "attend_first", [jax.ShapeDtypeStruct(num.shape, jnp.float32)] * 2,
        4 * rows * keys * HEAD_DIM, 2 * rows * HEAD_DIM * 8, rows * keys,
        in_specs=[SMEM] + [VMEM] * 5,
        out_specs=[VMEM] * 2,
    )(section, keep, query, cond, num, den)


def attend_second(section, place, keep, query, cond, num, den, seq):
    rows, keys = num.shape[0], cond.shape[1]
    return call(
        second_cond_kernel, "attend_second",
        jax.ShapeDtypeStruct((seq, rows // seq, HEAD_DIM), jnp.bfloat16),
        4 * rows * keys * HEAD_DIM, 2 * rows * HEAD_DIM * 8, rows * keys,
        in_specs=[SMEM, SMEM] + [VMEM] * 5,
        out_specs=VMEM,
    )(section, place, keep, query, cond, num, den)


def token_rows(attn_ref):
    return jnp.concatenate([attn_ref[h] for h in range(attn_ref.shape[0])], axis=1)


def product(half, attn_ref, w_hbm, w_ref, sems):
    depth, width = w_ref.shape
    rows = depth // sems.shape[0]
    columns = pl.ds(pl.multiple_of(half * width, width), width)
    finished(
        started(
            [
                (w_hbm.at[pl.ds(i * rows, rows), columns], w_ref.at[pl.ds(i * rows, rows), :])
                for i in range(sems.shape[0])
            ],
            sems,
        )
    )
    return jnp.dot(token_rows(attn_ref), w_ref[...], preferred_element_type=jnp.float32)


def sent_kernel(half_ref, attn_ref, w_hbm, out_ref, w_ref, sems):
    branch = product(1 - half_ref[0], attn_ref, w_hbm, w_ref, sems)
    out_ref[...] = branch.astype(jnp.bfloat16)


def kept_kernel(half_ref, attn_ref, w_hbm, image_ref, gate_ref, out_ref, w_ref, sems):
    branch = product(half_ref[0], attn_ref, w_hbm, w_ref, sems)
    out_ref[...] = image_ref[...].astype(jnp.float32) + gate_ref[...] * branch


def project_out(half, attn, w, image=None, gate=None):
    rows = attn.shape[1]
    depth, width = w.shape[0], w.shape[1] // 2
    kept = image is not None
    more = (image, gate) if kept else ()
    return call(
        kept_kernel if kept else sent_kernel, "out_kept" if kept else "out_sent",
        jax.ShapeDtypeStruct((rows, width), jnp.float32 if kept else jnp.bfloat16),
        2 * rows * depth * width, 2 * depth * width, 0,
        in_specs=[SMEM, VMEM, ANY] + [VMEM] * len(more),
        out_specs=VMEM,
        scratch_shapes=[pltpu.VMEM((depth, width), w.dtype), pltpu.SemaphoreType.DMA((8,))],
    )(half, attn, w, *more)


def lane_tables(row_ids, time_index):
    first = HEAD_DIM // 8
    rest = (HEAD_DIM - first) // 2
    freqs = jnp.concatenate([axis_freqs(first), axis_freqs(rest), axis_freqs(rest)])
    freqs = jnp.repeat(freqs, 2)[None]
    lane = jnp.arange(HEAD_DIM, dtype=jnp.int32)[None]
    rows = jnp.where(lane < first, time_index, row_ids.astype(jnp.float32)[:, None])
    columns = jnp.broadcast_to(jnp.arange(GRID_W, dtype=jnp.float32)[:, None], (GRID_W, HEAD_DIM))
    angles = jnp.concatenate([rows, columns], axis=0) * freqs
    return jnp.stack([jnp.cos(angles), jnp.sin(angles) * jnp.where(lane % 2 == 0, -1.0, 1.0)])


def z_pairs(seq, pairs):
    return [(2 * a + core, 2 * b + core) for a, b in pairs for core in range(2)]


def head_body(image, text_kv, modulation, w_qkv, w_out, q_gain, k_gain, region_mask):
    seq = lax.axis_size("seq")
    img_rows = image.shape[1]
    depth = w_qkv.shape[0]
    section = lax.axis_index("section")
    tp = lax.axis_index("tp")
    chip, core = lax.axis_index("seq") // 2, lax.axis_index("seq") % 2
    mods = modulation[0]
    section_at = section.astype(jnp.int32).reshape(1)
    tp_at = tp.astype(jnp.int32).reshape(1)
    both = [(0, 1), (1, 0)]

    upper = chip >= 2
    chips = jnp.stack([chip, chip ^ 1, jnp.where(upper, 1, 2), jnp.where(upper, 0, 3)])
    cores = jnp.stack([core, 1 - core])
    parts = jnp.stack([tp, 1 - tp])
    shards = chips[:, None, None] * 2 + cores[None, :, None] + 0 * parts[None, None, :]
    parts = parts[None, None, :] + 0 * shards
    shards, parts = shards.reshape(-1).astype(jnp.int32), parts.reshape(-1).astype(jnp.int32)
    size = img_rows // 2
    row_ids = shards * (img_rows // GRID_W) + parts * (size // GRID_W)
    tabs = lane_tables(row_ids, (section == 0).astype(jnp.float32))
    gains = jnp.stack([q_gain, k_gain])
    row_tiles = (shards[:, None] == jnp.arange(seq)[None]).astype(jnp.float32)
    key_tiles = jnp.arange(HEAD_DIM)[:, None] == shards[None]
    key_tiles = key_tiles.astype(jnp.float32)
    place = jnp.stack([shards, parts])

    rows3 = w_qkv.transpose(1, 0, 2)
    mine = lax.all_to_all(kv_weights(section_at, rows3), "seq", 0, 0)

    full, part = norm_tokens(tp_at, image[0], modulation.transpose(1, 0, 2))

    def along_z(x, pairs):
        return lax.ppermute(x, "seq", z_pairs(seq, pairs))

    def to_core(x):
        return lax.ppermute(x, "seq", [(s, s ^ 1) for s in range(seq)])

    def to_tp(x):
        return lax.ppermute(x, "tp", both)

    near = along_z(part, [(0, 1), (1, 0), (2, 3), (3, 2)])
    middle = along_z(part, [(1, 2), (2, 1)])
    far = along_z(near, [(1, 2), (2, 1)])
    middle_end = along_z(middle, [(1, 0), (2, 3)])
    far_end = along_z(far, [(1, 0), (2, 3)])
    inner = (chip == 1) | (chip == 2)
    third = jnp.where(inner, middle, middle_end)
    fourth = jnp.where(inner, far, far_end)

    text = text_kv[0].reshape(-1, 2, seq, HEAD_DIM).transpose(2, 1, 0, 3).reshape(seq, -1, HEAD_DIM)
    mask = jnp.pad(
        region_mask.astype(jnp.bfloat16), ((0, 15), (0, HEAD_DIM - region_mask.shape[1]))
    )
    direct = direct_rows(rows3, text, mask)

    near_tp = to_tp(near)
    third, near_tp, mine = lax.optimization_barrier((third, near_tp, mine))
    third_tp = to_tp(third)
    some = seq // 2
    peers = [lax.ppermute(mine[:some], "section", both), lax.ppermute(mine[some:], "section", both)]
    direct, mine = lax.optimization_barrier((direct, mine))
    direct = lax.all_to_all(direct, "seq", 0, 0)
    cols = w_out.shape[1] // 2
    gate = lax.dynamic_slice_in_dim(mods[2:3], tp * cols, cols, 1)
    residual = lax.dynamic_slice_in_dim(image[0], tp * cols, cols, 1)
    early = (tabs, gains, row_tiles, key_tiles, place, gate, residual)
    fourth, third_tp, peers[0], early = lax.optimization_barrier((fourth, third_tp, peers[0], early))
    tabs, gains, row_tiles, key_tiles, place, gate, residual = early
    fourth_tp = to_tp(fourth)
    fourth, fourth_tp, peers[1] = lax.optimization_barrier((fourth, fourth_tp, peers[1]))
    a = [full, to_core(full), near, near_tp, to_core(near), to_core(near_tp)]
    b = [third, third_tp, to_core(third), to_core(third_tp)]
    b += [fourth, fourth_tp, to_core(fourth), to_core(fourth_tp)]

    kv_a = project_kv(0, section_at, tabs, gains, mine, peers, a)
    cond_a = lax.ppermute(kv_a, "section", [(0, 1)])
    kv_b = project_kv(1, section_at, tabs, gains, mine, peers, b)
    cond_b = lax.ppermute(kv_b, "section", [(0, 1)])
    query, num, den, keep = attend_own(
        tabs, gains, row_tiles, key_tiles, (kv_a, kv_b), direct, a + b
    )
    num, den = attend_first(section_at, keep, query, cond_a, num, den)
    attn = attend_second(section_at, place, keep, query, cond_b, num, den, seq)

    attn = lax.all_to_all(attn, "seq", 0, 0)
    other = to_tp(project_out(tp_at, attn, w_out))
    kept = project_out(tp_at, attn, w_out, residual, gate)
    return (kept + gate * other.astype(jnp.float32)).astype(jnp.bfloat16)[None]


def rms_rows(x, gain):
    return x * lax.rsqrt(jnp.mean(x * x, axis=-1, keepdims=True) + 1e-06) * gain


def apply_rope(x, cosine, sine):
    rows, heads_here = (x.shape[0], x.shape[1])
    pairs = x.reshape(rows, heads_here, HEAD_DIM // 2, 2)
    first = pairs[..., 0]
    second = pairs[..., 1]
    cosine = cosine[:, None, :]
    sine = sine[:, None, :]
    rotated = jnp.stack([first * cosine - second * sine, first * sine + second * cosine], axis=-1)
    return rotated.reshape(rows, heads_here, HEAD_DIM)


def attend_piece(carry, keys_vals, query, keep):
    num, den = carry
    rows = keys_vals.shape[0]
    heads_local = query.shape[1]
    piece_k = keys_vals[:, 0].reshape(rows, heads_local, HEAD_DIM)
    piece_v = keys_vals[:, 1].reshape(rows, heads_local, HEAD_DIM)
    scores = jnp.einsum("qhd,khd->hqk", query, piece_k, preferred_element_type=jnp.float32) * (
        1.0 / HEAD_DIM**0.5
    )
    weights = jnp.exp(scores)
    if keep is not None:
        weights = jnp.where(keep[None], weights, 0.0)
    den = den + jnp.sum(weights, axis=-1)
    num = num + jnp.einsum(
        "hqk,khd->hqd", weights.astype(jnp.bfloat16), piece_v, preferred_element_type=jnp.float32
    )
    return (num, den)


def token_body(image, text_kv, modulation, w_qkv, w_out, q_gain, k_gain, region_mask):
    img_rows = image.shape[1]
    width_local = w_qkv.shape[2]
    heads_local = width_local // HEAD_DIM
    tokens = image[0].astype(jnp.float32)
    mods = modulation[0]
    normed = layer_norm(tokens, mods)
    qkv = jnp.einsum(
        "td,dcf->tcf",
        normed,
        lax.all_gather(w_qkv, "seq", axis=0, tiled=True),
        preferred_element_type=jnp.float32,
    )
    section_index = lax.axis_index("section")
    time_index = (section_index == 0).astype(jnp.float32)
    rows_index = lax.axis_index("seq") * img_rows + jnp.arange(img_rows, dtype=jnp.int32)
    cosine, sine = rope_tables(rows_index, time_index)
    query = apply_rope(
        rms_rows(qkv[:, 0].reshape(img_rows, heads_local, HEAD_DIM), q_gain), cosine, sine
    ).astype(jnp.bfloat16)
    keys = apply_rope(
        rms_rows(qkv[:, 1].reshape(img_rows, heads_local, HEAD_DIM), k_gain), cosine, sine
    ).astype(jnp.bfloat16)
    values = qkv[:, 2].astype(jnp.bfloat16)
    image_kv = jnp.stack([keys.reshape(img_rows, width_local), values], axis=1)
    own_kv = jnp.concatenate([image_kv, text_kv[0]], axis=0)
    enabled = (section_index == 1).astype(jnp.int32)
    local_mask = region_mask * enabled
    init = (
        jnp.zeros((heads_local, img_rows, HEAD_DIM), jnp.float32),
        jnp.zeros((heads_local, img_rows), jnp.float32),
    )
    carry = attend_piece(init, lax.all_gather(own_kv, "seq", axis=0, tiled=True), query, None)
    cond_local = lax.ppermute(image_kv, "section", [(0, 1)])
    keep = jnp.repeat(jnp.repeat(local_mask, TILE, axis=0), TILE, axis=1) > 0
    carry = attend_piece(carry, lax.all_gather(cond_local, "seq", axis=0, tiled=True), query, keep)
    num, den = carry
    attn = (num / den[..., None]).astype(jnp.bfloat16)
    attn = jnp.transpose(attn, (1, 0, 2)).reshape(img_rows, width_local)
    term = jnp.dot(attn, w_out, preferred_element_type=jnp.float32)
    branch = lax.psum_scatter(
        term.astype(jnp.bfloat16), "tp", scatter_dimension=1, tiled=True
    ).astype(jnp.float32)
    cols = branch.shape[1]
    offset = lax.axis_index("tp") * cols
    residual = lax.dynamic_slice_in_dim(tokens, offset, cols, 1)
    gate = lax.dynamic_slice_in_dim(mods[2], offset, cols, 0)
    out = residual + gate[None, :] * branch
    return out.astype(jnp.bfloat16)[None]


def body(*arrays):
    image, w_qkv, region_mask = arrays[0], arrays[3], arrays[7]
    seq = lax.axis_size("seq")
    one_head_each = (
        w_qkv.shape[2] // HEAD_DIM == seq == 8
        and lax.axis_size("section") == 2
        and lax.axis_size("tp") == 2
        and w_qkv.shape[0] % 128 == 0
        and image.shape[1] == TILE == 2 * GRID_W
        and region_mask.shape == (1, seq)
        and arrays[1].shape[1] % 16 == 0
        and arrays[4].shape[1] % 1024 == 0
    )
    return (head_body if one_head_each else token_body)(*arrays)


def solution(mesh):
    return jax.shard_map(
        body,
        mesh=mesh,
        in_specs=(
            P("section", "seq", None),
            P("section", "seq", None, "tp"),
            P("section", None, None),
            P("seq", None, "tp"),
            P("tp", None),
            P(),
            P(),
            P("seq", None),
        ),
        out_specs=P("section", "seq", "tp"),
        check_vma=False,
    )
```

```python
import jax
import jax.numpy as jnp
from jax import lax
from jax.experimental import pallas as pl
from jax.experimental.pallas import tpu as pltpu
from jax.sharding import PartitionSpec as P

HEAD_DIM = 128
GRID_W = 64
TILE = 128
VMEM_LIMIT = 24 * 1024 * 1024


def axis_freqs(width):
    return 10000.0 ** (-jnp.arange(0, width, 2).astype(jnp.float32) / width)


def rope_tables(rows_index, time_index):
    first = HEAD_DIM // 8
    rest = (HEAD_DIM - first) // 2
    row_pos = (rows_index // GRID_W).astype(jnp.float32)
    col_pos = (rows_index % GRID_W).astype(jnp.float32)
    time_pos = jnp.zeros_like(row_pos) + time_index
    angles = jnp.concatenate(
        [
            time_pos[:, None] * axis_freqs(first)[None],
            row_pos[:, None] * axis_freqs(rest)[None],
            col_pos[:, None] * axis_freqs(rest)[None],
        ],
        axis=-1,
    )
    return (jnp.cos(angles), jnp.sin(angles))


def layer_norm(tokens, mods):
    mean = jnp.mean(tokens, axis=-1, keepdims=True)
    var = jnp.mean((tokens - mean) ** 2, axis=-1, keepdims=True)
    return ((tokens - mean) * lax.rsqrt(var + 1e-06) * (1.0 + mods[1:2]) + mods[0:1]).astype(
        jnp.bfloat16
    )


VMEM = pl.BlockSpec(memory_space=pltpu.VMEM)
SMEM = pl.BlockSpec(memory_space=pltpu.SMEM)
HBM = pl.BlockSpec(memory_space=pltpu.HBM)


def call(kernel, name, out_shape, flops, moved, exps, limit=VMEM_LIMIT, **spec):
    return pl.pallas_call(
        kernel,
        out_shape=out_shape,
        compiler_params=pltpu.CompilerParams(vmem_limit_bytes=limit),
        cost_estimate=pl.CostEstimate(flops=flops, bytes_accessed=moved, transcendentals=exps),
        name=name,
        **spec,
    )


def started(pairs, sems, first=0):
    copies = [pltpu.make_async_copy(s, d, sems.at[first + i]) for i, (s, d) in enumerate(pairs)]
    for copy in copies:
        copy.start()
    return copies


def finished(copies):
    for copy in copies:
        copy.wait()


def norm_kernel(tp_ref, image_hbm, mods_hbm, full_ref, part_ref, image_ref, mods_ref, sems):
    rows = image_ref.shape[0] // 4
    pairs = [
        (image_hbm.at[pl.ds(i * rows, rows), :], image_ref.at[pl.ds(i * rows, rows), :])
        for i in range(4)
    ]
    finished(started(pairs + [(mods_hbm, mods_ref)], sems))
    mods = jnp.concatenate([mods_ref[0], mods_ref[1]], axis=0)
    normed = layer_norm(image_ref[...].astype(jnp.float32), mods)
    part = part_ref.shape[0]
    for t in range(2):

        @pl.when(tp_ref[0] == t)
        def _(t=t):
            ours, theirs = normed[t * part : (t + 1) * part], normed[(1 - t) * part : (2 - t) * part]
            full_ref[:part, :] = ours
            full_ref[part:, :] = theirs
            part_ref[...] = ours


def norm_tokens(tp, image, mods):
    rows, depth = image.shape
    return call(
        norm_kernel, "norm_tokens",
        [
            jax.ShapeDtypeStruct((rows, depth), jnp.bfloat16),
            jax.ShapeDtypeStruct((rows // 2, depth), jnp.bfloat16),
        ],
        10 * rows * depth, 4 * rows * depth, 0,
        in_specs=[SMEM, HBM, HBM],
        out_specs=[VMEM, VMEM],
        scratch_shapes=[
            pltpu.VMEM(image.shape, image.dtype),
            pltpu.VMEM(mods.shape, mods.dtype),
            pltpu.SemaphoreType.DMA((5,)),
        ],
    )(tp, image, mods)


def kv_weights_kernel(section_ref, w_hbm, out_ref, w_ref, sems):
    half = w_ref.shape[1]
    rows = pl.ds(pl.multiple_of(section_ref[0] * half, half), half)
    copies = started([(w_hbm.at[1 + k, rows, :], w_ref.at[k]) for k in range(2)], sems)
    for k in range(2):
        copies[k].wait()
        for s in range(out_ref.shape[0]):
            out_ref[s, k * half : (k + 1) * half, :] = w_ref[k, :, s * HEAD_DIM : (s + 1) * HEAD_DIM]


def kv_weights(section, w):
    _, depth, width = w.shape
    return call(
        kv_weights_kernel, "kv_weights",
        jax.ShapeDtypeStruct((width // HEAD_DIM, depth, HEAD_DIM), w.dtype),
        0, 4 * depth * width, 0,
        in_specs=[SMEM, HBM],
        out_specs=VMEM,
        scratch_shapes=[pltpu.VMEM((2, depth // 2, width), w.dtype), pltpu.SemaphoreType.DMA((2,))],
    )(section, w)


def direct_kernel(w_hbm, text_hbm, mask_ref, out_ref, w_ref, text_ref, sems):
    depth, count = w_ref.shape[0], text_ref.shape[1]
    copies = started([(w_hbm.at[0], w_ref), (text_hbm, text_ref)], sems)
    finished(copies)
    for s in range(out_ref.shape[0]):
        out_ref[s, :depth, :] = w_ref[:, s * HEAD_DIM : (s + 1) * HEAD_DIM]
        out_ref[s, depth : depth + count, :] = text_ref[s]
        out_ref[s, depth + count :, :] = mask_ref[...]


def direct_rows(w, text, mask):
    heads, count, _ = text.shape
    shape = (heads, w.shape[1] + count + mask.shape[0], HEAD_DIM)
    return call(
        direct_kernel, "direct_rows", jax.ShapeDtypeStruct(shape, w.dtype),
        0, 4 * heads * shape[1] * HEAD_DIM, 0,
        in_specs=[HBM, HBM, VMEM],
        out_specs=VMEM,
        scratch_shapes=[
            pltpu.VMEM(w.shape[1:], w.dtype),
            pltpu.VMEM(text.shape, text.dtype),
            pltpu.SemaphoreType.DMA((2,)),
        ],
    )(w, text, mask)


def normed_rotated(x, gain, cosine, sine):
    x = x * lax.rsqrt(jnp.mean(x * x, axis=-1, keepdims=True) + 1e-06) * gain
    even = lax.broadcasted_iota(jnp.int32, x.shape, 1) % 2 == 0
    other = jnp.where(even, pltpu.roll(x, HEAD_DIM - 1, 1), pltpu.roll(x, 1, 1))
    return (x * cosine + other * sine).astype(jnp.bfloat16)


def table_of(tabs_ref, which, start, rows):
    groups = tabs_ref.shape[1] - GRID_W
    columns = tabs_ref[which, groups:, :]
    lane = lax.broadcasted_iota(jnp.int32, columns.shape, 1)
    first = HEAD_DIM // 8
    by_row = lane < first + (HEAD_DIM - first) // 2
    return jnp.concatenate(
        [
            jnp.where(by_row, tabs_ref[which, g : g + 1, :], columns)
            for g in range(start // GRID_W, (start + rows) // GRID_W)
        ],
        axis=0,
    )


def piece_copies(piece_refs, x_ref):
    at, pairs = 0, []
    for ref in piece_refs:
        pairs.append((ref, x_ref.at[pl.ds(at, ref.shape[0]), :]))
        at += ref.shape[0]
    return pairs


def blocks(rows):
    return [(b, slice(b * BLOCK, (b + 1) * BLOCK)) for b in range(rows // BLOCK)]


def arrived(copies, piece_refs, rows):
    at = 0
    for copy, ref in zip(copies, piece_refs):
        if rows.start <= at < rows.stop:
            copy.wait()
        at += ref.shape[0]


def kv_kernel(chunk, section_ref, tabs_ref, gain_ref, mine_hbm, peer_a, peer_b, *refs):
    piece_refs, (kv_ref, x_ref, mine, peer, w_ref, sems) = refs[:-6], refs[-6:]
    sources, held, _ = mine.shape
    half = held // 2
    some = sources // 2
    weights = started(
        [
            (mine_hbm, mine),
            (peer_a, peer.at[pl.ds(0, some)]),
            (peer_b, peer.at[pl.ds(some, some)]),
        ],
        sems,
    )
    tokens = started(piece_copies(piece_refs, x_ref), sems, 3)
    finished(weights)
    first = section_ref[0] == 0
    for s in range(sources):
        for kind in range(2):
            at = slice(kind * half, (kind + 1) * half)
            lanes = slice(kind * HEAD_DIM, (kind + 1) * HEAD_DIM)
            a, b = mine[s, at, :], peer[s, at, :]
            w_ref[2 * s * half : (2 * s + 1) * half, lanes] = jnp.where(first, a, b)
            w_ref[(2 * s + 1) * half : (2 * s + 2) * half, lanes] = jnp.where(first, b, a)
    for b, at in blocks(x_ref.shape[0]):
        arrived(tokens, piece_refs, at)
        both = jnp.dot(x_ref[at, :], w_ref[...], preferred_element_type=jnp.float32)
        start = chunk * x_ref.shape[0] + b * BLOCK
        kv_ref[0, at, :] = normed_rotated(
            both[:, :HEAD_DIM],
            gain_ref[1:2, :],
            table_of(tabs_ref, 0, start, BLOCK),
            table_of(tabs_ref, 1, start, BLOCK),
        )
        kv_ref[1, at, :] = both[:, HEAD_DIM:].astype(jnp.bfloat16)


def project_kv(chunk, section, tabs, gains, mine, peers, pieces):
    depth = pieces[0].shape[1]
    rows = sum(p.shape[0] for p in pieces)
    return call(
        lambda *refs: kv_kernel(chunk, *refs), "project_kv" + "ab"[chunk],
        jax.ShapeDtypeStruct((2, rows, HEAD_DIM), jnp.bfloat16),
        4 * rows * depth * HEAD_DIM, 2 * (rows * depth + 2 * mine.size), 0,
        in_specs=[SMEM, VMEM, VMEM] + [HBM] * (3 + len(pieces)),
        out_specs=VMEM,
        scratch_shapes=[
            pltpu.VMEM((rows, depth), jnp.bfloat16),
            pltpu.VMEM(mine.shape, jnp.bfloat16),
            pltpu.VMEM(mine.shape, jnp.bfloat16),
            pltpu.VMEM((depth, 2 * HEAD_DIM), jnp.bfloat16),
            pltpu.SemaphoreType.DMA((3 + len(pieces),)),
        ],
    )(section, tabs, gains, mine, *peers, *pieces)


def weights_of(query, keys):
    scores = lax.dot_general(
        query, keys, (((1,), (1,)), ((), ())), preferred_element_type=jnp.float32
    )
    return jnp.exp(scores * (1.0 / HEAD_DIM**0.5))


def summed(weights, values):
    den = jnp.sum(weights, axis=-1, keepdims=True)
    num = jnp.dot(weights.astype(jnp.bfloat16), values, preferred_element_type=jnp.float32)
    return num, den


def kept_weights(query, cond_ref, keep):
    weights = weights_of(query, cond_ref[0])
    rows, keys = weights.shape
    groups = keep.shape[0]
    return (weights.reshape(groups, rows // groups, keys) * keep[:, None, :]).reshape(rows, keys)


BLOCK = 256


def own_kernel(tabs_ref, gain_ref, rows_ref, keys_ref, kva, kvb, direct_hbm, *refs):
    piece_refs = refs[:-7]
    q_ref, num_ref, den_ref, keep_ref, x_ref, direct, sems = refs[-7:]
    rows, depth = x_ref.shape
    sources, held, _ = direct.shape
    copies = started([(direct_hbm.at[s], direct.at[s]) for s in range(sources)], sems)
    tokens = started(piece_copies(piece_refs, x_ref), sems, sources)
    finished(copies)
    wide = depth // sources
    w = direct[:, :wide, :].reshape(depth, HEAD_DIM)
    count = (held - 16 - wide) // 2
    text = (
        direct[:, wide : wide + count, :].reshape(-1, HEAD_DIM),
        direct[:, wide + count : wide + 2 * count, :].reshape(-1, HEAD_DIM),
    )
    for b, at in blocks(rows):
        arrived(tokens, piece_refs, at)
        query = jnp.dot(x_ref[at, :], w, preferred_element_type=jnp.float32)
        query = normed_rotated(
            query,
            gain_ref[0:1, :],
            table_of(tabs_ref, 0, b * BLOCK, BLOCK),
            table_of(tabs_ref, 1, b * BLOCK, BLOCK),
        )
        q_ref[at, :] = query
        num, den = 0.0, 0.0
        for keys, values in ((kva[0], kva[1]), (kvb[0], kvb[1]), text):
            more = summed(weights_of(query, keys), values)
            num, den = num + more[0], den + more[1]
        num_ref[at, :] = num
        den_ref[at, :] = jnp.broadcast_to(den, num.shape)
    mask = jnp.concatenate(
        [direct[s, held - 16 : held, :].astype(jnp.float32)[:1] for s in range(sources)], axis=0
    )
    mask = jnp.dot(rows_ref[...], mask, preferred_element_type=jnp.float32)
    mask = jnp.dot(mask, keys_ref[...], preferred_element_type=jnp.float32)
    size = rows // keep_ref.shape[0]
    for g in range(keep_ref.shape[0]):
        keep_ref[:, g * size : (g + 1) * size] = jnp.broadcast_to(
            mask[:, g : g + 1], (keep_ref.shape[0], size)
        )


def cond_sum(keep_ref, q_ref, cond, chunk, b):
    groups = keep_ref.shape[0] * BLOCK // q_ref.shape[0]
    keys = cond.shape[1]
    keep = keep_ref[b * groups : (b + 1) * groups, chunk * keys : (chunk + 1) * keys]
    return summed(kept_weights(q_ref[b * BLOCK : (b + 1) * BLOCK, :], cond, keep), cond[1])


def first_cond_kernel(section_ref, keep_ref, q_ref, cond, num_in, den_in, num_ref, den_ref):
    @pl.when(section_ref[0] == 0)
    def _():
        num_ref[...] = num_in[...]
        den_ref[...] = den_in[...]

    @pl.when(section_ref[0] != 0)
    def _():
        for b in range(num_ref.shape[0] // BLOCK):
            at = slice(b * BLOCK, (b + 1) * BLOCK)
            num, den = cond_sum(keep_ref, q_ref, cond, 0, b)
            num_ref[at, :] = num_in[at, :] + num
            den_ref[at, :] = den_in[at, :] + den


def second_cond_kernel(section_ref, place_ref, keep_ref, q_ref, cond, num_ref, den_ref, out_ref):
    groups = keep_ref.shape[0] * BLOCK // num_ref.shape[0]
    size = BLOCK // groups

    def store(b, num, den):
        value = (num / den).astype(jnp.bfloat16)
        for g in range(groups):
            shard, part = place_ref[0, b * groups + g], place_ref[1, b * groups + g]
            at = pl.ds(pl.multiple_of(part * size, size), size)
            out_ref[shard, at, :] = value[g * size : (g + 1) * size]

    @pl.when(section_ref[0] == 0)
    def _():
        for b in range(num_ref.shape[0] // BLOCK):
            at = slice(b * BLOCK, (b + 1) * BLOCK)
            store(b, num_ref[at, :], den_ref[at, :])

    @pl.when(section_ref[0] != 0)
    def _():
        for b in range(num_ref.shape[0] // BLOCK):
            at = slice(b * BLOCK, (b + 1) * BLOCK)
            num, den = cond_sum(keep_ref, q_ref, cond, 1, b)
            store(b, num_ref[at, :] + num, den_ref[at, :] + den)


def attend_own(tabs, gains, row_tiles, key_tiles, kvs, direct, pieces):
    depth = pieces[0].shape[1]
    rows = sum(p.shape[0] for p in pieces)
    keys = rows + rows // 2
    return call(
        own_kernel, "attend_own",
        [
            jax.ShapeDtypeStruct((rows, HEAD_DIM), jnp.bfloat16),
            jax.ShapeDtypeStruct((rows, HEAD_DIM), jnp.float32),
            jax.ShapeDtypeStruct((rows, HEAD_DIM), jnp.float32),
            jax.ShapeDtypeStruct((row_tiles.shape[0], rows), jnp.float32),
        ],
        2 * rows * HEAD_DIM * (2 * keys + depth), 2 * rows * depth, rows * keys,
        in_specs=[VMEM] * 6 + [HBM] * (1 + len(pieces)),
        out_specs=[VMEM] * 4,
        scratch_shapes=[
            pltpu.VMEM((rows, depth), jnp.bfloat16),
            pltpu.VMEM(direct.shape, jnp.bfloat16),
            pltpu.SemaphoreType.DMA((direct.shape[0] + len(pieces),)),
        ],
    )(tabs, gains, row_tiles, key_tiles, *kvs, direct, *pieces)


def attend_first(section, keep, query, cond, num, den):
    rows, keys = num.shape[0], cond.shape[1]
    return call(
        first_cond_kernel, "attend_first", [jax.ShapeDtypeStruct(num.shape, jnp.float32)] * 2,
        4 * rows * keys * HEAD_DIM, 2 * rows * HEAD_DIM * 8, rows * keys,
        in_specs=[SMEM] + [VMEM] * 5,
        out_specs=[VMEM] * 2,
    )(section, keep, query, cond, num, den)


def attend_second(section, place, keep, query, cond, num, den, seq):
    rows, keys = num.shape[0], cond.shape[1]
    return call(
        second_cond_kernel, "attend_second",
        jax.ShapeDtypeStruct((seq, rows // seq, HEAD_DIM), jnp.bfloat16),
        4 * rows * keys * HEAD_DIM, 2 * rows * HEAD_DIM * 8, rows * keys,
        in_specs=[SMEM, SMEM] + [VMEM] * 5,
        out_specs=VMEM,
    )(section, place, keep, query, cond, num, den)


def token_rows(attn_ref):
    return jnp.concatenate([attn_ref[h] for h in range(attn_ref.shape[0])], axis=1)


def sent_kernel(attn_ref, w_ref, out_ref):
    branch = jnp.dot(token_rows(attn_ref), w_ref[...], preferred_element_type=jnp.float32)
    out_ref[...] = branch.astype(jnp.bfloat16)


def kept_kernel(attn_ref, w_ref, image_ref, gate_ref, out_ref):
    branch = jnp.dot(token_rows(attn_ref), w_ref[...], preferred_element_type=jnp.float32)
    out_ref[...] = image_ref[...].astype(jnp.float32) + gate_ref[...] * branch


def project_out(attn, w, image=None, gate=None):
    rows = attn.shape[1]
    depth, width = w.shape
    kept = image is not None
    args = (attn, w) + ((image, gate) if kept else ())
    return call(
        kept_kernel if kept else sent_kernel, "out_kept" if kept else "out_sent",
        jax.ShapeDtypeStruct((rows, width), jnp.float32 if kept else jnp.bfloat16),
        2 * rows * depth * width, 2 * depth * width, 0,
        in_specs=[VMEM] * len(args),
        out_specs=VMEM,
    )(*args)


def lane_tables(row_ids, time_index):
    first = HEAD_DIM // 8
    rest = (HEAD_DIM - first) // 2
    freqs = jnp.concatenate([axis_freqs(first), axis_freqs(rest), axis_freqs(rest)])
    freqs = jnp.repeat(freqs, 2)[None]
    lane = jnp.arange(HEAD_DIM, dtype=jnp.int32)[None]
    rows = jnp.where(lane < first, time_index, row_ids.astype(jnp.float32)[:, None])
    columns = jnp.broadcast_to(jnp.arange(GRID_W, dtype=jnp.float32)[:, None], (GRID_W, HEAD_DIM))
    angles = jnp.concatenate([rows, columns], axis=0) * freqs
    return jnp.stack([jnp.cos(angles), jnp.sin(angles) * jnp.where(lane % 2 == 0, -1.0, 1.0)])


def z_pairs(seq, pairs):
    return [(2 * a + core, 2 * b + core) for a, b in pairs for core in range(2)]


def head_body(image, text_kv, modulation, w_qkv, w_out, q_gain, k_gain, region_mask):
    seq = lax.axis_size("seq")
    img_rows = image.shape[1]
    depth = w_qkv.shape[0]
    section = lax.axis_index("section")
    tp = lax.axis_index("tp")
    chip, core = lax.axis_index("seq") // 2, lax.axis_index("seq") % 2
    mods = modulation[0]
    section_at = section.astype(jnp.int32).reshape(1)
    tp_at = tp.astype(jnp.int32).reshape(1)
    both = [(0, 1), (1, 0)]

    upper = chip >= 2
    chips = jnp.stack([chip, chip ^ 1, jnp.where(upper, 1, 2), jnp.where(upper, 0, 3)])
    cores = jnp.stack([core, 1 - core])
    parts = jnp.stack([tp, 1 - tp])
    shards = chips[:, None, None] * 2 + cores[None, :, None] + 0 * parts[None, None, :]
    parts = parts[None, None, :] + 0 * shards
    shards, parts = shards.reshape(-1).astype(jnp.int32), parts.reshape(-1).astype(jnp.int32)
    size = img_rows // 2
    row_ids = shards * (img_rows // GRID_W) + parts * (size // GRID_W)
    tabs = lane_tables(row_ids, (section == 0).astype(jnp.float32))
    gains = jnp.stack([q_gain, k_gain])
    row_tiles = (shards[:, None] == jnp.arange(seq)[None]).astype(jnp.float32)
    key_tiles = jnp.arange(HEAD_DIM)[:, None] == shards[None]
    key_tiles = key_tiles.astype(jnp.float32)
    place = jnp.stack([shards, parts])

    rows3 = w_qkv.transpose(1, 0, 2)
    mine = lax.all_to_all(kv_weights(section_at, rows3), "seq", 0, 0)

    full, part = norm_tokens(tp_at, image[0], modulation.transpose(1, 0, 2))

    def along_z(x, pairs):
        return lax.ppermute(x, "seq", z_pairs(seq, pairs))

    def to_core(x):
        return lax.ppermute(x, "seq", [(s, s ^ 1) for s in range(seq)])

    def to_tp(x):
        return lax.ppermute(x, "tp", both)

    near = along_z(part, [(0, 1), (1, 0), (2, 3), (3, 2)])
    middle = along_z(part, [(1, 2), (2, 1)])
    far = along_z(near, [(1, 2), (2, 1)])
    middle_end = along_z(middle, [(1, 0), (2, 3)])
    far_end = along_z(far, [(1, 0), (2, 3)])
    inner = (chip == 1) | (chip == 2)
    third = jnp.where(inner, middle, middle_end)
    fourth = jnp.where(inner, far, far_end)

    text = text_kv[0].reshape(-1, 2, seq, HEAD_DIM).transpose(2, 1, 0, 3).reshape(seq, -1, HEAD_DIM)
    mask = jnp.pad(
        region_mask.astype(jnp.bfloat16), ((0, 15), (0, HEAD_DIM - region_mask.shape[1]))
    )
    direct = direct_rows(rows3, text, mask)

    near_tp = to_tp(near)
    third, near_tp = lax.optimization_barrier((third, near_tp))
    third_tp = to_tp(third)
    some = seq // 2
    peers = [lax.ppermute(mine[:some], "section", both), lax.ppermute(mine[some:], "section", both)]
    direct, mine = lax.optimization_barrier((direct, mine))
    direct = lax.all_to_all(direct, "seq", 0, 0)
    cols = w_out.shape[1] // 2
    gate = lax.dynamic_slice_in_dim(mods[2:3], tp * cols, cols, 1)
    residual = lax.dynamic_slice_in_dim(image[0], tp * cols, cols, 1)
    w_sent = lax.dynamic_slice_in_dim(w_out, (1 - tp) * cols, cols, 1)
    w_kept = lax.dynamic_slice_in_dim(w_out, tp * cols, cols, 1)
    early = (tabs, gains, row_tiles, key_tiles, place, gate, residual, w_sent, w_kept)
    fourth, third_tp, peers[0], early = lax.optimization_barrier((fourth, third_tp, peers[0], early))
    tabs, gains, row_tiles, key_tiles, place, gate, residual, w_sent, w_kept = early
    fourth_tp = to_tp(fourth)
    fourth, fourth_tp, peers[1] = lax.optimization_barrier((fourth, fourth_tp, peers[1]))
    a = [full, to_core(full), near, near_tp, to_core(near), to_core(near_tp)]
    b = [third, third_tp, to_core(third), to_core(third_tp)]
    b += [fourth, fourth_tp, to_core(fourth), to_core(fourth_tp)]

    kv_a = project_kv(0, section_at, tabs, gains, mine, peers, a)
    cond_a = lax.ppermute(kv_a, "section", [(0, 1)])
    kv_b = project_kv(1, section_at, tabs, gains, mine, peers, b)
    cond_b = lax.ppermute(kv_b, "section", [(0, 1)])
    query, num, den, keep = attend_own(
        tabs, gains, row_tiles, key_tiles, (kv_a, kv_b), direct, a + b
    )
    num, den = attend_first(section_at, keep, query, cond_a, num, den)
    attn = attend_second(section_at, place, keep, query, cond_b, num, den, seq)

    attn = lax.all_to_all(attn, "seq", 0, 0)
    other = to_tp(project_out(attn, w_sent))
    kept = project_out(attn, w_kept, residual, gate)
    return (kept + gate * other.astype(jnp.float32)).astype(jnp.bfloat16)[None]


def rms_rows(x, gain):
    return x * lax.rsqrt(jnp.mean(x * x, axis=-1, keepdims=True) + 1e-06) * gain


def apply_rope(x, cosine, sine):
    rows, heads_here = (x.shape[0], x.shape[1])
    pairs = x.reshape(rows, heads_here, HEAD_DIM // 2, 2)
    first = pairs[..., 0]
    second = pairs[..., 1]
    cosine = cosine[:, None, :]
    sine = sine[:, None, :]
    rotated = jnp.stack([first * cosine - second * sine, first * sine + second * cosine], axis=-1)
    return rotated.reshape(rows, heads_here, HEAD_DIM)


def attend_piece(carry, keys_vals, query, keep):
    num, den = carry
    rows = keys_vals.shape[0]
    heads_local = query.shape[1]
    piece_k = keys_vals[:, 0].reshape(rows, heads_local, HEAD_DIM)
    piece_v = keys_vals[:, 1].reshape(rows, heads_local, HEAD_DIM)
    scores = jnp.einsum("qhd,khd->hqk", query, piece_k, preferred_element_type=jnp.float32) * (
        1.0 / HEAD_DIM**0.5
    )
    weights = jnp.exp(scores)
    if keep is not None:
        weights = jnp.where(keep[None], weights, 0.0)
    den = den + jnp.sum(weights, axis=-1)
    num = num + jnp.einsum(
        "hqk,khd->hqd", weights.astype(jnp.bfloat16), piece_v, preferred_element_type=jnp.float32
    )
    return (num, den)


def token_body(image, text_kv, modulation, w_qkv, w_out, q_gain, k_gain, region_mask):
    img_rows = image.shape[1]
    width_local = w_qkv.shape[2]
    heads_local = width_local // HEAD_DIM
    tokens = image[0].astype(jnp.float32)
    mods = modulation[0]
    normed = layer_norm(tokens, mods)
    qkv = jnp.einsum(
        "td,dcf->tcf",
        normed,
        lax.all_gather(w_qkv, "seq", axis=0, tiled=True),
        preferred_element_type=jnp.float32,
    )
    section_index = lax.axis_index("section")
    time_index = (section_index == 0).astype(jnp.float32)
    rows_index = lax.axis_index("seq") * img_rows + jnp.arange(img_rows, dtype=jnp.int32)
    cosine, sine = rope_tables(rows_index, time_index)
    query = apply_rope(
        rms_rows(qkv[:, 0].reshape(img_rows, heads_local, HEAD_DIM), q_gain), cosine, sine
    ).astype(jnp.bfloat16)
    keys = apply_rope(
        rms_rows(qkv[:, 1].reshape(img_rows, heads_local, HEAD_DIM), k_gain), cosine, sine
    ).astype(jnp.bfloat16)
    values = qkv[:, 2].astype(jnp.bfloat16)
    image_kv = jnp.stack([keys.reshape(img_rows, width_local), values], axis=1)
    own_kv = jnp.concatenate([image_kv, text_kv[0]], axis=0)
    enabled = (section_index == 1).astype(jnp.int32)
    local_mask = region_mask * enabled
    init = (
        jnp.zeros((heads_local, img_rows, HEAD_DIM), jnp.float32),
        jnp.zeros((heads_local, img_rows), jnp.float32),
    )
    carry = attend_piece(init, lax.all_gather(own_kv, "seq", axis=0, tiled=True), query, None)
    cond_local = lax.ppermute(image_kv, "section", [(0, 1)])
    keep = jnp.repeat(jnp.repeat(local_mask, TILE, axis=0), TILE, axis=1) > 0
    carry = attend_piece(carry, lax.all_gather(cond_local, "seq", axis=0, tiled=True), query, keep)
    num, den = carry
    attn = (num / den[..., None]).astype(jnp.bfloat16)
    attn = jnp.transpose(attn, (1, 0, 2)).reshape(img_rows, width_local)
    term = jnp.dot(attn, w_out, preferred_element_type=jnp.float32)
    branch = lax.psum_scatter(
        term.astype(jnp.bfloat16), "tp", scatter_dimension=1, tiled=True
    ).astype(jnp.float32)
    cols = branch.shape[1]
    offset = lax.axis_index("tp") * cols
    residual = lax.dynamic_slice_in_dim(tokens, offset, cols, 1)
    gate = lax.dynamic_slice_in_dim(mods[2], offset, cols, 0)
    out = residual + gate[None, :] * branch
    return out.astype(jnp.bfloat16)[None]


def body(*arrays):
    image, w_qkv, region_mask = arrays[0], arrays[3], arrays[7]
    seq = lax.axis_size("seq")
    one_head_each = (
        w_qkv.shape[2] // HEAD_DIM == seq == 8
        and lax.axis_size("section") == 2
        and lax.axis_size("tp") == 2
        and w_qkv.shape[0] % 128 == 0
        and image.shape[1] == TILE == 2 * GRID_W
        and region_mask.shape == (1, seq)
        and arrays[1].shape[1] % 16 == 0
        and arrays[4].shape[1] % 1024 == 0
    )
    return (head_body if one_head_each else token_body)(*arrays)


def solution(mesh):
    return jax.shard_map(
        body,
        mesh=mesh,
        in_specs=(
            P("section", "seq", None),
            P("section", "seq", None, "tp"),
            P("section", None, None),
            P("seq", None, "tp"),
            P("tp", None),
            P(),
            P(),
            P("seq", None),
        ),
        out_specs=P("section", "seq", "tp"),
        check_vma=False,
    )
```

```python
import jax
import jax.numpy as jnp
from jax import lax
from jax.experimental import pallas as pl
from jax.experimental.pallas import tpu as pltpu
from jax.sharding import PartitionSpec as P

HEAD_DIM = 128
GRID_W = 64
TILE = 128
VMEM_LIMIT = 24 * 1024 * 1024
VMEM_WHOLE = 56 * 1024 * 1024


def axis_freqs(width):
    return 10000.0 ** (-jnp.arange(0, width, 2).astype(jnp.float32) / width)


def rope_tables(rows_index, time_index):
    first = HEAD_DIM // 8
    rest = (HEAD_DIM - first) // 2
    row_pos = (rows_index // GRID_W).astype(jnp.float32)
    col_pos = (rows_index % GRID_W).astype(jnp.float32)
    time_pos = jnp.zeros_like(row_pos) + time_index
    angles = jnp.concatenate(
        [
            time_pos[:, None] * axis_freqs(first)[None],
            row_pos[:, None] * axis_freqs(rest)[None],
            col_pos[:, None] * axis_freqs(rest)[None],
        ],
        axis=-1,
    )
    return (jnp.cos(angles), jnp.sin(angles))


def layer_norm(tokens, mods):
    mean = jnp.mean(tokens, axis=-1, keepdims=True)
    var = jnp.mean((tokens - mean) ** 2, axis=-1, keepdims=True)
    return ((tokens - mean) * lax.rsqrt(var + 1e-06) * (1.0 + mods[1:2]) + mods[0:1]).astype(
        jnp.bfloat16
    )


VMEM = pl.BlockSpec(memory_space=pltpu.VMEM)
SMEM = pl.BlockSpec(memory_space=pltpu.SMEM)
HBM = pl.BlockSpec(memory_space=pltpu.HBM)


def call(kernel, name, out_shape, flops, moved, exps, limit=VMEM_LIMIT, **spec):
    return pl.pallas_call(
        kernel,
        out_shape=out_shape,
        compiler_params=pltpu.CompilerParams(vmem_limit_bytes=limit),
        cost_estimate=pl.CostEstimate(flops=flops, bytes_accessed=moved, transcendentals=exps),
        name=name,
        **spec,
    )


def started(pairs, sems, first=0):
    copies = [pltpu.make_async_copy(s, d, sems.at[first + i]) for i, (s, d) in enumerate(pairs)]
    for copy in copies:
        copy.start()
    return copies


def finished(copies):
    for copy in copies:
        copy.wait()


def norm_kernel(tp_ref, image_hbm, mods_hbm, full_ref, part_ref, image_ref, mods_ref, sems):
    rows = image_ref.shape[0] // 4
    pairs = [
        (image_hbm.at[pl.ds(i * rows, rows), :], image_ref.at[pl.ds(i * rows, rows), :])
        for i in range(4)
    ]
    finished(started(pairs + [(mods_hbm, mods_ref)], sems))
    mods = jnp.concatenate([mods_ref[0], mods_ref[1]], axis=0)
    normed = layer_norm(image_ref[...].astype(jnp.float32), mods)
    part = part_ref.shape[0]
    for t in range(2):

        @pl.when(tp_ref[0] == t)
        def _(t=t):
            ours, theirs = normed[t * part : (t + 1) * part], normed[(1 - t) * part : (2 - t) * part]
            full_ref[:part, :] = ours
            full_ref[part:, :] = theirs
            part_ref[...] = ours


def norm_tokens(tp, image, mods):
    rows, depth = image.shape
    return call(
        norm_kernel, "norm_tokens",
        [
            jax.ShapeDtypeStruct((rows, depth), jnp.bfloat16),
            jax.ShapeDtypeStruct((rows // 2, depth), jnp.bfloat16),
        ],
        10 * rows * depth, 4 * rows * depth, 0, VMEM_WHOLE,
        in_specs=[SMEM, HBM, HBM],
        out_specs=[VMEM, VMEM],
        scratch_shapes=[
            pltpu.VMEM(image.shape, image.dtype),
            pltpu.VMEM(mods.shape, mods.dtype),
            pltpu.SemaphoreType.DMA((5,)),
        ],
    )(tp, image, mods)


def kv_weights_kernel(section_ref, w_hbm, out_ref, w_ref, sems):
    half = w_ref.shape[1]
    rows = pl.ds(pl.multiple_of(section_ref[0] * half, half), half)
    copies = started([(w_hbm.at[1 + k, rows, :], w_ref.at[k]) for k in range(2)], sems)
    for k in range(2):
        copies[k].wait()
        for s in range(out_ref.shape[0]):
            out_ref[s, k * half : (k + 1) * half, :] = w_ref[k, :, s * HEAD_DIM : (s + 1) * HEAD_DIM]


def kv_weights(section, w):
    _, depth, width = w.shape
    return call(
        kv_weights_kernel, "kv_weights",
        jax.ShapeDtypeStruct((width // HEAD_DIM, depth, HEAD_DIM), w.dtype),
        0, 4 * depth * width, 0, VMEM_WHOLE,
        in_specs=[SMEM, HBM],
        out_specs=VMEM,
        scratch_shapes=[pltpu.VMEM((2, depth // 2, width), w.dtype), pltpu.SemaphoreType.DMA((2,))],
    )(section, w)


def direct_kernel(w_hbm, text_hbm, mask_ref, out_ref, w_ref, text_ref, sems):
    depth, count = w_ref.shape[0], text_ref.shape[1]
    copies = started([(w_hbm.at[0], w_ref), (text_hbm, text_ref)], sems)
    finished(copies)
    for s in range(out_ref.shape[0]):
        out_ref[s, :depth, :] = w_ref[:, s * HEAD_DIM : (s + 1) * HEAD_DIM]
        out_ref[s, depth : depth + count, :] = text_ref[s]
        out_ref[s, depth + count :, :] = mask_ref[...]


def direct_rows(w, text, mask):
    heads, count, _ = text.shape
    shape = (heads, w.shape[1] + count + mask.shape[0], HEAD_DIM)
    return call(
        direct_kernel, "direct_rows", jax.ShapeDtypeStruct(shape, w.dtype),
        0, 4 * heads * shape[1] * HEAD_DIM, 0, VMEM_WHOLE,
        in_specs=[HBM, HBM, VMEM],
        out_specs=VMEM,
        scratch_shapes=[
            pltpu.VMEM(w.shape[1:], w.dtype),
            pltpu.VMEM(text.shape, text.dtype),
            pltpu.SemaphoreType.DMA((2,)),
        ],
    )(w, text, mask)


def normed_rotated(x, gain, cosine, sine):
    x = x * lax.rsqrt(jnp.mean(x * x, axis=-1, keepdims=True) + 1e-06) * gain
    even = lax.broadcasted_iota(jnp.int32, x.shape, 1) % 2 == 0
    other = jnp.where(even, pltpu.roll(x, HEAD_DIM - 1, 1), pltpu.roll(x, 1, 1))
    return (x * cosine + other * sine).astype(jnp.bfloat16)


def table_of(tabs_ref, which, start, rows):
    groups = tabs_ref.shape[1] - GRID_W
    columns = tabs_ref[which, groups:, :]
    lane = lax.broadcasted_iota(jnp.int32, columns.shape, 1)
    first = HEAD_DIM // 8
    by_row = lane < first + (HEAD_DIM - first) // 2
    return jnp.concatenate(
        [
            jnp.where(by_row, tabs_ref[which, g : g + 1, :], columns)
            for g in range(start // GRID_W, (start + rows) // GRID_W)
        ],
        axis=0,
    )


def piece_copies(piece_refs, x_ref):
    at, pairs = 0, []
    for ref in piece_refs:
        pairs.append((ref, x_ref.at[pl.ds(at, ref.shape[0]), :]))
        at += ref.shape[0]
    return pairs


def blocks(rows):
    return [(b, slice(b * BLOCK, (b + 1) * BLOCK)) for b in range(rows // BLOCK)]


def arrived(copies, piece_refs, rows):
    at = 0
    for copy, ref in zip(copies, piece_refs):
        if rows.start <= at < rows.stop:
            copy.wait()
        at += ref.shape[0]


def kv_kernel(chunk, section_ref, tabs_ref, gain_ref, mine_hbm, peer_a, peer_b, *refs):
    piece_refs, (kv_ref, x_ref, mine, peer, w_ref, sems) = refs[:-6], refs[-6:]
    sources, held, _ = mine.shape
    half = held // 2
    some = sources // 2
    weights = started(
        [
            (mine_hbm, mine),
            (peer_a, peer.at[pl.ds(0, some)]),
            (peer_b, peer.at[pl.ds(some, some)]),
        ],
        sems,
    )
    tokens = started(piece_copies(piece_refs, x_ref), sems, 3)
    finished(weights)
    first = section_ref[0] == 0
    for s in range(sources):
        for kind in range(2):
            at = slice(kind * half, (kind + 1) * half)
            lanes = slice(kind * HEAD_DIM, (kind + 1) * HEAD_DIM)
            a, b = mine[s, at, :], peer[s, at, :]
            w_ref[2 * s * half : (2 * s + 1) * half, lanes] = jnp.where(first, a, b)
            w_ref[(2 * s + 1) * half : (2 * s + 2) * half, lanes] = jnp.where(first, b, a)
    for b, at in blocks(x_ref.shape[0]):
        arrived(tokens, piece_refs, at)
        both = jnp.dot(x_ref[at, :], w_ref[...], preferred_element_type=jnp.float32)
        start = chunk * x_ref.shape[0] + b * BLOCK
        kv_ref[0, at, :] = normed_rotated(
            both[:, :HEAD_DIM],
            gain_ref[1:2, :],
            table_of(tabs_ref, 0, start, BLOCK),
            table_of(tabs_ref, 1, start, BLOCK),
        )
        kv_ref[1, at, :] = both[:, HEAD_DIM:].astype(jnp.bfloat16)


def project_kv(chunk, section, tabs, gains, mine, peers, pieces):
    depth = pieces[0].shape[1]
    rows = sum(p.shape[0] for p in pieces)
    return call(
        lambda *refs: kv_kernel(chunk, *refs), "project_kv" + "ab"[chunk],
        jax.ShapeDtypeStruct((2, rows, HEAD_DIM), jnp.bfloat16),
        4 * rows * depth * HEAD_DIM, 2 * (rows * depth + 2 * mine.size), 0, VMEM_WHOLE,
        in_specs=[SMEM, VMEM, VMEM] + [HBM] * (3 + len(pieces)),
        out_specs=VMEM,
        scratch_shapes=[
            pltpu.VMEM((rows, depth), jnp.bfloat16),
            pltpu.VMEM(mine.shape, jnp.bfloat16),
            pltpu.VMEM(mine.shape, jnp.bfloat16),
            pltpu.VMEM((depth, 2 * HEAD_DIM), jnp.bfloat16),
            pltpu.SemaphoreType.DMA((3 + len(pieces),)),
        ],
    )(section, tabs, gains, mine, *peers, *pieces)


def weights_of(query, keys):
    scores = lax.dot_general(
        query, keys, (((1,), (1,)), ((), ())), preferred_element_type=jnp.float32
    )
    return jnp.exp(scores * (1.0 / HEAD_DIM**0.5))


def summed(weights, values):
    den = jnp.sum(weights, axis=-1, keepdims=True)
    num = jnp.dot(weights.astype(jnp.bfloat16), values, preferred_element_type=jnp.float32)
    return num, den


def kept_weights(query, cond_ref, keep):
    weights = weights_of(query, cond_ref[0])
    rows, keys = weights.shape
    groups = keep.shape[0]
    return (weights.reshape(groups, rows // groups, keys) * keep[:, None, :]).reshape(rows, keys)


BLOCK = 256


def own_kernel(tabs_ref, gain_ref, rows_ref, keys_ref, kva, kvb, direct_hbm, *refs):
    piece_refs = refs[:-7]
    q_ref, num_ref, den_ref, keep_ref, x_ref, direct, sems = refs[-7:]
    rows, depth = x_ref.shape
    sources, held, _ = direct.shape
    copies = started([(direct_hbm.at[s], direct.at[s]) for s in range(sources)], sems)
    tokens = started(piece_copies(piece_refs, x_ref), sems, sources)
    finished(copies)
    wide = depth // sources
    w = direct[:, :wide, :].reshape(depth, HEAD_DIM)
    count = (held - 16 - wide) // 2
    text = (
        direct[:, wide : wide + count, :].reshape(-1, HEAD_DIM),
        direct[:, wide + count : wide + 2 * count, :].reshape(-1, HEAD_DIM),
    )
    for b, at in blocks(rows):
        arrived(tokens, piece_refs, at)
        query = jnp.dot(x_ref[at, :], w, preferred_element_type=jnp.float32)
        query = normed_rotated(
            query,
            gain_ref[0:1, :],
            table_of(tabs_ref, 0, b * BLOCK, BLOCK),
            table_of(tabs_ref, 1, b * BLOCK, BLOCK),
        )
        q_ref[at, :] = query
        num, den = 0.0, 0.0
        for keys, values in ((kva[0], kva[1]), (kvb[0], kvb[1]), text):
            more = summed(weights_of(query, keys), values)
            num, den = num + more[0], den + more[1]
        num_ref[at, :] = num
        den_ref[at, :] = jnp.broadcast_to(den, num.shape)
    mask = jnp.concatenate(
        [direct[s, held - 16 : held, :].astype(jnp.float32)[:1] for s in range(sources)], axis=0
    )
    mask = jnp.dot(rows_ref[...], mask, preferred_element_type=jnp.float32)
    mask = jnp.dot(mask, keys_ref[...], preferred_element_type=jnp.float32)
    size = rows // keep_ref.shape[0]
    for g in range(keep_ref.shape[0]):
        keep_ref[:, g * size : (g + 1) * size] = jnp.broadcast_to(
            mask[:, g : g + 1], (keep_ref.shape[0], size)
        )


def cond_sum(keep_ref, q_ref, cond, chunk, b):
    groups = keep_ref.shape[0] * BLOCK // q_ref.shape[0]
    keys = cond.shape[1]
    keep = keep_ref[b * groups : (b + 1) * groups, chunk * keys : (chunk + 1) * keys]
    return summed(kept_weights(q_ref[b * BLOCK : (b + 1) * BLOCK, :], cond, keep), cond[1])


def first_cond_kernel(section_ref, keep_ref, q_ref, cond, num_in, den_in, num_ref, den_ref):
    @pl.when(section_ref[0] == 0)
    def _():
        num_ref[...] = num_in[...]
        den_ref[...] = den_in[...]

    @pl.when(section_ref[0] != 0)
    def _():
        for b in range(num_ref.shape[0] // BLOCK):
            at = slice(b * BLOCK, (b + 1) * BLOCK)
            num, den = cond_sum(keep_ref, q_ref, cond, 0, b)
            num_ref[at, :] = num_in[at, :] + num
            den_ref[at, :] = den_in[at, :] + den


def second_cond_kernel(section_ref, place_ref, keep_ref, q_ref, cond, num_ref, den_ref, out_ref):
    groups = keep_ref.shape[0] * BLOCK // num_ref.shape[0]
    size = BLOCK // groups

    def store(b, num, den):
        value = (num / den).astype(jnp.bfloat16)
        for g in range(groups):
            shard, part = place_ref[0, b * groups + g], place_ref[1, b * groups + g]
            at = pl.ds(pl.multiple_of(part * size, size), size)
            out_ref[shard, at, :] = value[g * size : (g + 1) * size]

    @pl.when(section_ref[0] == 0)
    def _():
        for b in range(num_ref.shape[0] // BLOCK):
            at = slice(b * BLOCK, (b + 1) * BLOCK)
            store(b, num_ref[at, :], den_ref[at, :])

    @pl.when(section_ref[0] != 0)
    def _():
        for b in range(num_ref.shape[0] // BLOCK):
            at = slice(b * BLOCK, (b + 1) * BLOCK)
            num, den = cond_sum(keep_ref, q_ref, cond, 1, b)
            store(b, num_ref[at, :] + num, den_ref[at, :] + den)


def attend_own(tabs, gains, row_tiles, key_tiles, kvs, direct, pieces):
    depth = pieces[0].shape[1]
    rows = sum(p.shape[0] for p in pieces)
    keys = rows + rows // 2
    return call(
        own_kernel, "attend_own",
        [
            jax.ShapeDtypeStruct((rows, HEAD_DIM), jnp.bfloat16),
            jax.ShapeDtypeStruct((rows, HEAD_DIM), jnp.float32),
            jax.ShapeDtypeStruct((rows, HEAD_DIM), jnp.float32),
            jax.ShapeDtypeStruct((row_tiles.shape[0], rows), jnp.float32),
        ],
        2 * rows * HEAD_DIM * (2 * keys + depth), 2 * rows * depth, rows * keys, VMEM_WHOLE,
        in_specs=[VMEM] * 6 + [HBM] * (1 + len(pieces)),
        out_specs=[VMEM] * 4,
        scratch_shapes=[
            pltpu.VMEM((rows, depth), jnp.bfloat16),
            pltpu.VMEM(direct.shape, jnp.bfloat16),
            pltpu.SemaphoreType.DMA((direct.shape[0] + len(pieces),)),
        ],
    )(tabs, gains, row_tiles, key_tiles, *kvs, direct, *pieces)


def attend_first(section, keep, query, cond, num, den):
    rows, keys = num.shape[0], cond.shape[1]
    return call(
        first_cond_kernel, "attend_first", [jax.ShapeDtypeStruct(num.shape, jnp.float32)] * 2,
        4 * rows * keys * HEAD_DIM, 2 * rows * HEAD_DIM * 8, rows * keys,
        in_specs=[SMEM] + [VMEM] * 5,
        out_specs=[VMEM] * 2,
    )(section, keep, query, cond, num, den)


def attend_second(section, place, keep, query, cond, num, den, seq):
    rows, keys = num.shape[0], cond.shape[1]
    return call(
        second_cond_kernel, "attend_second",
        jax.ShapeDtypeStruct((seq, rows // seq, HEAD_DIM), jnp.bfloat16),
        4 * rows * keys * HEAD_DIM, 2 * rows * HEAD_DIM * 8, rows * keys,
        in_specs=[SMEM, SMEM] + [VMEM] * 5,
        out_specs=VMEM,
    )(section, place, keep, query, cond, num, den)


def token_rows(attn_ref):
    return jnp.concatenate([attn_ref[h] for h in range(attn_ref.shape[0])], axis=1)


def sent_kernel(attn_ref, w_ref, out_ref):
    branch = jnp.dot(token_rows(attn_ref), w_ref[...], preferred_element_type=jnp.float32)
    out_ref[...] = branch.astype(jnp.bfloat16)


def kept_kernel(attn_ref, w_ref, image_ref, gate_ref, out_ref):
    branch = jnp.dot(token_rows(attn_ref), w_ref[...], preferred_element_type=jnp.float32)
    out_ref[...] = image_ref[...].astype(jnp.float32) + gate_ref[...] * branch


def project_out(attn, w, image=None, gate=None):
    rows = attn.shape[1]
    depth, width = w.shape
    kept = image is not None
    args = (attn, w) + ((image, gate) if kept else ())
    return call(
        kept_kernel if kept else sent_kernel, "out_kept" if kept else "out_sent",
        jax.ShapeDtypeStruct((rows, width), jnp.float32 if kept else jnp.bfloat16),
        2 * rows * depth * width, 2 * depth * width, 0,
        in_specs=[VMEM] * len(args),
        out_specs=VMEM,
    )(*args)


def lane_tables(row_ids, time_index):
    first = HEAD_DIM // 8
    rest = (HEAD_DIM - first) // 2
    freqs = jnp.concatenate([axis_freqs(first), axis_freqs(rest), axis_freqs(rest)])
    freqs = jnp.repeat(freqs, 2)[None]
    lane = jnp.arange(HEAD_DIM, dtype=jnp.int32)[None]
    rows = jnp.where(lane < first, time_index, row_ids.astype(jnp.float32)[:, None])
    columns = jnp.broadcast_to(jnp.arange(GRID_W, dtype=jnp.float32)[:, None], (GRID_W, HEAD_DIM))
    angles = jnp.concatenate([rows, columns], axis=0) * freqs
    return jnp.stack([jnp.cos(angles), jnp.sin(angles) * jnp.where(lane % 2 == 0, -1.0, 1.0)])


def z_pairs(seq, pairs):
    return [(2 * a + core, 2 * b + core) for a, b in pairs for core in range(2)]


def head_body(image, text_kv, modulation, w_qkv, w_out, q_gain, k_gain, region_mask):
    seq = lax.axis_size("seq")
    img_rows = image.shape[1]
    depth = w_qkv.shape[0]
    section = lax.axis_index("section")
    tp = lax.axis_index("tp")
    chip, core = lax.axis_index("seq") // 2, lax.axis_index("seq") % 2
    mods = modulation[0]
    section_at = section.astype(jnp.int32).reshape(1)
    tp_at = tp.astype(jnp.int32).reshape(1)
    both = [(0, 1), (1, 0)]

    upper = chip >= 2
    chips = jnp.stack([chip, chip ^ 1, jnp.where(upper, 1, 2), jnp.where(upper, 0, 3)])
    cores = jnp.stack([core, 1 - core])
    parts = jnp.stack([tp, 1 - tp])
    shards = chips[:, None, None] * 2 + cores[None, :, None] + 0 * parts[None, None, :]
    parts = parts[None, None, :] + 0 * shards
    shards, parts = shards.reshape(-1).astype(jnp.int32), parts.reshape(-1).astype(jnp.int32)
    size = img_rows // 2
    row_ids = shards * (img_rows // GRID_W) + parts * (size // GRID_W)
    tabs = lane_tables(row_ids, (section == 0).astype(jnp.float32))
    gains = jnp.stack([q_gain, k_gain])
    row_tiles = (shards[:, None] == jnp.arange(seq)[None]).astype(jnp.float32)
    key_tiles = jnp.arange(HEAD_DIM)[:, None] == shards[None]
    key_tiles = key_tiles.astype(jnp.float32)
    place = jnp.stack([shards, parts])

    rows3 = w_qkv.transpose(1, 0, 2)
    mine = lax.all_to_all(kv_weights(section_at, rows3), "seq", 0, 0)

    full, part = norm_tokens(tp_at, image[0], modulation.transpose(1, 0, 2))

    def along_z(x, pairs):
        return lax.ppermute(x, "seq", z_pairs(seq, pairs))

    def to_core(x):
        return lax.ppermute(x, "seq", [(s, s ^ 1) for s in range(seq)])

    def to_tp(x):
        return lax.ppermute(x, "tp", both)

    near = along_z(part, [(0, 1), (1, 0), (2, 3), (3, 2)])
    middle = along_z(part, [(1, 2), (2, 1)])
    far = along_z(near, [(1, 2), (2, 1)])
    middle_end = along_z(middle, [(1, 0), (2, 3)])
    far_end = along_z(far, [(1, 0), (2, 3)])
    inner = (chip == 1) | (chip == 2)
    third = jnp.where(inner, middle, middle_end)
    fourth = jnp.where(inner, far, far_end)

    text = text_kv[0].reshape(-1, 2, seq, HEAD_DIM).transpose(2, 1, 0, 3).reshape(seq, -1, HEAD_DIM)
    mask = jnp.pad(
        region_mask.astype(jnp.bfloat16), ((0, 15), (0, HEAD_DIM - region_mask.shape[1]))
    )
    direct = direct_rows(rows3, text, mask)

    near_tp = to_tp(near)
    some = seq // 2
    peers = [lax.ppermute(mine[:some], "section", both), lax.ppermute(mine[some:], "section", both)]
    third, near_tp, peers[0] = lax.optimization_barrier((third, near_tp, peers[0]))
    third_tp = to_tp(third)
    direct, mine = lax.optimization_barrier((direct, mine))
    direct = lax.all_to_all(direct, "seq", 0, 0)
    cols = w_out.shape[1] // 2
    gate = lax.dynamic_slice_in_dim(mods[2:3], tp * cols, cols, 1)
    residual = lax.dynamic_slice_in_dim(image[0], tp * cols, cols, 1)
    w_sent = lax.dynamic_slice_in_dim(w_out, (1 - tp) * cols, cols, 1)
    w_kept = lax.dynamic_slice_in_dim(w_out, tp * cols, cols, 1)
    early = (tabs, gains, row_tiles, key_tiles, place, gate, residual, w_sent, w_kept)
    fourth, third_tp, peers[1], early = lax.optimization_barrier((fourth, third_tp, peers[1], early))
    tabs, gains, row_tiles, key_tiles, place, gate, residual, w_sent, w_kept = early
    fourth_tp = to_tp(fourth)
    a = [full, to_core(full), near, near_tp, to_core(near), to_core(near_tp)]
    b = [third, third_tp, to_core(third), to_core(third_tp)]
    b += [fourth, fourth_tp, to_core(fourth), to_core(fourth_tp)]

    kv_a = project_kv(0, section_at, tabs, gains, mine, peers, a)
    cond_a = lax.ppermute(kv_a, "section", [(0, 1)])
    kv_b = project_kv(1, section_at, tabs, gains, mine, peers, b)
    cond_b = lax.ppermute(kv_b, "section", [(0, 1)])
    query, num, den, keep = attend_own(
        tabs, gains, row_tiles, key_tiles, (kv_a, kv_b), direct, a + b
    )
    num, den = attend_first(section_at, keep, query, cond_a, num, den)
    attn = attend_second(section_at, place, keep, query, cond_b, num, den, seq)

    attn = lax.all_to_all(attn, "seq", 0, 0)
    other = to_tp(project_out(attn, w_sent))
    kept = project_out(attn, w_kept, residual, gate)
    return (kept + gate * other.astype(jnp.float32)).astype(jnp.bfloat16)[None]


def rms_rows(x, gain):
    return x * lax.rsqrt(jnp.mean(x * x, axis=-1, keepdims=True) + 1e-06) * gain


def apply_rope(x, cosine, sine):
    rows, heads_here = (x.shape[0], x.shape[1])
    pairs = x.reshape(rows, heads_here, HEAD_DIM // 2, 2)
    first = pairs[..., 0]
    second = pairs[..., 1]
    cosine = cosine[:, None, :]
    sine = sine[:, None, :]
    rotated = jnp.stack([first * cosine - second * sine, first * sine + second * cosine], axis=-1)
    return rotated.reshape(rows, heads_here, HEAD_DIM)


def attend_piece(carry, keys_vals, query, keep):
    num, den = carry
    rows = keys_vals.shape[0]
    heads_local = query.shape[1]
    piece_k = keys_vals[:, 0].reshape(rows, heads_local, HEAD_DIM)
    piece_v = keys_vals[:, 1].reshape(rows, heads_local, HEAD_DIM)
    scores = jnp.einsum("qhd,khd->hqk", query, piece_k, preferred_element_type=jnp.float32) * (
        1.0 / HEAD_DIM**0.5
    )
    weights = jnp.exp(scores)
    if keep is not None:
        weights = jnp.where(keep[None], weights, 0.0)
    den = den + jnp.sum(weights, axis=-1)
    num = num + jnp.einsum(
        "hqk,khd->hqd", weights.astype(jnp.bfloat16), piece_v, preferred_element_type=jnp.float32
    )
    return (num, den)


def token_body(image, text_kv, modulation, w_qkv, w_out, q_gain, k_gain, region_mask):
    img_rows = image.shape[1]
    width_local = w_qkv.shape[2]
    heads_local = width_local // HEAD_DIM
    tokens = image[0].astype(jnp.float32)
    mods = modulation[0]
    normed = layer_norm(tokens, mods)
    qkv = jnp.einsum(
        "td,dcf->tcf",
        normed,
        lax.all_gather(w_qkv, "seq", axis=0, tiled=True),
        preferred_element_type=jnp.float32,
    )
    section_index = lax.axis_index("section")
    time_index = (section_index == 0).astype(jnp.float32)
    rows_index = lax.axis_index("seq") * img_rows + jnp.arange(img_rows, dtype=jnp.int32)
    cosine, sine = rope_tables(rows_index, time_index)
    query = apply_rope(
        rms_rows(qkv[:, 0].reshape(img_rows, heads_local, HEAD_DIM), q_gain), cosine, sine
    ).astype(jnp.bfloat16)
    keys = apply_rope(
        rms_rows(qkv[:, 1].reshape(img_rows, heads_local, HEAD_DIM), k_gain), cosine, sine
    ).astype(jnp.bfloat16)
    values = qkv[:, 2].astype(jnp.bfloat16)
    image_kv = jnp.stack([keys.reshape(img_rows, width_local), values], axis=1)
    own_kv = jnp.concatenate([image_kv, text_kv[0]], axis=0)
    enabled = (section_index == 1).astype(jnp.int32)
    local_mask = region_mask * enabled
    init = (
        jnp.zeros((heads_local, img_rows, HEAD_DIM), jnp.float32),
        jnp.zeros((heads_local, img_rows), jnp.float32),
    )
    carry = attend_piece(init, lax.all_gather(own_kv, "seq", axis=0, tiled=True), query, None)
    cond_local = lax.ppermute(image_kv, "section", [(0, 1)])
    keep = jnp.repeat(jnp.repeat(local_mask, TILE, axis=0), TILE, axis=1) > 0
    carry = attend_piece(carry, lax.all_gather(cond_local, "seq", axis=0, tiled=True), query, keep)
    num, den = carry
    attn = (num / den[..., None]).astype(jnp.bfloat16)
    attn = jnp.transpose(attn, (1, 0, 2)).reshape(img_rows, width_local)
    term = jnp.dot(attn, w_out, preferred_element_type=jnp.float32)
    branch = lax.psum_scatter(
        term.astype(jnp.bfloat16), "tp", scatter_dimension=1, tiled=True
    ).astype(jnp.float32)
    cols = branch.shape[1]
    offset = lax.axis_index("tp") * cols
    residual = lax.dynamic_slice_in_dim(tokens, offset, cols, 1)
    gate = lax.dynamic_slice_in_dim(mods[2], offset, cols, 0)
    out = residual + gate[None, :] * branch
    return out.astype(jnp.bfloat16)[None]


def body(*arrays):
    image, w_qkv, region_mask = arrays[0], arrays[3], arrays[7]
    seq = lax.axis_size("seq")
    one_head_each = (
        w_qkv.shape[2] // HEAD_DIM == seq == 8
        and lax.axis_size("section") == 2
        and lax.axis_size("tp") == 2
        and w_qkv.shape[0] % 128 == 0
        and image.shape[1] == TILE == 2 * GRID_W
        and region_mask.shape == (1, seq)
        and arrays[1].shape[1] % 16 == 0
        and arrays[4].shape[1] % 1024 == 0
    )
    return (head_body if one_head_each else token_body)(*arrays)


def solution(mesh):
    return jax.shard_map(
        body,
        mesh=mesh,
        in_specs=(
            P("section", "seq", None),
            P("section", "seq", None, "tp"),
            P("section", None, None),
            P("seq", None, "tp"),
            P("tp", None),
            P(),
            P(),
            P("seq", None),
        ),
        out_specs=P("section", "seq", "tp"),
        check_vma=False,
    )
```

```python
import jax
import jax.numpy as jnp
from jax import lax
from jax.experimental import pallas as pl
from jax.experimental.pallas import tpu as pltpu
from jax.sharding import PartitionSpec as P

HEAD_DIM = 128
GRID_W = 64
TILE = 128
VMEM_LIMIT = 24 * 1024 * 1024
VMEM_WHOLE = 56 * 1024 * 1024


def axis_freqs(width):
    return 10000.0 ** (-jnp.arange(0, width, 2).astype(jnp.float32) / width)


def rope_tables(rows_index, time_index):
    first = HEAD_DIM // 8
    rest = (HEAD_DIM - first) // 2
    row_pos = (rows_index // GRID_W).astype(jnp.float32)
    col_pos = (rows_index % GRID_W).astype(jnp.float32)
    time_pos = jnp.zeros_like(row_pos) + time_index
    angles = jnp.concatenate(
        [
            time_pos[:, None] * axis_freqs(first)[None],
            row_pos[:, None] * axis_freqs(rest)[None],
            col_pos[:, None] * axis_freqs(rest)[None],
        ],
        axis=-1,
    )
    return (jnp.cos(angles), jnp.sin(angles))


def layer_norm(tokens, mods):
    mean = jnp.mean(tokens, axis=-1, keepdims=True)
    var = jnp.mean((tokens - mean) ** 2, axis=-1, keepdims=True)
    return ((tokens - mean) * lax.rsqrt(var + 1e-06) * (1.0 + mods[1:2]) + mods[0:1]).astype(
        jnp.bfloat16
    )


VMEM = pl.BlockSpec(memory_space=pltpu.VMEM)
SMEM = pl.BlockSpec(memory_space=pltpu.SMEM)
HBM = pl.BlockSpec(memory_space=pltpu.HBM)


def call(kernel, name, out_shape, flops, moved, exps, limit=VMEM_LIMIT, **spec):
    return pl.pallas_call(
        kernel,
        out_shape=out_shape,
        compiler_params=pltpu.CompilerParams(vmem_limit_bytes=limit),
        cost_estimate=pl.CostEstimate(flops=flops, bytes_accessed=moved, transcendentals=exps),
        name=name,
        **spec,
    )


def started(pairs, sems, first=0):
    copies = [pltpu.make_async_copy(s, d, sems.at[first + i]) for i, (s, d) in enumerate(pairs)]
    for copy in copies:
        copy.start()
    return copies


def finished(copies):
    for copy in copies:
        copy.wait()


def norm_kernel(tp_ref, image_hbm, mods_hbm, full_ref, part_ref, image_ref, mods_ref, sems):
    rows = image_ref.shape[0] // 4
    pairs = [
        (image_hbm.at[pl.ds(i * rows, rows), :], image_ref.at[pl.ds(i * rows, rows), :])
        for i in range(4)
    ]
    finished(started(pairs + [(mods_hbm, mods_ref)], sems))
    mods = jnp.concatenate([mods_ref[0], mods_ref[1]], axis=0)
    normed = layer_norm(image_ref[...].astype(jnp.float32), mods)
    part = part_ref.shape[0]
    for t in range(2):

        @pl.when(tp_ref[0] == t)
        def _(t=t):
            ours, theirs = normed[t * part : (t + 1) * part], normed[(1 - t) * part : (2 - t) * part]
            full_ref[:part, :] = ours
            full_ref[part:, :] = theirs
            part_ref[...] = ours


def norm_tokens(tp, image, mods):
    rows, depth = image.shape
    return call(
        norm_kernel, "norm_tokens",
        [
            jax.ShapeDtypeStruct((rows, depth), jnp.bfloat16),
            jax.ShapeDtypeStruct((rows // 2, depth), jnp.bfloat16),
        ],
        10 * rows * depth, 4 * rows * depth, 0, VMEM_WHOLE,
        in_specs=[SMEM, HBM, HBM],
        out_specs=[VMEM, VMEM],
        scratch_shapes=[
            pltpu.VMEM(image.shape, image.dtype),
            pltpu.VMEM(mods.shape, mods.dtype),
            pltpu.SemaphoreType.DMA((5,)),
        ],
    )(tp, image, mods)


def kv_weights_kernel(section_ref, w_hbm, out_ref, w_ref, sems):
    half = w_ref.shape[1]
    rows = pl.ds(pl.multiple_of(section_ref[0] * half, half), half)
    copies = started([(w_hbm.at[1 + k, rows, :], w_ref.at[k]) for k in range(2)], sems)
    for k in range(2):
        copies[k].wait()
        for s in range(out_ref.shape[0]):
            out_ref[s, k * half : (k + 1) * half, :] = w_ref[k, :, s * HEAD_DIM : (s + 1) * HEAD_DIM]


def kv_weights(section, w):
    _, depth, width = w.shape
    return call(
        kv_weights_kernel, "kv_weights",
        jax.ShapeDtypeStruct((width // HEAD_DIM, depth, HEAD_DIM), w.dtype),
        0, 4 * depth * width, 0, VMEM_WHOLE,
        in_specs=[SMEM, HBM],
        out_specs=VMEM,
        scratch_shapes=[pltpu.VMEM((2, depth // 2, width), w.dtype), pltpu.SemaphoreType.DMA((2,))],
    )(section, w)


def direct_kernel(w_hbm, text_hbm, mask_ref, out_ref, w_ref, text_ref, sems):
    depth, count = w_ref.shape[0], text_ref.shape[1]
    copies = started([(w_hbm.at[0], w_ref), (text_hbm, text_ref)], sems)
    finished(copies)
    for s in range(out_ref.shape[0]):
        out_ref[s, :depth, :] = w_ref[:, s * HEAD_DIM : (s + 1) * HEAD_DIM]
        out_ref[s, depth : depth + count, :] = text_ref[s]
        out_ref[s, depth + count :, :] = mask_ref[...]


def direct_rows(w, text, mask):
    heads, count, _ = text.shape
    shape = (heads, w.shape[1] + count + mask.shape[0], HEAD_DIM)
    return call(
        direct_kernel, "direct_rows", jax.ShapeDtypeStruct(shape, w.dtype),
        0, 4 * heads * shape[1] * HEAD_DIM, 0, VMEM_WHOLE,
        in_specs=[HBM, HBM, VMEM],
        out_specs=VMEM,
        scratch_shapes=[
            pltpu.VMEM(w.shape[1:], w.dtype),
            pltpu.VMEM(text.shape, text.dtype),
            pltpu.SemaphoreType.DMA((2,)),
        ],
    )(w, text, mask)


def normed_rotated(x, gain, cosine, sine):
    x = x * lax.rsqrt(jnp.mean(x * x, axis=-1, keepdims=True) + 1e-06) * gain
    even = lax.broadcasted_iota(jnp.int32, x.shape, 1) % 2 == 0
    other = jnp.where(even, pltpu.roll(x, HEAD_DIM - 1, 1), pltpu.roll(x, 1, 1))
    return (x * cosine + other * sine).astype(jnp.bfloat16)


def table_of(tabs_ref, which, start, rows):
    groups = tabs_ref.shape[1] - GRID_W
    columns = tabs_ref[which, groups:, :]
    lane = lax.broadcasted_iota(jnp.int32, columns.shape, 1)
    first = HEAD_DIM // 8
    by_row = lane < first + (HEAD_DIM - first) // 2
    return jnp.concatenate(
        [
            jnp.where(by_row, tabs_ref[which, g : g + 1, :], columns)
            for g in range(start // GRID_W, (start + rows) // GRID_W)
        ],
        axis=0,
    )


def piece_copies(piece_refs, x_ref):
    at, pairs = 0, []
    for ref in piece_refs:
        pairs.append((ref, x_ref.at[pl.ds(at, ref.shape[0]), :]))
        at += ref.shape[0]
    return pairs


def blocks(rows):
    return [(b, slice(b * BLOCK, (b + 1) * BLOCK)) for b in range(rows // BLOCK)]


def arrived(copies, piece_refs, rows):
    at = 0
    for copy, ref in zip(copies, piece_refs):
        if rows.start <= at < rows.stop:
            copy.wait()
        at += ref.shape[0]


def kv_kernel(chunk, section_ref, tabs_hbm, gain_hbm, mine_hbm, peer_a, peer_b, *refs):
    piece_refs = refs[:-8]
    kv_ref, x_ref, mine, peer, w_ref, tabs_ref, gain_ref, sems = refs[-8:]
    sources, held, _ = mine.shape
    half = held // 2
    some = sources // 2
    weights = started(
        [
            (mine_hbm, mine),
            (peer_a, peer.at[pl.ds(0, some)]),
            (peer_b, peer.at[pl.ds(some, some)]),
            (tabs_hbm, tabs_ref),
            (gain_hbm, gain_ref),
        ],
        sems,
    )
    tokens = started(piece_copies(piece_refs, x_ref), sems, 5)
    finished(weights)
    first = section_ref[0] == 0
    for s in range(sources):
        for kind in range(2):
            at = slice(kind * half, (kind + 1) * half)
            lanes = slice(kind * HEAD_DIM, (kind + 1) * HEAD_DIM)
            a, b = mine[s, at, :], peer[s, at, :]
            w_ref[2 * s * half : (2 * s + 1) * half, lanes] = jnp.where(first, a, b)
            w_ref[(2 * s + 1) * half : (2 * s + 2) * half, lanes] = jnp.where(first, b, a)
    for b, at in blocks(x_ref.shape[0]):
        arrived(tokens, piece_refs, at)
        both = jnp.dot(x_ref[at, :], w_ref[...], preferred_element_type=jnp.float32)
        start = chunk * x_ref.shape[0] + b * BLOCK
        kv_ref[0, at, :] = normed_rotated(
            both[:, :HEAD_DIM],
            gain_ref[1:2, :],
            table_of(tabs_ref, 0, start, BLOCK),
            table_of(tabs_ref, 1, start, BLOCK),
        )
        kv_ref[1, at, :] = both[:, HEAD_DIM:].astype(jnp.bfloat16)


def project_kv(chunk, section, tabs, gains, mine, peers, pieces):
    depth = pieces[0].shape[1]
    rows = sum(p.shape[0] for p in pieces)
    return call(
        lambda *refs: kv_kernel(chunk, *refs), "project_kv" + "ab"[chunk],
        jax.ShapeDtypeStruct((2, rows, HEAD_DIM), jnp.bfloat16),
        4 * rows * depth * HEAD_DIM, 2 * (rows * depth + 2 * mine.size), 0, VMEM_WHOLE,
        in_specs=[SMEM] + [HBM] * (5 + len(pieces)),
        out_specs=VMEM,
        scratch_shapes=[
            pltpu.VMEM((rows, depth), jnp.bfloat16),
            pltpu.VMEM(mine.shape, jnp.bfloat16),
            pltpu.VMEM(mine.shape, jnp.bfloat16),
            pltpu.VMEM((depth, 2 * HEAD_DIM), jnp.bfloat16),
            pltpu.VMEM(tabs.shape, tabs.dtype),
            pltpu.VMEM(gains.shape, gains.dtype),
            pltpu.SemaphoreType.DMA((5 + len(pieces),)),
        ],
    )(section, tabs, gains, mine, *peers, *pieces)


def weights_of(query, keys):
    scores = lax.dot_general(
        query, keys, (((1,), (1,)), ((), ())), preferred_element_type=jnp.float32
    )
    return jnp.exp(scores * (1.0 / HEAD_DIM**0.5))


def summed(weights, values):
    den = jnp.sum(weights, axis=-1, keepdims=True)
    num = jnp.dot(weights.astype(jnp.bfloat16), values, preferred_element_type=jnp.float32)
    return num, den


def kept_weights(query, cond_ref, keep):
    weights = weights_of(query, cond_ref[0])
    rows, keys = weights.shape
    groups = keep.shape[0]
    return (weights.reshape(groups, rows // groups, keys) * keep[:, None, :]).reshape(rows, keys)


BLOCK = 256


def own_kernel(
    section_ref, rows_ref, keys_ref, kva, kvb, cond, tabs_hbm, gain_hbm, direct_hbm, *refs
):
    piece_refs = refs[:-9]
    q_ref, num_ref, den_ref, keep_ref, x_ref, direct, tabs_ref, gain_ref, sems = refs[-9:]
    rows, depth = x_ref.shape
    sources, held, _ = direct.shape
    copies = started([(direct_hbm.at[s], direct.at[s]) for s in range(sources)], sems)
    copies += started([(tabs_hbm, tabs_ref), (gain_hbm, gain_ref)], sems, sources)
    tokens = started(piece_copies(piece_refs, x_ref), sems, sources + 2)
    finished(copies)
    wide = depth // sources
    w = direct[:, :wide, :].reshape(depth, HEAD_DIM)
    count = (held - 16 - wide) // 2
    text = (
        direct[:, wide : wide + count, :].reshape(-1, HEAD_DIM),
        direct[:, wide + count : wide + 2 * count, :].reshape(-1, HEAD_DIM),
    )
    for b, at in blocks(rows):
        arrived(tokens, piece_refs, at)
        query = jnp.dot(x_ref[at, :], w, preferred_element_type=jnp.float32)
        query = normed_rotated(
            query,
            gain_ref[0:1, :],
            table_of(tabs_ref, 0, b * BLOCK, BLOCK),
            table_of(tabs_ref, 1, b * BLOCK, BLOCK),
        )
        q_ref[at, :] = query
        num, den = 0.0, 0.0
        for keys, values in ((kva[0], kva[1]), (kvb[0], kvb[1]), text):
            more = summed(weights_of(query, keys), values)
            num, den = num + more[0], den + more[1]
        num_ref[at, :] = num
        den_ref[at, :] = jnp.broadcast_to(den, num.shape)
    mask = jnp.concatenate(
        [direct[s, held - 16 : held, :].astype(jnp.float32)[:1] for s in range(sources)], axis=0
    )
    mask = jnp.dot(rows_ref[...], mask, preferred_element_type=jnp.float32)
    mask = jnp.dot(mask, keys_ref[...], preferred_element_type=jnp.float32)
    size = rows // keep_ref.shape[0]
    for g in range(keep_ref.shape[0]):
        keep_ref[:, g * size : (g + 1) * size] = jnp.broadcast_to(
            mask[:, g : g + 1], (keep_ref.shape[0], size)
        )

    @pl.when(section_ref[0] != 0)
    def _():
        for b, at in blocks(rows):
            num, den = cond_sum(keep_ref, q_ref, cond, 0, b)
            num_ref[at, :] += num
            den_ref[at, :] += jnp.broadcast_to(den, num.shape)


def cond_sum(keep_ref, q_ref, cond, chunk, b):
    groups = keep_ref.shape[0] * BLOCK // q_ref.shape[0]
    keys = cond.shape[1]
    keep = keep_ref[b * groups : (b + 1) * groups, chunk * keys : (chunk + 1) * keys]
    return summed(kept_weights(q_ref[b * BLOCK : (b + 1) * BLOCK, :], cond, keep), cond[1])


def second_cond_kernel(
    section_ref, place_ref, keep_hbm, q_hbm, num_hbm, den_hbm, cond, out_ref,
    keep_ref, q_ref, num_ref, den_ref, sems,
):
    groups = keep_ref.shape[0] * BLOCK // num_ref.shape[0]
    size = BLOCK // groups
    finished(
        started(
            [(num_hbm, num_ref), (den_hbm, den_ref), (q_hbm, q_ref), (keep_hbm, keep_ref)], sems
        )
    )

    def store(b, num, den):
        value = (num / den).astype(jnp.bfloat16)
        for g in range(groups):
            shard, part = place_ref[0, b * groups + g], place_ref[1, b * groups + g]
            at = pl.ds(pl.multiple_of(part * size, size), size)
            out_ref[shard, at, :] = value[g * size : (g + 1) * size]

    @pl.when(section_ref[0] == 0)
    def _():
        for b, at in blocks(num_ref.shape[0]):
            store(b, num_ref[at, :], den_ref[at, :])

    @pl.when(section_ref[0] != 0)
    def _():
        for b, at in blocks(num_ref.shape[0]):
            num, den = cond_sum(keep_ref, q_ref, cond, 1, b)
            store(b, num_ref[at, :] + num, den_ref[at, :] + den)


def attend_own(section, tabs, gains, row_tiles, key_tiles, kvs, cond, direct, pieces):
    depth = pieces[0].shape[1]
    rows = sum(p.shape[0] for p in pieces)
    keys = 2 * rows
    return call(
        own_kernel, "attend_own",
        [
            jax.ShapeDtypeStruct((rows, HEAD_DIM), jnp.bfloat16),
            jax.ShapeDtypeStruct((rows, HEAD_DIM), jnp.float32),
            jax.ShapeDtypeStruct((rows, HEAD_DIM), jnp.float32),
            jax.ShapeDtypeStruct((row_tiles.shape[0], rows), jnp.float32),
        ],
        2 * rows * HEAD_DIM * (2 * keys + depth), 2 * rows * depth, rows * keys, VMEM_WHOLE,
        in_specs=[SMEM] + [VMEM] * 5 + [HBM] * (3 + len(pieces)),
        out_specs=[VMEM] * 4,
        scratch_shapes=[
            pltpu.VMEM((rows, depth), jnp.bfloat16),
            pltpu.VMEM(direct.shape, jnp.bfloat16),
            pltpu.VMEM(tabs.shape, tabs.dtype),
            pltpu.VMEM(gains.shape, gains.dtype),
            pltpu.SemaphoreType.DMA((direct.shape[0] + 2 + len(pieces),)),
        ],
    )(section, row_tiles, key_tiles, *kvs, cond, tabs, gains, direct, *pieces)


def attend_second(section, place, keep, query, cond, num, den, seq):
    rows, keys = num.shape[0], cond.shape[1]
    return call(
        second_cond_kernel, "attend_second",
        jax.ShapeDtypeStruct((seq, rows // seq, HEAD_DIM), jnp.bfloat16),
        4 * rows * keys * HEAD_DIM, 2 * rows * HEAD_DIM * 8, rows * keys, VMEM_WHOLE,
        in_specs=[SMEM, SMEM] + [HBM] * 4 + [VMEM],
        out_specs=VMEM,
        scratch_shapes=[pltpu.VMEM(x.shape, x.dtype) for x in (keep, query, num, den)]
        + [pltpu.SemaphoreType.DMA((4,))],
    )(section, place, keep, query, num, den, cond)


def token_rows(attn_ref):
    return jnp.concatenate([attn_ref[h] for h in range(attn_ref.shape[0])], axis=1)


def sent_kernel(attn_ref, w_ref, out_ref):
    branch = jnp.dot(token_rows(attn_ref), w_ref[...], preferred_element_type=jnp.float32)
    out_ref[...] = branch.astype(jnp.bfloat16)


def kept_kernel(attn_ref, w_ref, image_ref, gate_ref, out_ref):
    branch = jnp.dot(token_rows(attn_ref), w_ref[...], preferred_element_type=jnp.float32)
    out_ref[...] = image_ref[...].astype(jnp.float32) + gate_ref[...] * branch


def project_out(attn, w, image=None, gate=None):
    rows = attn.shape[1]
    depth, width = w.shape
    kept = image is not None
    args = (attn, w) + ((image, gate) if kept else ())
    return call(
        kept_kernel if kept else sent_kernel, "out_kept" if kept else "out_sent",
        jax.ShapeDtypeStruct((rows, width), jnp.float32 if kept else jnp.bfloat16),
        2 * rows * depth * width, 2 * depth * width, 0,
        in_specs=[VMEM] * len(args),
        out_specs=VMEM,
    )(*args)


def lane_tables(row_ids, time_index):
    first = HEAD_DIM // 8
    rest = (HEAD_DIM - first) // 2
    freqs = jnp.concatenate([axis_freqs(first), axis_freqs(rest), axis_freqs(rest)])
    freqs = jnp.repeat(freqs, 2)[None]
    lane = jnp.arange(HEAD_DIM, dtype=jnp.int32)[None]
    rows = jnp.where(lane < first, time_index, row_ids.astype(jnp.float32)[:, None])
    columns = jnp.broadcast_to(jnp.arange(GRID_W, dtype=jnp.float32)[:, None], (GRID_W, HEAD_DIM))
    angles = jnp.concatenate([rows, columns], axis=0) * freqs
    return jnp.stack([jnp.cos(angles), jnp.sin(angles) * jnp.where(lane % 2 == 0, -1.0, 1.0)])


def z_pairs(seq, pairs):
    return [(2 * a + core, 2 * b + core) for a, b in pairs for core in range(2)]


def head_body(image, text_kv, modulation, w_qkv, w_out, q_gain, k_gain, region_mask):
    seq = lax.axis_size("seq")
    img_rows = image.shape[1]
    depth = w_qkv.shape[0]
    section = lax.axis_index("section")
    tp = lax.axis_index("tp")
    chip, core = lax.axis_index("seq") // 2, lax.axis_index("seq") % 2
    mods = modulation[0]
    section_at = section.astype(jnp.int32).reshape(1)
    tp_at = tp.astype(jnp.int32).reshape(1)
    both = [(0, 1), (1, 0)]

    rows3 = w_qkv.transpose(1, 0, 2)
    mine = lax.all_to_all(kv_weights(section_at, rows3), "seq", 0, 0)

    full, part = norm_tokens(tp_at, image[0], modulation.transpose(1, 0, 2))

    def along_z(x, pairs):
        return lax.ppermute(x, "seq", z_pairs(seq, pairs))

    def to_core(x):
        return lax.ppermute(x, "seq", [(s, s ^ 1) for s in range(seq)])

    def to_tp(x):
        return lax.ppermute(x, "tp", both)

    near = along_z(part, [(0, 1), (1, 0), (2, 3), (3, 2)])
    middle = along_z(part, [(1, 2), (2, 1)])
    far = along_z(near, [(1, 2), (2, 1)])
    middle_end = along_z(middle, [(1, 0), (2, 3)])
    far_end = along_z(far, [(1, 0), (2, 3)])
    inner = (chip == 1) | (chip == 2)
    third = jnp.where(inner, middle, middle_end)
    fourth = jnp.where(inner, far, far_end)

    text = text_kv[0].reshape(-1, 2, seq, HEAD_DIM).transpose(2, 1, 0, 3).reshape(seq, -1, HEAD_DIM)
    mask = jnp.pad(
        region_mask.astype(jnp.bfloat16), ((0, 15), (0, HEAD_DIM - region_mask.shape[1]))
    )
    direct = direct_rows(rows3, text, mask)

    near_tp = to_tp(near)
    direct, mine, w_late, at_chip = lax.optimization_barrier(
        (direct, mine, w_out, chip.astype(jnp.int32))
    )
    direct = lax.all_to_all(direct, "seq", 0, 0)
    some = seq // 2
    peers = [lax.ppermute(mine[:some], "section", both), lax.ppermute(mine[some:], "section", both)]
    cols = w_out.shape[1] // 2
    w_sent = lax.dynamic_slice_in_dim(w_late, (1 - tp) * cols, cols, 1)
    w_kept = lax.dynamic_slice_in_dim(w_late, tp * cols, cols, 1)

    upper = at_chip >= 2
    chips = jnp.stack([at_chip, at_chip ^ 1, jnp.where(upper, 1, 2), jnp.where(upper, 0, 3)])
    cores = jnp.stack([core, 1 - core])
    parts = jnp.stack([tp, 1 - tp])
    shards = chips[:, None, None] * 2 + cores[None, :, None] + 0 * parts[None, None, :]
    parts = parts[None, None, :] + 0 * shards
    shards, parts = shards.reshape(-1).astype(jnp.int32), parts.reshape(-1).astype(jnp.int32)
    size = img_rows // 2
    row_ids = shards * (img_rows // GRID_W) + parts * (size // GRID_W)
    tabs = lane_tables(row_ids, (section == 0).astype(jnp.float32))
    gains = jnp.stack([q_gain, k_gain])
    row_tiles = (shards[:, None] == jnp.arange(seq)[None]).astype(jnp.float32)
    key_tiles = jnp.arange(HEAD_DIM)[:, None] == shards[None]
    key_tiles = key_tiles.astype(jnp.float32)
    place = jnp.stack([shards, parts])

    early = (tabs, gains, row_tiles, key_tiles, place, w_sent, w_kept)
    third, near_tp, peers[0], early = lax.optimization_barrier((third, near_tp, peers[0], early))
    tabs, gains, row_tiles, key_tiles, place, w_sent, w_kept = early
    third_tp = to_tp(third)
    fourth, third_tp, peers[1] = lax.optimization_barrier((fourth, third_tp, peers[1]))
    fourth_tp = to_tp(fourth)
    a = [full, to_core(full), near, near_tp, to_core(near), to_core(near_tp)]
    kv_a = project_kv(0, section_at, tabs, gains, mine, peers, a)
    cond_a = lax.ppermute(kv_a, "section", [(0, 1)])
    b = [third, third_tp, to_core(third), to_core(third_tp), fourth, fourth_tp, to_core(fourth)]
    fourth_tp, kv_a = lax.optimization_barrier((fourth_tp, kv_a))
    b[5] = fourth_tp
    b.append(to_core(fourth_tp))
    kv_b = project_kv(1, section_at, tabs, gains, mine, peers, b)
    cond_b = lax.ppermute(kv_b, "section", [(0, 1)])
    query, num, den, keep = attend_own(
        section_at, tabs, gains, row_tiles, key_tiles, (kv_a, kv_b), cond_a, direct, a + b
    )
    attn = attend_second(section_at, place, keep, query, cond_b, num, den, seq)

    attn = lax.all_to_all(attn, "seq", 0, 0)
    gate = lax.dynamic_slice_in_dim(mods[2:3], tp * cols, cols, 1)
    residual = lax.dynamic_slice_in_dim(image[0], tp * cols, cols, 1)
    other = to_tp(project_out(attn, w_sent))
    kept = project_out(attn, w_kept, residual, gate)
    return (kept + gate * other.astype(jnp.float32)).astype(jnp.bfloat16)[None]


def rms_rows(x, gain):
    return x * lax.rsqrt(jnp.mean(x * x, axis=-1, keepdims=True) + 1e-06) * gain


def apply_rope(x, cosine, sine):
    rows, heads_here = (x.shape[0], x.shape[1])
    pairs = x.reshape(rows, heads_here, HEAD_DIM // 2, 2)
    first = pairs[..., 0]
    second = pairs[..., 1]
    cosine = cosine[:, None, :]
    sine = sine[:, None, :]
    rotated = jnp.stack([first * cosine - second * sine, first * sine + second * cosine], axis=-1)
    return rotated.reshape(rows, heads_here, HEAD_DIM)


def attend_piece(carry, keys_vals, query, keep):
    num, den = carry
    rows = keys_vals.shape[0]
    heads_local = query.shape[1]
    piece_k = keys_vals[:, 0].reshape(rows, heads_local, HEAD_DIM)
    piece_v = keys_vals[:, 1].reshape(rows, heads_local, HEAD_DIM)
    scores = jnp.einsum("qhd,khd->hqk", query, piece_k, preferred_element_type=jnp.float32) * (
        1.0 / HEAD_DIM**0.5
    )
    weights = jnp.exp(scores)
    if keep is not None:
        weights = jnp.where(keep[None], weights, 0.0)
    den = den + jnp.sum(weights, axis=-1)
    num = num + jnp.einsum(
        "hqk,khd->hqd", weights.astype(jnp.bfloat16), piece_v, preferred_element_type=jnp.float32
    )
    return (num, den)


def token_body(image, text_kv, modulation, w_qkv, w_out, q_gain, k_gain, region_mask):
    img_rows = image.shape[1]
    width_local = w_qkv.shape[2]
    heads_local = width_local // HEAD_DIM
    tokens = image[0].astype(jnp.float32)
    mods = modulation[0]
    normed = layer_norm(tokens, mods)
    qkv = jnp.einsum(
        "td,dcf->tcf",
        normed,
        lax.all_gather(w_qkv, "seq", axis=0, tiled=True),
        preferred_element_type=jnp.float32,
    )
    section_index = lax.axis_index("section")
    time_index = (section_index == 0).astype(jnp.float32)
    rows_index = lax.axis_index("seq") * img_rows + jnp.arange(img_rows, dtype=jnp.int32)
    cosine, sine = rope_tables(rows_index, time_index)
    query = apply_rope(
        rms_rows(qkv[:, 0].reshape(img_rows, heads_local, HEAD_DIM), q_gain), cosine, sine
    ).astype(jnp.bfloat16)
    keys = apply_rope(
        rms_rows(qkv[:, 1].reshape(img_rows, heads_local, HEAD_DIM), k_gain), cosine, sine
    ).astype(jnp.bfloat16)
    values = qkv[:, 2].astype(jnp.bfloat16)
    image_kv = jnp.stack([keys.reshape(img_rows, width_local), values], axis=1)
    own_kv = jnp.concatenate([image_kv, text_kv[0]], axis=0)
    enabled = (section_index == 1).astype(jnp.int32)
    local_mask = region_mask * enabled
    init = (
        jnp.zeros((heads_local, img_rows, HEAD_DIM), jnp.float32),
        jnp.zeros((heads_local, img_rows), jnp.float32),
    )
    carry = attend_piece(init, lax.all_gather(own_kv, "seq", axis=0, tiled=True), query, None)
    cond_local = lax.ppermute(image_kv, "section", [(0, 1)])
    keep = jnp.repeat(jnp.repeat(local_mask, TILE, axis=0), TILE, axis=1) > 0
    carry = attend_piece(carry, lax.all_gather(cond_local, "seq", axis=0, tiled=True), query, keep)
    num, den = carry
    attn = (num / den[..., None]).astype(jnp.bfloat16)
    attn = jnp.transpose(attn, (1, 0, 2)).reshape(img_rows, width_local)
    term = jnp.dot(attn, w_out, preferred_element_type=jnp.float32)
    branch = lax.psum_scatter(
        term.astype(jnp.bfloat16), "tp", scatter_dimension=1, tiled=True
    ).astype(jnp.float32)
    cols = branch.shape[1]
    offset = lax.axis_index("tp") * cols
    residual = lax.dynamic_slice_in_dim(tokens, offset, cols, 1)
    gate = lax.dynamic_slice_in_dim(mods[2], offset, cols, 0)
    out = residual + gate[None, :] * branch
    return out.astype(jnp.bfloat16)[None]


def body(*arrays):
    image, w_qkv, region_mask = arrays[0], arrays[3], arrays[7]
    seq = lax.axis_size("seq")
    one_head_each = (
        w_qkv.shape[2] // HEAD_DIM == seq == 8
        and lax.axis_size("section") == 2
        and lax.axis_size("tp") == 2
        and w_qkv.shape[0] % 128 == 0
        and image.shape[1] == TILE == 2 * GRID_W
        and region_mask.shape == (1, seq)
        and arrays[1].shape[1] % 16 == 0
        and arrays[4].shape[1] % 1024 == 0
    )
    return (head_body if one_head_each else token_body)(*arrays)


def solution(mesh):
    return jax.shard_map(
        body,
        mesh=mesh,
        in_specs=(
            P("section", "seq", None),
            P("section", "seq", None, "tp"),
            P("section", None, None),
            P("seq", None, "tp"),
            P("tp", None),
            P(),
            P(),
            P("seq", None),
        ),
        out_specs=P("section", "seq", "tp"),
        check_vma=False,
    )
```

```python
import jax
import jax.numpy as jnp
from jax import lax
from jax.experimental import pallas as pl
from jax.experimental.pallas import tpu as pltpu
from jax.sharding import PartitionSpec as P

HEAD_DIM = 128
GRID_W = 64
TILE = 128
VMEM_LIMIT = 24 * 1024 * 1024
VMEM_WHOLE = 56 * 1024 * 1024


def axis_freqs(width):
    return 10000.0 ** (-jnp.arange(0, width, 2).astype(jnp.float32) / width)


def rope_tables(rows_index, time_index):
    first = HEAD_DIM // 8
    rest = (HEAD_DIM - first) // 2
    row_pos = (rows_index // GRID_W).astype(jnp.float32)
    col_pos = (rows_index % GRID_W).astype(jnp.float32)
    time_pos = jnp.zeros_like(row_pos) + time_index
    angles = jnp.concatenate(
        [
            time_pos[:, None] * axis_freqs(first)[None],
            row_pos[:, None] * axis_freqs(rest)[None],
            col_pos[:, None] * axis_freqs(rest)[None],
        ],
        axis=-1,
    )
    return (jnp.cos(angles), jnp.sin(angles))


def layer_norm(tokens, mods):
    mean = jnp.mean(tokens, axis=-1, keepdims=True)
    var = jnp.mean((tokens - mean) ** 2, axis=-1, keepdims=True)
    return ((tokens - mean) * lax.rsqrt(var + 1e-06) * (1.0 + mods[1:2]) + mods[0:1]).astype(
        jnp.bfloat16
    )


VMEM = pl.BlockSpec(memory_space=pltpu.VMEM)
SMEM = pl.BlockSpec(memory_space=pltpu.SMEM)
HBM = pl.BlockSpec(memory_space=pltpu.HBM)


def call(kernel, name, out_shape, flops, moved, exps, limit=VMEM_LIMIT, **spec):
    return pl.pallas_call(
        kernel,
        out_shape=out_shape,
        compiler_params=pltpu.CompilerParams(vmem_limit_bytes=limit),
        cost_estimate=pl.CostEstimate(flops=flops, bytes_accessed=moved, transcendentals=exps),
        name=name,
        **spec,
    )


def started(pairs, sems, first=0):
    copies = [pltpu.make_async_copy(s, d, sems.at[first + i]) for i, (s, d) in enumerate(pairs)]
    for copy in copies:
        copy.start()
    return copies


def finished(copies):
    for copy in copies:
        copy.wait()


def norm_kernel(tp_ref, image_hbm, mods_hbm, full_ref, part_ref, image_ref, mods_ref, sems):
    rows = image_ref.shape[0] // 4
    pairs = [
        (image_hbm.at[pl.ds(i * rows, rows), :], image_ref.at[pl.ds(i * rows, rows), :])
        for i in range(4)
    ]
    finished(started(pairs + [(mods_hbm, mods_ref)], sems))
    mods = jnp.concatenate([mods_ref[0], mods_ref[1]], axis=0)
    normed = layer_norm(image_ref[...].astype(jnp.float32), mods)
    part = part_ref.shape[0]
    for t in range(2):

        @pl.when(tp_ref[0] == t)
        def _(t=t):
            ours, theirs = normed[t * part : (t + 1) * part], normed[(1 - t) * part : (2 - t) * part]
            full_ref[:part, :] = ours
            full_ref[part:, :] = theirs
            part_ref[...] = ours


def norm_tokens(tp, image, mods):
    rows, depth = image.shape
    return call(
        norm_kernel, "norm_tokens",
        [
            jax.ShapeDtypeStruct((rows, depth), jnp.bfloat16),
            jax.ShapeDtypeStruct((rows // 2, depth), jnp.bfloat16),
        ],
        10 * rows * depth, 4 * rows * depth, 0, VMEM_WHOLE,
        in_specs=[SMEM, HBM, HBM],
        out_specs=[VMEM, VMEM],
        scratch_shapes=[
            pltpu.VMEM(image.shape, image.dtype),
            pltpu.VMEM(mods.shape, mods.dtype),
            pltpu.SemaphoreType.DMA((5,)),
        ],
    )(tp, image, mods)


def kv_weights_kernel(section_ref, w_hbm, out_ref, w_ref, sems):
    half = w_ref.shape[1]
    rows = pl.ds(pl.multiple_of(section_ref[0] * half, half), half)
    copies = started([(w_hbm.at[1 + k, rows, :], w_ref.at[k]) for k in range(2)], sems)
    for k in range(2):
        copies[k].wait()
        for s in range(out_ref.shape[0]):
            out_ref[s, k * half : (k + 1) * half, :] = w_ref[k, :, s * HEAD_DIM : (s + 1) * HEAD_DIM]


def kv_weights(section, w):
    _, depth, width = w.shape
    return call(
        kv_weights_kernel, "kv_weights",
        jax.ShapeDtypeStruct((width // HEAD_DIM, depth, HEAD_DIM), w.dtype),
        0, 4 * depth * width, 0, VMEM_WHOLE,
        in_specs=[SMEM, HBM],
        out_specs=VMEM,
        scratch_shapes=[pltpu.VMEM((2, depth // 2, width), w.dtype), pltpu.SemaphoreType.DMA((2,))],
    )(section, w)


def direct_kernel(w_hbm, text_hbm, mask_ref, out_ref, w_ref, text_ref, sems):
    depth, count = w_ref.shape[0], text_ref.shape[1]
    copies = started([(w_hbm.at[0], w_ref), (text_hbm, text_ref)], sems)
    finished(copies)
    for s in range(out_ref.shape[0]):
        out_ref[s, :depth, :] = w_ref[:, s * HEAD_DIM : (s + 1) * HEAD_DIM]
        out_ref[s, depth : depth + count, :] = text_ref[s]
        out_ref[s, depth + count :, :] = mask_ref[...]


def direct_rows(w, text, mask):
    heads, count, _ = text.shape
    shape = (heads, w.shape[1] + count + mask.shape[0], HEAD_DIM)
    return call(
        direct_kernel, "direct_rows", jax.ShapeDtypeStruct(shape, w.dtype),
        0, 4 * heads * shape[1] * HEAD_DIM, 0, VMEM_WHOLE,
        in_specs=[HBM, HBM, VMEM],
        out_specs=VMEM,
        scratch_shapes=[
            pltpu.VMEM(w.shape[1:], w.dtype),
            pltpu.VMEM(text.shape, text.dtype),
            pltpu.SemaphoreType.DMA((2,)),
        ],
    )(w, text, mask)


def normed_rotated(x, gain, cosine, sine):
    x = x * lax.rsqrt(jnp.mean(x * x, axis=-1, keepdims=True) + 1e-06) * gain
    even = lax.broadcasted_iota(jnp.int32, x.shape, 1) % 2 == 0
    other = jnp.where(even, pltpu.roll(x, HEAD_DIM - 1, 1), pltpu.roll(x, 1, 1))
    return (x * cosine + other * sine).astype(jnp.bfloat16)


def table_of(tabs_ref, which, start, rows):
    groups = tabs_ref.shape[1] - GRID_W
    columns = tabs_ref[which, groups:, :]
    lane = lax.broadcasted_iota(jnp.int32, columns.shape, 1)
    first = HEAD_DIM // 8
    by_row = lane < first + (HEAD_DIM - first) // 2
    return jnp.concatenate(
        [
            jnp.where(by_row, tabs_ref[which, g : g + 1, :], columns)
            for g in range(start // GRID_W, (start + rows) // GRID_W)
        ],
        axis=0,
    )


def piece_copies(piece_refs, x_ref):
    at, pairs = 0, []
    for ref in piece_refs:
        pairs.append((ref, x_ref.at[pl.ds(at, ref.shape[0]), :]))
        at += ref.shape[0]
    return pairs


def blocks(rows):
    return [(b, slice(b * BLOCK, (b + 1) * BLOCK)) for b in range(rows // BLOCK)]


def arrived(copies, piece_refs, rows):
    at = 0
    for copy, ref in zip(copies, piece_refs):
        if rows.start <= at < rows.stop:
            copy.wait()
        at += ref.shape[0]


def kv_kernel(chunk, section_ref, tabs_hbm, gain_hbm, mine_hbm, peer_hbm, *refs):
    piece_refs = refs[:-8]
    kv_ref, x_ref, mine, peer, w_ref, tabs_ref, gain_ref, sems = refs[-8:]
    sources, held, _ = mine.shape
    half = held // 2
    weights = started(
        [(mine_hbm, mine), (peer_hbm, peer), (tabs_hbm, tabs_ref), (gain_hbm, gain_ref)], sems
    )
    tokens = started(piece_copies(piece_refs, x_ref), sems, 4)
    finished(weights)
    first = section_ref[0] == 0
    for s in range(sources):
        for kind in range(2):
            at = slice(kind * half, (kind + 1) * half)
            lanes = slice(kind * HEAD_DIM, (kind + 1) * HEAD_DIM)
            a, b = mine[s, at, :], peer[s, at, :]
            w_ref[2 * s * half : (2 * s + 1) * half, lanes] = jnp.where(first, a, b)
            w_ref[(2 * s + 1) * half : (2 * s + 2) * half, lanes] = jnp.where(first, b, a)
    for b, at in blocks(x_ref.shape[0]):
        arrived(tokens, piece_refs, at)
        both = jnp.dot(x_ref[at, :], w_ref[...], preferred_element_type=jnp.float32)
        start = chunk * x_ref.shape[0] + b * BLOCK
        kv_ref[0, at, :] = normed_rotated(
            both[:, :HEAD_DIM],
            gain_ref[1:2, :],
            table_of(tabs_ref, 0, start, BLOCK),
            table_of(tabs_ref, 1, start, BLOCK),
        )
        kv_ref[1, at, :] = both[:, HEAD_DIM:].astype(jnp.bfloat16)


def project_kv(chunk, section, tabs, gains, mine, peer, pieces):
    depth = pieces[0].shape[1]
    rows = sum(p.shape[0] for p in pieces)
    return call(
        lambda *refs: kv_kernel(chunk, *refs), "project_kv" + "ab"[chunk],
        jax.ShapeDtypeStruct((2, rows, HEAD_DIM), jnp.bfloat16),
        4 * rows * depth * HEAD_DIM, 2 * (rows * depth + 2 * mine.size), 0, VMEM_WHOLE,
        in_specs=[SMEM] + [HBM] * (4 + len(pieces)),
        out_specs=VMEM,
        scratch_shapes=[
            pltpu.VMEM((rows, depth), jnp.bfloat16),
            pltpu.VMEM(mine.shape, jnp.bfloat16),
            pltpu.VMEM(mine.shape, jnp.bfloat16),
            pltpu.VMEM((depth, 2 * HEAD_DIM), jnp.bfloat16),
            pltpu.VMEM(tabs.shape, tabs.dtype),
            pltpu.VMEM(gains.shape, gains.dtype),
            pltpu.SemaphoreType.DMA((4 + len(pieces),)),
        ],
    )(section, tabs, gains, mine, peer, *pieces)


def weights_of(query, keys):
    scores = lax.dot_general(
        query, keys, (((1,), (1,)), ((), ())), preferred_element_type=jnp.float32
    )
    return jnp.exp(scores * (1.0 / HEAD_DIM**0.5))


def summed(weights, values):
    den = jnp.sum(weights, axis=-1, keepdims=True)
    num = jnp.dot(weights.astype(jnp.bfloat16), values, preferred_element_type=jnp.float32)
    return num, den


def kept_weights(query, cond_ref, keep):
    weights = weights_of(query, cond_ref[0])
    rows, keys = weights.shape
    groups = keep.shape[0]
    return (weights.reshape(groups, rows // groups, keys) * keep[:, None, :]).reshape(rows, keys)


BLOCK = 256


def own_kernel(
    section_ref, rows_ref, keys_ref, kva, kvb, cond, tabs_hbm, gain_hbm, direct_hbm, *refs
):
    piece_refs = refs[:-9]
    q_ref, num_ref, den_ref, keep_ref, x_ref, direct, tabs_ref, gain_ref, sems = refs[-9:]
    rows, depth = x_ref.shape
    sources, held, _ = direct.shape
    copies = started([(direct_hbm.at[s], direct.at[s]) for s in range(sources)], sems)
    copies += started([(tabs_hbm, tabs_ref), (gain_hbm, gain_ref)], sems, sources)
    tokens = started(piece_copies(piece_refs, x_ref), sems, sources + 2)
    finished(copies)
    wide = depth // sources
    w = direct[:, :wide, :].reshape(depth, HEAD_DIM)
    count = (held - 16 - wide) // 2
    text = (
        direct[:, wide : wide + count, :].reshape(-1, HEAD_DIM),
        direct[:, wide + count : wide + 2 * count, :].reshape(-1, HEAD_DIM),
    )
    for b, at in blocks(rows):
        arrived(tokens, piece_refs, at)
        query = jnp.dot(x_ref[at, :], w, preferred_element_type=jnp.float32)
        query = normed_rotated(
            query,
            gain_ref[0:1, :],
            table_of(tabs_ref, 0, b * BLOCK, BLOCK),
            table_of(tabs_ref, 1, b * BLOCK, BLOCK),
        )
        q_ref[at, :] = query
        num, den = 0.0, 0.0
        for keys, values in ((kva[0], kva[1]), (kvb[0], kvb[1]), text):
            more = summed(weights_of(query, keys), values)
            num, den = num + more[0], den + more[1]
        num_ref[at, :] = num
        den_ref[at, :] = jnp.broadcast_to(den, num.shape)
    mask = jnp.concatenate(
        [direct[s, held - 16 : held, :].astype(jnp.float32)[:1] for s in range(sources)], axis=0
    )
    mask = jnp.dot(rows_ref[...], mask, preferred_element_type=jnp.float32)
    mask = jnp.dot(mask, keys_ref[...], preferred_element_type=jnp.float32)
    size = rows // keep_ref.shape[0]
    for g in range(keep_ref.shape[0]):
        keep_ref[:, g * size : (g + 1) * size] = jnp.broadcast_to(
            mask[:, g : g + 1], (keep_ref.shape[0], size)
        )

    @pl.when(section_ref[0] != 0)
    def _():
        for b, at in blocks(rows):
            num, den = cond_sum(keep_ref, q_ref, cond, 0, b)
            num_ref[at, :] += num
            den_ref[at, :] += jnp.broadcast_to(den, num.shape)


def cond_sum(keep_ref, q_ref, cond, chunk, b):
    groups = keep_ref.shape[0] * BLOCK // q_ref.shape[0]
    keys = cond.shape[1]
    keep = keep_ref[b * groups : (b + 1) * groups, chunk * keys : (chunk + 1) * keys]
    return summed(kept_weights(q_ref[b * BLOCK : (b + 1) * BLOCK, :], cond, keep), cond[1])


def second_cond_kernel(
    section_ref, place_ref, keep_hbm, q_hbm, num_hbm, den_hbm, cond, out_ref,
    keep_ref, q_ref, num_ref, den_ref, sems,
):
    groups = keep_ref.shape[0] * BLOCK // num_ref.shape[0]
    size = BLOCK // groups
    finished(
        started(
            [(num_hbm, num_ref), (den_hbm, den_ref), (q_hbm, q_ref), (keep_hbm, keep_ref)], sems
        )
    )

    def store(b, num, den):
        value = (num / den).astype(jnp.bfloat16)
        for g in range(groups):
            shard, part = place_ref[0, b * groups + g], place_ref[1, b * groups + g]
            at = pl.ds(pl.multiple_of(part * size, size), size)
            out_ref[shard, at, :] = value[g * size : (g + 1) * size]

    @pl.when(section_ref[0] == 0)
    def _():
        for b, at in blocks(num_ref.shape[0]):
            store(b, num_ref[at, :], den_ref[at, :])

    @pl.when(section_ref[0] != 0)
    def _():
        for b, at in blocks(num_ref.shape[0]):
            num, den = cond_sum(keep_ref, q_ref, cond, 1, b)
            store(b, num_ref[at, :] + num, den_ref[at, :] + den)


def attend_own(section, tabs, gains, row_tiles, key_tiles, kvs, cond, direct, pieces):
    depth = pieces[0].shape[1]
    rows = sum(p.shape[0] for p in pieces)
    keys = 2 * rows
    return call(
        own_kernel, "attend_own",
        [
            jax.ShapeDtypeStruct((rows, HEAD_DIM), jnp.bfloat16),
            jax.ShapeDtypeStruct((rows, HEAD_DIM), jnp.float32),
            jax.ShapeDtypeStruct((rows, HEAD_DIM), jnp.float32),
            jax.ShapeDtypeStruct((row_tiles.shape[0], rows), jnp.float32),
        ],
        2 * rows * HEAD_DIM * (2 * keys + depth), 2 * rows * depth, rows * keys, VMEM_WHOLE,
        in_specs=[SMEM] + [VMEM] * 5 + [HBM] * (3 + len(pieces)),
        out_specs=[VMEM] * 4,
        scratch_shapes=[
            pltpu.VMEM((rows, depth), jnp.bfloat16),
            pltpu.VMEM(direct.shape, jnp.bfloat16),
            pltpu.VMEM(tabs.shape, tabs.dtype),
            pltpu.VMEM(gains.shape, gains.dtype),
            pltpu.SemaphoreType.DMA((direct.shape[0] + 2 + len(pieces),)),
        ],
    )(section, row_tiles, key_tiles, *kvs, cond, tabs, gains, direct, *pieces)


def attend_second(section, place, keep, query, cond, num, den, seq):
    rows, keys = num.shape[0], cond.shape[1]
    return call(
        second_cond_kernel, "attend_second",
        jax.ShapeDtypeStruct((seq, rows // seq, HEAD_DIM), jnp.bfloat16),
        4 * rows * keys * HEAD_DIM, 2 * rows * HEAD_DIM * 8, rows * keys, VMEM_WHOLE,
        in_specs=[SMEM, SMEM] + [HBM] * 4 + [VMEM],
        out_specs=VMEM,
        scratch_shapes=[pltpu.VMEM(x.shape, x.dtype) for x in (keep, query, num, den)]
        + [pltpu.SemaphoreType.DMA((4,))],
    )(section, place, keep, query, num, den, cond)


def token_rows(attn_ref):
    return jnp.concatenate([attn_ref[h] for h in range(attn_ref.shape[0])], axis=1)


def sent_kernel(attn_ref, w_ref, out_ref):
    branch = jnp.dot(token_rows(attn_ref), w_ref[...], preferred_element_type=jnp.float32)
    out_ref[...] = branch.astype(jnp.bfloat16)


def kept_kernel(attn_ref, w_ref, image_ref, gate_ref, out_ref):
    branch = jnp.dot(token_rows(attn_ref), w_ref[...], preferred_element_type=jnp.float32)
    out_ref[...] = image_ref[...].astype(jnp.float32) + gate_ref[...] * branch


def project_out(attn, w, image=None, gate=None):
    rows = attn.shape[1]
    depth, width = w.shape
    kept = image is not None
    args = (attn, w) + ((image, gate) if kept else ())
    return call(
        kept_kernel if kept else sent_kernel, "out_kept" if kept else "out_sent",
        jax.ShapeDtypeStruct((rows, width), jnp.float32 if kept else jnp.bfloat16),
        2 * rows * depth * width, 2 * depth * width, 0,
        in_specs=[VMEM] * len(args),
        out_specs=VMEM,
    )(*args)


def lane_tables(row_ids, time_index):
    first = HEAD_DIM // 8
    rest = (HEAD_DIM - first) // 2
    freqs = jnp.concatenate([axis_freqs(first), axis_freqs(rest), axis_freqs(rest)])
    freqs = jnp.repeat(freqs, 2)[None]
    lane = jnp.arange(HEAD_DIM, dtype=jnp.int32)[None]
    rows = jnp.where(lane < first, time_index, row_ids.astype(jnp.float32)[:, None])
    columns = jnp.broadcast_to(jnp.arange(GRID_W, dtype=jnp.float32)[:, None], (GRID_W, HEAD_DIM))
    angles = jnp.concatenate([rows, columns], axis=0) * freqs
    return jnp.stack([jnp.cos(angles), jnp.sin(angles) * jnp.where(lane % 2 == 0, -1.0, 1.0)])


def z_pairs(seq, pairs):
    return [(2 * a + core, 2 * b + core) for a, b in pairs for core in range(2)]


def head_body(image, text_kv, modulation, w_qkv, w_out, q_gain, k_gain, region_mask):
    seq = lax.axis_size("seq")
    img_rows = image.shape[1]
    depth = w_qkv.shape[0]
    section = lax.axis_index("section")
    tp = lax.axis_index("tp")
    chip, core = lax.axis_index("seq") // 2, lax.axis_index("seq") % 2
    mods = modulation[0]
    section_at = section.astype(jnp.int32).reshape(1)
    tp_at = tp.astype(jnp.int32).reshape(1)
    both = [(0, 1), (1, 0)]

    rows3 = w_qkv.transpose(1, 0, 2)
    mine = lax.all_to_all(kv_weights(section_at, rows3), "seq", 0, 0)

    full, part = norm_tokens(tp_at, image[0], modulation.transpose(1, 0, 2))

    def along_z(x, pairs):
        return lax.ppermute(x, "seq", z_pairs(seq, pairs))

    def to_core(x):
        return lax.ppermute(x, "seq", [(s, s ^ 1) for s in range(seq)])

    def to_tp(x):
        return lax.ppermute(x, "tp", both)

    near = along_z(part, [(0, 1), (1, 0), (2, 3), (3, 2)])
    near, w_late, at_chip = lax.optimization_barrier((near, w_out, chip.astype(jnp.int32)))
    middle = along_z(part, [(1, 2), (2, 1)])
    far = along_z(near, [(1, 2), (2, 1)])
    middle_end = along_z(middle, [(1, 0), (2, 3)])
    far_end = along_z(far, [(1, 0), (2, 3)])
    inner = (chip == 1) | (chip == 2)
    third = jnp.where(inner, middle, middle_end)
    fourth = jnp.where(inner, far, far_end)
    near_tp = to_tp(near)
    peer = lax.ppermute(mine, "section", both)
    cols = w_out.shape[1] // 2
    w_sent = lax.dynamic_slice_in_dim(w_late, (1 - tp) * cols, cols, 1)
    w_kept = lax.dynamic_slice_in_dim(w_late, tp * cols, cols, 1)

    upper = at_chip >= 2
    chips = jnp.stack([at_chip, at_chip ^ 1, jnp.where(upper, 1, 2), jnp.where(upper, 0, 3)])
    cores = jnp.stack([core, 1 - core])
    parts = jnp.stack([tp, 1 - tp])
    shards = chips[:, None, None] * 2 + cores[None, :, None] + 0 * parts[None, None, :]
    parts = parts[None, None, :] + 0 * shards
    shards, parts = shards.reshape(-1).astype(jnp.int32), parts.reshape(-1).astype(jnp.int32)
    size = img_rows // 2
    row_ids = shards * (img_rows // GRID_W) + parts * (size // GRID_W)
    tabs = lane_tables(row_ids, (section == 0).astype(jnp.float32))
    gains = jnp.stack([q_gain, k_gain])
    row_tiles = (shards[:, None] == jnp.arange(seq)[None]).astype(jnp.float32)
    key_tiles = jnp.arange(HEAD_DIM)[:, None] == shards[None]
    key_tiles = key_tiles.astype(jnp.float32)
    place = jnp.stack([shards, parts])

    early = (tabs, gains, row_tiles, key_tiles, place, w_sent, w_kept)
    third, near_tp, text_late, early = lax.optimization_barrier((third, near_tp, text_kv, early))
    tabs, gains, row_tiles, key_tiles, place, w_sent, w_kept = early
    third_tp = to_tp(third)

    text = text_late[0].reshape(-1, 2, seq, HEAD_DIM).transpose(2, 1, 0, 3).reshape(seq, -1, HEAD_DIM)
    mask = jnp.pad(
        region_mask.astype(jnp.bfloat16), ((0, 15), (0, HEAD_DIM - region_mask.shape[1]))
    )
    direct = direct_rows(rows3, text, mask)

    direct, third_tp = lax.optimization_barrier((direct, third_tp))
    direct = lax.all_to_all(direct, "seq", 0, 0)
    fourth, third_tp, peer = lax.optimization_barrier((fourth, third_tp, peer))
    fourth_tp = to_tp(fourth)
    a = [full, to_core(full), near, near_tp, to_core(near), to_core(near_tp)]
    kv_a = project_kv(0, section_at, tabs, gains, mine, peer, a)
    cond_a = lax.ppermute(kv_a, "section", [(0, 1)])
    b = [third, third_tp, to_core(third), to_core(third_tp), fourth, fourth_tp, to_core(fourth)]
    fourth_tp, kv_a = lax.optimization_barrier((fourth_tp, kv_a))
    b[5] = fourth_tp
    b.append(to_core(fourth_tp))
    kv_b = project_kv(1, section_at, tabs, gains, mine, peer, b)
    cond_b = lax.ppermute(kv_b, "section", [(0, 1)])
    query, num, den, keep = attend_own(
        section_at, tabs, gains, row_tiles, key_tiles, (kv_a, kv_b), cond_a, direct, a + b
    )
    attn = attend_second(section_at, place, keep, query, cond_b, num, den, seq)

    attn = lax.all_to_all(attn, "seq", 0, 0)
    gate = lax.dynamic_slice_in_dim(mods[2:3], tp * cols, cols, 1)
    residual = lax.dynamic_slice_in_dim(image[0], tp * cols, cols, 1)
    other = to_tp(project_out(attn, w_sent))
    kept = project_out(attn, w_kept, residual, gate)
    return (kept + gate * other.astype(jnp.float32)).astype(jnp.bfloat16)[None]


def rms_rows(x, gain):
    return x * lax.rsqrt(jnp.mean(x * x, axis=-1, keepdims=True) + 1e-06) * gain


def apply_rope(x, cosine, sine):
    rows, heads_here = (x.shape[0], x.shape[1])
    pairs = x.reshape(rows, heads_here, HEAD_DIM // 2, 2)
    first = pairs[..., 0]
    second = pairs[..., 1]
    cosine = cosine[:, None, :]
    sine = sine[:, None, :]
    rotated = jnp.stack([first * cosine - second * sine, first * sine + second * cosine], axis=-1)
    return rotated.reshape(rows, heads_here, HEAD_DIM)


def attend_piece(carry, keys_vals, query, keep):
    num, den = carry
    rows = keys_vals.shape[0]
    heads_local = query.shape[1]
    piece_k = keys_vals[:, 0].reshape(rows, heads_local, HEAD_DIM)
    piece_v = keys_vals[:, 1].reshape(rows, heads_local, HEAD_DIM)
    scores = jnp.einsum("qhd,khd->hqk", query, piece_k, preferred_element_type=jnp.float32) * (
        1.0 / HEAD_DIM**0.5
    )
    weights = jnp.exp(scores)
    if keep is not None:
        weights = jnp.where(keep[None], weights, 0.0)
    den = den + jnp.sum(weights, axis=-1)
    num = num + jnp.einsum(
        "hqk,khd->hqd", weights.astype(jnp.bfloat16), piece_v, preferred_element_type=jnp.float32
    )
    return (num, den)


def token_body(image, text_kv, modulation, w_qkv, w_out, q_gain, k_gain, region_mask):
    img_rows = image.shape[1]
    width_local = w_qkv.shape[2]
    heads_local = width_local // HEAD_DIM
    tokens = image[0].astype(jnp.float32)
    mods = modulation[0]
    normed = layer_norm(tokens, mods)
    qkv = jnp.einsum(
        "td,dcf->tcf",
        normed,
        lax.all_gather(w_qkv, "seq", axis=0, tiled=True),
        preferred_element_type=jnp.float32,
    )
    section_index = lax.axis_index("section")
    time_index = (section_index == 0).astype(jnp.float32)
    rows_index = lax.axis_index("seq") * img_rows + jnp.arange(img_rows, dtype=jnp.int32)
    cosine, sine = rope_tables(rows_index, time_index)
    query = apply_rope(
        rms_rows(qkv[:, 0].reshape(img_rows, heads_local, HEAD_DIM), q_gain), cosine, sine
    ).astype(jnp.bfloat16)
    keys = apply_rope(
        rms_rows(qkv[:, 1].reshape(img_rows, heads_local, HEAD_DIM), k_gain), cosine, sine
    ).astype(jnp.bfloat16)
    values = qkv[:, 2].astype(jnp.bfloat16)
    image_kv = jnp.stack([keys.reshape(img_rows, width_local), values], axis=1)
    own_kv = jnp.concatenate([image_kv, text_kv[0]], axis=0)
    enabled = (section_index == 1).astype(jnp.int32)
    local_mask = region_mask * enabled
    init = (
        jnp.zeros((heads_local, img_rows, HEAD_DIM), jnp.float32),
        jnp.zeros((heads_local, img_rows), jnp.float32),
    )
    carry = attend_piece(init, lax.all_gather(own_kv, "seq", axis=0, tiled=True), query, None)
    cond_local = lax.ppermute(image_kv, "section", [(0, 1)])
    keep = jnp.repeat(jnp.repeat(local_mask, TILE, axis=0), TILE, axis=1) > 0
    carry = attend_piece(carry, lax.all_gather(cond_local, "seq", axis=0, tiled=True), query, keep)
    num, den = carry
    attn = (num / den[..., None]).astype(jnp.bfloat16)
    attn = jnp.transpose(attn, (1, 0, 2)).reshape(img_rows, width_local)
    term = jnp.dot(attn, w_out, preferred_element_type=jnp.float32)
    branch = lax.psum_scatter(
        term.astype(jnp.bfloat16), "tp", scatter_dimension=1, tiled=True
    ).astype(jnp.float32)
    cols = branch.shape[1]
    offset = lax.axis_index("tp") * cols
    residual = lax.dynamic_slice_in_dim(tokens, offset, cols, 1)
    gate = lax.dynamic_slice_in_dim(mods[2], offset, cols, 0)
    out = residual + gate[None, :] * branch
    return out.astype(jnp.bfloat16)[None]


def body(*arrays):
    image, w_qkv, region_mask = arrays[0], arrays[3], arrays[7]
    seq = lax.axis_size("seq")
    one_head_each = (
        w_qkv.shape[2] // HEAD_DIM == seq == 8
        and lax.axis_size("section") == 2
        and lax.axis_size("tp") == 2
        and w_qkv.shape[0] % 128 == 0
        and image.shape[1] == TILE == 2 * GRID_W
        and region_mask.shape == (1, seq)
        and arrays[1].shape[1] % 16 == 0
        and arrays[4].shape[1] % 1024 == 0
    )
    return (head_body if one_head_each else token_body)(*arrays)


def solution(mesh):
    return jax.shard_map(
        body,
        mesh=mesh,
        in_specs=(
            P("section", "seq", None),
            P("section", "seq", None, "tp"),
            P("section", None, None),
            P("seq", None, "tp"),
            P("tp", None),
            P(),
            P(),
            P("seq", None),
        ),
        out_specs=P("section", "seq", "tp"),
        check_vma=False,
    )
```

```python
import jax
import jax.numpy as jnp
from jax import lax
from jax.experimental import pallas as pl
from jax.experimental.pallas import tpu as pltpu
from jax.sharding import PartitionSpec as P

HEAD_DIM = 128
GRID_W = 64
TILE = 128
VMEM_LIMIT = 24 * 1024 * 1024
VMEM_WHOLE = 56 * 1024 * 1024


def axis_freqs(width):
    return 10000.0 ** (-jnp.arange(0, width, 2).astype(jnp.float32) / width)


def rope_tables(rows_index, time_index):
    first = HEAD_DIM // 8
    rest = (HEAD_DIM - first) // 2
    row_pos = (rows_index // GRID_W).astype(jnp.float32)
    col_pos = (rows_index % GRID_W).astype(jnp.float32)
    time_pos = jnp.zeros_like(row_pos) + time_index
    angles = jnp.concatenate(
        [
            time_pos[:, None] * axis_freqs(first)[None],
            row_pos[:, None] * axis_freqs(rest)[None],
            col_pos[:, None] * axis_freqs(rest)[None],
        ],
        axis=-1,
    )
    return (jnp.cos(angles), jnp.sin(angles))


def layer_norm(tokens, mods):
    mean = jnp.mean(tokens, axis=-1, keepdims=True)
    var = jnp.mean((tokens - mean) ** 2, axis=-1, keepdims=True)
    return ((tokens - mean) * lax.rsqrt(var + 1e-06) * (1.0 + mods[1:2]) + mods[0:1]).astype(
        jnp.bfloat16
    )


VMEM = pl.BlockSpec(memory_space=pltpu.VMEM)
SMEM = pl.BlockSpec(memory_space=pltpu.SMEM)
HBM = pl.BlockSpec(memory_space=pltpu.HBM)


def call(kernel, name, out_shape, flops, moved, exps, limit=VMEM_LIMIT, **spec):
    return pl.pallas_call(
        kernel,
        out_shape=out_shape,
        compiler_params=pltpu.CompilerParams(vmem_limit_bytes=limit),
        cost_estimate=pl.CostEstimate(flops=flops, bytes_accessed=moved, transcendentals=exps),
        name=name,
        **spec,
    )


def started(pairs, sems, first=0):
    copies = [pltpu.make_async_copy(s, d, sems.at[first + i]) for i, (s, d) in enumerate(pairs)]
    for copy in copies:
        copy.start()
    return copies


def finished(copies):
    for copy in copies:
        copy.wait()


def norm_kernel(tp_ref, image_hbm, mods_hbm, full_ref, part_ref, image_ref, mods_ref, sems):
    rows = image_ref.shape[0] // 4
    pairs = [
        (image_hbm.at[pl.ds(i * rows, rows), :], image_ref.at[pl.ds(i * rows, rows), :])
        for i in range(4)
    ]
    finished(started(pairs + [(mods_hbm, mods_ref)], sems))
    mods = jnp.concatenate([mods_ref[0], mods_ref[1]], axis=0)
    normed = layer_norm(image_ref[...].astype(jnp.float32), mods)
    part = part_ref.shape[0]
    for t in range(2):

        @pl.when(tp_ref[0] == t)
        def _(t=t):
            ours, theirs = normed[t * part : (t + 1) * part], normed[(1 - t) * part : (2 - t) * part]
            full_ref[:part, :] = ours
            full_ref[part:, :] = theirs
            part_ref[...] = ours


def norm_tokens(tp, image, mods):
    rows, depth = image.shape
    return call(
        norm_kernel, "norm_tokens",
        [
            jax.ShapeDtypeStruct((rows, depth), jnp.bfloat16),
            jax.ShapeDtypeStruct((rows // 2, depth), jnp.bfloat16),
        ],
        10 * rows * depth, 4 * rows * depth, 0, VMEM_WHOLE,
        in_specs=[SMEM, HBM, HBM],
        out_specs=[VMEM, VMEM],
        scratch_shapes=[
            pltpu.VMEM(image.shape, image.dtype),
            pltpu.VMEM(mods.shape, mods.dtype),
            pltpu.SemaphoreType.DMA((5,)),
        ],
    )(tp, image, mods)


def kv_weights_kernel(section_ref, w_hbm, out_ref, w_ref, sems):
    half = w_ref.shape[1]
    rows = pl.ds(pl.multiple_of(section_ref[0] * half, half), half)
    copies = started([(w_hbm.at[1 + k, rows, :], w_ref.at[k]) for k in range(2)], sems)
    for k in range(2):
        copies[k].wait()
        for s in range(out_ref.shape[0]):
            out_ref[s, k * half : (k + 1) * half, :] = w_ref[k, :, s * HEAD_DIM : (s + 1) * HEAD_DIM]


def kv_weights(section, w):
    _, depth, width = w.shape
    return call(
        kv_weights_kernel, "kv_weights",
        jax.ShapeDtypeStruct((width // HEAD_DIM, depth, HEAD_DIM), w.dtype),
        0, 4 * depth * width, 0, VMEM_WHOLE,
        in_specs=[SMEM, HBM],
        out_specs=VMEM,
        scratch_shapes=[pltpu.VMEM((2, depth // 2, width), w.dtype), pltpu.SemaphoreType.DMA((2,))],
    )(section, w)


def direct_kernel(w_hbm, text_hbm, mask_ref, out_ref, w_ref, text_ref, sems):
    depth, count = w_ref.shape[0], text_ref.shape[1]
    copies = started([(w_hbm.at[0], w_ref), (text_hbm, text_ref)], sems)
    finished(copies)
    for s in range(out_ref.shape[0]):
        out_ref[s, :depth, :] = w_ref[:, s * HEAD_DIM : (s + 1) * HEAD_DIM]
        out_ref[s, depth : depth + count, :] = text_ref[s]
        out_ref[s, depth + count :, :] = mask_ref[...]


def direct_rows(w, text, mask):
    heads, count, _ = text.shape
    shape = (heads, w.shape[1] + count + mask.shape[0], HEAD_DIM)
    return call(
        direct_kernel, "direct_rows", jax.ShapeDtypeStruct(shape, w.dtype),
        0, 4 * heads * shape[1] * HEAD_DIM, 0, VMEM_WHOLE,
        in_specs=[HBM, HBM, VMEM],
        out_specs=VMEM,
        scratch_shapes=[
            pltpu.VMEM(w.shape[1:], w.dtype),
            pltpu.VMEM(text.shape, text.dtype),
            pltpu.SemaphoreType.DMA((2,)),
        ],
    )(w, text, mask)


def normed_rotated(x, gain, cosine, sine):
    x = x * lax.rsqrt(jnp.mean(x * x, axis=-1, keepdims=True) + 1e-06) * gain
    even = lax.broadcasted_iota(jnp.int32, x.shape, 1) % 2 == 0
    other = jnp.where(even, pltpu.roll(x, HEAD_DIM - 1, 1), pltpu.roll(x, 1, 1))
    return (x * cosine + other * sine).astype(jnp.bfloat16)


def table_of(tabs_ref, which, start, rows):
    groups = tabs_ref.shape[1] - GRID_W
    columns = tabs_ref[which, groups:, :]
    lane = lax.broadcasted_iota(jnp.int32, columns.shape, 1)
    first = HEAD_DIM // 8
    by_row = lane < first + (HEAD_DIM - first) // 2
    return jnp.concatenate(
        [
            jnp.where(by_row, tabs_ref[which, g : g + 1, :], columns)
            for g in range(start // GRID_W, (start + rows) // GRID_W)
        ],
        axis=0,
    )


def piece_copies(piece_refs, x_ref):
    at, pairs = 0, []
    for ref in piece_refs:
        pairs.append((ref, x_ref.at[pl.ds(at, ref.shape[0]), :]))
        at += ref.shape[0]
    return pairs


def blocks(rows):
    return [(b, slice(b * BLOCK, (b + 1) * BLOCK)) for b in range(rows // BLOCK)]


def arrived(copies, piece_refs, rows):
    at = 0
    for copy, ref in zip(copies, piece_refs):
        if rows.start <= at < rows.stop:
            copy.wait()
        at += ref.shape[0]


def kv_kernel(chunk, section_ref, tabs_hbm, gain_hbm, mine_hbm, peer_a, peer_b, *refs):
    piece_refs = refs[:-8]
    kv_ref, x_ref, mine, peer, w_ref, tabs_ref, gain_ref, sems = refs[-8:]
    sources, held, _ = mine.shape
    half = held // 2
    some = sources // 2
    weights = started(
        [
            (mine_hbm, mine),
            (peer_a, peer.at[pl.ds(0, some)]),
            (peer_b, peer.at[pl.ds(some, some)]),
            (tabs_hbm, tabs_ref),
            (gain_hbm, gain_ref),
        ],
        sems,
    )
    tokens = started(piece_copies(piece_refs, x_ref), sems, 5)
    finished(weights)
    first = section_ref[0] == 0
    for s in range(sources):
        for kind in range(2):
            at = slice(kind * half, (kind + 1) * half)
            lanes = slice(kind * HEAD_DIM, (kind + 1) * HEAD_DIM)
            a, b = mine[s, at, :], peer[s, at, :]
            w_ref[2 * s * half : (2 * s + 1) * half, lanes] = jnp.where(first, a, b)
            w_ref[(2 * s + 1) * half : (2 * s + 2) * half, lanes] = jnp.where(first, b, a)
    for b, at in blocks(x_ref.shape[0]):
        arrived(tokens, piece_refs, at)
        both = jnp.dot(x_ref[at, :], w_ref[...], preferred_element_type=jnp.float32)
        start = chunk * x_ref.shape[0] + b * BLOCK
        kv_ref[0, at, :] = normed_rotated(
            both[:, :HEAD_DIM],
            gain_ref[1:2, :],
            table_of(tabs_ref, 0, start, BLOCK),
            table_of(tabs_ref, 1, start, BLOCK),
        )
        kv_ref[1, at, :] = both[:, HEAD_DIM:].astype(jnp.bfloat16)


def project_kv(chunk, section, tabs, gains, mine, peers, pieces):
    depth = pieces[0].shape[1]
    rows = sum(p.shape[0] for p in pieces)
    return call(
        lambda *refs: kv_kernel(chunk, *refs), "project_kv" + "ab"[chunk],
        jax.ShapeDtypeStruct((2, rows, HEAD_DIM), jnp.bfloat16),
        4 * rows * depth * HEAD_DIM, 2 * (rows * depth + 2 * mine.size), 0, VMEM_WHOLE,
        in_specs=[SMEM] + [HBM] * (5 + len(pieces)),
        out_specs=VMEM,
        scratch_shapes=[
            pltpu.VMEM((rows, depth), jnp.bfloat16),
            pltpu.VMEM(mine.shape, jnp.bfloat16),
            pltpu.VMEM(mine.shape, jnp.bfloat16),
            pltpu.VMEM((depth, 2 * HEAD_DIM), jnp.bfloat16),
            pltpu.VMEM(tabs.shape, tabs.dtype),
            pltpu.VMEM(gains.shape, gains.dtype),
            pltpu.SemaphoreType.DMA((5 + len(pieces),)),
        ],
    )(section, tabs, gains, mine, *peers, *pieces)


def weights_of(query, keys):
    scores = lax.dot_general(
        query, keys, (((1,), (1,)), ((), ())), preferred_element_type=jnp.float32
    )
    return jnp.exp(scores * (1.0 / HEAD_DIM**0.5))


def summed(weights, values):
    den = jnp.sum(weights, axis=-1, keepdims=True)
    num = jnp.dot(weights.astype(jnp.bfloat16), values, preferred_element_type=jnp.float32)
    return num, den


def kept_weights(query, cond_ref, keep):
    weights = weights_of(query, cond_ref[0])
    rows, keys = weights.shape
    groups = keep.shape[0]
    return (weights.reshape(groups, rows // groups, keys) * keep[:, None, :]).reshape(rows, keys)


BLOCK = 256


def own_kernel(
    section_ref, rows_ref, keys_ref, kva, kvb, cond, tabs_hbm, gain_hbm, direct_hbm, *refs
):
    piece_refs = refs[:-9]
    q_ref, num_ref, den_ref, keep_ref, x_ref, direct, tabs_ref, gain_ref, sems = refs[-9:]
    rows, depth = x_ref.shape
    sources, held, _ = direct.shape
    copies = started([(direct_hbm.at[s], direct.at[s]) for s in range(sources)], sems)
    copies += started([(tabs_hbm, tabs_ref), (gain_hbm, gain_ref)], sems, sources)
    tokens = started(piece_copies(piece_refs, x_ref), sems, sources + 2)
    finished(copies)
    wide = depth // sources
    w = direct[:, :wide, :].reshape(depth, HEAD_DIM)
    count = (held - 16 - wide) // 2
    text = (
        direct[:, wide : wide + count, :].reshape(-1, HEAD_DIM),
        direct[:, wide + count : wide + 2 * count, :].reshape(-1, HEAD_DIM),
    )
    for b, at in blocks(rows):
        arrived(tokens, piece_refs, at)
        query = jnp.dot(x_ref[at, :], w, preferred_element_type=jnp.float32)
        query = normed_rotated(
            query,
            gain_ref[0:1, :],
            table_of(tabs_ref, 0, b * BLOCK, BLOCK),
            table_of(tabs_ref, 1, b * BLOCK, BLOCK),
        )
        q_ref[at, :] = query
        num, den = 0.0, 0.0
        for keys, values in ((kva[0], kva[1]), (kvb[0], kvb[1]), text):
            more = summed(weights_of(query, keys), values)
            num, den = num + more[0], den + more[1]
        num_ref[at, :] = num
        den_ref[at, :] = jnp.broadcast_to(den, num.shape)
    mask = jnp.concatenate(
        [direct[s, held - 16 : held, :].astype(jnp.float32)[:1] for s in range(sources)], axis=0
    )
    mask = jnp.dot(rows_ref[...], mask, preferred_element_type=jnp.float32)
    mask = jnp.dot(mask, keys_ref[...], preferred_element_type=jnp.float32)
    size = rows // keep_ref.shape[0]
    for g in range(keep_ref.shape[0]):
        keep_ref[:, g * size : (g + 1) * size] = jnp.broadcast_to(
            mask[:, g : g + 1], (keep_ref.shape[0], size)
        )

    @pl.when(section_ref[0] != 0)
    def _():
        for b, at in blocks(rows):
            num, den = cond_sum(keep_ref, q_ref, cond, 0, b)
            num_ref[at, :] += num
            den_ref[at, :] += jnp.broadcast_to(den, num.shape)


def cond_sum(keep_ref, q_ref, cond, chunk, b):
    groups = keep_ref.shape[0] * BLOCK // q_ref.shape[0]
    keys = cond.shape[1]
    keep = keep_ref[b * groups : (b + 1) * groups, chunk * keys : (chunk + 1) * keys]
    return summed(kept_weights(q_ref[b * BLOCK : (b + 1) * BLOCK, :], cond, keep), cond[1])


def second_cond_kernel(
    section_ref, place_ref, keep_hbm, q_hbm, num_hbm, den_hbm, cond, out_ref,
    keep_ref, q_ref, num_ref, den_ref, sems,
):
    groups = keep_ref.shape[0] * BLOCK // num_ref.shape[0]
    size = BLOCK // groups
    finished(
        started(
            [(num_hbm, num_ref), (den_hbm, den_ref), (q_hbm, q_ref), (keep_hbm, keep_ref)], sems
        )
    )

    def store(b, num, den):
        value = (num / den).astype(jnp.bfloat16)
        for g in range(groups):
            shard, part = place_ref[0, b * groups + g], place_ref[1, b * groups + g]
            at = pl.ds(pl.multiple_of(part * size, size), size)
            out_ref[shard, at, :] = value[g * size : (g + 1) * size]

    @pl.when(section_ref[0] == 0)
    def _():
        for b, at in blocks(num_ref.shape[0]):
            store(b, num_ref[at, :], den_ref[at, :])

    @pl.when(section_ref[0] != 0)
    def _():
        for b, at in blocks(num_ref.shape[0]):
            num, den = cond_sum(keep_ref, q_ref, cond, 1, b)
            store(b, num_ref[at, :] + num, den_ref[at, :] + den)


def attend_own(section, tabs, gains, row_tiles, key_tiles, kvs, cond, direct, pieces):
    depth = pieces[0].shape[1]
    rows = sum(p.shape[0] for p in pieces)
    keys = 2 * rows
    return call(
        own_kernel, "attend_own",
        [
            jax.ShapeDtypeStruct((rows, HEAD_DIM), jnp.bfloat16),
            jax.ShapeDtypeStruct((rows, HEAD_DIM), jnp.float32),
            jax.ShapeDtypeStruct((rows, HEAD_DIM), jnp.float32),
            jax.ShapeDtypeStruct((row_tiles.shape[0], rows), jnp.float32),
        ],
        2 * rows * HEAD_DIM * (2 * keys + depth), 2 * rows * depth, rows * keys, VMEM_WHOLE,
        in_specs=[SMEM] + [VMEM] * 5 + [HBM] * (3 + len(pieces)),
        out_specs=[VMEM] * 4,
        scratch_shapes=[
            pltpu.VMEM((rows, depth), jnp.bfloat16),
            pltpu.VMEM(direct.shape, jnp.bfloat16),
            pltpu.VMEM(tabs.shape, tabs.dtype),
            pltpu.VMEM(gains.shape, gains.dtype),
            pltpu.SemaphoreType.DMA((direct.shape[0] + 2 + len(pieces),)),
        ],
    )(section, row_tiles, key_tiles, *kvs, cond, tabs, gains, direct, *pieces)


def attend_second(section, place, keep, query, cond, num, den, seq):
    rows, keys = num.shape[0], cond.shape[1]
    return call(
        second_cond_kernel, "attend_second",
        jax.ShapeDtypeStruct((seq, rows // seq, HEAD_DIM), jnp.bfloat16),
        4 * rows * keys * HEAD_DIM, 2 * rows * HEAD_DIM * 8, rows * keys, VMEM_WHOLE,
        in_specs=[SMEM, SMEM] + [HBM] * 4 + [VMEM],
        out_specs=VMEM,
        scratch_shapes=[pltpu.VMEM(x.shape, x.dtype) for x in (keep, query, num, den)]
        + [pltpu.SemaphoreType.DMA((4,))],
    )(section, place, keep, query, num, den, cond)


def token_rows(attn_ref):
    return jnp.concatenate([attn_ref[h] for h in range(attn_ref.shape[0])], axis=1)


def sent_kernel(attn_ref, w_ref, out_ref):
    branch = jnp.dot(token_rows(attn_ref), w_ref[...], preferred_element_type=jnp.float32)
    out_ref[...] = branch.astype(jnp.bfloat16)


def kept_kernel(attn_ref, w_ref, image_ref, gate_ref, out_ref):
    branch = jnp.dot(token_rows(attn_ref), w_ref[...], preferred_element_type=jnp.float32)
    out_ref[...] = image_ref[...].astype(jnp.float32) + gate_ref[...] * branch


def project_out(attn, w, image=None, gate=None):
    rows = attn.shape[1]
    depth, width = w.shape
    kept = image is not None
    args = (attn, w) + ((image, gate) if kept else ())
    return call(
        kept_kernel if kept else sent_kernel, "out_kept" if kept else "out_sent",
        jax.ShapeDtypeStruct((rows, width), jnp.float32 if kept else jnp.bfloat16),
        2 * rows * depth * width, 2 * depth * width, 0,
        in_specs=[VMEM] * len(args),
        out_specs=VMEM,
    )(*args)


def lane_tables(row_ids, time_index):
    first = HEAD_DIM // 8
    rest = (HEAD_DIM - first) // 2
    freqs = jnp.concatenate([axis_freqs(first), axis_freqs(rest), axis_freqs(rest)])
    freqs = jnp.repeat(freqs, 2)[None]
    lane = jnp.arange(HEAD_DIM, dtype=jnp.int32)[None]
    rows = jnp.where(lane < first, time_index, row_ids.astype(jnp.float32)[:, None])
    columns = jnp.broadcast_to(jnp.arange(GRID_W, dtype=jnp.float32)[:, None], (GRID_W, HEAD_DIM))
    angles = jnp.concatenate([rows, columns], axis=0) * freqs
    return jnp.stack([jnp.cos(angles), jnp.sin(angles) * jnp.where(lane % 2 == 0, -1.0, 1.0)])


def z_pairs(seq, pairs):
    return [(2 * a + core, 2 * b + core) for a, b in pairs for core in range(2)]


def head_body(image, text_kv, modulation, w_qkv, w_out, q_gain, k_gain, region_mask):
    seq = lax.axis_size("seq")
    img_rows = image.shape[1]
    depth = w_qkv.shape[0]
    section = lax.axis_index("section")
    tp = lax.axis_index("tp")
    chip, core = lax.axis_index("seq") // 2, lax.axis_index("seq") % 2
    mods = modulation[0]
    section_at = section.astype(jnp.int32).reshape(1)
    tp_at = tp.astype(jnp.int32).reshape(1)
    both = [(0, 1), (1, 0)]

    rows3 = w_qkv.transpose(1, 0, 2)
    mine = lax.all_to_all(kv_weights(section_at, rows3), "seq", 0, 0)

    full, part = norm_tokens(tp_at, image[0], modulation.transpose(1, 0, 2))

    def along_z(x, pairs):
        return lax.ppermute(x, "seq", z_pairs(seq, pairs))

    def to_core(x):
        return lax.ppermute(x, "seq", [(s, s ^ 1) for s in range(seq)])

    def to_tp(x):
        return lax.ppermute(x, "tp", both)

    near = along_z(part, [(0, 1), (1, 0), (2, 3), (3, 2)])
    near, w_late, at_chip = lax.optimization_barrier((near, w_out, chip.astype(jnp.int32)))
    middle = along_z(part, [(1, 2), (2, 1)])
    far = along_z(near, [(1, 2), (2, 1)])
    middle_end = along_z(middle, [(1, 0), (2, 3)])
    far_end = along_z(far, [(1, 0), (2, 3)])
    inner = (chip == 1) | (chip == 2)
    third = jnp.where(inner, middle, middle_end)
    fourth = jnp.where(inner, far, far_end)

    text = text_kv[0].reshape(-1, 2, seq, HEAD_DIM).transpose(2, 1, 0, 3).reshape(seq, -1, HEAD_DIM)
    mask = jnp.pad(
        region_mask.astype(jnp.bfloat16), ((0, 15), (0, HEAD_DIM - region_mask.shape[1]))
    )
    direct = direct_rows(rows3, text, mask)

    near_tp = to_tp(near)
    direct, mine = lax.optimization_barrier((direct, mine))
    direct = lax.all_to_all(direct, "seq", 0, 0)
    some = seq // 2
    peers = [lax.ppermute(mine[:some], "section", both), lax.ppermute(mine[some:], "section", both)]
    cols = w_out.shape[1] // 2
    w_sent = lax.dynamic_slice_in_dim(w_late, (1 - tp) * cols, cols, 1)
    w_kept = lax.dynamic_slice_in_dim(w_late, tp * cols, cols, 1)

    upper = at_chip >= 2
    chips = jnp.stack([at_chip, at_chip ^ 1, jnp.where(upper, 1, 2), jnp.where(upper, 0, 3)])
    cores = jnp.stack([core, 1 - core])
    parts = jnp.stack([tp, 1 - tp])
    shards = chips[:, None, None] * 2 + cores[None, :, None] + 0 * parts[None, None, :]
    parts = parts[None, None, :] + 0 * shards
    shards, parts = shards.reshape(-1).astype(jnp.int32), parts.reshape(-1).astype(jnp.int32)
    size = img_rows // 2
    row_ids = shards * (img_rows // GRID_W) + parts * (size // GRID_W)
    tabs = lane_tables(row_ids, (section == 0).astype(jnp.float32))
    gains = jnp.stack([q_gain, k_gain])
    row_tiles = (shards[:, None] == jnp.arange(seq)[None]).astype(jnp.float32)
    key_tiles = jnp.arange(HEAD_DIM)[:, None] == shards[None]
    key_tiles = key_tiles.astype(jnp.float32)
    place = jnp.stack([shards, parts])

    early = (tabs, gains, row_tiles, key_tiles, place, w_sent, w_kept)
    third, near_tp, peers[0], early = lax.optimization_barrier((third, near_tp, peers[0], early))
    tabs, gains, row_tiles, key_tiles, place, w_sent, w_kept = early
    third_tp = to_tp(third)
    fourth, third_tp, peers[1] = lax.optimization_barrier((fourth, third_tp, peers[1]))
    fourth_tp = to_tp(fourth)
    a = [full, to_core(full), near, near_tp, to_core(near), to_core(near_tp)]
    kv_a = project_kv(0, section_at, tabs, gains, mine, peers, a)
    cond_a = lax.ppermute(kv_a, "section", [(0, 1)])
    b = [third, third_tp, to_core(third), to_core(third_tp), fourth, fourth_tp, to_core(fourth)]
    fourth_tp, kv_a = lax.optimization_barrier((fourth_tp, kv_a))
    b[5] = fourth_tp
    b.append(to_core(fourth_tp))
    kv_b = project_kv(1, section_at, tabs, gains, mine, peers, b)
    cond_b = lax.ppermute(kv_b, "section", [(0, 1)])
    query, num, den, keep = attend_own(
        section_at, tabs, gains, row_tiles, key_tiles, (kv_a, kv_b), cond_a, direct, a + b
    )
    attn = attend_second(section_at, place, keep, query, cond_b, num, den, seq)

    attn = lax.all_to_all(attn, "seq", 0, 0)
    gate = lax.dynamic_slice_in_dim(mods[2:3], tp * cols, cols, 1)
    residual = lax.dynamic_slice_in_dim(image[0], tp * cols, cols, 1)
    other = to_tp(project_out(attn, w_sent))
    kept = project_out(attn, w_kept, residual, gate)
    return (kept + gate * other.astype(jnp.float32)).astype(jnp.bfloat16)[None]


def rms_rows(x, gain):
    return x * lax.rsqrt(jnp.mean(x * x, axis=-1, keepdims=True) + 1e-06) * gain


def apply_rope(x, cosine, sine):
    rows, heads_here = (x.shape[0], x.shape[1])
    pairs = x.reshape(rows, heads_here, HEAD_DIM // 2, 2)
    first = pairs[..., 0]
    second = pairs[..., 1]
    cosine = cosine[:, None, :]
    sine = sine[:, None, :]
    rotated = jnp.stack([first * cosine - second * sine, first * sine + second * cosine], axis=-1)
    return rotated.reshape(rows, heads_here, HEAD_DIM)


def attend_piece(carry, keys_vals, query, keep):
    num, den = carry
    rows = keys_vals.shape[0]
    heads_local = query.shape[1]
    piece_k = keys_vals[:, 0].reshape(rows, heads_local, HEAD_DIM)
    piece_v = keys_vals[:, 1].reshape(rows, heads_local, HEAD_DIM)
    scores = jnp.einsum("qhd,khd->hqk", query, piece_k, preferred_element_type=jnp.float32) * (
        1.0 / HEAD_DIM**0.5
    )
    weights = jnp.exp(scores)
    if keep is not None:
        weights = jnp.where(keep[None], weights, 0.0)
    den = den + jnp.sum(weights, axis=-1)
    num = num + jnp.einsum(
        "hqk,khd->hqd", weights.astype(jnp.bfloat16), piece_v, preferred_element_type=jnp.float32
    )
    return (num, den)


def token_body(image, text_kv, modulation, w_qkv, w_out, q_gain, k_gain, region_mask):
    img_rows = image.shape[1]
    width_local = w_qkv.shape[2]
    heads_local = width_local // HEAD_DIM
    tokens = image[0].astype(jnp.float32)
    mods = modulation[0]
    normed = layer_norm(tokens, mods)
    qkv = jnp.einsum(
        "td,dcf->tcf",
        normed,
        lax.all_gather(w_qkv, "seq", axis=0, tiled=True),
        preferred_element_type=jnp.float32,
    )
    section_index = lax.axis_index("section")
    time_index = (section_index == 0).astype(jnp.float32)
    rows_index = lax.axis_index("seq") * img_rows + jnp.arange(img_rows, dtype=jnp.int32)
    cosine, sine = rope_tables(rows_index, time_index)
    query = apply_rope(
        rms_rows(qkv[:, 0].reshape(img_rows, heads_local, HEAD_DIM), q_gain), cosine, sine
    ).astype(jnp.bfloat16)
    keys = apply_rope(
        rms_rows(qkv[:, 1].reshape(img_rows, heads_local, HEAD_DIM), k_gain), cosine, sine
    ).astype(jnp.bfloat16)
    values = qkv[:, 2].astype(jnp.bfloat16)
    image_kv = jnp.stack([keys.reshape(img_rows, width_local), values], axis=1)
    own_kv = jnp.concatenate([image_kv, text_kv[0]], axis=0)
    enabled = (section_index == 1).astype(jnp.int32)
    local_mask = region_mask * enabled
    init = (
        jnp.zeros((heads_local, img_rows, HEAD_DIM), jnp.float32),
        jnp.zeros((heads_local, img_rows), jnp.float32),
    )
    carry = attend_piece(init, lax.all_gather(own_kv, "seq", axis=0, tiled=True), query, None)
    cond_local = lax.ppermute(image_kv, "section", [(0, 1)])
    keep = jnp.repeat(jnp.repeat(local_mask, TILE, axis=0), TILE, axis=1) > 0
    carry = attend_piece(carry, lax.all_gather(cond_local, "seq", axis=0, tiled=True), query, keep)
    num, den = carry
    attn = (num / den[..., None]).astype(jnp.bfloat16)
    attn = jnp.transpose(attn, (1, 0, 2)).reshape(img_rows, width_local)
    term = jnp.dot(attn, w_out, preferred_element_type=jnp.float32)
    branch = lax.psum_scatter(
        term.astype(jnp.bfloat16), "tp", scatter_dimension=1, tiled=True
    ).astype(jnp.float32)
    cols = branch.shape[1]
    offset = lax.axis_index("tp") * cols
    residual = lax.dynamic_slice_in_dim(tokens, offset, cols, 1)
    gate = lax.dynamic_slice_in_dim(mods[2], offset, cols, 0)
    out = residual + gate[None, :] * branch
    return out.astype(jnp.bfloat16)[None]


def body(*arrays):
    image, w_qkv, region_mask = arrays[0], arrays[3], arrays[7]
    seq = lax.axis_size("seq")
    one_head_each = (
        w_qkv.shape[2] // HEAD_DIM == seq == 8
        and lax.axis_size("section") == 2
        and lax.axis_size("tp") == 2
        and w_qkv.shape[0] % 128 == 0
        and image.shape[1] == TILE == 2 * GRID_W
        and region_mask.shape == (1, seq)
        and arrays[1].shape[1] % 16 == 0
        and arrays[4].shape[1] % 1024 == 0
    )
    return (head_body if one_head_each else token_body)(*arrays)


def solution(mesh):
    return jax.shard_map(
        body,
        mesh=mesh,
        in_specs=(
            P("section", "seq", None),
            P("section", "seq", None, "tp"),
            P("section", None, None),
            P("seq", None, "tp"),
            P("tp", None),
            P(),
            P(),
            P("seq", None),
        ),
        out_specs=P("section", "seq", "tp"),
        check_vma=False,
    )
```

```python
import jax
import jax.numpy as jnp
from jax import lax
from jax.experimental import pallas as pl
from jax.experimental.pallas import tpu as pltpu
from jax.sharding import PartitionSpec as P

HEAD_DIM = 128
GRID_W = 64
TILE = 128
VMEM_LIMIT = 24 * 1024 * 1024
VMEM_WHOLE = 56 * 1024 * 1024


def axis_freqs(width):
    return 10000.0 ** (-jnp.arange(0, width, 2).astype(jnp.float32) / width)


def rope_tables(rows_index, time_index):
    first = HEAD_DIM // 8
    rest = (HEAD_DIM - first) // 2
    row_pos = (rows_index // GRID_W).astype(jnp.float32)
    col_pos = (rows_index % GRID_W).astype(jnp.float32)
    time_pos = jnp.zeros_like(row_pos) + time_index
    angles = jnp.concatenate(
        [
            time_pos[:, None] * axis_freqs(first)[None],
            row_pos[:, None] * axis_freqs(rest)[None],
            col_pos[:, None] * axis_freqs(rest)[None],
        ],
        axis=-1,
    )
    return (jnp.cos(angles), jnp.sin(angles))


def layer_norm(tokens, mods):
    mean = jnp.mean(tokens, axis=-1, keepdims=True)
    var = jnp.mean((tokens - mean) ** 2, axis=-1, keepdims=True)
    return ((tokens - mean) * lax.rsqrt(var + 1e-06) * (1.0 + mods[1:2]) + mods[0:1]).astype(
        jnp.bfloat16
    )


VMEM = pl.BlockSpec(memory_space=pltpu.VMEM)
SMEM = pl.BlockSpec(memory_space=pltpu.SMEM)
HBM = pl.BlockSpec(memory_space=pltpu.HBM)


def call(kernel, name, out_shape, flops, moved, exps, limit=VMEM_LIMIT, **spec):
    return pl.pallas_call(
        kernel,
        out_shape=out_shape,
        compiler_params=pltpu.CompilerParams(vmem_limit_bytes=limit),
        cost_estimate=pl.CostEstimate(flops=flops, bytes_accessed=moved, transcendentals=exps),
        name=name,
        **spec,
    )


def started(pairs, sems, first=0):
    copies = [pltpu.make_async_copy(s, d, sems.at[first + i]) for i, (s, d) in enumerate(pairs)]
    for copy in copies:
        copy.start()
    return copies


def finished(copies):
    for copy in copies:
        copy.wait()


def norm_kernel(tp_ref, image_hbm, mods_hbm, full_ref, part_ref, image_ref, mods_ref, sems):
    rows = image_ref.shape[0] // 4
    pairs = [
        (image_hbm.at[pl.ds(i * rows, rows), :], image_ref.at[pl.ds(i * rows, rows), :])
        for i in range(4)
    ]
    finished(started(pairs + [(mods_hbm, mods_ref)], sems))
    mods = jnp.concatenate([mods_ref[0], mods_ref[1]], axis=0)
    normed = layer_norm(image_ref[...].astype(jnp.float32), mods)
    part = part_ref.shape[0]
    for t in range(2):

        @pl.when(tp_ref[0] == t)
        def _(t=t):
            ours, theirs = normed[t * part : (t + 1) * part], normed[(1 - t) * part : (2 - t) * part]
            full_ref[:part, :] = ours
            full_ref[part:, :] = theirs
            part_ref[...] = ours


def norm_tokens(tp, image, mods):
    rows, depth = image.shape
    return call(
        norm_kernel, "norm_tokens",
        [
            jax.ShapeDtypeStruct((rows, depth), jnp.bfloat16),
            jax.ShapeDtypeStruct((rows // 2, depth), jnp.bfloat16),
        ],
        10 * rows * depth, 4 * rows * depth, 0, VMEM_WHOLE,
        in_specs=[SMEM, HBM, HBM],
        out_specs=[VMEM, VMEM],
        scratch_shapes=[
            pltpu.VMEM(image.shape, image.dtype),
            pltpu.VMEM(mods.shape, mods.dtype),
            pltpu.SemaphoreType.DMA((5,)),
        ],
    )(tp, image, mods)


def kv_weights_kernel(section_ref, w_hbm, out_ref, w_ref, sems):
    half = w_ref.shape[1]
    rows = pl.ds(pl.multiple_of(section_ref[0] * half, half), half)
    copies = started([(w_hbm.at[1 + k, rows, :], w_ref.at[k]) for k in range(2)], sems)
    for k in range(2):
        copies[k].wait()
        for s in range(out_ref.shape[0]):
            out_ref[s, k * half : (k + 1) * half, :] = w_ref[k, :, s * HEAD_DIM : (s + 1) * HEAD_DIM]


def kv_weights(section, w):
    _, depth, width = w.shape
    return call(
        kv_weights_kernel, "kv_weights",
        jax.ShapeDtypeStruct((width // HEAD_DIM, depth, HEAD_DIM), w.dtype),
        0, 4 * depth * width, 0, VMEM_WHOLE,
        in_specs=[SMEM, HBM],
        out_specs=VMEM,
        scratch_shapes=[pltpu.VMEM((2, depth // 2, width), w.dtype), pltpu.SemaphoreType.DMA((2,))],
    )(section, w)


def direct_kernel(w_hbm, text_hbm, mask_ref, out_ref, w_ref, text_ref, sems):
    depth, count = w_ref.shape[0], text_ref.shape[1]
    copies = started([(w_hbm.at[0], w_ref), (text_hbm, text_ref)], sems)
    finished(copies)
    for s in range(out_ref.shape[0]):
        out_ref[s, :depth, :] = w_ref[:, s * HEAD_DIM : (s + 1) * HEAD_DIM]
        out_ref[s, depth : depth + count, :] = text_ref[s]
        out_ref[s, depth + count :, :] = mask_ref[...]


def direct_rows(w, text, mask):
    heads, count, _ = text.shape
    shape = (heads, w.shape[1] + count + mask.shape[0], HEAD_DIM)
    return call(
        direct_kernel, "direct_rows", jax.ShapeDtypeStruct(shape, w.dtype),
        0, 4 * heads * shape[1] * HEAD_DIM, 0, VMEM_WHOLE,
        in_specs=[HBM, HBM, VMEM],
        out_specs=VMEM,
        scratch_shapes=[
            pltpu.VMEM(w.shape[1:], w.dtype),
            pltpu.VMEM(text.shape, text.dtype),
            pltpu.SemaphoreType.DMA((2,)),
        ],
    )(w, text, mask)


def normed_rotated(x, gain, cosine, sine):
    x = x * lax.rsqrt(jnp.mean(x * x, axis=-1, keepdims=True) + 1e-06) * gain
    even = lax.broadcasted_iota(jnp.int32, x.shape, 1) % 2 == 0
    other = jnp.where(even, pltpu.roll(x, HEAD_DIM - 1, 1), pltpu.roll(x, 1, 1))
    return (x * cosine + other * sine).astype(jnp.bfloat16)


def table_of(tabs_ref, which, start, rows):
    groups = tabs_ref.shape[1] - GRID_W
    columns = tabs_ref[which, groups:, :]
    lane = lax.broadcasted_iota(jnp.int32, columns.shape, 1)
    first = HEAD_DIM // 8
    by_row = lane < first + (HEAD_DIM - first) // 2
    return jnp.concatenate(
        [
            jnp.where(by_row, tabs_ref[which, g : g + 1, :], columns)
            for g in range(start // GRID_W, (start + rows) // GRID_W)
        ],
        axis=0,
    )


def piece_copies(piece_refs, x_ref):
    at, pairs = 0, []
    for ref in piece_refs:
        pairs.append((ref, x_ref.at[pl.ds(at, ref.shape[0]), :]))
        at += ref.shape[0]
    return pairs


def blocks(rows):
    return [(b, slice(b * BLOCK, (b + 1) * BLOCK)) for b in range(rows // BLOCK)]


def arrived(copies, piece_refs, rows):
    at = 0
    for copy, ref in zip(copies, piece_refs):
        if rows.start <= at < rows.stop:
            copy.wait()
        at += ref.shape[0]


def kv_kernel(chunk, section_ref, tabs_hbm, gain_hbm, mine_hbm, peer_a, peer_b, *refs):
    piece_refs = refs[:-8]
    kv_ref, x_ref, mine, peer, w_ref, tabs_ref, gain_ref, sems = refs[-8:]
    sources, held, _ = mine.shape
    half = held // 2
    some = sources // 2
    weights = started(
        [
            (mine_hbm, mine),
            (peer_a, peer.at[pl.ds(0, some)]),
            (peer_b, peer.at[pl.ds(some, some)]),
            (tabs_hbm, tabs_ref),
            (gain_hbm, gain_ref),
        ],
        sems,
    )
    tokens = started(piece_copies(piece_refs, x_ref), sems, 5)
    finished(weights)
    first = section_ref[0] == 0
    for s in range(sources):
        for kind in range(2):
            at = slice(kind * half, (kind + 1) * half)
            lanes = slice(kind * HEAD_DIM, (kind + 1) * HEAD_DIM)
            a, b = mine[s, at, :], peer[s, at, :]
            w_ref[2 * s * half : (2 * s + 1) * half, lanes] = jnp.where(first, a, b)
            w_ref[(2 * s + 1) * half : (2 * s + 2) * half, lanes] = jnp.where(first, b, a)
    for b, at in blocks(x_ref.shape[0]):
        arrived(tokens, piece_refs, at)
        both = jnp.dot(x_ref[at, :], w_ref[...], preferred_element_type=jnp.float32)
        start = chunk * x_ref.shape[0] + b * BLOCK
        kv_ref[0, at, :] = normed_rotated(
            both[:, :HEAD_DIM],
            gain_ref[1:2, :],
            table_of(tabs_ref, 0, start, BLOCK),
            table_of(tabs_ref, 1, start, BLOCK),
        )
        kv_ref[1, at, :] = both[:, HEAD_DIM:].astype(jnp.bfloat16)


def project_kv(chunk, section, tabs, gains, mine, peers, pieces):
    depth = pieces[0].shape[1]
    rows = sum(p.shape[0] for p in pieces)
    return call(
        lambda *refs: kv_kernel(chunk, *refs), "project_kv" + "ab"[chunk],
        jax.ShapeDtypeStruct((2, rows, HEAD_DIM), jnp.bfloat16),
        4 * rows * depth * HEAD_DIM, 2 * (rows * depth + 2 * mine.size), 0, VMEM_WHOLE,
        in_specs=[SMEM] + [HBM] * (5 + len(pieces)),
        out_specs=VMEM,
        scratch_shapes=[
            pltpu.VMEM((rows, depth), jnp.bfloat16),
            pltpu.VMEM(mine.shape, jnp.bfloat16),
            pltpu.VMEM(mine.shape, jnp.bfloat16),
            pltpu.VMEM((depth, 2 * HEAD_DIM), jnp.bfloat16),
            pltpu.VMEM(tabs.shape, tabs.dtype),
            pltpu.VMEM(gains.shape, gains.dtype),
            pltpu.SemaphoreType.DMA((5 + len(pieces),)),
        ],
    )(section, tabs, gains, mine, *peers, *pieces)


def weights_of(query, keys):
    scores = lax.dot_general(
        query, keys, (((1,), (1,)), ((), ())), preferred_element_type=jnp.float32
    )
    return jnp.exp(scores * (1.0 / HEAD_DIM**0.5))


def summed(weights, values):
    den = jnp.sum(weights, axis=-1, keepdims=True)
    num = jnp.dot(weights.astype(jnp.bfloat16), values, preferred_element_type=jnp.float32)
    return num, den


def kept_weights(query, cond_ref, keep):
    weights = weights_of(query, cond_ref[0])
    rows, keys = weights.shape
    groups = keep.shape[0]
    return (weights.reshape(groups, rows // groups, keys) * keep[:, None, :]).reshape(rows, keys)


BLOCK = 256


def own_kernel(
    section_ref, rows_ref, keys_ref, kva, kvb, cond, tabs_hbm, gain_hbm, direct_hbm, *refs
):
    piece_refs = refs[:-9]
    q_ref, num_ref, den_ref, keep_ref, x_ref, direct, tabs_ref, gain_ref, sems = refs[-9:]
    rows, depth = x_ref.shape
    sources, held, _ = direct.shape
    copies = started([(direct_hbm.at[s], direct.at[s]) for s in range(sources)], sems)
    copies += started([(tabs_hbm, tabs_ref), (gain_hbm, gain_ref)], sems, sources)
    tokens = started(piece_copies(piece_refs, x_ref), sems, sources + 2)
    finished(copies)
    wide = depth // sources
    w = direct[:, :wide, :].reshape(depth, HEAD_DIM)
    count = (held - 16 - wide) // 2
    text = (
        direct[:, wide : wide + count, :].reshape(-1, HEAD_DIM),
        direct[:, wide + count : wide + 2 * count, :].reshape(-1, HEAD_DIM),
    )
    for b, at in blocks(rows):
        arrived(tokens, piece_refs, at)
        query = jnp.dot(x_ref[at, :], w, preferred_element_type=jnp.float32)
        query = normed_rotated(
            query,
            gain_ref[0:1, :],
            table_of(tabs_ref, 0, b * BLOCK, BLOCK),
            table_of(tabs_ref, 1, b * BLOCK, BLOCK),
        )
        q_ref[at, :] = query
        num, den = 0.0, 0.0
        for keys, values in ((kva[0], kva[1]), (kvb[0], kvb[1]), text):
            more = summed(weights_of(query, keys), values)
            num, den = num + more[0], den + more[1]
        num_ref[at, :] = num
        den_ref[at, :] = jnp.broadcast_to(den, num.shape)
    mask = jnp.concatenate(
        [direct[s, held - 16 : held, :].astype(jnp.float32)[:1] for s in range(sources)], axis=0
    )
    mask = jnp.dot(rows_ref[...], mask, preferred_element_type=jnp.float32)
    mask = jnp.dot(mask, keys_ref[...], preferred_element_type=jnp.float32)
    size = rows // keep_ref.shape[0]
    for g in range(keep_ref.shape[0]):
        keep_ref[:, g * size : (g + 1) * size] = jnp.broadcast_to(
            mask[:, g : g + 1], (keep_ref.shape[0], size)
        )

    @pl.when(section_ref[0] != 0)
    def _():
        for b, at in blocks(rows):
            num, den = cond_sum(keep_ref, q_ref, cond, 0, b)
            num_ref[at, :] += num
            den_ref[at, :] += jnp.broadcast_to(den, num.shape)


def cond_sum(keep_ref, q_ref, cond, chunk, b):
    groups = keep_ref.shape[0] * BLOCK // q_ref.shape[0]
    keys = cond.shape[1]
    keep = keep_ref[b * groups : (b + 1) * groups, chunk * keys : (chunk + 1) * keys]
    return summed(kept_weights(q_ref[b * BLOCK : (b + 1) * BLOCK, :], cond, keep), cond[1])


def second_cond_kernel(
    section_ref, place_ref, keep_hbm, q_hbm, num_hbm, den_hbm, cond, out_ref,
    keep_ref, q_ref, num_ref, den_ref, sems,
):
    groups = keep_ref.shape[0] * BLOCK // num_ref.shape[0]
    size = BLOCK // groups
    finished(
        started(
            [(num_hbm, num_ref), (den_hbm, den_ref), (q_hbm, q_ref), (keep_hbm, keep_ref)], sems
        )
    )

    def store(b, num, den):
        value = (num / den).astype(jnp.bfloat16)
        for g in range(groups):
            shard, part = place_ref[0, b * groups + g], place_ref[1, b * groups + g]
            at = pl.ds(pl.multiple_of(part * size, size), size)
            out_ref[shard, at, :] = value[g * size : (g + 1) * size]

    @pl.when(section_ref[0] == 0)
    def _():
        for b, at in blocks(num_ref.shape[0]):
            store(b, num_ref[at, :], den_ref[at, :])

    @pl.when(section_ref[0] != 0)
    def _():
        for b, at in blocks(num_ref.shape[0]):
            num, den = cond_sum(keep_ref, q_ref, cond, 1, b)
            store(b, num_ref[at, :] + num, den_ref[at, :] + den)


def attend_own(section, tabs, gains, row_tiles, key_tiles, kvs, cond, direct, pieces):
    depth = pieces[0].shape[1]
    rows = sum(p.shape[0] for p in pieces)
    keys = 2 * rows
    return call(
        own_kernel, "attend_own",
        [
            jax.ShapeDtypeStruct((rows, HEAD_DIM), jnp.bfloat16),
            jax.ShapeDtypeStruct((rows, HEAD_DIM), jnp.float32),
            jax.ShapeDtypeStruct((rows, HEAD_DIM), jnp.float32),
            jax.ShapeDtypeStruct((row_tiles.shape[0], rows), jnp.float32),
        ],
        2 * rows * HEAD_DIM * (2 * keys + depth), 2 * rows * depth, rows * keys, VMEM_WHOLE,
        in_specs=[SMEM] + [VMEM] * 5 + [HBM] * (3 + len(pieces)),
        out_specs=[VMEM] * 4,
        scratch_shapes=[
            pltpu.VMEM((rows, depth), jnp.bfloat16),
            pltpu.VMEM(direct.shape, jnp.bfloat16),
            pltpu.VMEM(tabs.shape, tabs.dtype),
            pltpu.VMEM(gains.shape, gains.dtype),
            pltpu.SemaphoreType.DMA((direct.shape[0] + 2 + len(pieces),)),
        ],
    )(section, row_tiles, key_tiles, *kvs, cond, tabs, gains, direct, *pieces)


def attend_second(section, place, keep, query, cond, num, den, seq):
    rows, keys = num.shape[0], cond.shape[1]
    return call(
        second_cond_kernel, "attend_second",
        jax.ShapeDtypeStruct((seq, rows // seq, HEAD_DIM), jnp.bfloat16),
        4 * rows * keys * HEAD_DIM, 2 * rows * HEAD_DIM * 8, rows * keys, VMEM_WHOLE,
        in_specs=[SMEM, SMEM] + [HBM] * 4 + [VMEM],
        out_specs=VMEM,
        scratch_shapes=[pltpu.VMEM(x.shape, x.dtype) for x in (keep, query, num, den)]
        + [pltpu.SemaphoreType.DMA((4,))],
    )(section, place, keep, query, num, den, cond)


def token_rows(attn_ref):
    return jnp.concatenate([attn_ref[h] for h in range(attn_ref.shape[0])], axis=1)


def sent_kernel(attn_ref, w_ref, out_ref):
    branch = jnp.dot(token_rows(attn_ref), w_ref[...], preferred_element_type=jnp.float32)
    out_ref[...] = branch.astype(jnp.bfloat16)


def kept_kernel(attn_ref, w_ref, image_ref, gate_ref, out_ref):
    branch = jnp.dot(token_rows(attn_ref), w_ref[...], preferred_element_type=jnp.float32)
    out_ref[...] = image_ref[...].astype(jnp.float32) + gate_ref[...] * branch


def project_out(attn, w, image=None, gate=None):
    rows = attn.shape[1]
    depth, width = w.shape
    kept = image is not None
    args = (attn, w) + ((image, gate) if kept else ())
    return call(
        kept_kernel if kept else sent_kernel, "out_kept" if kept else "out_sent",
        jax.ShapeDtypeStruct((rows, width), jnp.float32 if kept else jnp.bfloat16),
        2 * rows * depth * width, 2 * depth * width, 0,
        in_specs=[VMEM] * len(args),
        out_specs=VMEM,
    )(*args)


def lane_tables(row_ids, time_index):
    first = HEAD_DIM // 8
    rest = (HEAD_DIM - first) // 2
    freqs = jnp.concatenate([axis_freqs(first), axis_freqs(rest), axis_freqs(rest)])
    freqs = jnp.repeat(freqs, 2)[None]
    lane = jnp.arange(HEAD_DIM, dtype=jnp.int32)[None]
    rows = jnp.where(lane < first, time_index, row_ids.astype(jnp.float32)[:, None])
    columns = jnp.broadcast_to(jnp.arange(GRID_W, dtype=jnp.float32)[:, None], (GRID_W, HEAD_DIM))
    angles = jnp.concatenate([rows, columns], axis=0) * freqs
    return jnp.stack([jnp.cos(angles), jnp.sin(angles) * jnp.where(lane % 2 == 0, -1.0, 1.0)])


def z_pairs(seq, pairs):
    return [(2 * a + core, 2 * b + core) for a, b in pairs for core in range(2)]


def head_body(image, text_kv, modulation, w_qkv, w_out, q_gain, k_gain, region_mask):
    seq = lax.axis_size("seq")
    img_rows = image.shape[1]
    depth = w_qkv.shape[0]
    section = lax.axis_index("section")
    tp = lax.axis_index("tp")
    chip, core = lax.axis_index("seq") // 2, lax.axis_index("seq") % 2
    mods = modulation[0]
    section_at = section.astype(jnp.int32).reshape(1)
    tp_at = tp.astype(jnp.int32).reshape(1)
    both = [(0, 1), (1, 0)]

    rows3 = w_qkv.transpose(1, 0, 2)
    mine = lax.all_to_all(kv_weights(section_at, rows3), "seq", 0, 0)

    full, part = norm_tokens(tp_at, image[0], modulation.transpose(1, 0, 2))

    def along_z(x, pairs):
        return lax.ppermute(x, "seq", z_pairs(seq, pairs))

    def to_core(x):
        return lax.ppermute(x, "seq", [(s, s ^ 1) for s in range(seq)])

    def to_tp(x):
        return lax.ppermute(x, "tp", both)

    near = along_z(part, [(0, 1), (1, 0), (2, 3), (3, 2)])
    near, w_late, at_chip = lax.optimization_barrier((near, w_out, chip.astype(jnp.int32)))
    middle = along_z(part, [(1, 2), (2, 1)])
    far = along_z(near, [(1, 2), (2, 1)])
    middle_end = along_z(middle, [(1, 0), (2, 3)])
    far_end = along_z(far, [(1, 0), (2, 3)])
    inner = (chip == 1) | (chip == 2)
    third = jnp.where(inner, middle, middle_end)
    fourth = jnp.where(inner, far, far_end)

    text = text_kv[0].reshape(-1, 2, seq, HEAD_DIM).transpose(2, 1, 0, 3).reshape(seq, -1, HEAD_DIM)
    mask = jnp.pad(
        region_mask.astype(jnp.bfloat16), ((0, 15), (0, HEAD_DIM - region_mask.shape[1]))
    )
    direct = direct_rows(rows3, text, mask)

    near_tp = to_tp(near)
    some = seq // 2
    peers = [lax.ppermute(mine[:some], "section", both), lax.ppermute(mine[some:], "section", both)]
    direct, peers[0] = lax.optimization_barrier((direct, peers[0]))
    direct = lax.all_to_all(direct, "seq", 0, 0)
    cols = w_out.shape[1] // 2
    w_sent = lax.dynamic_slice_in_dim(w_late, (1 - tp) * cols, cols, 1)
    w_kept = lax.dynamic_slice_in_dim(w_late, tp * cols, cols, 1)

    upper = at_chip >= 2
    chips = jnp.stack([at_chip, at_chip ^ 1, jnp.where(upper, 1, 2), jnp.where(upper, 0, 3)])
    cores = jnp.stack([core, 1 - core])
    parts = jnp.stack([tp, 1 - tp])
    shards = chips[:, None, None] * 2 + cores[None, :, None] + 0 * parts[None, None, :]
    parts = parts[None, None, :] + 0 * shards
    shards, parts = shards.reshape(-1).astype(jnp.int32), parts.reshape(-1).astype(jnp.int32)
    size = img_rows // 2
    row_ids = shards * (img_rows // GRID_W) + parts * (size // GRID_W)
    tabs = lane_tables(row_ids, (section == 0).astype(jnp.float32))
    gains = jnp.stack([q_gain, k_gain])
    row_tiles = (shards[:, None] == jnp.arange(seq)[None]).astype(jnp.float32)
    key_tiles = jnp.arange(HEAD_DIM)[:, None] == shards[None]
    key_tiles = key_tiles.astype(jnp.float32)
    place = jnp.stack([shards, parts])

    early = (tabs, gains, row_tiles, key_tiles, place, w_sent, w_kept)
    third, near_tp, early = lax.optimization_barrier((third, near_tp, early))
    tabs, gains, row_tiles, key_tiles, place, w_sent, w_kept = early
    third_tp = to_tp(third)
    fourth, third_tp, peers[0] = lax.optimization_barrier((fourth, third_tp, peers[0]))
    fourth_tp = to_tp(fourth)
    a = [full, to_core(full), near, near_tp, to_core(near), to_core(near_tp)]
    kv_a = project_kv(0, section_at, tabs, gains, mine, peers, a)
    cond_a = lax.ppermute(kv_a, "section", [(0, 1)])
    b = [third, third_tp, to_core(third), to_core(third_tp), fourth, fourth_tp, to_core(fourth)]
    fourth_tp, kv_a = lax.optimization_barrier((fourth_tp, kv_a))
    b[5] = fourth_tp
    b.append(to_core(fourth_tp))
    kv_b = project_kv(1, section_at, tabs, gains, mine, peers, b)
    cond_b = lax.ppermute(kv_b, "section", [(0, 1)])
    query, num, den, keep = attend_own(
        section_at, tabs, gains, row_tiles, key_tiles, (kv_a, kv_b), cond_a, direct, a + b
    )
    attn = attend_second(section_at, place, keep, query, cond_b, num, den, seq)

    attn = lax.all_to_all(attn, "seq", 0, 0)
    gate = lax.dynamic_slice_in_dim(mods[2:3], tp * cols, cols, 1)
    residual = lax.dynamic_slice_in_dim(image[0], tp * cols, cols, 1)
    other = to_tp(project_out(attn, w_sent))
    kept = project_out(attn, w_kept, residual, gate)
    return (kept + gate * other.astype(jnp.float32)).astype(jnp.bfloat16)[None]


def rms_rows(x, gain):
    return x * lax.rsqrt(jnp.mean(x * x, axis=-1, keepdims=True) + 1e-06) * gain


def apply_rope(x, cosine, sine):
    rows, heads_here = (x.shape[0], x.shape[1])
    pairs = x.reshape(rows, heads_here, HEAD_DIM // 2, 2)
    first = pairs[..., 0]
    second = pairs[..., 1]
    cosine = cosine[:, None, :]
    sine = sine[:, None, :]
    rotated = jnp.stack([first * cosine - second * sine, first * sine + second * cosine], axis=-1)
    return rotated.reshape(rows, heads_here, HEAD_DIM)


def attend_piece(carry, keys_vals, query, keep):
    num, den = carry
    rows = keys_vals.shape[0]
    heads_local = query.shape[1]
    piece_k = keys_vals[:, 0].reshape(rows, heads_local, HEAD_DIM)
    piece_v = keys_vals[:, 1].reshape(rows, heads_local, HEAD_DIM)
    scores = jnp.einsum("qhd,khd->hqk", query, piece_k, preferred_element_type=jnp.float32) * (
        1.0 / HEAD_DIM**0.5
    )
    weights = jnp.exp(scores)
    if keep is not None:
        weights = jnp.where(keep[None], weights, 0.0)
    den = den + jnp.sum(weights, axis=-1)
    num = num + jnp.einsum(
        "hqk,khd->hqd", weights.astype(jnp.bfloat16), piece_v, preferred_element_type=jnp.float32
    )
    return (num, den)


def token_body(image, text_kv, modulation, w_qkv, w_out, q_gain, k_gain, region_mask):
    img_rows = image.shape[1]
    width_local = w_qkv.shape[2]
    heads_local = width_local // HEAD_DIM
    tokens = image[0].astype(jnp.float32)
    mods = modulation[0]
    normed = layer_norm(tokens, mods)
    qkv = jnp.einsum(
        "td,dcf->tcf",
        normed,
        lax.all_gather(w_qkv, "seq", axis=0, tiled=True),
        preferred_element_type=jnp.float32,
    )
    section_index = lax.axis_index("section")
    time_index = (section_index == 0).astype(jnp.float32)
    rows_index = lax.axis_index("seq") * img_rows + jnp.arange(img_rows, dtype=jnp.int32)
    cosine, sine = rope_tables(rows_index, time_index)
    query = apply_rope(
        rms_rows(qkv[:, 0].reshape(img_rows, heads_local, HEAD_DIM), q_gain), cosine, sine
    ).astype(jnp.bfloat16)
    keys = apply_rope(
        rms_rows(qkv[:, 1].reshape(img_rows, heads_local, HEAD_DIM), k_gain), cosine, sine
    ).astype(jnp.bfloat16)
    values = qkv[:, 2].astype(jnp.bfloat16)
    image_kv = jnp.stack([keys.reshape(img_rows, width_local), values], axis=1)
    own_kv = jnp.concatenate([image_kv, text_kv[0]], axis=0)
    enabled = (section_index == 1).astype(jnp.int32)
    local_mask = region_mask * enabled
    init = (
        jnp.zeros((heads_local, img_rows, HEAD_DIM), jnp.float32),
        jnp.zeros((heads_local, img_rows), jnp.float32),
    )
    carry = attend_piece(init, lax.all_gather(own_kv, "seq", axis=0, tiled=True), query, None)
    cond_local = lax.ppermute(image_kv, "section", [(0, 1)])
    keep = jnp.repeat(jnp.repeat(local_mask, TILE, axis=0), TILE, axis=1) > 0
    carry = attend_piece(carry, lax.all_gather(cond_local, "seq", axis=0, tiled=True), query, keep)
    num, den = carry
    attn = (num / den[..., None]).astype(jnp.bfloat16)
    attn = jnp.transpose(attn, (1, 0, 2)).reshape(img_rows, width_local)
    term = jnp.dot(attn, w_out, preferred_element_type=jnp.float32)
    branch = lax.psum_scatter(
        term.astype(jnp.bfloat16), "tp", scatter_dimension=1, tiled=True
    ).astype(jnp.float32)
    cols = branch.shape[1]
    offset = lax.axis_index("tp") * cols
    residual = lax.dynamic_slice_in_dim(tokens, offset, cols, 1)
    gate = lax.dynamic_slice_in_dim(mods[2], offset, cols, 0)
    out = residual + gate[None, :] * branch
    return out.astype(jnp.bfloat16)[None]


def body(*arrays):
    image, w_qkv, region_mask = arrays[0], arrays[3], arrays[7]
    seq = lax.axis_size("seq")
    one_head_each = (
        w_qkv.shape[2] // HEAD_DIM == seq == 8
        and lax.axis_size("section") == 2
        and lax.axis_size("tp") == 2
        and w_qkv.shape[0] % 128 == 0
        and image.shape[1] == TILE == 2 * GRID_W
        and region_mask.shape == (1, seq)
        and arrays[1].shape[1] % 16 == 0
        and arrays[4].shape[1] % 1024 == 0
    )
    return (head_body if one_head_each else token_body)(*arrays)


def solution(mesh):
    return jax.shard_map(
        body,
        mesh=mesh,
        in_specs=(
            P("section", "seq", None),
            P("section", "seq", None, "tp"),
            P("section", None, None),
            P("seq", None, "tp"),
            P("tp", None),
            P(),
            P(),
            P("seq", None),
        ),
        out_specs=P("section", "seq", "tp"),
        check_vma=False,
    )
```

```python
import jax
import jax.numpy as jnp
from jax import lax
from jax.experimental import pallas as pl
from jax.experimental.pallas import tpu as pltpu
from jax.sharding import PartitionSpec as P

HEAD_DIM = 128
GRID_W = 64
TILE = 128
VMEM_LIMIT = 24 * 1024 * 1024
VMEM_WHOLE = 56 * 1024 * 1024


def axis_freqs(width):
    return 10000.0 ** (-jnp.arange(0, width, 2).astype(jnp.float32) / width)


def rope_tables(rows_index, time_index):
    first = HEAD_DIM // 8
    rest = (HEAD_DIM - first) // 2
    row_pos = (rows_index // GRID_W).astype(jnp.float32)
    col_pos = (rows_index % GRID_W).astype(jnp.float32)
    time_pos = jnp.zeros_like(row_pos) + time_index
    angles = jnp.concatenate(
        [
            time_pos[:, None] * axis_freqs(first)[None],
            row_pos[:, None] * axis_freqs(rest)[None],
            col_pos[:, None] * axis_freqs(rest)[None],
        ],
        axis=-1,
    )
    return (jnp.cos(angles), jnp.sin(angles))


def layer_norm(tokens, mods):
    mean = jnp.mean(tokens, axis=-1, keepdims=True)
    var = jnp.mean((tokens - mean) ** 2, axis=-1, keepdims=True)
    return ((tokens - mean) * lax.rsqrt(var + 1e-06) * (1.0 + mods[1:2]) + mods[0:1]).astype(
        jnp.bfloat16
    )


VMEM = pl.BlockSpec(memory_space=pltpu.VMEM)
SMEM = pl.BlockSpec(memory_space=pltpu.SMEM)
HBM = pl.BlockSpec(memory_space=pltpu.HBM)


def call(kernel, name, out_shape, flops, moved, exps, limit=VMEM_LIMIT, **spec):
    return pl.pallas_call(
        kernel,
        out_shape=out_shape,
        compiler_params=pltpu.CompilerParams(vmem_limit_bytes=limit),
        cost_estimate=pl.CostEstimate(flops=flops, bytes_accessed=moved, transcendentals=exps),
        name=name,
        **spec,
    )


def started(pairs, sems, first=0):
    copies = [pltpu.make_async_copy(s, d, sems.at[first + i]) for i, (s, d) in enumerate(pairs)]
    for copy in copies:
        copy.start()
    return copies


def finished(copies):
    for copy in copies:
        copy.wait()


def norm_kernel(tp_ref, image_hbm, mods_hbm, full_ref, part_ref, image_ref, mods_ref, sems):
    rows = image_ref.shape[0] // 4
    pairs = [
        (image_hbm.at[pl.ds(i * rows, rows), :], image_ref.at[pl.ds(i * rows, rows), :])
        for i in range(4)
    ]
    finished(started(pairs + [(mods_hbm, mods_ref)], sems))
    mods = jnp.concatenate([mods_ref[0], mods_ref[1]], axis=0)
    normed = layer_norm(image_ref[...].astype(jnp.float32), mods)
    part = part_ref.shape[0]
    for t in range(2):

        @pl.when(tp_ref[0] == t)
        def _(t=t):
            ours, theirs = normed[t * part : (t + 1) * part], normed[(1 - t) * part : (2 - t) * part]
            full_ref[:part, :] = ours
            full_ref[part:, :] = theirs
            part_ref[...] = ours


def norm_tokens(tp, image, mods):
    rows, depth = image.shape
    return call(
        norm_kernel, "norm_tokens",
        [
            jax.ShapeDtypeStruct((rows, depth), jnp.bfloat16),
            jax.ShapeDtypeStruct((rows // 2, depth), jnp.bfloat16),
        ],
        10 * rows * depth, 4 * rows * depth, 0, VMEM_WHOLE,
        in_specs=[SMEM, HBM, HBM],
        out_specs=[VMEM, VMEM],
        scratch_shapes=[
            pltpu.VMEM(image.shape, image.dtype),
            pltpu.VMEM(mods.shape, mods.dtype),
            pltpu.SemaphoreType.DMA((5,)),
        ],
    )(tp, image, mods)


def kv_weights_kernel(section_ref, w_hbm, out_ref, w_ref, sems):
    half = w_ref.shape[1]
    rows = pl.ds(pl.multiple_of(section_ref[0] * half, half), half)
    copies = started([(w_hbm.at[1 + k, rows, :], w_ref.at[k]) for k in range(2)], sems)
    for k in range(2):
        copies[k].wait()
        for s in range(out_ref.shape[0]):
            out_ref[s, k * half : (k + 1) * half, :] = w_ref[k, :, s * HEAD_DIM : (s + 1) * HEAD_DIM]


def kv_weights(section, w):
    _, depth, width = w.shape
    return call(
        kv_weights_kernel, "kv_weights",
        jax.ShapeDtypeStruct((width // HEAD_DIM, depth, HEAD_DIM), w.dtype),
        0, 4 * depth * width, 0, VMEM_WHOLE,
        in_specs=[SMEM, HBM],
        out_specs=VMEM,
        scratch_shapes=[pltpu.VMEM((2, depth // 2, width), w.dtype), pltpu.SemaphoreType.DMA((2,))],
    )(section, w)


def direct_kernel(w_hbm, text_hbm, mask_ref, out_ref, w_ref, text_ref, sems):
    depth, count = w_ref.shape[0], text_ref.shape[1]
    copies = started([(w_hbm.at[0], w_ref), (text_hbm, text_ref)], sems)
    finished(copies)
    for s in range(out_ref.shape[0]):
        out_ref[s, :depth, :] = w_ref[:, s * HEAD_DIM : (s + 1) * HEAD_DIM]
        out_ref[s, depth : depth + count, :] = text_ref[s]
        out_ref[s, depth + count :, :] = mask_ref[...]


def direct_rows(w, text, mask):
    heads, count, _ = text.shape
    shape = (heads, w.shape[1] + count + mask.shape[0], HEAD_DIM)
    return call(
        direct_kernel, "direct_rows", jax.ShapeDtypeStruct(shape, w.dtype),
        0, 4 * heads * shape[1] * HEAD_DIM, 0, VMEM_WHOLE,
        in_specs=[HBM, HBM, VMEM],
        out_specs=VMEM,
        scratch_shapes=[
            pltpu.VMEM(w.shape[1:], w.dtype),
            pltpu.VMEM(text.shape, text.dtype),
            pltpu.SemaphoreType.DMA((2,)),
        ],
    )(w, text, mask)


def normed_rotated(x, gain, cosine, sine):
    x = x * lax.rsqrt(jnp.mean(x * x, axis=-1, keepdims=True) + 1e-06) * gain
    even = lax.broadcasted_iota(jnp.int32, x.shape, 1) % 2 == 0
    other = jnp.where(even, pltpu.roll(x, HEAD_DIM - 1, 1), pltpu.roll(x, 1, 1))
    return (x * cosine + other * sine).astype(jnp.bfloat16)


def table_of(tabs_ref, which, start, rows):
    groups = tabs_ref.shape[1] - GRID_W
    columns = tabs_ref[which, groups:, :]
    lane = lax.broadcasted_iota(jnp.int32, columns.shape, 1)
    first = HEAD_DIM // 8
    by_row = lane < first + (HEAD_DIM - first) // 2
    return jnp.concatenate(
        [
            jnp.where(by_row, tabs_ref[which, g : g + 1, :], columns)
            for g in range(start // GRID_W, (start + rows) // GRID_W)
        ],
        axis=0,
    )


def piece_copies(piece_refs, x_ref):
    at, pairs = 0, []
    for ref in piece_refs:
        pairs.append((ref, x_ref.at[pl.ds(at, ref.shape[0]), :]))
        at += ref.shape[0]
    return pairs


def blocks(rows):
    return [(b, slice(b * BLOCK, (b + 1) * BLOCK)) for b in range(rows // BLOCK)]


def arrived(copies, piece_refs, rows):
    at = 0
    for copy, ref in zip(copies, piece_refs):
        if rows.start <= at < rows.stop:
            copy.wait()
        at += ref.shape[0]


def kv_kernel(chunk, section_ref, tabs_hbm, gain_hbm, mine_hbm, peer_a, peer_b, *refs):
    piece_refs = refs[:-8]
    kv_ref, x_ref, mine, peer, w_ref, tabs_ref, gain_ref, sems = refs[-8:]
    sources, held, _ = mine.shape
    half = held // 2
    some = sources // 2
    weights = started(
        [
            (mine_hbm, mine),
            (peer_a, peer.at[pl.ds(0, some)]),
            (peer_b, peer.at[pl.ds(some, some)]),
            (tabs_hbm, tabs_ref),
            (gain_hbm, gain_ref),
        ],
        sems,
    )
    tokens = started(piece_copies(piece_refs, x_ref), sems, 5)
    finished(weights)
    first = section_ref[0] == 0
    for s in range(sources):
        for kind in range(2):
            at = slice(kind * half, (kind + 1) * half)
            lanes = slice(kind * HEAD_DIM, (kind + 1) * HEAD_DIM)
            a, b = mine[s, at, :], peer[s, at, :]
            w_ref[2 * s * half : (2 * s + 1) * half, lanes] = jnp.where(first, a, b)
            w_ref[(2 * s + 1) * half : (2 * s + 2) * half, lanes] = jnp.where(first, b, a)
    for b, at in blocks(x_ref.shape[0]):
        arrived(tokens, piece_refs, at)
        both = jnp.dot(x_ref[at, :], w_ref[...], preferred_element_type=jnp.float32)
        start = chunk * x_ref.shape[0] + b * BLOCK
        kv_ref[0, at, :] = normed_rotated(
            both[:, :HEAD_DIM],
            gain_ref[1:2, :],
            table_of(tabs_ref, 0, start, BLOCK),
            table_of(tabs_ref, 1, start, BLOCK),
        )
        kv_ref[1, at, :] = both[:, HEAD_DIM:].astype(jnp.bfloat16)


def project_kv(chunk, section, tabs, gains, mine, peers, pieces):
    depth = pieces[0].shape[1]
    rows = sum(p.shape[0] for p in pieces)
    return call(
        lambda *refs: kv_kernel(chunk, *refs), "project_kv" + "ab"[chunk],
        jax.ShapeDtypeStruct((2, rows, HEAD_DIM), jnp.bfloat16),
        4 * rows * depth * HEAD_DIM, 2 * (rows * depth + 2 * mine.size), 0, VMEM_WHOLE,
        in_specs=[SMEM] + [HBM] * (5 + len(pieces)),
        out_specs=VMEM,
        scratch_shapes=[
            pltpu.VMEM((rows, depth), jnp.bfloat16),
            pltpu.VMEM(mine.shape, jnp.bfloat16),
            pltpu.VMEM(mine.shape, jnp.bfloat16),
            pltpu.VMEM((depth, 2 * HEAD_DIM), jnp.bfloat16),
            pltpu.VMEM(tabs.shape, tabs.dtype),
            pltpu.VMEM(gains.shape, gains.dtype),
            pltpu.SemaphoreType.DMA((5 + len(pieces),)),
        ],
    )(section, tabs, gains, mine, *peers, *pieces)


def weights_of(query, keys):
    scores = lax.dot_general(
        query, keys, (((1,), (1,)), ((), ())), preferred_element_type=jnp.float32
    )
    return jnp.exp(scores * (1.0 / HEAD_DIM**0.5))


def summed(weights, values):
    den = jnp.sum(weights, axis=-1, keepdims=True)
    num = jnp.dot(weights.astype(jnp.bfloat16), values, preferred_element_type=jnp.float32)
    return num, den


def kept_weights(query, cond_ref, keep):
    weights = weights_of(query, cond_ref[0])
    rows, keys = weights.shape
    groups = keep.shape[0]
    return (weights.reshape(groups, rows // groups, keys) * keep[:, None, :]).reshape(rows, keys)


BLOCK = 512


def own_kernel(
    section_ref, rows_ref, keys_ref, kva, kvb, cond, tabs_hbm, gain_hbm, direct_hbm, *refs
):
    piece_refs = refs[:-9]
    q_ref, num_ref, den_ref, keep_ref, x_ref, direct, tabs_ref, gain_ref, sems = refs[-9:]
    rows, depth = x_ref.shape
    sources, held, _ = direct.shape
    copies = started([(direct_hbm.at[s], direct.at[s]) for s in range(sources)], sems)
    copies += started([(tabs_hbm, tabs_ref), (gain_hbm, gain_ref)], sems, sources)
    tokens = started(piece_copies(piece_refs, x_ref), sems, sources + 2)
    finished(copies)
    wide = depth // sources
    w = direct[:, :wide, :].reshape(depth, HEAD_DIM)
    count = (held - 16 - wide) // 2
    text = (
        direct[:, wide : wide + count, :].reshape(-1, HEAD_DIM),
        direct[:, wide + count : wide + 2 * count, :].reshape(-1, HEAD_DIM),
    )
    for b, at in blocks(rows):
        arrived(tokens, piece_refs, at)
        query = jnp.dot(x_ref[at, :], w, preferred_element_type=jnp.float32)
        query = normed_rotated(
            query,
            gain_ref[0:1, :],
            table_of(tabs_ref, 0, b * BLOCK, BLOCK),
            table_of(tabs_ref, 1, b * BLOCK, BLOCK),
        )
        q_ref[at, :] = query
        num, den = 0.0, 0.0
        for keys, values in ((kva[0], kva[1]), (kvb[0], kvb[1]), text):
            more = summed(weights_of(query, keys), values)
            num, den = num + more[0], den + more[1]
        num_ref[at, :] = num
        den_ref[at, :] = jnp.broadcast_to(den, num.shape)
    mask = jnp.concatenate(
        [direct[s, held - 16 : held, :].astype(jnp.float32)[:1] for s in range(sources)], axis=0
    )
    mask = jnp.dot(rows_ref[...], mask, preferred_element_type=jnp.float32)
    mask = jnp.dot(mask, keys_ref[...], preferred_element_type=jnp.float32)
    size = rows // keep_ref.shape[0]
    for g in range(keep_ref.shape[0]):
        keep_ref[:, g * size : (g + 1) * size] = jnp.broadcast_to(
            mask[:, g : g + 1], (keep_ref.shape[0], size)
        )

    @pl.when(section_ref[0] != 0)
    def _():
        for b, at in blocks(rows):
            num, den = cond_sum(keep_ref, q_ref, cond, 0, b)
            num_ref[at, :] += num
            den_ref[at, :] += jnp.broadcast_to(den, num.shape)


def cond_sum(keep_ref, q_ref, cond, chunk, b):
    groups = keep_ref.shape[0] * BLOCK // q_ref.shape[0]
    keys = cond.shape[1]
    keep = keep_ref[b * groups : (b + 1) * groups, chunk * keys : (chunk + 1) * keys]
    return summed(kept_weights(q_ref[b * BLOCK : (b + 1) * BLOCK, :], cond, keep), cond[1])


def second_cond_kernel(
    section_ref, place_ref, keep_hbm, q_hbm, num_hbm, den_hbm, cond, out_ref,
    keep_ref, q_ref, num_ref, den_ref, sems,
):
    groups = keep_ref.shape[0] * BLOCK // num_ref.shape[0]
    size = BLOCK // groups
    finished(
        started(
            [(num_hbm, num_ref), (den_hbm, den_ref), (q_hbm, q_ref), (keep_hbm, keep_ref)], sems
        )
    )

    def store(b, num, den):
        value = (num / den).astype(jnp.bfloat16)
        for g in range(groups):
            shard, part = place_ref[0, b * groups + g], place_ref[1, b * groups + g]
            at = pl.ds(pl.multiple_of(part * size, size), size)
            out_ref[shard, at, :] = value[g * size : (g + 1) * size]

    @pl.when(section_ref[0] == 0)
    def _():
        for b, at in blocks(num_ref.shape[0]):
            store(b, num_ref[at, :], den_ref[at, :])

    @pl.when(section_ref[0] != 0)
    def _():
        for b, at in blocks(num_ref.shape[0]):
            num, den = cond_sum(keep_ref, q_ref, cond, 1, b)
            store(b, num_ref[at, :] + num, den_ref[at, :] + den)


def attend_own(section, tabs, gains, row_tiles, key_tiles, kvs, cond, direct, pieces):
    depth = pieces[0].shape[1]
    rows = sum(p.shape[0] for p in pieces)
    keys = 2 * rows
    return call(
        own_kernel, "attend_own",
        [
            jax.ShapeDtypeStruct((rows, HEAD_DIM), jnp.bfloat16),
            jax.ShapeDtypeStruct((rows, HEAD_DIM), jnp.float32),
            jax.ShapeDtypeStruct((rows, HEAD_DIM), jnp.float32),
            jax.ShapeDtypeStruct((row_tiles.shape[0], rows), jnp.float32),
        ],
        2 * rows * HEAD_DIM * (2 * keys + depth), 2 * rows * depth, rows * keys, VMEM_WHOLE,
        in_specs=[SMEM] + [VMEM] * 5 + [HBM] * (3 + len(pieces)),
        out_specs=[VMEM] * 4,
        scratch_shapes=[
            pltpu.VMEM((rows, depth), jnp.bfloat16),
            pltpu.VMEM(direct.shape, jnp.bfloat16),
            pltpu.VMEM(tabs.shape, tabs.dtype),
            pltpu.VMEM(gains.shape, gains.dtype),
            pltpu.SemaphoreType.DMA((direct.shape[0] + 2 + len(pieces),)),
        ],
    )(section, row_tiles, key_tiles, *kvs, cond, tabs, gains, direct, *pieces)


def attend_second(section, place, keep, query, cond, num, den, seq):
    rows, keys = num.shape[0], cond.shape[1]
    return call(
        second_cond_kernel, "attend_second",
        jax.ShapeDtypeStruct((seq, rows // seq, HEAD_DIM), jnp.bfloat16),
        4 * rows * keys * HEAD_DIM, 2 * rows * HEAD_DIM * 8, rows * keys, VMEM_WHOLE,
        in_specs=[SMEM, SMEM] + [HBM] * 4 + [VMEM],
        out_specs=VMEM,
        scratch_shapes=[pltpu.VMEM(x.shape, x.dtype) for x in (keep, query, num, den)]
        + [pltpu.SemaphoreType.DMA((4,))],
    )(section, place, keep, query, num, den, cond)


def token_rows(attn_ref):
    return jnp.concatenate([attn_ref[h] for h in range(attn_ref.shape[0])], axis=1)


def sent_kernel(attn_ref, w_ref, out_ref):
    branch = jnp.dot(token_rows(attn_ref), w_ref[...], preferred_element_type=jnp.float32)
    out_ref[...] = branch.astype(jnp.bfloat16)


def kept_kernel(attn_ref, w_ref, image_ref, gate_ref, out_ref):
    branch = jnp.dot(token_rows(attn_ref), w_ref[...], preferred_element_type=jnp.float32)
    out_ref[...] = image_ref[...].astype(jnp.float32) + gate_ref[...] * branch


def project_out(attn, w, image=None, gate=None):
    rows = attn.shape[1]
    depth, width = w.shape
    kept = image is not None
    args = (attn, w) + ((image, gate) if kept else ())
    return call(
        kept_kernel if kept else sent_kernel, "out_kept" if kept else "out_sent",
        jax.ShapeDtypeStruct((rows, width), jnp.float32 if kept else jnp.bfloat16),
        2 * rows * depth * width, 2 * depth * width, 0,
        in_specs=[VMEM] * len(args),
        out_specs=VMEM,
    )(*args)


def lane_tables(row_ids, time_index):
    first = HEAD_DIM // 8
    rest = (HEAD_DIM - first) // 2
    freqs = jnp.concatenate([axis_freqs(first), axis_freqs(rest), axis_freqs(rest)])
    freqs = jnp.repeat(freqs, 2)[None]
    lane = jnp.arange(HEAD_DIM, dtype=jnp.int32)[None]
    rows = jnp.where(lane < first, time_index, row_ids.astype(jnp.float32)[:, None])
    columns = jnp.broadcast_to(jnp.arange(GRID_W, dtype=jnp.float32)[:, None], (GRID_W, HEAD_DIM))
    angles = jnp.concatenate([rows, columns], axis=0) * freqs
    return jnp.stack([jnp.cos(angles), jnp.sin(angles) * jnp.where(lane % 2 == 0, -1.0, 1.0)])


def z_pairs(seq, pairs):
    return [(2 * a + core, 2 * b + core) for a, b in pairs for core in range(2)]


def head_body(image, text_kv, modulation, w_qkv, w_out, q_gain, k_gain, region_mask):
    seq = lax.axis_size("seq")
    img_rows = image.shape[1]
    depth = w_qkv.shape[0]
    section = lax.axis_index("section")
    tp = lax.axis_index("tp")
    chip, core = lax.axis_index("seq") // 2, lax.axis_index("seq") % 2
    mods = modulation[0]
    section_at = section.astype(jnp.int32).reshape(1)
    tp_at = tp.astype(jnp.int32).reshape(1)
    both = [(0, 1), (1, 0)]

    rows3 = w_qkv.transpose(1, 0, 2)
    mine = lax.all_to_all(kv_weights(section_at, rows3), "seq", 0, 0)

    full, part = norm_tokens(tp_at, image[0], modulation.transpose(1, 0, 2))

    def along_z(x, pairs):
        return lax.ppermute(x, "seq", z_pairs(seq, pairs))

    def to_core(x):
        return lax.ppermute(x, "seq", [(s, s ^ 1) for s in range(seq)])

    def to_tp(x):
        return lax.ppermute(x, "tp", both)

    near = along_z(part, [(0, 1), (1, 0), (2, 3), (3, 2)])
    near, w_late, at_chip = lax.optimization_barrier((near, w_out, chip.astype(jnp.int32)))
    middle = along_z(part, [(1, 2), (2, 1)])
    far = along_z(near, [(1, 2), (2, 1)])
    middle_end = along_z(middle, [(1, 0), (2, 3)])
    far_end = along_z(far, [(1, 0), (2, 3)])
    inner = (chip == 1) | (chip == 2)
    third = jnp.where(inner, middle, middle_end)
    fourth = jnp.where(inner, far, far_end)

    text = text_kv[0].reshape(-1, 2, seq, HEAD_DIM).transpose(2, 1, 0, 3).reshape(seq, -1, HEAD_DIM)
    mask = jnp.pad(
        region_mask.astype(jnp.bfloat16), ((0, 15), (0, HEAD_DIM - region_mask.shape[1]))
    )
    direct = direct_rows(rows3, text, mask)

    near_tp = to_tp(near)
    some = seq // 2
    peers = [lax.ppermute(mine[:some], "section", both), lax.ppermute(mine[some:], "section", both)]
    direct, peers[0] = lax.optimization_barrier((direct, peers[0]))
    direct = lax.all_to_all(direct, "seq", 0, 0)
    cols = w_out.shape[1] // 2
    w_sent = lax.dynamic_slice_in_dim(w_late, (1 - tp) * cols, cols, 1)
    w_kept = lax.dynamic_slice_in_dim(w_late, tp * cols, cols, 1)

    upper = at_chip >= 2
    chips = jnp.stack([at_chip, at_chip ^ 1, jnp.where(upper, 1, 2), jnp.where(upper, 0, 3)])
    cores = jnp.stack([core, 1 - core])
    parts = jnp.stack([tp, 1 - tp])
    shards = chips[:, None, None] * 2 + cores[None, :, None] + 0 * parts[None, None, :]
    parts = parts[None, None, :] + 0 * shards
    shards, parts = shards.reshape(-1).astype(jnp.int32), parts.reshape(-1).astype(jnp.int32)
    size = img_rows // 2
    row_ids = shards * (img_rows // GRID_W) + parts * (size // GRID_W)
    tabs = lane_tables(row_ids, (section == 0).astype(jnp.float32))
    gains = jnp.stack([q_gain, k_gain])
    row_tiles = (shards[:, None] == jnp.arange(seq)[None]).astype(jnp.float32)
    key_tiles = jnp.arange(HEAD_DIM)[:, None] == shards[None]
    key_tiles = key_tiles.astype(jnp.float32)
    place = jnp.stack([shards, parts])

    early = (tabs, gains, row_tiles, key_tiles, place, w_sent, w_kept)
    third, near_tp, early = lax.optimization_barrier((third, near_tp, early))
    tabs, gains, row_tiles, key_tiles, place, w_sent, w_kept = early
    third_tp = to_tp(third)
    fourth, third_tp, peers[0] = lax.optimization_barrier((fourth, third_tp, peers[0]))
    fourth_tp = to_tp(fourth)
    a = [full, to_core(full), near, near_tp, to_core(near), to_core(near_tp)]
    kv_a = project_kv(0, section_at, tabs, gains, mine, peers, a)
    cond_a = lax.ppermute(kv_a, "section", [(0, 1)])
    b = [third, third_tp, to_core(third), to_core(third_tp), fourth, fourth_tp, to_core(fourth)]
    fourth_tp, kv_a = lax.optimization_barrier((fourth_tp, kv_a))
    b[5] = fourth_tp
    b.append(to_core(fourth_tp))
    kv_b = project_kv(1, section_at, tabs, gains, mine, peers, b)
    cond_b = lax.ppermute(kv_b, "section", [(0, 1)])
    query, num, den, keep = attend_own(
        section_at, tabs, gains, row_tiles, key_tiles, (kv_a, kv_b), cond_a, direct, a + b
    )
    attn = attend_second(section_at, place, keep, query, cond_b, num, den, seq)

    attn = lax.all_to_all(attn, "seq", 0, 0)
    gate = lax.dynamic_slice_in_dim(mods[2:3], tp * cols, cols, 1)
    residual = lax.dynamic_slice_in_dim(image[0], tp * cols, cols, 1)
    other = to_tp(project_out(attn, w_sent))
    kept = project_out(attn, w_kept, residual, gate)
    return (kept + gate * other.astype(jnp.float32)).astype(jnp.bfloat16)[None]


def rms_rows(x, gain):
    return x * lax.rsqrt(jnp.mean(x * x, axis=-1, keepdims=True) + 1e-06) * gain


def apply_rope(x, cosine, sine):
    rows, heads_here = (x.shape[0], x.shape[1])
    pairs = x.reshape(rows, heads_here, HEAD_DIM // 2, 2)
    first = pairs[..., 0]
    second = pairs[..., 1]
    cosine = cosine[:, None, :]
    sine = sine[:, None, :]
    rotated = jnp.stack([first * cosine - second * sine, first * sine + second * cosine], axis=-1)
    return rotated.reshape(rows, heads_here, HEAD_DIM)


def attend_piece(carry, keys_vals, query, keep):
    num, den = carry
    rows = keys_vals.shape[0]
    heads_local = query.shape[1]
    piece_k = keys_vals[:, 0].reshape(rows, heads_local, HEAD_DIM)
    piece_v = keys_vals[:, 1].reshape(rows, heads_local, HEAD_DIM)
    scores = jnp.einsum("qhd,khd->hqk", query, piece_k, preferred_element_type=jnp.float32) * (
        1.0 / HEAD_DIM**0.5
    )
    weights = jnp.exp(scores)
    if keep is not None:
        weights = jnp.where(keep[None], weights, 0.0)
    den = den + jnp.sum(weights, axis=-1)
    num = num + jnp.einsum(
        "hqk,khd->hqd", weights.astype(jnp.bfloat16), piece_v, preferred_element_type=jnp.float32
    )
    return (num, den)


def token_body(image, text_kv, modulation, w_qkv, w_out, q_gain, k_gain, region_mask):
    img_rows = image.shape[1]
    width_local = w_qkv.shape[2]
    heads_local = width_local // HEAD_DIM
    tokens = image[0].astype(jnp.float32)
    mods = modulation[0]
    normed = layer_norm(tokens, mods)
    qkv = jnp.einsum(
        "td,dcf->tcf",
        normed,
        lax.all_gather(w_qkv, "seq", axis=0, tiled=True),
        preferred_element_type=jnp.float32,
    )
    section_index = lax.axis_index("section")
    time_index = (section_index == 0).astype(jnp.float32)
    rows_index = lax.axis_index("seq") * img_rows + jnp.arange(img_rows, dtype=jnp.int32)
    cosine, sine = rope_tables(rows_index, time_index)
    query = apply_rope(
        rms_rows(qkv[:, 0].reshape(img_rows, heads_local, HEAD_DIM), q_gain), cosine, sine
    ).astype(jnp.bfloat16)
    keys = apply_rope(
        rms_rows(qkv[:, 1].reshape(img_rows, heads_local, HEAD_DIM), k_gain), cosine, sine
    ).astype(jnp.bfloat16)
    values = qkv[:, 2].astype(jnp.bfloat16)
    image_kv = jnp.stack([keys.reshape(img_rows, width_local), values], axis=1)
    own_kv = jnp.concatenate([image_kv, text_kv[0]], axis=0)
    enabled = (section_index == 1).astype(jnp.int32)
    local_mask = region_mask * enabled
    init = (
        jnp.zeros((heads_local, img_rows, HEAD_DIM), jnp.float32),
        jnp.zeros((heads_local, img_rows), jnp.float32),
    )
    carry = attend_piece(init, lax.all_gather(own_kv, "seq", axis=0, tiled=True), query, None)
    cond_local = lax.ppermute(image_kv, "section", [(0, 1)])
    keep = jnp.repeat(jnp.repeat(local_mask, TILE, axis=0), TILE, axis=1) > 0
    carry = attend_piece(carry, lax.all_gather(cond_local, "seq", axis=0, tiled=True), query, keep)
    num, den = carry
    attn = (num / den[..., None]).astype(jnp.bfloat16)
    attn = jnp.transpose(attn, (1, 0, 2)).reshape(img_rows, width_local)
    term = jnp.dot(attn, w_out, preferred_element_type=jnp.float32)
    branch = lax.psum_scatter(
        term.astype(jnp.bfloat16), "tp", scatter_dimension=1, tiled=True
    ).astype(jnp.float32)
    cols = branch.shape[1]
    offset = lax.axis_index("tp") * cols
    residual = lax.dynamic_slice_in_dim(tokens, offset, cols, 1)
    gate = lax.dynamic_slice_in_dim(mods[2], offset, cols, 0)
    out = residual + gate[None, :] * branch
    return out.astype(jnp.bfloat16)[None]


def body(*arrays):
    image, w_qkv, region_mask = arrays[0], arrays[3], arrays[7]
    seq = lax.axis_size("seq")
    one_head_each = (
        w_qkv.shape[2] // HEAD_DIM == seq == 8
        and lax.axis_size("section") == 2
        and lax.axis_size("tp") == 2
        and w_qkv.shape[0] % 128 == 0
        and image.shape[1] == TILE == 2 * GRID_W
        and region_mask.shape == (1, seq)
        and arrays[1].shape[1] % 16 == 0
        and arrays[4].shape[1] % 1024 == 0
    )
    return (head_body if one_head_each else token_body)(*arrays)


def solution(mesh):
    return jax.shard_map(
        body,
        mesh=mesh,
        in_specs=(
            P("section", "seq", None),
            P("section", "seq", None, "tp"),
            P("section", None, None),
            P("seq", None, "tp"),
            P("tp", None),
            P(),
            P(),
            P("seq", None),
        ),
        out_specs=P("section", "seq", "tp"),
        check_vma=False,
    )
```

```python
import jax
import jax.numpy as jnp
from jax import lax
from jax.experimental import pallas as pl
from jax.experimental.pallas import tpu as pltpu
from jax.sharding import PartitionSpec as P

HEAD_DIM = 128
GRID_W = 64
TILE = 128
BLOCK = 512
OWN_BLOCK = 256
VMEM_LIMIT = 24 * 1024 * 1024
VMEM_WHOLE = 56 * 1024 * 1024


def axis_freqs(width):
    return 10000.0 ** (-jnp.arange(0, width, 2).astype(jnp.float32) / width)


def rope_tables(rows_index, time_index):
    first = HEAD_DIM // 8
    rest = (HEAD_DIM - first) // 2
    row_pos = (rows_index // GRID_W).astype(jnp.float32)
    col_pos = (rows_index % GRID_W).astype(jnp.float32)
    time_pos = jnp.zeros_like(row_pos) + time_index
    angles = jnp.concatenate(
        [
            time_pos[:, None] * axis_freqs(first)[None],
            row_pos[:, None] * axis_freqs(rest)[None],
            col_pos[:, None] * axis_freqs(rest)[None],
        ],
        axis=-1,
    )
    return (jnp.cos(angles), jnp.sin(angles))


def layer_norm(tokens, mods):
    mean = jnp.mean(tokens, axis=-1, keepdims=True)
    var = jnp.mean((tokens - mean) ** 2, axis=-1, keepdims=True)
    return ((tokens - mean) * lax.rsqrt(var + 1e-06) * (1.0 + mods[1:2]) + mods[0:1]).astype(
        jnp.bfloat16
    )


VMEM = pl.BlockSpec(memory_space=pltpu.VMEM)
SMEM = pl.BlockSpec(memory_space=pltpu.SMEM)
HBM = pl.BlockSpec(memory_space=pltpu.HBM)


def call(kernel, name, out_shape, flops, moved, exps, limit=VMEM_LIMIT, **spec):
    return pl.pallas_call(
        kernel,
        out_shape=out_shape,
        compiler_params=pltpu.CompilerParams(vmem_limit_bytes=limit),
        cost_estimate=pl.CostEstimate(flops=flops, bytes_accessed=moved, transcendentals=exps),
        name=name,
        **spec,
    )


def started(pairs, sems, first=0):
    copies = [pltpu.make_async_copy(s, d, sems.at[first + i]) for i, (s, d) in enumerate(pairs)]
    for copy in copies:
        copy.start()
    return copies


def finished(copies):
    for copy in copies:
        copy.wait()


def norm_kernel(tp_ref, image_hbm, mods_hbm, full_ref, part_ref, image_ref, mods_ref, sems):
    rows = image_ref.shape[0] // 4
    pairs = [
        (image_hbm.at[pl.ds(i * rows, rows), :], image_ref.at[pl.ds(i * rows, rows), :])
        for i in range(4)
    ]
    finished(started(pairs + [(mods_hbm, mods_ref)], sems))
    mods = jnp.concatenate([mods_ref[0], mods_ref[1]], axis=0)
    normed = layer_norm(image_ref[...].astype(jnp.float32), mods)
    part = part_ref.shape[0]
    for t in range(2):

        @pl.when(tp_ref[0] == t)
        def _(t=t):
            ours, theirs = normed[t * part : (t + 1) * part], normed[(1 - t) * part : (2 - t) * part]
            full_ref[:part, :] = ours
            full_ref[part:, :] = theirs
            part_ref[...] = ours


def norm_tokens(tp, image, mods):
    rows, depth = image.shape
    return call(
        norm_kernel, "norm_tokens",
        [
            jax.ShapeDtypeStruct((rows, depth), jnp.bfloat16),
            jax.ShapeDtypeStruct((rows // 2, depth), jnp.bfloat16),
        ],
        10 * rows * depth, 4 * rows * depth, 0, VMEM_WHOLE,
        in_specs=[SMEM, HBM, HBM],
        out_specs=[VMEM, VMEM],
        scratch_shapes=[
            pltpu.VMEM(image.shape, image.dtype),
            pltpu.VMEM(mods.shape, mods.dtype),
            pltpu.SemaphoreType.DMA((5,)),
        ],
    )(tp, image, mods)


def kv_weights_kernel(section_ref, w_hbm, out_ref, w_ref, sems):
    half = w_ref.shape[1]
    rows = pl.ds(pl.multiple_of(section_ref[0] * half, half), half)
    copies = started([(w_hbm.at[1 + k, rows, :], w_ref.at[k]) for k in range(2)], sems)
    for k in range(2):
        copies[k].wait()
        for s in range(out_ref.shape[0]):
            out_ref[s, k * half : (k + 1) * half, :] = w_ref[k, :, s * HEAD_DIM : (s + 1) * HEAD_DIM]


def kv_weights(section, w):
    _, depth, width = w.shape
    return call(
        kv_weights_kernel, "kv_weights",
        jax.ShapeDtypeStruct((width // HEAD_DIM, depth, HEAD_DIM), w.dtype),
        0, 4 * depth * width, 0, VMEM_WHOLE,
        in_specs=[SMEM, HBM],
        out_specs=VMEM,
        scratch_shapes=[pltpu.VMEM((2, depth // 2, width), w.dtype), pltpu.SemaphoreType.DMA((2,))],
    )(section, w)


def direct_kernel(w_hbm, text_hbm, mask_ref, out_ref, w_ref, text_ref, sems):
    depth, count = w_ref.shape[0], text_ref.shape[1]
    copies = started([(w_hbm.at[0], w_ref), (text_hbm, text_ref)], sems)
    finished(copies)
    for s in range(out_ref.shape[0]):
        out_ref[s, :depth, :] = w_ref[:, s * HEAD_DIM : (s + 1) * HEAD_DIM]
        out_ref[s, depth : depth + count, :] = text_ref[s]
        out_ref[s, depth + count :, :] = mask_ref[...]


def direct_rows(w, text, mask):
    heads, count, _ = text.shape
    shape = (heads, w.shape[1] + count + mask.shape[0], HEAD_DIM)
    return call(
        direct_kernel, "direct_rows", jax.ShapeDtypeStruct(shape, w.dtype),
        0, 4 * heads * shape[1] * HEAD_DIM, 0, VMEM_WHOLE,
        in_specs=[HBM, HBM, VMEM],
        out_specs=VMEM,
        scratch_shapes=[
            pltpu.VMEM(w.shape[1:], w.dtype),
            pltpu.VMEM(text.shape, text.dtype),
            pltpu.SemaphoreType.DMA((2,)),
        ],
    )(w, text, mask)


def normed_rotated(x, gain, cosine, sine):
    x = x * lax.rsqrt(jnp.mean(x * x, axis=-1, keepdims=True) + 1e-06) * gain
    even = lax.broadcasted_iota(jnp.int32, x.shape, 1) % 2 == 0
    other = jnp.where(even, pltpu.roll(x, HEAD_DIM - 1, 1), pltpu.roll(x, 1, 1))
    return (x * cosine + other * sine).astype(jnp.bfloat16)


def table_of(tabs_ref, which, start, rows):
    groups = tabs_ref.shape[1] - GRID_W
    columns = tabs_ref[which, groups:, :]
    lane = lax.broadcasted_iota(jnp.int32, columns.shape, 1)
    first = HEAD_DIM // 8
    by_row = lane < first + (HEAD_DIM - first) // 2
    return jnp.concatenate(
        [
            jnp.where(by_row, tabs_ref[which, g : g + 1, :], columns)
            for g in range(start // GRID_W, (start + rows) // GRID_W)
        ],
        axis=0,
    )


def piece_copies(piece_refs, x_ref):
    at, pairs = 0, []
    for ref in piece_refs:
        pairs.append((ref, x_ref.at[pl.ds(at, ref.shape[0]), :]))
        at += ref.shape[0]
    return pairs


def blocks(rows, block=BLOCK):
    return [(b, slice(b * block, (b + 1) * block)) for b in range(rows // block)]


def arrived(copies, piece_refs, rows):
    at = 0
    for copy, ref in zip(copies, piece_refs):
        if rows.start <= at < rows.stop:
            copy.wait()
        at += ref.shape[0]


def kv_kernel(chunk, section_ref, tabs_hbm, gain_hbm, mine_hbm, peer_a, peer_b, *refs):
    piece_refs = refs[:-8]
    kv_ref, x_ref, mine, peer, w_ref, tabs_ref, gain_ref, sems = refs[-8:]
    sources, held, _ = mine.shape
    half = held // 2
    some = sources // 2
    weights = started(
        [
            (mine_hbm, mine),
            (peer_a, peer.at[pl.ds(0, some)]),
            (peer_b, peer.at[pl.ds(some, some)]),
            (tabs_hbm, tabs_ref),
            (gain_hbm, gain_ref),
        ],
        sems,
    )
    tokens = started(piece_copies(piece_refs, x_ref), sems, 5)
    finished(weights)
    first = section_ref[0] == 0
    for s in range(sources):
        for kind in range(2):
            at = slice(kind * half, (kind + 1) * half)
            lanes = slice(kind * HEAD_DIM, (kind + 1) * HEAD_DIM)
            a, b = mine[s, at, :], peer[s, at, :]
            w_ref[2 * s * half : (2 * s + 1) * half, lanes] = jnp.where(first, a, b)
            w_ref[(2 * s + 1) * half : (2 * s + 2) * half, lanes] = jnp.where(first, b, a)
    for b, at in blocks(x_ref.shape[0]):
        arrived(tokens, piece_refs, at)
        both = jnp.dot(x_ref[at, :], w_ref[...], preferred_element_type=jnp.float32)
        start = chunk * x_ref.shape[0] + b * BLOCK
        kv_ref[0, at, :] = normed_rotated(
            both[:, :HEAD_DIM],
            gain_ref[1:2, :],
            table_of(tabs_ref, 0, start, BLOCK),
            table_of(tabs_ref, 1, start, BLOCK),
        )
        kv_ref[1, at, :] = both[:, HEAD_DIM:].astype(jnp.bfloat16)


def project_kv(chunk, section, tabs, gains, mine, peers, pieces):
    depth = pieces[0].shape[1]
    rows = sum(p.shape[0] for p in pieces)
    return call(
        lambda *refs: kv_kernel(chunk, *refs), "project_kv" + "ab"[chunk],
        jax.ShapeDtypeStruct((2, rows, HEAD_DIM), jnp.bfloat16),
        4 * rows * depth * HEAD_DIM, 2 * (rows * depth + 2 * mine.size), 0, VMEM_WHOLE,
        in_specs=[SMEM] + [HBM] * (5 + len(pieces)),
        out_specs=VMEM,
        scratch_shapes=[
            pltpu.VMEM((rows, depth), jnp.bfloat16),
            pltpu.VMEM(mine.shape, jnp.bfloat16),
            pltpu.VMEM(mine.shape, jnp.bfloat16),
            pltpu.VMEM((depth, 2 * HEAD_DIM), jnp.bfloat16),
            pltpu.VMEM(tabs.shape, tabs.dtype),
            pltpu.VMEM(gains.shape, gains.dtype),
            pltpu.SemaphoreType.DMA((5 + len(pieces),)),
        ],
    )(section, tabs, gains, mine, *peers, *pieces)


def weights_of(query, keys):
    scores = lax.dot_general(
        query, keys, (((1,), (1,)), ((), ())), preferred_element_type=jnp.float32
    )
    return jnp.exp(scores * (1.0 / HEAD_DIM**0.5))


def summed(weights, values):
    den = jnp.sum(weights, axis=-1, keepdims=True)
    num = jnp.dot(weights.astype(jnp.bfloat16), values, preferred_element_type=jnp.float32)
    return num, den


def kept_weights(query, cond_ref, keep):
    weights = weights_of(query, cond_ref[0])
    rows, keys = weights.shape
    groups = keep.shape[0]
    return (weights.reshape(groups, rows // groups, keys) * keep[:, None, :]).reshape(rows, keys)


def own_kernel(
    section_ref, rows_ref, keys_ref, kva, kvb, cond, tabs_hbm, gain_hbm, direct_hbm, *refs
):
    piece_refs = refs[:-9]
    q_ref, num_ref, den_ref, keep_ref, x_ref, direct, tabs_ref, gain_ref, sems = refs[-9:]
    rows, depth = x_ref.shape
    sources, held, _ = direct.shape
    copies = started([(direct_hbm.at[s], direct.at[s]) for s in range(sources)], sems)
    copies += started([(tabs_hbm, tabs_ref), (gain_hbm, gain_ref)], sems, sources)
    tokens = started(piece_copies(piece_refs, x_ref), sems, sources + 2)
    finished(copies)
    wide = depth // sources
    w = direct[:, :wide, :].reshape(depth, HEAD_DIM)
    count = (held - 16 - wide) // 2
    text = (
        direct[:, wide : wide + count, :].reshape(-1, HEAD_DIM),
        direct[:, wide + count : wide + 2 * count, :].reshape(-1, HEAD_DIM),
    )
    for b, at in blocks(rows, OWN_BLOCK):
        arrived(tokens, piece_refs, at)
        query = jnp.dot(x_ref[at, :], w, preferred_element_type=jnp.float32)
        query = normed_rotated(
            query,
            gain_ref[0:1, :],
            table_of(tabs_ref, 0, b * OWN_BLOCK, OWN_BLOCK),
            table_of(tabs_ref, 1, b * OWN_BLOCK, OWN_BLOCK),
        )
        q_ref[at, :] = query
        num, den = 0.0, 0.0
        for keys, values in ((kva[0], kva[1]), (kvb[0], kvb[1]), text):
            more = summed(weights_of(query, keys), values)
            num, den = num + more[0], den + more[1]
        num_ref[at, :] = num
        den_ref[at, :] = jnp.broadcast_to(den, num.shape)
    mask = jnp.concatenate(
        [direct[s, held - 16 : held, :].astype(jnp.float32)[:1] for s in range(sources)], axis=0
    )
    mask = jnp.dot(rows_ref[...], mask, preferred_element_type=jnp.float32)
    mask = jnp.dot(mask, keys_ref[...], preferred_element_type=jnp.float32)
    size = rows // keep_ref.shape[0]
    for g in range(keep_ref.shape[0]):
        keep_ref[:, g * size : (g + 1) * size] = jnp.broadcast_to(
            mask[:, g : g + 1], (keep_ref.shape[0], size)
        )

    @pl.when(section_ref[0] != 0)
    def _():
        for b, at in blocks(rows, OWN_BLOCK):
            num, den = cond_sum(keep_ref, q_ref, cond, 0, b, OWN_BLOCK)
            num_ref[at, :] += num
            den_ref[at, :] += jnp.broadcast_to(den, num.shape)


def cond_sum(keep_ref, q_ref, cond, chunk, b, block=BLOCK):
    groups = keep_ref.shape[0] * block // q_ref.shape[0]
    keys = cond.shape[1]
    keep = keep_ref[b * groups : (b + 1) * groups, chunk * keys : (chunk + 1) * keys]
    return summed(kept_weights(q_ref[b * block : (b + 1) * block, :], cond, keep), cond[1])


def second_cond_kernel(
    section_ref, place_ref, keep_hbm, q_hbm, num_hbm, den_hbm, cond, out_ref,
    keep_ref, q_ref, num_ref, den_ref, sems,
):
    groups = keep_ref.shape[0] * BLOCK // num_ref.shape[0]
    size = BLOCK // groups
    finished(
        started(
            [(num_hbm, num_ref), (den_hbm, den_ref), (q_hbm, q_ref), (keep_hbm, keep_ref)], sems
        )
    )

    def store(b, num, den):
        value = (num / den).astype(jnp.bfloat16)
        for g in range(groups):
            shard, part = place_ref[0, b * groups + g], place_ref[1, b * groups + g]
            at = pl.ds(pl.multiple_of(part * size, size), size)
            out_ref[shard, at, :] = value[g * size : (g + 1) * size]

    @pl.when(section_ref[0] == 0)
    def _():
        for b, at in blocks(num_ref.shape[0]):
            store(b, num_ref[at, :], den_ref[at, :])

    @pl.when(section_ref[0] != 0)
    def _():
        for b, at in blocks(num_ref.shape[0]):
            num, den = cond_sum(keep_ref, q_ref, cond, 1, b)
            store(b, num_ref[at, :] + num, den_ref[at, :] + den)


def attend_own(section, tabs, gains, row_tiles, key_tiles, kvs, cond, direct, pieces):
    depth = pieces[0].shape[1]
    rows = sum(p.shape[0] for p in pieces)
    keys = 2 * rows
    return call(
        own_kernel, "attend_own",
        [
            jax.ShapeDtypeStruct((rows, HEAD_DIM), jnp.bfloat16),
            jax.ShapeDtypeStruct((rows, HEAD_DIM), jnp.float32),
            jax.ShapeDtypeStruct((rows, HEAD_DIM), jnp.float32),
            jax.ShapeDtypeStruct((row_tiles.shape[0], rows), jnp.float32),
        ],
        2 * rows * HEAD_DIM * (2 * keys + depth), 2 * rows * depth, rows * keys, VMEM_WHOLE,
        in_specs=[SMEM] + [VMEM] * 5 + [HBM] * (3 + len(pieces)),
        out_specs=[VMEM] * 4,
        scratch_shapes=[
            pltpu.VMEM((rows, depth), jnp.bfloat16),
            pltpu.VMEM(direct.shape, jnp.bfloat16),
            pltpu.VMEM(tabs.shape, tabs.dtype),
            pltpu.VMEM(gains.shape, gains.dtype),
            pltpu.SemaphoreType.DMA((direct.shape[0] + 2 + len(pieces),)),
        ],
    )(section, row_tiles, key_tiles, *kvs, cond, tabs, gains, direct, *pieces)


def attend_second(section, place, keep, query, cond, num, den, seq):
    rows, keys = num.shape[0], cond.shape[1]
    return call(
        second_cond_kernel, "attend_second",
        jax.ShapeDtypeStruct((seq, rows // seq, HEAD_DIM), jnp.bfloat16),
        4 * rows * keys * HEAD_DIM, 2 * rows * HEAD_DIM * 8, rows * keys, VMEM_WHOLE,
        in_specs=[SMEM, SMEM] + [HBM] * 4 + [VMEM],
        out_specs=VMEM,
        scratch_shapes=[pltpu.VMEM(x.shape, x.dtype) for x in (keep, query, num, den)]
        + [pltpu.SemaphoreType.DMA((4,))],
    )(section, place, keep, query, num, den, cond)


def token_rows(attn_ref):
    return jnp.concatenate([attn_ref[h] for h in range(attn_ref.shape[0])], axis=1)


def sent_kernel(attn_ref, w_ref, out_ref):
    branch = jnp.dot(token_rows(attn_ref), w_ref[...], preferred_element_type=jnp.float32)
    out_ref[...] = branch.astype(jnp.bfloat16)


def kept_kernel(attn_ref, w_ref, image_ref, gate_ref, out_ref):
    branch = jnp.dot(token_rows(attn_ref), w_ref[...], preferred_element_type=jnp.float32)
    out_ref[...] = image_ref[...].astype(jnp.float32) + gate_ref[...] * branch


def project_out(attn, w, image=None, gate=None):
    rows = attn.shape[1]
    depth, width = w.shape
    kept = image is not None
    args = (attn, w) + ((image, gate) if kept else ())
    return call(
        kept_kernel if kept else sent_kernel, "out_kept" if kept else "out_sent",
        jax.ShapeDtypeStruct((rows, width), jnp.float32 if kept else jnp.bfloat16),
        2 * rows * depth * width, 2 * depth * width, 0,
        in_specs=[VMEM] * len(args),
        out_specs=VMEM,
    )(*args)


def lane_tables(row_ids, time_index):
    first = HEAD_DIM // 8
    rest = (HEAD_DIM - first) // 2
    freqs = jnp.concatenate([axis_freqs(first), axis_freqs(rest), axis_freqs(rest)])
    freqs = jnp.repeat(freqs, 2)[None]
    lane = jnp.arange(HEAD_DIM, dtype=jnp.int32)[None]
    rows = jnp.where(lane < first, time_index, row_ids.astype(jnp.float32)[:, None])
    columns = jnp.broadcast_to(jnp.arange(GRID_W, dtype=jnp.float32)[:, None], (GRID_W, HEAD_DIM))
    angles = jnp.concatenate([rows, columns], axis=0) * freqs
    return jnp.stack([jnp.cos(angles), jnp.sin(angles) * jnp.where(lane % 2 == 0, -1.0, 1.0)])


def z_pairs(seq, pairs):
    return [(2 * a + core, 2 * b + core) for a, b in pairs for core in range(2)]


def head_body(image, text_kv, modulation, w_qkv, w_out, q_gain, k_gain, region_mask):
    seq = lax.axis_size("seq")
    img_rows = image.shape[1]
    depth = w_qkv.shape[0]
    section = lax.axis_index("section")
    tp = lax.axis_index("tp")
    chip, core = lax.axis_index("seq") // 2, lax.axis_index("seq") % 2
    mods = modulation[0]
    section_at = section.astype(jnp.int32).reshape(1)
    tp_at = tp.astype(jnp.int32).reshape(1)
    both = [(0, 1), (1, 0)]

    rows3 = w_qkv.transpose(1, 0, 2)
    mine = lax.all_to_all(kv_weights(section_at, rows3), "seq", 0, 0)

    full, part = norm_tokens(tp_at, image[0], modulation.transpose(1, 0, 2))

    def along_z(x, pairs):
        return lax.ppermute(x, "seq", z_pairs(seq, pairs))

    def to_core(x):
        return lax.ppermute(x, "seq", [(s, s ^ 1) for s in range(seq)])

    def to_tp(x):
        return lax.ppermute(x, "tp", both)

    near = along_z(part, [(0, 1), (1, 0), (2, 3), (3, 2)])
    near, w_late, at_chip = lax.optimization_barrier((near, w_out, chip.astype(jnp.int32)))
    middle = along_z(part, [(1, 2), (2, 1)])
    far = along_z(near, [(1, 2), (2, 1)])
    middle_end = along_z(middle, [(1, 0), (2, 3)])
    far_end = along_z(far, [(1, 0), (2, 3)])
    inner = (chip == 1) | (chip == 2)
    third = jnp.where(inner, middle, middle_end)
    fourth = jnp.where(inner, far, far_end)

    text = text_kv[0].reshape(-1, 2, seq, HEAD_DIM).transpose(2, 1, 0, 3).reshape(seq, -1, HEAD_DIM)
    mask = jnp.pad(
        region_mask.astype(jnp.bfloat16), ((0, 15), (0, HEAD_DIM - region_mask.shape[1]))
    )
    direct = direct_rows(rows3, text, mask)

    near_tp = to_tp(near)
    some = seq // 2
    peers = [lax.ppermute(mine[:some], "section", both), lax.ppermute(mine[some:], "section", both)]
    cols = w_out.shape[1] // 2
    w_sent = lax.dynamic_slice_in_dim(w_late, (1 - tp) * cols, cols, 1)
    w_kept = lax.dynamic_slice_in_dim(w_late, tp * cols, cols, 1)

    upper = at_chip >= 2
    chips = jnp.stack([at_chip, at_chip ^ 1, jnp.where(upper, 1, 2), jnp.where(upper, 0, 3)])
    cores = jnp.stack([core, 1 - core])
    parts = jnp.stack([tp, 1 - tp])
    shards = chips[:, None, None] * 2 + cores[None, :, None] + 0 * parts[None, None, :]
    parts = parts[None, None, :] + 0 * shards
    shards, parts = shards.reshape(-1).astype(jnp.int32), parts.reshape(-1).astype(jnp.int32)
    size = img_rows // 2
    row_ids = shards * (img_rows // GRID_W) + parts * (size // GRID_W)
    tabs = lane_tables(row_ids, (section == 0).astype(jnp.float32))
    gains = jnp.stack([q_gain, k_gain])
    row_tiles = (shards[:, None] == jnp.arange(seq)[None]).astype(jnp.float32)
    key_tiles = jnp.arange(HEAD_DIM)[:, None] == shards[None]
    key_tiles = key_tiles.astype(jnp.float32)
    place = jnp.stack([shards, parts])

    early = (tabs, gains, row_tiles, key_tiles, place, w_sent, w_kept)
    third, near_tp, early = lax.optimization_barrier((third, near_tp, early))
    tabs, gains, row_tiles, key_tiles, place, w_sent, w_kept = early
    third_tp = to_tp(third)
    direct, third_tp, peers = lax.optimization_barrier((direct, third_tp, peers))
    direct = lax.all_to_all(direct, "seq", 0, 0)
    fourth, third_tp, peers[0] = lax.optimization_barrier((fourth, third_tp, peers[0]))
    fourth_tp = to_tp(fourth)
    a = [full, to_core(full), near, near_tp, to_core(near), to_core(near_tp)]
    kv_a = project_kv(0, section_at, tabs, gains, mine, peers, a)
    cond_a = lax.ppermute(kv_a, "section", [(0, 1)])
    b = [third, third_tp, to_core(third), to_core(third_tp), fourth, fourth_tp, to_core(fourth)]
    fourth_tp, kv_a = lax.optimization_barrier((fourth_tp, kv_a))
    b[5] = fourth_tp
    b.append(to_core(fourth_tp))
    kv_b = project_kv(1, section_at, tabs, gains, mine, peers, b)
    cond_b = lax.ppermute(kv_b, "section", [(0, 1)])
    query, num, den, keep = attend_own(
        section_at, tabs, gains, row_tiles, key_tiles, (kv_a, kv_b), cond_a, direct, a + b
    )
    attn = attend_second(section_at, place, keep, query, cond_b, num, den, seq)

    attn = lax.all_to_all(attn, "seq", 0, 0)
    gate = lax.dynamic_slice_in_dim(mods[2:3], tp * cols, cols, 1)
    residual = lax.dynamic_slice_in_dim(image[0], tp * cols, cols, 1)
    other = to_tp(project_out(attn, w_sent))
    kept = project_out(attn, w_kept, residual, gate)
    return (kept + gate * other.astype(jnp.float32)).astype(jnp.bfloat16)[None]


def rms_rows(x, gain):
    return x * lax.rsqrt(jnp.mean(x * x, axis=-1, keepdims=True) + 1e-06) * gain


def apply_rope(x, cosine, sine):
    rows, heads_here = (x.shape[0], x.shape[1])
    pairs = x.reshape(rows, heads_here, HEAD_DIM // 2, 2)
    first = pairs[..., 0]
    second = pairs[..., 1]
    cosine = cosine[:, None, :]
    sine = sine[:, None, :]
    rotated = jnp.stack([first * cosine - second * sine, first * sine + second * cosine], axis=-1)
    return rotated.reshape(rows, heads_here, HEAD_DIM)


def attend_piece(carry, keys_vals, query, keep):
    num, den = carry
    rows = keys_vals.shape[0]
    heads_local = query.shape[1]
    piece_k = keys_vals[:, 0].reshape(rows, heads_local, HEAD_DIM)
    piece_v = keys_vals[:, 1].reshape(rows, heads_local, HEAD_DIM)
    scores = jnp.einsum("qhd,khd->hqk", query, piece_k, preferred_element_type=jnp.float32) * (
        1.0 / HEAD_DIM**0.5
    )
    weights = jnp.exp(scores)
    if keep is not None:
        weights = jnp.where(keep[None], weights, 0.0)
    den = den + jnp.sum(weights, axis=-1)
    num = num + jnp.einsum(
        "hqk,khd->hqd", weights.astype(jnp.bfloat16), piece_v, preferred_element_type=jnp.float32
    )
    return (num, den)


def token_body(image, text_kv, modulation, w_qkv, w_out, q_gain, k_gain, region_mask):
    img_rows = image.shape[1]
    width_local = w_qkv.shape[2]
    heads_local = width_local // HEAD_DIM
    tokens = image[0].astype(jnp.float32)
    mods = modulation[0]
    normed = layer_norm(tokens, mods)
    qkv = jnp.einsum(
        "td,dcf->tcf",
        normed,
        lax.all_gather(w_qkv, "seq", axis=0, tiled=True),
        preferred_element_type=jnp.float32,
    )
    section_index = lax.axis_index("section")
    time_index = (section_index == 0).astype(jnp.float32)
    rows_index = lax.axis_index("seq") * img_rows + jnp.arange(img_rows, dtype=jnp.int32)
    cosine, sine = rope_tables(rows_index, time_index)
    query = apply_rope(
        rms_rows(qkv[:, 0].reshape(img_rows, heads_local, HEAD_DIM), q_gain), cosine, sine
    ).astype(jnp.bfloat16)
    keys = apply_rope(
        rms_rows(qkv[:, 1].reshape(img_rows, heads_local, HEAD_DIM), k_gain), cosine, sine
    ).astype(jnp.bfloat16)
    values = qkv[:, 2].astype(jnp.bfloat16)
    image_kv = jnp.stack([keys.reshape(img_rows, width_local), values], axis=1)
    own_kv = jnp.concatenate([image_kv, text_kv[0]], axis=0)
    enabled = (section_index == 1).astype(jnp.int32)
    local_mask = region_mask * enabled
    init = (
        jnp.zeros((heads_local, img_rows, HEAD_DIM), jnp.float32),
        jnp.zeros((heads_local, img_rows), jnp.float32),
    )
    carry = attend_piece(init, lax.all_gather(own_kv, "seq", axis=0, tiled=True), query, None)
    cond_local = lax.ppermute(image_kv, "section", [(0, 1)])
    keep = jnp.repeat(jnp.repeat(local_mask, TILE, axis=0), TILE, axis=1) > 0
    carry = attend_piece(carry, lax.all_gather(cond_local, "seq", axis=0, tiled=True), query, keep)
    num, den = carry
    attn = (num / den[..., None]).astype(jnp.bfloat16)
    attn = jnp.transpose(attn, (1, 0, 2)).reshape(img_rows, width_local)
    term = jnp.dot(attn, w_out, preferred_element_type=jnp.float32)
    branch = lax.psum_scatter(
        term.astype(jnp.bfloat16), "tp", scatter_dimension=1, tiled=True
    ).astype(jnp.float32)
    cols = branch.shape[1]
    offset = lax.axis_index("tp") * cols
    residual = lax.dynamic_slice_in_dim(tokens, offset, cols, 1)
    gate = lax.dynamic_slice_in_dim(mods[2], offset, cols, 0)
    out = residual + gate[None, :] * branch
    return out.astype(jnp.bfloat16)[None]


def body(*arrays):
    image, w_qkv, region_mask = arrays[0], arrays[3], arrays[7]
    seq = lax.axis_size("seq")
    one_head_each = (
        w_qkv.shape[2] // HEAD_DIM == seq == 8
        and lax.axis_size("section") == 2
        and lax.axis_size("tp") == 2
        and w_qkv.shape[0] % 128 == 0
        and image.shape[1] == TILE == 2 * GRID_W
        and region_mask.shape == (1, seq)
        and arrays[1].shape[1] % 16 == 0
        and arrays[4].shape[1] % 1024 == 0
    )
    return (head_body if one_head_each else token_body)(*arrays)


def solution(mesh):
    return jax.shard_map(
        body,
        mesh=mesh,
        in_specs=(
            P("section", "seq", None),
            P("section", "seq", None, "tp"),
            P("section", None, None),
            P("seq", None, "tp"),
            P("tp", None),
            P(),
            P(),
            P("seq", None),
        ),
        out_specs=P("section", "seq", "tp"),
        check_vma=False,
    )
```

```python
import jax
import jax.numpy as jnp
from jax import lax
from jax.experimental import pallas as pl
from jax.experimental.pallas import tpu as pltpu
from jax.sharding import PartitionSpec as P

HEAD_DIM = 128
GRID_W = 64
TILE = 128
BLOCK = 512
OWN_BLOCK = 256
VMEM_LIMIT = 24 * 1024 * 1024
VMEM_WHOLE = 56 * 1024 * 1024


def axis_freqs(width):
    return 10000.0 ** (-jnp.arange(0, width, 2).astype(jnp.float32) / width)


def rope_tables(rows_index, time_index):
    first = HEAD_DIM // 8
    rest = (HEAD_DIM - first) // 2
    row_pos = (rows_index // GRID_W).astype(jnp.float32)
    col_pos = (rows_index % GRID_W).astype(jnp.float32)
    time_pos = jnp.zeros_like(row_pos) + time_index
    angles = jnp.concatenate(
        [
            time_pos[:, None] * axis_freqs(first)[None],
            row_pos[:, None] * axis_freqs(rest)[None],
            col_pos[:, None] * axis_freqs(rest)[None],
        ],
        axis=-1,
    )
    return (jnp.cos(angles), jnp.sin(angles))


def layer_norm(tokens, mods):
    mean = jnp.mean(tokens, axis=-1, keepdims=True)
    var = jnp.mean((tokens - mean) ** 2, axis=-1, keepdims=True)
    return ((tokens - mean) * lax.rsqrt(var + 1e-06) * (1.0 + mods[1:2]) + mods[0:1]).astype(
        jnp.bfloat16
    )


VMEM = pl.BlockSpec(memory_space=pltpu.VMEM)
SMEM = pl.BlockSpec(memory_space=pltpu.SMEM)
HBM = pl.BlockSpec(memory_space=pltpu.HBM)


def call(kernel, name, out_shape, flops, moved, exps, limit=VMEM_LIMIT, **spec):
    return pl.pallas_call(
        kernel,
        out_shape=out_shape,
        compiler_params=pltpu.CompilerParams(vmem_limit_bytes=limit),
        cost_estimate=pl.CostEstimate(flops=flops, bytes_accessed=moved, transcendentals=exps),
        name=name,
        **spec,
    )


def started(pairs, sems, first=0):
    copies = [pltpu.make_async_copy(s, d, sems.at[first + i]) for i, (s, d) in enumerate(pairs)]
    for copy in copies:
        copy.start()
    return copies


def finished(copies):
    for copy in copies:
        copy.wait()


def norm_kernel(tp_ref, image_hbm, mods_hbm, full_ref, part_ref, image_ref, mods_ref, sems):
    rows = image_ref.shape[0] // 4
    pairs = [
        (image_hbm.at[pl.ds(i * rows, rows), :], image_ref.at[pl.ds(i * rows, rows), :])
        for i in range(4)
    ]
    finished(started(pairs + [(mods_hbm, mods_ref)], sems))
    mods = jnp.concatenate([mods_ref[0], mods_ref[1]], axis=0)
    normed = layer_norm(image_ref[...].astype(jnp.float32), mods)
    part = part_ref.shape[0]
    for t in range(2):

        @pl.when(tp_ref[0] == t)
        def _(t=t):
            ours, theirs = normed[t * part : (t + 1) * part], normed[(1 - t) * part : (2 - t) * part]
            full_ref[:part, :] = ours
            full_ref[part:, :] = theirs
            part_ref[...] = ours


def norm_tokens(tp, image, mods):
    rows, depth = image.shape
    return call(
        norm_kernel, "norm_tokens",
        [
            jax.ShapeDtypeStruct((rows, depth), jnp.bfloat16),
            jax.ShapeDtypeStruct((rows // 2, depth), jnp.bfloat16),
        ],
        10 * rows * depth, 4 * rows * depth, 0, VMEM_WHOLE,
        in_specs=[SMEM, HBM, HBM],
        out_specs=[VMEM, VMEM],
        scratch_shapes=[
            pltpu.VMEM(image.shape, image.dtype),
            pltpu.VMEM(mods.shape, mods.dtype),
            pltpu.SemaphoreType.DMA((5,)),
        ],
    )(tp, image, mods)


def kv_weights_kernel(section_ref, w_hbm, out_ref, w_ref, sems):
    half = w_ref.shape[1]
    rows = pl.ds(pl.multiple_of(section_ref[0] * half, half), half)
    copies = started([(w_hbm.at[1 + k, rows, :], w_ref.at[k]) for k in range(2)], sems)
    for k in range(2):
        copies[k].wait()
        for s in range(out_ref.shape[0]):
            out_ref[s, k * half : (k + 1) * half, :] = w_ref[k, :, s * HEAD_DIM : (s + 1) * HEAD_DIM]


def kv_weights(section, w):
    _, depth, width = w.shape
    return call(
        kv_weights_kernel, "kv_weights",
        jax.ShapeDtypeStruct((width // HEAD_DIM, depth, HEAD_DIM), w.dtype),
        0, 4 * depth * width, 0, VMEM_WHOLE,
        in_specs=[SMEM, HBM],
        out_specs=VMEM,
        scratch_shapes=[pltpu.VMEM((2, depth // 2, width), w.dtype), pltpu.SemaphoreType.DMA((2,))],
    )(section, w)


def direct_kernel(w_hbm, text_hbm, mask_ref, out_ref, w_ref, text_ref, sems):
    depth, count = w_ref.shape[0], text_ref.shape[1]
    copies = started([(w_hbm.at[0], w_ref), (text_hbm, text_ref)], sems)
    finished(copies)
    for s in range(out_ref.shape[0]):
        out_ref[s, :depth, :] = w_ref[:, s * HEAD_DIM : (s + 1) * HEAD_DIM]
        out_ref[s, depth : depth + count, :] = text_ref[s]
        out_ref[s, depth + count :, :] = mask_ref[...]


def direct_rows(w, text, mask):
    heads, count, _ = text.shape
    shape = (heads, w.shape[1] + count + mask.shape[0], HEAD_DIM)
    return call(
        direct_kernel, "direct_rows", jax.ShapeDtypeStruct(shape, w.dtype),
        0, 4 * heads * shape[1] * HEAD_DIM, 0, VMEM_WHOLE,
        in_specs=[HBM, HBM, VMEM],
        out_specs=VMEM,
        scratch_shapes=[
            pltpu.VMEM(w.shape[1:], w.dtype),
            pltpu.VMEM(text.shape, text.dtype),
            pltpu.SemaphoreType.DMA((2,)),
        ],
    )(w, text, mask)


def normed_rotated(x, gain, cosine, sine):
    x = x * lax.rsqrt(jnp.mean(x * x, axis=-1, keepdims=True) + 1e-06) * gain
    even = lax.broadcasted_iota(jnp.int32, x.shape, 1) % 2 == 0
    other = jnp.where(even, pltpu.roll(x, HEAD_DIM - 1, 1), pltpu.roll(x, 1, 1))
    return (x * cosine + other * sine).astype(jnp.bfloat16)


def table_of(tabs_ref, which, start, rows):
    groups = tabs_ref.shape[1] - GRID_W
    columns = tabs_ref[which, groups:, :]
    lane = lax.broadcasted_iota(jnp.int32, columns.shape, 1)
    first = HEAD_DIM // 8
    by_row = lane < first + (HEAD_DIM - first) // 2
    return jnp.concatenate(
        [
            jnp.where(by_row, tabs_ref[which, g : g + 1, :], columns)
            for g in range(start // GRID_W, (start + rows) // GRID_W)
        ],
        axis=0,
    )


def piece_copies(piece_refs, x_ref):
    at, pairs = 0, []
    for ref in piece_refs:
        pairs.append((ref, x_ref.at[pl.ds(at, ref.shape[0]), :]))
        at += ref.shape[0]
    return pairs


def blocks(rows, block=BLOCK):
    return [(b, slice(b * block, (b + 1) * block)) for b in range(rows // block)]


def arrived(copies, piece_refs, rows):
    at = 0
    for copy, ref in zip(copies, piece_refs):
        if rows.start <= at < rows.stop:
            copy.wait()
        at += ref.shape[0]


def kv_kernel(chunk, section_ref, tabs_hbm, gain_hbm, mine_hbm, peer_a, peer_b, *refs):
    piece_refs = refs[:-8]
    kv_ref, x_ref, mine, peer, w_ref, tabs_ref, gain_ref, sems = refs[-8:]
    sources, held, _ = mine.shape
    half = held // 2
    some = sources // 2
    weights = started(
        [
            (mine_hbm, mine),
            (peer_a, peer.at[pl.ds(0, some)]),
            (peer_b, peer.at[pl.ds(some, some)]),
            (tabs_hbm, tabs_ref),
            (gain_hbm, gain_ref),
        ],
        sems,
    )
    tokens = started(piece_copies(piece_refs, x_ref), sems, 5)
    finished(weights)
    first = section_ref[0] == 0
    for s in range(sources):
        for kind in range(2):
            at = slice(kind * half, (kind + 1) * half)
            lanes = slice(kind * HEAD_DIM, (kind + 1) * HEAD_DIM)
            a, b = mine[s, at, :], peer[s, at, :]
            w_ref[2 * s * half : (2 * s + 1) * half, lanes] = jnp.where(first, a, b)
            w_ref[(2 * s + 1) * half : (2 * s + 2) * half, lanes] = jnp.where(first, b, a)
    for b, at in blocks(x_ref.shape[0]):
        arrived(tokens, piece_refs, at)
        both = jnp.dot(x_ref[at, :], w_ref[...], preferred_element_type=jnp.float32)
        start = chunk * x_ref.shape[0] + b * BLOCK
        kv_ref[0, at, :] = normed_rotated(
            both[:, :HEAD_DIM],
            gain_ref[1:2, :],
            table_of(tabs_ref, 0, start, BLOCK),
            table_of(tabs_ref, 1, start, BLOCK),
        )
        kv_ref[1, at, :] = both[:, HEAD_DIM:].astype(jnp.bfloat16)


def project_kv(chunk, section, tabs, gains, mine, peers, pieces):
    depth = pieces[0].shape[1]
    rows = sum(p.shape[0] for p in pieces)
    return call(
        lambda *refs: kv_kernel(chunk, *refs), "project_kv" + "ab"[chunk],
        jax.ShapeDtypeStruct((2, rows, HEAD_DIM), jnp.bfloat16),
        4 * rows * depth * HEAD_DIM, 2 * (rows * depth + 2 * mine.size), 0, VMEM_WHOLE,
        in_specs=[SMEM] + [HBM] * (5 + len(pieces)),
        out_specs=VMEM,
        scratch_shapes=[
            pltpu.VMEM((rows, depth), jnp.bfloat16),
            pltpu.VMEM(mine.shape, jnp.bfloat16),
            pltpu.VMEM(mine.shape, jnp.bfloat16),
            pltpu.VMEM((depth, 2 * HEAD_DIM), jnp.bfloat16),
            pltpu.VMEM(tabs.shape, tabs.dtype),
            pltpu.VMEM(gains.shape, gains.dtype),
            pltpu.SemaphoreType.DMA((5 + len(pieces),)),
        ],
    )(section, tabs, gains, mine, *peers, *pieces)


def weights_of(query, keys):
    scores = lax.dot_general(
        query, keys, (((1,), (1,)), ((), ())), preferred_element_type=jnp.float32
    )
    return jnp.exp(scores * (1.0 / HEAD_DIM**0.5))


def summed(weights, values):
    den = jnp.sum(weights, axis=-1, keepdims=True)
    num = jnp.dot(weights.astype(jnp.bfloat16), values, preferred_element_type=jnp.float32)
    return num, den


def kept_weights(query, cond_ref, keep):
    weights = weights_of(query, cond_ref[0])
    rows, keys = weights.shape
    groups = keep.shape[0]
    return (weights.reshape(groups, rows // groups, keys) * keep[:, None, :]).reshape(rows, keys)


def own_kernel(
    section_ref, rows_ref, keys_ref, kva, kvb, cond, tabs_hbm, gain_hbm, direct_hbm, *refs
):
    piece_refs = refs[:-9]
    q_ref, num_ref, den_ref, keep_ref, x_ref, direct, tabs_ref, gain_ref, sems = refs[-9:]
    rows, depth = x_ref.shape
    sources, held, _ = direct.shape
    copies = started([(direct_hbm.at[s], direct.at[s]) for s in range(sources)], sems)
    copies += started([(tabs_hbm, tabs_ref), (gain_hbm, gain_ref)], sems, sources)
    tokens = started(piece_copies(piece_refs, x_ref), sems, sources + 2)
    finished(copies)
    wide = depth // sources
    w = direct[:, :wide, :].reshape(depth, HEAD_DIM)
    count = (held - 16 - wide) // 2
    text = (
        direct[:, wide : wide + count, :].reshape(-1, HEAD_DIM),
        direct[:, wide + count : wide + 2 * count, :].reshape(-1, HEAD_DIM),
    )
    for b, at in blocks(rows, OWN_BLOCK):
        arrived(tokens, piece_refs, at)
        query = jnp.dot(x_ref[at, :], w, preferred_element_type=jnp.float32)
        query = normed_rotated(
            query,
            gain_ref[0:1, :],
            table_of(tabs_ref, 0, b * OWN_BLOCK, OWN_BLOCK),
            table_of(tabs_ref, 1, b * OWN_BLOCK, OWN_BLOCK),
        )
        q_ref[at, :] = query
        num, den = 0.0, 0.0
        for keys, values in ((kva[0], kva[1]), (kvb[0], kvb[1]), text):
            more = summed(weights_of(query, keys), values)
            num, den = num + more[0], den + more[1]
        num_ref[at, :] = num
        den_ref[at, :] = jnp.broadcast_to(den, num.shape)
    mask = jnp.concatenate(
        [direct[s, held - 16 : held, :].astype(jnp.float32)[:1] for s in range(sources)], axis=0
    )
    mask = jnp.dot(rows_ref[...], mask, preferred_element_type=jnp.float32)
    mask = jnp.dot(mask, keys_ref[...], preferred_element_type=jnp.float32)
    size = rows // keep_ref.shape[0]
    for g in range(keep_ref.shape[0]):
        keep_ref[:, g * size : (g + 1) * size] = jnp.broadcast_to(
            mask[:, g : g + 1], (keep_ref.shape[0], size)
        )

    @pl.when(section_ref[0] != 0)
    def _():
        for b, at in blocks(rows, OWN_BLOCK):
            num, den = cond_sum(keep_ref, q_ref, cond, 0, b, OWN_BLOCK)
            num_ref[at, :] += num
            den_ref[at, :] += jnp.broadcast_to(den, num.shape)


def cond_sum(keep_ref, q_ref, cond, chunk, b, block=BLOCK):
    groups = keep_ref.shape[0] * block // q_ref.shape[0]
    keys = cond.shape[1]
    keep = keep_ref[b * groups : (b + 1) * groups, chunk * keys : (chunk + 1) * keys]
    return summed(kept_weights(q_ref[b * block : (b + 1) * block, :], cond, keep), cond[1])


def second_cond_kernel(
    section_ref, place_ref, keep_hbm, q_hbm, num_hbm, den_hbm, cond, out_ref,
    keep_ref, q_ref, num_ref, den_ref, sems,
):
    groups = keep_ref.shape[0] * BLOCK // num_ref.shape[0]
    size = BLOCK // groups
    finished(
        started(
            [(num_hbm, num_ref), (den_hbm, den_ref), (q_hbm, q_ref), (keep_hbm, keep_ref)], sems
        )
    )

    def store(b, num, den):
        value = (num / den).astype(jnp.bfloat16)
        for g in range(groups):
            shard, part = place_ref[0, b * groups + g], place_ref[1, b * groups + g]
            at = pl.ds(pl.multiple_of(part * size, size), size)
            out_ref[shard, at, :] = value[g * size : (g + 1) * size]

    @pl.when(section_ref[0] == 0)
    def _():
        for b, at in blocks(num_ref.shape[0]):
            store(b, num_ref[at, :], den_ref[at, :])

    @pl.when(section_ref[0] != 0)
    def _():
        for b, at in blocks(num_ref.shape[0]):
            num, den = cond_sum(keep_ref, q_ref, cond, 1, b)
            store(b, num_ref[at, :] + num, den_ref[at, :] + den)


def attend_own(section, tabs, gains, row_tiles, key_tiles, kvs, cond, direct, pieces):
    depth = pieces[0].shape[1]
    rows = sum(p.shape[0] for p in pieces)
    keys = 2 * rows
    return call(
        own_kernel, "attend_own",
        [
            jax.ShapeDtypeStruct((rows, HEAD_DIM), jnp.bfloat16),
            jax.ShapeDtypeStruct((rows, HEAD_DIM), jnp.float32),
            jax.ShapeDtypeStruct((rows, HEAD_DIM), jnp.float32),
            jax.ShapeDtypeStruct((row_tiles.shape[0], rows), jnp.float32),
        ],
        2 * rows * HEAD_DIM * (2 * keys + depth), 2 * rows * depth, rows * keys, VMEM_WHOLE,
        in_specs=[SMEM] + [VMEM] * 5 + [HBM] * (3 + len(pieces)),
        out_specs=[VMEM] * 4,
        scratch_shapes=[
            pltpu.VMEM((rows, depth), jnp.bfloat16),
            pltpu.VMEM(direct.shape, jnp.bfloat16),
            pltpu.VMEM(tabs.shape, tabs.dtype),
            pltpu.VMEM(gains.shape, gains.dtype),
            pltpu.SemaphoreType.DMA((direct.shape[0] + 2 + len(pieces),)),
        ],
    )(section, row_tiles, key_tiles, *kvs, cond, tabs, gains, direct, *pieces)


def attend_second(section, place, keep, query, cond, num, den, seq):
    rows, keys = num.shape[0], cond.shape[1]
    return call(
        second_cond_kernel, "attend_second",
        jax.ShapeDtypeStruct((seq, rows // seq, HEAD_DIM), jnp.bfloat16),
        4 * rows * keys * HEAD_DIM, 2 * rows * HEAD_DIM * 8, rows * keys, VMEM_WHOLE,
        in_specs=[SMEM, SMEM] + [HBM] * 4 + [VMEM],
        out_specs=VMEM,
        scratch_shapes=[pltpu.VMEM(x.shape, x.dtype) for x in (keep, query, num, den)]
        + [pltpu.SemaphoreType.DMA((4,))],
    )(section, place, keep, query, num, den, cond)


def token_rows(attn_ref):
    return jnp.concatenate([attn_ref[h] for h in range(attn_ref.shape[0])], axis=1)


def sent_kernel(attn_ref, w_ref, out_ref):
    branch = jnp.dot(token_rows(attn_ref), w_ref[...], preferred_element_type=jnp.float32)
    out_ref[...] = branch.astype(jnp.bfloat16)


def kept_kernel(attn_ref, w_ref, image_ref, gate_ref, out_ref):
    branch = jnp.dot(token_rows(attn_ref), w_ref[...], preferred_element_type=jnp.float32)
    out_ref[...] = image_ref[...].astype(jnp.float32) + gate_ref[...] * branch


def project_out(attn, w, image=None, gate=None):
    rows = attn.shape[1]
    depth, width = w.shape
    kept = image is not None
    args = (attn, w) + ((image, gate) if kept else ())
    return call(
        kept_kernel if kept else sent_kernel, "out_kept" if kept else "out_sent",
        jax.ShapeDtypeStruct((rows, width), jnp.float32 if kept else jnp.bfloat16),
        2 * rows * depth * width, 2 * depth * width, 0,
        in_specs=[VMEM] * len(args),
        out_specs=VMEM,
    )(*args)


def lane_tables(row_ids, time_index):
    first = HEAD_DIM // 8
    rest = (HEAD_DIM - first) // 2
    freqs = jnp.concatenate([axis_freqs(first), axis_freqs(rest), axis_freqs(rest)])
    freqs = jnp.repeat(freqs, 2)[None]
    lane = jnp.arange(HEAD_DIM, dtype=jnp.int32)[None]
    rows = jnp.where(lane < first, time_index, row_ids.astype(jnp.float32)[:, None])
    columns = jnp.broadcast_to(jnp.arange(GRID_W, dtype=jnp.float32)[:, None], (GRID_W, HEAD_DIM))
    angles = jnp.concatenate([rows, columns], axis=0) * freqs
    return jnp.stack([jnp.cos(angles), jnp.sin(angles) * jnp.where(lane % 2 == 0, -1.0, 1.0)])


def z_pairs(seq, pairs):
    return [(2 * a + core, 2 * b + core) for a, b in pairs for core in range(2)]


def head_body(image, text_kv, modulation, w_qkv, w_out, q_gain, k_gain, region_mask):
    seq = lax.axis_size("seq")
    img_rows = image.shape[1]
    depth = w_qkv.shape[0]
    section = lax.axis_index("section")
    tp = lax.axis_index("tp")
    chip, core = lax.axis_index("seq") // 2, lax.axis_index("seq") % 2
    mods = modulation[0]
    section_at = section.astype(jnp.int32).reshape(1)
    tp_at = tp.astype(jnp.int32).reshape(1)
    both = [(0, 1), (1, 0)]

    rows3 = w_qkv.transpose(1, 0, 2)
    mine = lax.all_to_all(kv_weights(section_at, rows3), "seq", 0, 0)

    full, part = norm_tokens(tp_at, image[0], modulation.transpose(1, 0, 2))

    def along_z(x, pairs):
        return lax.ppermute(x, "seq", z_pairs(seq, pairs))

    def to_core(x):
        return lax.ppermute(x, "seq", [(s, s ^ 1) for s in range(seq)])

    def to_tp(x):
        return lax.ppermute(x, "tp", both)

    near = along_z(part, [(0, 1), (1, 0), (2, 3), (3, 2)])
    near, w_late, at_chip = lax.optimization_barrier((near, w_out, chip.astype(jnp.int32)))
    middle = along_z(part, [(1, 2), (2, 1)])
    far = along_z(near, [(1, 2), (2, 1)])
    middle_end = along_z(middle, [(1, 0), (2, 3)])
    far_end = along_z(far, [(1, 0), (2, 3)])
    inner = (chip == 1) | (chip == 2)
    third = jnp.where(inner, middle, middle_end)
    fourth = jnp.where(inner, far, far_end)

    text = text_kv[0].reshape(-1, 2, seq, HEAD_DIM).transpose(2, 1, 0, 3).reshape(seq, -1, HEAD_DIM)
    mask = jnp.pad(
        region_mask.astype(jnp.bfloat16), ((0, 15), (0, HEAD_DIM - region_mask.shape[1]))
    )
    direct = direct_rows(rows3, text, mask)

    near_tp = to_tp(near)
    some = seq // 2
    peers = [lax.ppermute(mine[:some], "section", both), lax.ppermute(mine[some:], "section", both)]
    direct, peers[0] = lax.optimization_barrier((direct, peers[0]))
    direct = lax.all_to_all(direct, "seq", 0, 0)
    cols = w_out.shape[1] // 2
    w_sent = lax.dynamic_slice_in_dim(w_late, (1 - tp) * cols, cols, 1)
    w_kept = lax.dynamic_slice_in_dim(w_late, tp * cols, cols, 1)

    upper = at_chip >= 2
    chips = jnp.stack([at_chip, at_chip ^ 1, jnp.where(upper, 1, 2), jnp.where(upper, 0, 3)])
    cores = jnp.stack([core, 1 - core])
    parts = jnp.stack([tp, 1 - tp])
    shards = chips[:, None, None] * 2 + cores[None, :, None] + 0 * parts[None, None, :]
    parts = parts[None, None, :] + 0 * shards
    shards, parts = shards.reshape(-1).astype(jnp.int32), parts.reshape(-1).astype(jnp.int32)
    size = img_rows // 2
    row_ids = shards * (img_rows // GRID_W) + parts * (size // GRID_W)
    tabs = lane_tables(row_ids, (section == 0).astype(jnp.float32))
    gains = jnp.stack([q_gain, k_gain])
    row_tiles = (shards[:, None] == jnp.arange(seq)[None]).astype(jnp.float32)
    key_tiles = jnp.arange(HEAD_DIM)[:, None] == shards[None]
    key_tiles = key_tiles.astype(jnp.float32)
    place = jnp.stack([shards, parts])

    early = (tabs, gains, row_tiles, key_tiles, place, w_sent, w_kept)
    third, near_tp, early = lax.optimization_barrier((third, near_tp, early))
    tabs, gains, row_tiles, key_tiles, place, w_sent, w_kept = early
    third_tp = to_tp(third)
    fourth, third_tp, peers[0] = lax.optimization_barrier((fourth, third_tp, peers[0]))
    fourth_tp = to_tp(fourth)
    a = [full, to_core(full), near, near_tp, to_core(near), to_core(near_tp)]
    kv_a = project_kv(0, section_at, tabs, gains, mine, peers, a)
    cond_a = lax.ppermute(kv_a, "section", [(0, 1)])
    b = [third, third_tp, to_core(third), to_core(third_tp), fourth, fourth_tp, to_core(fourth)]
    fourth_tp, kv_a = lax.optimization_barrier((fourth_tp, kv_a))
    b[5] = fourth_tp
    b.append(to_core(fourth_tp))
    kv_b = project_kv(1, section_at, tabs, gains, mine, peers, b)
    cond_b = lax.ppermute(kv_b, "section", [(0, 1)])
    query, num, den, keep = attend_own(
        section_at, tabs, gains, row_tiles, key_tiles, (kv_a, kv_b), cond_a, direct, a + b
    )
    attn = attend_second(section_at, place, keep, query, cond_b, num, den, seq)

    attn = lax.all_to_all(attn, "seq", 0, 0)
    gate = lax.dynamic_slice_in_dim(mods[2:3], tp * cols, cols, 1)
    residual = lax.dynamic_slice_in_dim(image[0], tp * cols, cols, 1)
    other = to_tp(project_out(attn, w_sent))
    kept = project_out(attn, w_kept, residual, gate)
    return (kept + gate * other.astype(jnp.float32)).astype(jnp.bfloat16)[None]


def rms_rows(x, gain):
    return x * lax.rsqrt(jnp.mean(x * x, axis=-1, keepdims=True) + 1e-06) * gain


def apply_rope(x, cosine, sine):
    rows, heads_here = (x.shape[0], x.shape[1])
    pairs = x.reshape(rows, heads_here, HEAD_DIM // 2, 2)
    first = pairs[..., 0]
    second = pairs[..., 1]
    cosine = cosine[:, None, :]
    sine = sine[:, None, :]
    rotated = jnp.stack([first * cosine - second * sine, first * sine + second * cosine], axis=-1)
    return rotated.reshape(rows, heads_here, HEAD_DIM)


def attend_piece(carry, keys_vals, query, keep):
    num, den = carry
    rows = keys_vals.shape[0]
    heads_local = query.shape[1]
    piece_k = keys_vals[:, 0].reshape(rows, heads_local, HEAD_DIM)
    piece_v = keys_vals[:, 1].reshape(rows, heads_local, HEAD_DIM)
    scores = jnp.einsum("qhd,khd->hqk", query, piece_k, preferred_element_type=jnp.float32) * (
        1.0 / HEAD_DIM**0.5
    )
    weights = jnp.exp(scores)
    if keep is not None:
        weights = jnp.where(keep[None], weights, 0.0)
    den = den + jnp.sum(weights, axis=-1)
    num = num + jnp.einsum(
        "hqk,khd->hqd", weights.astype(jnp.bfloat16), piece_v, preferred_element_type=jnp.float32
    )
    return (num, den)


def token_body(image, text_kv, modulation, w_qkv, w_out, q_gain, k_gain, region_mask):
    img_rows = image.shape[1]
    width_local = w_qkv.shape[2]
    heads_local = width_local // HEAD_DIM
    tokens = image[0].astype(jnp.float32)
    mods = modulation[0]
    normed = layer_norm(tokens, mods)
    qkv = jnp.einsum(
        "td,dcf->tcf",
        normed,
        lax.all_gather(w_qkv, "seq", axis=0, tiled=True),
        preferred_element_type=jnp.float32,
    )
    section_index = lax.axis_index("section")
    time_index = (section_index == 0).astype(jnp.float32)
    rows_index = lax.axis_index("seq") * img_rows + jnp.arange(img_rows, dtype=jnp.int32)
    cosine, sine = rope_tables(rows_index, time_index)
    query = apply_rope(
        rms_rows(qkv[:, 0].reshape(img_rows, heads_local, HEAD_DIM), q_gain), cosine, sine
    ).astype(jnp.bfloat16)
    keys = apply_rope(
        rms_rows(qkv[:, 1].reshape(img_rows, heads_local, HEAD_DIM), k_gain), cosine, sine
    ).astype(jnp.bfloat16)
    values = qkv[:, 2].astype(jnp.bfloat16)
    image_kv = jnp.stack([keys.reshape(img_rows, width_local), values], axis=1)
    own_kv = jnp.concatenate([image_kv, text_kv[0]], axis=0)
    enabled = (section_index == 1).astype(jnp.int32)
    local_mask = region_mask * enabled
    init = (
        jnp.zeros((heads_local, img_rows, HEAD_DIM), jnp.float32),
        jnp.zeros((heads_local, img_rows), jnp.float32),
    )
    carry = attend_piece(init, lax.all_gather(own_kv, "seq", axis=0, tiled=True), query, None)
    cond_local = lax.ppermute(image_kv, "section", [(0, 1)])
    keep = jnp.repeat(jnp.repeat(local_mask, TILE, axis=0), TILE, axis=1) > 0
    carry = attend_piece(carry, lax.all_gather(cond_local, "seq", axis=0, tiled=True), query, keep)
    num, den = carry
    attn = (num / den[..., None]).astype(jnp.bfloat16)
    attn = jnp.transpose(attn, (1, 0, 2)).reshape(img_rows, width_local)
    term = jnp.dot(attn, w_out, preferred_element_type=jnp.float32)
    branch = lax.psum_scatter(
        term.astype(jnp.bfloat16), "tp", scatter_dimension=1, tiled=True
    ).astype(jnp.float32)
    cols = branch.shape[1]
    offset = lax.axis_index("tp") * cols
    residual = lax.dynamic_slice_in_dim(tokens, offset, cols, 1)
    gate = lax.dynamic_slice_in_dim(mods[2], offset, cols, 0)
    out = residual + gate[None, :] * branch
    return out.astype(jnp.bfloat16)[None]


def body(*arrays):
    image, w_qkv, region_mask = arrays[0], arrays[3], arrays[7]
    seq = lax.axis_size("seq")
    one_head_each = (
        w_qkv.shape[2] // HEAD_DIM == seq == 8
        and lax.axis_size("section") == 2
        and lax.axis_size("tp") == 2
        and w_qkv.shape[0] % 128 == 0
        and image.shape[1] == TILE == 2 * GRID_W
        and region_mask.shape == (1, seq)
        and arrays[1].shape[1] % 16 == 0
        and arrays[4].shape[1] % 1024 == 0
    )
    return (head_body if one_head_each else token_body)(*arrays)


def solution(mesh):
    return jax.shard_map(
        body,
        mesh=mesh,
        in_specs=(
            P("section", "seq", None),
            P("section", "seq", None, "tp"),
            P("section", None, None),
            P("seq", None, "tp"),
            P("tp", None),
            P(),
            P(),
            P("seq", None),
        ),
        out_specs=P("section", "seq", "tp"),
        check_vma=False,
    )
```
